32 devices in a mesh: group: 2 (over x), dp: 16 (over z, y, core).
Axes of the slice: x: 2, y: 2, z: 4, core: 2. Of those that a mesh axis runs over, the one named last changes fastest.
Arguments:
- queries: bfloat16 [256, 4096], P(('group', 'dp')), parts along dimension 0, may hold values from -80 to 80
- new_keys: bfloat16 [256, 1024], P(('group', 'dp')), parts along dimension 0, may hold values from -6 to 6
- new_values: bfloat16 [256, 1024], P(('group', 'dp')), parts along dimension 0, may hold values from -6 to 6
- cache_keys: bfloat16 [256, 32, 1024], P(('group', 'dp')), parts along dimension 0, may hold values from -4 to 4
- cache_values: bfloat16 [256, 32, 1024], P(('group', 'dp')), parts along dimension 0, may hold values from -6 to 6
- lengths: int32 [256], P(('group', 'dp')), parts along dimension 0, may hold values from 2 to 32, as said below
- residual: bfloat16 [256, 4096], P(('group', 'dp')), parts along dimension 0, may hold values from -6 to 6
- norm_gain: bfloat16 [4096], replicated, may hold values from 0.099609375 to 1.8984375
- router_weight: bfloat16 [4096, 4], replicated, may hold values from -0.09375 to 0.09375
- gate_weight: bfloat16 [4096, 28672], P(None, 'dp'), may hold values from -0.09375 to 0.09375
- up_weight: bfloat16 [4096, 28672], P(None, 'dp'), may hold values from -0.09375 to 0.09375
- down_weight: bfloat16 [28672, 4096], P('dp'), may hold values from -0.0625 to 0.0625
- routes: int32 [256, 2], P('group'), parts along dimension 0, may hold values from 0 to 3, all different within a row; in each aligned block of 8 rows (0 to 7, 8 to 15, ...) at most 6 rows name the same one
Outputs:
- attended: bfloat16 [256, 4096], P(('group', 'dp')), parts along dimension 0
- expert_out: bfloat16 [256, 4096], P(('group', 'dp')), parts along dimension 0
The draws below stay inside these ranges and needn't reach their ends.
There are 2 independent parts, one for each index of `group`. The reference program is written for one: setup_inputs(seed, part) draws one part's arguments, and reference() takes and returns one part's arrays. A program takes and returns all parts, laid end to end along the dimension named above; an argument that names none is the same for every part. Nothing has to cross between parts.
Inputs may be any that keep to these rules, and one draw needn't show every extreme that they name: `routes`: each row names two different experts; among the rows of one device no expert is named by more than 6 rows, and some expert reaches 6. `lengths`: some row has exactly 32 valid positions.
All inputs are finite; a program needn't handle non-finite values.
Results may differ from the reference program's by a relative error of at most 0.0095.
Values may be sent and summed in bfloat16 or wider, within the bound.
No kernel may reach another device: no remote copies, remote signals or barrier semaphores. Data moves between devices by JAX's collectives and lax.ppermute only.
A program may use at most 128 MiB of HBM per device.

```python
import math
import jax
import jax.numpy as jnp
import numpy as np
from jax import lax

D = 4096
HEADS = 32
KV_HEADS = 8
HEAD_DIM = 128
EXPERTS = 4
FF = 7168
ROWS_DEV = 8
CACHE_LEN = 32
MOST = 6
ROWS = 128


def shared_keys(key):
    return jnp.clip(jax.random.normal(key, (ROWS, CACHE_LEN, KV_HEADS * HEAD_DIM), jnp.float32), -4.0, 4.0)


def draw_cache_keys(key, part):
    base = shared_keys(key)
    return base.astype(jnp.bfloat16)


def draw_queries(key, part):
    key = jax.random.fold_in(key, 1)
    first_key = jax.random.fold_in(key, 0)
    values = jnp.clip(jax.random.normal(first_key, (ROWS, D), jnp.float32), -6.0, 6.0)
    return values.astype(jnp.bfloat16)


def draw_lengths(key, part):
    key = jax.random.fold_in(key, 3)
    found = jax.random.randint(key, (ROWS,), 2, CACHE_LEN + 1, jnp.int32)
    return found.at[0].set(CACHE_LEN)


def levels(stream_key, extent, shards, smallest, high):
    def one(position, blocks):
        heights = jax.random.uniform(jax.random.fold_in(jax.random.fold_in(stream_key, 6), position), (blocks,), jnp.float32, smallest / len(shards), high / len(shards))
        return jnp.repeat(jnp.exp(heights), extent[position] // blocks).reshape((-1,) + (1,) * (len(extent) - position - 1))

    gain = one(*shards[0])
    for cut in shards[1:]:
        gain = gain * one(*cut)
    return gain


def assign_block(key, own, number, rows, count, top, bound, skew):
    order = jax.random.permutation(key, count)
    crowded, usual = load_shares(count, rows * top, bound, skew, True), load_shares(count, rows * top, bound, skew, False)
    places = jnp.arange(count)

    def named(sizes, rotation):
        used = int((sizes > 0).sum())
        fixed = max(1, used // 4)
        moved = fixed + (places - fixed + rotation * (used - fixed)) % max(1, count - fixed)
        return jnp.zeros((count,), jnp.int32).at[order[jnp.where(places < fixed, places, moved)]].set(jnp.asarray(sizes, jnp.int32))

    sizes = jnp.where(number % 4 == 0, named(crowded, number // 4), named(usual, number - number // 4 - 1))
    mixed = jax.random.permutation(jax.random.fold_in(own, 3), count)
    giver, receiver = mixed[0:count // 2 * 2:2], mixed[1:count // 2 * 2:2]
    margin = jnp.minimum(sizes[giver] - 1, bound - sizes[receiver]) // 2
    margin = jnp.where((giver == order[0]) | (receiver == order[0]) | (sizes[receiver] == 0), 0, jnp.maximum(margin, 0))
    moved = jax.random.randint(jax.random.fold_in(own, 4), (count // 2,), 0, 1 << 20) % (margin + 1)
    sizes = sizes.at[giver].add(-moved).at[receiver].add(moved)
    members = jnp.searchsorted(jnp.cumsum(sizes), jnp.arange(rows * top), side="right").astype(jnp.int32)
    listing = members.reshape(top, rows).T
    listing = listing[jax.random.permutation(jax.random.fold_in(own, 1), rows)]
    rotation = jax.random.randint(jax.random.fold_in(own, 2), (rows, 1), 0, top)
    return jnp.take_along_axis(listing, (jnp.arange(top)[None, :] + rotation) % top, axis=1)


def load_shares(number_of, total, limit, slope, full):
    loads = [(1 << 20) // math.isqrt(rank ** slope) + 1 for rank in range(1, number_of + 1)]
    largest = limit if full else min(limit, max(-(-total // number_of), total * loads[0] // sum(loads)))
    least = 1 if total - largest >= number_of - 1 else 0
    given, spare = [largest] + [least] * (number_of - 1), total - largest - least * (number_of - 1)
    while spare > 0:
        candidates = [i for i in range(1, number_of) if given[i] < largest] or [i for i in range(1, number_of) if given[i] < limit]
        pool, budget = sum([loads[i] for i in candidates]), spare
        for i in candidates:
            addition = min(limit - given[i], max(1, budget * loads[i] // pool), spare)
            given[i] = given[i] + addition
            spare = spare - addition
    return np.array(given)


def normal_values(key, shape, scale, reach, cuts=(), kind=jnp.bfloat16):
    entries = scale * jax.random.normal(key, shape, jnp.float32)
    if cuts:
        entries = entries * levels(key, shape, cuts, -0.22, 0.18)
    return jnp.clip(entries, -reach, reach).astype(kind)


def setup_inputs(seed: int = 0, part: int = 0) -> dict:
    keys = jax.random.split(jax.random.key(seed), 14)
    part_keys = jax.random.split(jax.random.fold_in(keys[13], part), 14)
    queries = draw_queries(jax.random.fold_in(jax.random.fold_in(keys[13], part), 71), part)
    new_keys = normal_values(part_keys[1], (ROWS, KV_HEADS * HEAD_DIM), 1.0, 6.0, ((0, 16),))
    new_values = normal_values(part_keys[2], (ROWS, KV_HEADS * HEAD_DIM), 1.0, 6.0, ((0, 16),))
    cache_keys = draw_cache_keys(jax.random.fold_in(jax.random.fold_in(keys[13], part), 71), part)
    cache_values = normal_values(part_keys[4], (ROWS, CACHE_LEN, KV_HEADS * HEAD_DIM), 1.0, 6.0, ((0, 16),))
    lengths = draw_lengths(jax.random.fold_in(jax.random.fold_in(keys[13], part), 71), part)
    residual = normal_values(part_keys[6], (ROWS, D), 1.0, 6.0, ((0, 16),))
    norm_gain = jnp.clip(1.0 + 0.18 * jax.random.normal(keys[7], (D,), jnp.float32), 0.099609375, 1.8984375).astype(jnp.bfloat16)
    router_weight = normal_values(keys[8], (D, EXPERTS), D ** -0.5, 0.09375)
    gate_weight = normal_values(keys[9], (D, EXPERTS * FF), D ** -0.5, 0.09375, ((1, 16),))
    up_weight = normal_values(keys[10], (D, EXPERTS * FF), D ** -0.5, 0.09375, ((1, 16),))
    down_weight = normal_values(keys[11], (EXPERTS * FF, D), FF ** -0.5, 0.0625, ((0, 16),))
    routes_keys = jax.random.split(jax.random.fold_in(part_keys[12], 1), ROWS // ROWS_DEV)
    routes_turns = jax.random.permutation(jax.random.fold_in(part_keys[12], 3), ROWS // ROWS_DEV)
    routes = jax.vmap(lambda own, number: assign_block(jax.random.fold_in(part_keys[12], 2), own, number, ROWS_DEV, EXPERTS, 2, MOST, 2))(routes_keys, routes_turns).reshape((ROWS, 2))
    return {"queries": queries, "new_keys": new_keys, "new_values": new_values, "cache_keys": cache_keys, "cache_values": cache_values, "lengths": lengths, "residual": residual, "norm_gain": norm_gain, "router_weight": router_weight, "gate_weight": gate_weight, "up_weight": up_weight, "down_weight": down_weight, "routes": routes}


def attend(queries, new_keys, new_values, cache_keys, cache_values, lengths, residual, norm_gain):
    row_count = queries.shape[0]
    positions = cache_keys.shape[1]
    groups = HEADS // KV_HEADS
    score_scale = 1.0 / HEAD_DIM ** 0.5
    query_f = queries.astype(jnp.float32).reshape(row_count, KV_HEADS, groups, HEAD_DIM)
    keys_f = cache_keys.astype(jnp.float32).reshape(row_count, positions, KV_HEADS, HEAD_DIM)
    values_f = cache_values.astype(jnp.float32).reshape(row_count, positions, KV_HEADS, HEAD_DIM)
    newk_f = new_keys.astype(jnp.float32).reshape(row_count, KV_HEADS, HEAD_DIM)
    newv_f = new_values.astype(jnp.float32).reshape(row_count, KV_HEADS, HEAD_DIM)
    scores = jnp.einsum('rgjd,rtgd->rgjt', query_f, keys_f) * score_scale
    in_cache = (jnp.arange(positions)[None, :] < lengths[:, None])[:, None, None, :]
    scores = jnp.where(in_cache, scores, -jnp.inf)
    new_score = jnp.einsum('rgjd,rgd->rgj', query_f, newk_f) * score_scale
    peak = jnp.maximum(lax.optimization_barrier(jnp.max(scores, axis=-1)), new_score)
    weights = jnp.exp(scores - peak[..., None])
    new_weight = jnp.exp(new_score - peak)
    total = lax.optimization_barrier(jnp.sum(weights, axis=-1)) + new_weight
    probs = (weights / total[..., None]).astype(jnp.bfloat16)
    new_prob = (new_weight / total).astype(jnp.bfloat16)
    mixed = jnp.einsum('rgjt,rtgd->rgjd', probs.astype(jnp.float32), values_f)
    mixed = mixed + new_prob.astype(jnp.float32)[..., None] * newv_f[:, :, None, :]
    attended = (residual.astype(jnp.float32) + mixed.reshape(row_count, D)).astype(jnp.bfloat16)
    states = attended.astype(jnp.float32)
    normed = states * lax.rsqrt(lax.optimization_barrier(jnp.mean(states * states, axis=-1, keepdims=True)) + 1e-05)
    normed = (normed * norm_gain.astype(jnp.float32)).astype(jnp.bfloat16)
    return (attended, normed)

def reference(queries, new_keys, new_values, cache_keys, cache_values, lengths, residual, norm_gain, router_weight, gate_weight, up_weight, down_weight, routes):
    attended, normed = attend(queries, new_keys, new_values, cache_keys, cache_values, lengths, residual, norm_gain)
    logits = jnp.dot(normed, router_weight, preferred_element_type=jnp.float32)
    expert_ids = jnp.arange(EXPERTS, dtype=jnp.int32)
    first_hot = routes[:, 0:1] == expert_ids[None, :]
    second_hot = routes[:, 1:2] == expert_ids[None, :]
    first_logit = lax.optimization_barrier(jnp.sum(jnp.where(first_hot, logits, 0.0), axis=1))
    second_logit = lax.optimization_barrier(jnp.sum(jnp.where(second_hot, logits, 0.0), axis=1))
    first_share = jax.nn.sigmoid(first_logit - second_logit)
    second_share = jax.nn.sigmoid(second_logit - first_logit)
    share = jnp.where(first_hot, first_share[:, None], 0.0) + jnp.where(second_hot, second_share[:, None], 0.0)

    def one_expert(expert, total):
        first_col = (expert * FF).astype(jnp.int32)
        gate_part = lax.dynamic_slice_in_dim(gate_weight, first_col, FF, 1)
        up_part = lax.dynamic_slice_in_dim(up_weight, first_col, FF, 1)
        down_part = lax.dynamic_slice_in_dim(down_weight, first_col, FF, 0)
        gate = jnp.dot(normed, gate_part, preferred_element_type=jnp.float32)
        upper = jnp.dot(normed, up_part, preferred_element_type=jnp.float32)
        hidden = (jax.nn.silu(gate) * upper).astype(jnp.bfloat16)
        result = jnp.dot(hidden, down_part, preferred_element_type=jnp.float32)
        column = lax.dynamic_slice_in_dim(share, expert.astype(jnp.int32), 1, 1)
        return total + column * result
    summed = lax.fori_loop(0, EXPERTS, one_expert, jnp.zeros((normed.shape[0], D), jnp.float32))
    return (attended, summed.astype(jnp.bfloat16))
```

```python
import jax
import jax.numpy as jnp
from jax import lax
from jax.sharding import PartitionSpec as P

D = 4096
HEADS = 32
KV_HEADS = 8
HEAD_DIM = 128
EXPERTS = 4
FF = 7168


def attend(queries, new_keys, new_values, cache_keys, cache_values, lengths, residual, norm_gain):
    row_count = queries.shape[0]
    positions = cache_keys.shape[1]
    groups = HEADS // KV_HEADS
    score_scale = 1.0 / HEAD_DIM**0.5
    query_b = queries.reshape(row_count, KV_HEADS, groups, HEAD_DIM)
    keys_b = cache_keys.reshape(row_count, positions, KV_HEADS, HEAD_DIM)
    values_b = cache_values.reshape(row_count, positions, KV_HEADS, HEAD_DIM)
    newk_b = new_keys.reshape(row_count, KV_HEADS, HEAD_DIM)
    newv_f = new_values.astype(jnp.float32).reshape(row_count, KV_HEADS, HEAD_DIM)
    scores = (
        jnp.einsum("rgjd,rtgd->rgjt", query_b, keys_b, preferred_element_type=jnp.float32)
        * score_scale
    )
    in_cache = (jnp.arange(positions)[None, :] < lengths[:, None])[:, None, None, :]
    scores = jnp.where(in_cache, scores, -jnp.inf)
    new_score = (
        jnp.einsum("rgjd,rgd->rgj", query_b, newk_b, preferred_element_type=jnp.float32)
        * score_scale
    )
    peak = jnp.maximum(jnp.max(scores, axis=-1), new_score)
    weights = jnp.exp(scores - peak[..., None])
    new_weight = jnp.exp(new_score - peak)
    total = jnp.sum(weights, axis=-1) + new_weight
    probs = (weights / total[..., None]).astype(jnp.bfloat16)
    new_prob = (new_weight / total).astype(jnp.bfloat16)
    mixed = jnp.einsum("rgjt,rtgd->rgjd", probs, values_b, preferred_element_type=jnp.float32)
    mixed = mixed + new_prob.astype(jnp.float32)[..., None] * newv_f[:, :, None, :]
    attended = (residual.astype(jnp.float32) + mixed.reshape(row_count, D)).astype(jnp.bfloat16)
    states = attended.astype(jnp.float32)
    normed = states * lax.rsqrt(jnp.mean(states * states, axis=-1, keepdims=True) + 1e-05)
    normed = (normed * norm_gain.astype(jnp.float32)).astype(jnp.bfloat16)
    return (attended, normed)


def expert_rows(inputs, gate_weight, up_weight, down_weight):
    gate = jnp.dot(inputs, gate_weight, preferred_element_type=jnp.float32)
    upper = jnp.dot(inputs, up_weight, preferred_element_type=jnp.float32)
    hidden = (jax.nn.silu(gate) * upper).astype(jnp.bfloat16)
    return jnp.dot(hidden, down_weight, preferred_element_type=jnp.float32)


def row_shares(normed, router_weight, routes):
    logits = jnp.dot(normed, router_weight, preferred_element_type=jnp.float32)
    expert_ids = jnp.arange(EXPERTS, dtype=jnp.int32)
    first_hot = routes[:, 0:1] == expert_ids[None, :]
    second_hot = routes[:, 1:2] == expert_ids[None, :]
    first_logit = jnp.sum(jnp.where(first_hot, logits, 0.0), axis=1)
    second_logit = jnp.sum(jnp.where(second_hot, logits, 0.0), axis=1)
    first_share = jax.nn.sigmoid(first_logit - second_logit)
    second_share = jax.nn.sigmoid(second_logit - first_logit)
    return jnp.where(first_hot, first_share[:, None], 0.0) + jnp.where(
        second_hot, second_share[:, None], 0.0
    )


def plane_shift(value, count, offset):
    plane = count // EXPERTS
    return lax.ppermute(
        value, "dp", [(i, (i + offset * plane) % count) for i in range(count)]
    )


def swap(value, count, bit):
    return lax.ppermute(value, "dp", [(i, i ^ bit) for i in range(count)])


def body(
    queries,
    new_keys,
    new_values,
    cache_keys,
    cache_values,
    lengths,
    residual,
    norm_gain,
    router_weight,
    gate_weight,
    up_weight,
    down_weight,
    routes,
):
    rows = queries.shape[0]
    count = lax.axis_size("dp")
    index = lax.axis_index("dp")
    plane = count // EXPERTS
    bits = [1 << k for k in reversed(range(plane.bit_length() - 1))]
    attended, normed = attend(
        queries, new_keys, new_values, cache_keys, cache_values, lengths, residual, norm_gain
    )
    own_routes = lax.dynamic_slice_in_dim(routes, index * rows, rows, 0)
    share = row_shares(normed, router_weight, own_routes)

    gathered = jnp.concatenate(
        [normed] + [plane_shift(normed, count, k) for k in range(1, EXPERTS)], axis=0
    )
    for bit in bits:
        gathered = jnp.concatenate([gathered, swap(gathered, count, bit)], axis=0)

    terms = expert_rows(gathered, gate_weight, up_weight, down_weight)
    for bit in reversed(bits):
        half = terms.shape[0] // 2
        other = swap(terms[half:].astype(jnp.bfloat16), count, bit)
        terms = terms[:half] + other.astype(jnp.float32)
    terms = terms.astype(jnp.bfloat16).reshape(EXPERTS, rows, D)

    expert = index // plane
    total = jnp.zeros((rows, D), jnp.float32)
    for k in range(EXPERTS):
        result = terms[k] if k == 0 else plane_shift(terms[k], count, -k)
        column = lax.dynamic_slice_in_dim(share, (expert + k) % EXPERTS, 1, 1)
        total = total + column * result.astype(jnp.float32)
    return (attended, total.astype(jnp.bfloat16))


def solution(mesh):
    placed = (
        P(("group", "dp"), None),
        P(("group", "dp"), None),
        P(("group", "dp"), None),
        P(("group", "dp"), None, None),
        P(("group", "dp"), None, None),
        P(("group", "dp")),
        P(("group", "dp"), None),
        P(),
        P(),
        P(None, "dp"),
        P(None, "dp"),
        P("dp", None),
        P("group", None),
    )
    return jax.shard_map(
        body,
        mesh=mesh,
        in_specs=placed,
        out_specs=(P(("group", "dp"), None), P(("group", "dp"), None)),
        check_vma=False,
    )
```

```python
import functools

import jax
import jax.numpy as jnp
from jax import lax
from jax.experimental import pallas as pl
from jax.experimental.pallas import tpu as pltpu
from jax.sharding import PartitionSpec as P

HEADS = 32
KV_HEADS = 8
HEAD_DIM = 128
EXPERTS = 4
MIB = 1 << 20
F32 = jnp.float32
BF16 = jnp.bfloat16
VMEM = pl.BlockSpec(memory_space=pltpu.VMEM)
ANY = pl.BlockSpec(memory_space=pl.ANY)


def dot(a, b, contract_last=False):
    dims = (((1,), (1 if contract_last else 0,)), ((), ()))
    return lax.dot_general(a, b, dims, preferred_element_type=F32)


def attend_kernel(plane, *refs):
    sources, (attended, normed, share), held, semaphores = (
        refs[:10], refs[10:13], refs[13:23], refs[23]
    )
    copies = [
        pltpu.make_async_copy(source, target, semaphores.at[i])
        for i, (source, target) in enumerate(zip(sources, held))
    ]
    for copy in copies:
        copy.start()
    (queries, cache_keys, new_keys, lengths, cache_values, new_values, residual, gain, router,
     routes) = held
    for copy in copies:
        copy.wait()
    rows, width = queries.shape
    positions = cache_keys.shape[1]
    groups = HEADS // KV_HEADS
    scale = 1.0 / HEAD_DIM**0.5
    every = rows * positions
    block = groups * rows

    query = queries[...].astype(F32)
    stacked = jnp.concatenate(
        [query[:, h * HEAD_DIM : (h + 1) * HEAD_DIM] for h in range(HEADS)], axis=0
    )
    stacked_b = stacked.astype(BF16)
    keys = cache_keys[...].reshape(every, KV_HEADS * HEAD_DIM)
    values = cache_values[...].reshape(every, KV_HEADS * HEAD_DIM)
    newk = new_keys[...].astype(F32)
    newv = new_values[...].astype(F32)

    row_of = lax.broadcasted_iota(jnp.int32, (block, every), 0) % rows
    column = lax.broadcasted_iota(jnp.int32, (block, every), 1)
    position = column % positions
    column_row = column // positions
    limit = jnp.zeros((block, every), jnp.int32)
    for r in range(rows):
        limit = jnp.where(column_row == r, lengths[r], limit)
    valid = (row_of == column_row) & (position < limit)

    pieces = []
    for g in range(KV_HEADS):
        lanes = slice(g * HEAD_DIM, (g + 1) * HEAD_DIM)
        mine = slice(g * block, (g + 1) * block)
        scores = dot(stacked_b[mine], keys[:, lanes], contract_last=True) * scale
        scores = jnp.where(valid, scores, -jnp.inf)
        own_key = jnp.concatenate([newk[:, lanes]] * groups, axis=0)
        new_score = jnp.sum(stacked[mine] * own_key, axis=1, keepdims=True) * scale
        peak = jnp.maximum(jnp.max(scores, axis=1, keepdims=True), new_score)
        weights = jnp.exp(scores - peak)
        new_weight = jnp.exp(new_score - peak)
        total = jnp.sum(weights, axis=1, keepdims=True) + new_weight
        probs = (weights / total).astype(BF16)
        new_prob = (new_weight / total).astype(BF16).astype(F32)
        own_value = jnp.concatenate([newv[:, lanes]] * groups, axis=0)
        mixed = dot(probs, values[:, lanes]) + new_prob * own_value
        pieces += [mixed[j * rows : (j + 1) * rows] for j in range(groups)]

    states = (residual[...].astype(F32) + jnp.concatenate(pieces, axis=1)).astype(BF16)
    attended[...] = states
    states = states.astype(F32)
    norm = lax.rsqrt(jnp.mean(states * states, axis=1, keepdims=True) + 1e-05)
    gains = gain[...].astype(F32)
    logits = [jnp.zeros((rows, 128), F32) for _ in range(EXPERTS)]
    for c in range(width // 128):
        lanes = slice(c * 128, (c + 1) * 128)
        part = (states[:, lanes] * norm * gains[c : c + 1]).astype(BF16)
        normed[:, lanes] = part
        part = part.astype(F32)
        for e in range(EXPERTS):
            logits[e] += part * router[e : e + 1, lanes].astype(F32)
    logits = [jnp.sum(value, axis=1, keepdims=True) for value in logits]

    index = lax.axis_index("dp")
    base = index * rows
    row = lax.broadcasted_iota(jnp.int32, (rows, 1), 0)
    first = jnp.zeros((rows, 1), jnp.int32)
    second = jnp.zeros((rows, 1), jnp.int32)
    for r in range(rows):
        first = jnp.where(row == r, routes[0, base + r], first)
        second = jnp.where(row == r, routes[1, base + r], second)
    first_logit = jnp.zeros((rows, 1), F32)
    second_logit = jnp.zeros((rows, 1), F32)
    for e in range(EXPERTS):
        first_logit = jnp.where(first == e, logits[e], first_logit)
        second_logit = jnp.where(second == e, logits[e], second_logit)
    first_share = 1.0 / (1.0 + jnp.exp(second_logit - first_logit))
    second_share = 1.0 / (1.0 + jnp.exp(first_logit - second_logit))
    lane = lax.broadcasted_iota(jnp.int32, (rows, 128), 1)
    expert = (index // plane + lane) % EXPERTS
    expert = jnp.where(lane < EXPERTS, expert, -1)
    share[...] = jnp.where(first == expert, first_share, 0.0) + jnp.where(
        second == expert, second_share, 0.0
    )


def attend(plane, queries, new_keys, new_values, cache_keys, cache_values, lengths, residual,
           norm_gain, router_weight, routes):
    rows, width = queries.shape
    operands = (
        queries,
        cache_keys,
        new_keys,
        lengths,
        cache_values,
        new_values,
        residual,
        norm_gain.reshape(-1, 128),
        router_weight.T,
        routes.T,
    )
    in_smem = (3, 9)
    return pl.pallas_call(
        functools.partial(attend_kernel, plane),
        out_shape=(
            jax.ShapeDtypeStruct((rows, width), BF16),
            jax.ShapeDtypeStruct((rows, width), BF16),
            jax.ShapeDtypeStruct((rows, 128), F32),
        ),
        in_specs=[ANY] * len(operands),
        out_specs=(VMEM, VMEM, VMEM),
        scratch_shapes=[
            (pltpu.SMEM if i in in_smem else pltpu.VMEM)(operand.shape, operand.dtype)
            for i, operand in enumerate(operands)
        ]
        + [pltpu.SemaphoreType.DMA((len(operands),))],
        compiler_params=pltpu.CompilerParams(vmem_limit_bytes=5 * MIB),
        name="attend",
    )(*[pltpu.with_memory_space_constraint(operand, pltpu.HBM) for operand in operands])


def expert_kernel(inputs, gate_weight, up_weight, down_weight, keep, send, hidden):
    columns = gate_weight.shape[1]
    width = down_weight.shape[1]
    half = keep.shape[0]
    step = 256 if columns % 256 == 0 else columns
    x = inputs[...]
    for f in range(0, columns, step):
        gate = dot(x, gate_weight[:, f : f + step])
        upper = dot(x, up_weight[:, f : f + step])
        hidden[:, f : f + step] = (gate / (1.0 + jnp.exp(-gate)) * upper).astype(BF16)
    h = hidden[...]
    for n in range(0, width, 512):
        terms = dot(h, down_weight[:, n : n + 512])
        keep[:, n : n + 512] = terms[:half]
        send[:, n : n + 512] = terms[half:].astype(BF16)


def expert_rows(inputs, gate_weight, up_weight, down_weight):
    rows, width = inputs.shape
    columns = gate_weight.shape[1]
    half = rows // 2
    return pl.pallas_call(
        expert_kernel,
        out_shape=(
            jax.ShapeDtypeStruct((half, width), F32),
            jax.ShapeDtypeStruct((half, width), BF16),
        ),
        in_specs=[VMEM] * 4,
        out_specs=(VMEM, VMEM),
        scratch_shapes=[pltpu.VMEM((rows, columns), BF16)],
        compiler_params=pltpu.CompilerParams(vmem_limit_bytes=4 * MIB * max(1, rows // 128)),
        cost_estimate=pl.CostEstimate(
            flops=6 * rows * width * columns, bytes_accessed=0, transcendentals=rows * columns
        ),
        name="experts",
    )(inputs, gate_weight, up_weight, down_weight)


def load_kernel(source, after, target, token, semaphore):
    copy = pltpu.make_async_copy(source, target, semaphore)
    copy.start()
    token[...] = jnp.zeros(token.shape, token.dtype)
    copy.wait()


def load(source, after):
    return pl.pallas_call(
        load_kernel,
        out_shape=(
            pltpu.VMEM(source.shape, source.dtype),
            jax.ShapeDtypeStruct((8, 128), F32),
        ),
        in_specs=[ANY, ANY],
        out_specs=(VMEM, VMEM),
        scratch_shapes=[pltpu.SemaphoreType.DMA],
        compiler_params=pltpu.CompilerParams(vmem_limit_bytes=MIB),
        cost_estimate=pl.CostEstimate(
            flops=0, bytes_accessed=2 * source.size, transcendentals=0
        ),
        name="load",
    )(pltpu.with_memory_space_constraint(source, pltpu.HBM), after)


def join_kernel(*refs):
    out, row = refs[-1], 0
    for piece in refs[1:-1]:
        out[row : row + piece.shape[0]] = piece[...]
        row += piece.shape[0]


def join(after, *pieces):
    rows = sum(piece.shape[0] for piece in pieces)
    return pl.pallas_call(
        join_kernel,
        out_shape=jax.ShapeDtypeStruct((rows, pieces[0].shape[1]), BF16),
        in_specs=[ANY] + [VMEM] * len(pieces),
        out_specs=VMEM,
        compiler_params=pltpu.CompilerParams(vmem_limit_bytes=1 * MIB),
        name="join",
    )(after, *pieces)


def fold_kernel(held, arrived, keep, send):
    half = keep.shape[0]
    keep[...] = held[:half] + arrived[:half].astype(F32)
    send[...] = (held[half:] + arrived[half:].astype(F32)).astype(BF16)


def fold(held, arrived):
    half, width = held.shape[0] // 2, held.shape[1]
    return pl.pallas_call(
        fold_kernel,
        out_shape=(
            jax.ShapeDtypeStruct((half, width), F32),
            jax.ShapeDtypeStruct((half, width), BF16),
        ),
        in_specs=[VMEM] * 2,
        out_specs=(VMEM, VMEM),
        compiler_params=pltpu.CompilerParams(vmem_limit_bytes=4 * MIB * max(1, half // 32)),
        name="fold",
    )(held, arrived)


def last_fold_kernel(held, arrived, *outs):
    rows = outs[0].shape[0]
    for k, out in enumerate(outs):
        block = slice(k * rows, (k + 1) * rows)
        out[...] = (held[block] + arrived[block].astype(F32)).astype(BF16)


def last_fold(held, arrived):
    rows, width = held.shape[0] // EXPERTS, held.shape[1]
    return pl.pallas_call(
        last_fold_kernel,
        out_shape=(jax.ShapeDtypeStruct((rows, width), BF16),) * EXPERTS,
        in_specs=[VMEM] * 2,
        out_specs=(VMEM,) * EXPERTS,
        compiler_params=pltpu.CompilerParams(vmem_limit_bytes=4 * MIB),
        name="last_fold",
    )(held, arrived)


def combine_kernel(share, *refs):
    results, out = refs[:-1], refs[-1]
    total = jnp.zeros(out.shape, F32)
    for k, result in enumerate(results):
        total = total + share[:, k : k + 1] * result[...].astype(F32)
    out[...] = total.astype(BF16)


def combine(share, results):
    return pl.pallas_call(
        combine_kernel,
        out_shape=jax.ShapeDtypeStruct(results[0].shape, BF16),
        in_specs=[VMEM] * (1 + EXPERTS),
        out_specs=VMEM,
        compiler_params=pltpu.CompilerParams(vmem_limit_bytes=4 * MIB),
        name="combine",
    )(share, *results)


def plane_shift(value, count, offset):
    plane = count // EXPERTS
    return lax.ppermute(
        value, "dp", [(i, (i + offset * plane) % count) for i in range(count)]
    )


def swap(value, count, bit):
    return lax.ppermute(value, "dp", [(i, i ^ bit) for i in range(count)])


def body(
    queries,
    new_keys,
    new_values,
    cache_keys,
    cache_values,
    lengths,
    residual,
    norm_gain,
    router_weight,
    gate_weight,
    up_weight,
    down_weight,
    routes,
):
    count = lax.axis_size("dp")
    plane = count // EXPERTS
    bits = [1 << k for k in reversed(range(plane.bit_length() - 1))]
    attended, normed, share = attend(
        plane, queries, new_keys, new_values, cache_keys, cache_values, lengths, residual,
        norm_gain, router_weight, routes,
    )

    gate, token = load(gate_weight, normed)
    gathered = join(token, normed, *[plane_shift(normed, count, k) for k in range(1, EXPERTS)])
    up, token = load(up_weight, gathered)
    gathered = join(token, gathered, swap(gathered, count, bits[0]))
    down, token = load(down_weight, gathered)
    for bit in bits[1:]:
        gathered = join(token, gathered, swap(gathered, count, bit))

    held, send = expert_rows(gathered, gate, up, down)
    for bit in bits[:0:-1]:
        held, send = fold(held, swap(send, count, bit))
    terms = last_fold(held, swap(send, count, bits[0]))
    results = [terms[0]] + [plane_shift(terms[k], count, -k) for k in range(1, EXPERTS)]
    return (attended, combine(share, results))


def solution(mesh):
    placed = (
        P(("group", "dp"), None),
        P(("group", "dp"), None),
        P(("group", "dp"), None),
        P(("group", "dp"), None, None),
        P(("group", "dp"), None, None),
        P(("group", "dp")),
        P(("group", "dp"), None),
        P(),
        P(),
        P(None, "dp"),
        P(None, "dp"),
        P("dp", None),
        P("group", None),
    )
    return jax.shard_map(
        body,
        mesh=mesh,
        in_specs=placed,
        out_specs=(P(("group", "dp"), None), P(("group", "dp"), None)),
        check_vma=False,
    )
```

```python
import functools

import jax
import jax.numpy as jnp
from jax import lax
from jax.experimental import pallas as pl
from jax.experimental.pallas import tpu as pltpu
from jax.sharding import PartitionSpec as P

HEADS = 32
KV_HEADS = 8
HEAD_DIM = 128
EXPERTS = 4
MIB = 1 << 20
WAYS = 4
PARTS = 2
F32 = jnp.float32
BF16 = jnp.bfloat16
VMEM = pl.BlockSpec(memory_space=pltpu.VMEM)
ANY = pl.BlockSpec(memory_space=pl.ANY)


def dot(a, b, contract_last=False):
    dims = (((1,), (1 if contract_last else 0,)), ((), ()))
    return lax.dot_general(a, b, dims, preferred_element_type=F32)


def weight_copies(source, target, semaphores):
    step = source.shape[0] // WAYS
    return [
        pltpu.make_async_copy(
            source.at[pl.ds(i * step, step)], target.at[pl.ds(i * step, step)], semaphores.at[i]
        )
        for i in range(WAYS)
    ]


def attend_kernel(plane, *refs):
    sources, (attended, normed, share), held, semaphores = (
        refs[:10], refs[11:14], refs[15:25], refs[25]
    )
    weight = weight_copies(refs[10], refs[14], refs[26])
    copies = [
        pltpu.make_async_copy(source, target, semaphores.at[i])
        for i, (source, target) in enumerate(zip(sources, held))
    ]
    for copy in copies + weight:
        copy.start()
    (queries, cache_keys, new_keys, lengths, cache_values, new_values, residual, gain, router,
     routes) = held
    for copy in copies:
        copy.wait()
    rows, width = queries.shape
    positions = cache_keys.shape[1]
    groups = HEADS // KV_HEADS
    scale = 1.0 / HEAD_DIM**0.5
    every = rows * positions
    block = groups * rows

    query = queries[...].astype(F32)
    stacked = jnp.concatenate(
        [query[:, h * HEAD_DIM : (h + 1) * HEAD_DIM] for h in range(HEADS)], axis=0
    )
    stacked_b = stacked.astype(BF16)
    keys = cache_keys[...].reshape(every, KV_HEADS * HEAD_DIM)
    values = cache_values[...].reshape(every, KV_HEADS * HEAD_DIM)
    newk = new_keys[...].astype(F32)
    newv = new_values[...].astype(F32)

    row_of = lax.broadcasted_iota(jnp.int32, (block, every), 0) % rows
    column = lax.broadcasted_iota(jnp.int32, (block, every), 1)
    position = column % positions
    column_row = column // positions
    limit = jnp.zeros((block, every), jnp.int32)
    for r in range(rows):
        limit = jnp.where(column_row == r, lengths[r], limit)
    valid = (row_of == column_row) & (position < limit)

    pieces = []
    for g in range(KV_HEADS):
        lanes = slice(g * HEAD_DIM, (g + 1) * HEAD_DIM)
        mine = slice(g * block, (g + 1) * block)
        scores = dot(stacked_b[mine], keys[:, lanes], contract_last=True) * scale
        scores = jnp.where(valid, scores, -jnp.inf)
        own_key = jnp.concatenate([newk[:, lanes]] * groups, axis=0)
        new_score = jnp.sum(stacked[mine] * own_key, axis=1, keepdims=True) * scale
        peak = jnp.maximum(jnp.max(scores, axis=1, keepdims=True), new_score)
        weights = jnp.exp(scores - peak)
        new_weight = jnp.exp(new_score - peak)
        total = jnp.sum(weights, axis=1, keepdims=True) + new_weight
        probs = (weights / total).astype(BF16)
        new_prob = (new_weight / total).astype(BF16).astype(F32)
        own_value = jnp.concatenate([newv[:, lanes]] * groups, axis=0)
        mixed = dot(probs, values[:, lanes]) + new_prob * own_value
        pieces += [mixed[j * rows : (j + 1) * rows] for j in range(groups)]

    states = (residual[...].astype(F32) + jnp.concatenate(pieces, axis=1)).astype(BF16)
    attended[...] = states
    states = states.astype(F32)
    norm = lax.rsqrt(jnp.mean(states * states, axis=1, keepdims=True) + 1e-05)
    gains = gain[...].astype(F32)
    logits = [jnp.zeros((rows, 128), F32) for _ in range(EXPERTS)]
    for c in range(width // 128):
        lanes = slice(c * 128, (c + 1) * 128)
        part = (states[:, lanes] * norm * gains[c : c + 1]).astype(BF16)
        normed[:, lanes] = part
        part = part.astype(F32)
        for e in range(EXPERTS):
            logits[e] += part * router[e : e + 1, lanes].astype(F32)
    logits = [jnp.sum(value, axis=1, keepdims=True) for value in logits]

    index = lax.axis_index("dp")
    base = index * rows
    row = lax.broadcasted_iota(jnp.int32, (rows, 1), 0)
    first = jnp.zeros((rows, 1), jnp.int32)
    second = jnp.zeros((rows, 1), jnp.int32)
    for r in range(rows):
        first = jnp.where(row == r, routes[0, base + r], first)
        second = jnp.where(row == r, routes[1, base + r], second)
    first_logit = jnp.zeros((rows, 1), F32)
    second_logit = jnp.zeros((rows, 1), F32)
    for e in range(EXPERTS):
        first_logit = jnp.where(first == e, logits[e], first_logit)
        second_logit = jnp.where(second == e, logits[e], second_logit)
    first_share = 1.0 / (1.0 + jnp.exp(second_logit - first_logit))
    second_share = 1.0 / (1.0 + jnp.exp(first_logit - second_logit))
    lane = lax.broadcasted_iota(jnp.int32, (rows, 128), 1)
    expert = (index // plane + lane) % EXPERTS
    expert = jnp.where(lane < EXPERTS, expert, -1)
    share[...] = jnp.where(first == expert, first_share, 0.0) + jnp.where(
        second == expert, second_share, 0.0
    )
    for copy in weight:
        copy.wait()


def attend(plane, queries, new_keys, new_values, cache_keys, cache_values, lengths, residual,
           norm_gain, router_weight, routes, weight):
    rows, width = queries.shape
    operands = (
        queries,
        cache_keys,
        new_keys,
        lengths,
        cache_values,
        new_values,
        residual,
        norm_gain.reshape(-1, 128),
        router_weight.T,
        routes.T,
    )
    in_smem = (3, 9)
    return pl.pallas_call(
        functools.partial(attend_kernel, plane),
        out_shape=(
            jax.ShapeDtypeStruct((rows, width), BF16),
            jax.ShapeDtypeStruct((rows, width), BF16),
            jax.ShapeDtypeStruct((rows, 128), F32),
            pltpu.VMEM(weight.shape, weight.dtype),
        ),
        in_specs=[ANY] * (len(operands) + 1),
        out_specs=(VMEM,) * 4,
        scratch_shapes=[
            (pltpu.SMEM if i in in_smem else pltpu.VMEM)(operand.shape, operand.dtype)
            for i, operand in enumerate(operands)
        ]
        + [pltpu.SemaphoreType.DMA((len(operands),)), pltpu.SemaphoreType.DMA((WAYS,))],
        compiler_params=pltpu.CompilerParams(vmem_limit_bytes=5 * MIB),
        name="attend",
    )(*[pltpu.with_memory_space_constraint(x, pltpu.HBM) for x in (*operands, weight)])


def hidden_kernel(inputs, gate_weight, up_weight, hidden):
    columns = gate_weight.shape[1]
    step = 256 if columns % 256 == 0 else columns
    x = inputs[...]
    for f in range(0, columns, step):
        gate = dot(x, gate_weight[:, f : f + step])
        upper = dot(x, up_weight[:, f : f + step])
        hidden[:, f : f + step] = (gate / (1.0 + jnp.exp(-gate)) * upper).astype(BF16)


def hidden_rows(inputs, gate_weight, up_weight):
    rows, width = inputs.shape
    columns = gate_weight.shape[1]
    return pl.pallas_call(
        hidden_kernel,
        out_shape=jax.ShapeDtypeStruct((rows, columns), BF16),
        in_specs=[VMEM] * 3,
        out_specs=VMEM,
        compiler_params=pltpu.CompilerParams(vmem_limit_bytes=4 * MIB * max(1, rows // 128)),
        cost_estimate=pl.CostEstimate(
            flops=4 * rows * width * columns, bytes_accessed=0, transcendentals=rows * columns
        ),
        name="hidden",
    )(inputs, gate_weight, up_weight)


def down_kernel(first, hidden, down_weight, keep, send):
    half, width = keep.shape
    h = hidden[...]
    for n in range(0, width, 512):
        terms = dot(h, down_weight[:, first + n : first + n + 512])
        keep[:, n : n + 512] = terms[:half]
        send[:, n : n + 512] = terms[half:].astype(BF16)


def down_rows(hidden, down_weight, part):
    rows, columns = hidden.shape
    half, width = rows // 2, down_weight.shape[1] // PARTS
    return pl.pallas_call(
        functools.partial(down_kernel, part * width),
        out_shape=(
            jax.ShapeDtypeStruct((half, width), F32),
            jax.ShapeDtypeStruct((half, width), BF16),
        ),
        in_specs=[VMEM] * 2,
        out_specs=(VMEM, VMEM),
        compiler_params=pltpu.CompilerParams(vmem_limit_bytes=4 * MIB * max(1, rows // 128)),
        cost_estimate=pl.CostEstimate(
            flops=2 * rows * width * columns, bytes_accessed=0, transcendentals=0
        ),
        name="down",
    )(hidden, down_weight)


def load_kernel(source, after, target, token, semaphores):
    copies = weight_copies(source, target, semaphores)
    for copy in copies:
        copy.start()
    token[...] = jnp.zeros(token.shape, token.dtype)
    for copy in copies:
        copy.wait()


def load(source, after):
    return pl.pallas_call(
        load_kernel,
        out_shape=(
            pltpu.VMEM(source.shape, source.dtype),
            jax.ShapeDtypeStruct((8, 128), F32),
        ),
        in_specs=[ANY, ANY],
        out_specs=(VMEM, VMEM),
        scratch_shapes=[pltpu.SemaphoreType.DMA((WAYS,))],
        compiler_params=pltpu.CompilerParams(vmem_limit_bytes=MIB),
        cost_estimate=pl.CostEstimate(
            flops=0, bytes_accessed=2 * source.size, transcendentals=0
        ),
        name="load",
    )(pltpu.with_memory_space_constraint(source, pltpu.HBM), after)


def join_kernel(*refs):
    out, row = refs[-1], 0
    for piece in refs[1:-1]:
        out[row : row + piece.shape[0]] = piece[...]
        row += piece.shape[0]


def join(after, *pieces):
    rows = sum(piece.shape[0] for piece in pieces)
    return pl.pallas_call(
        join_kernel,
        out_shape=jax.ShapeDtypeStruct((rows, pieces[0].shape[1]), BF16),
        in_specs=[ANY] + [VMEM] * len(pieces),
        out_specs=VMEM,
        compiler_params=pltpu.CompilerParams(vmem_limit_bytes=1 * MIB),
        name="join",
    )(after, *pieces)


def fold_kernel(held, arrived, keep, send):
    half = keep.shape[0]
    keep[...] = held[:half] + arrived[:half].astype(F32)
    send[...] = (held[half:] + arrived[half:].astype(F32)).astype(BF16)


def fold(held, arrived):
    half, width = held.shape[0] // 2, held.shape[1]
    return pl.pallas_call(
        fold_kernel,
        out_shape=(
            jax.ShapeDtypeStruct((half, width), F32),
            jax.ShapeDtypeStruct((half, width), BF16),
        ),
        in_specs=[VMEM] * 2,
        out_specs=(VMEM, VMEM),
        compiler_params=pltpu.CompilerParams(vmem_limit_bytes=4 * MIB * max(1, half // 32)),
        name="fold",
    )(held, arrived)


def last_fold_kernel(held, arrived, *outs):
    rows = outs[0].shape[0]
    for k, out in enumerate(outs):
        block = slice(k * rows, (k + 1) * rows)
        out[...] = (held[block] + arrived[block].astype(F32)).astype(BF16)


def last_fold(held, arrived):
    rows, width = held.shape[0] // EXPERTS, held.shape[1]
    return pl.pallas_call(
        last_fold_kernel,
        out_shape=(jax.ShapeDtypeStruct((rows, width), BF16),) * EXPERTS,
        in_specs=[VMEM] * 2,
        out_specs=(VMEM,) * EXPERTS,
        compiler_params=pltpu.CompilerParams(vmem_limit_bytes=4 * MIB),
        name="last_fold",
    )(held, arrived)


def combine_kernel(share, *refs):
    results, out = refs[:-1], refs[-1]
    width = results[0].shape[1]
    for part in range(PARTS):
        total = jnp.zeros(results[0].shape, F32)
        for k in range(EXPERTS):
            total = total + share[:, k : k + 1] * results[part * EXPERTS + k][...].astype(F32)
        out[:, part * width : (part + 1) * width] = total.astype(BF16)


def combine(share, results):
    rows, width = results[0].shape
    return pl.pallas_call(
        combine_kernel,
        out_shape=jax.ShapeDtypeStruct((rows, width * PARTS), BF16),
        in_specs=[VMEM] * (1 + len(results)),
        out_specs=VMEM,
        compiler_params=pltpu.CompilerParams(vmem_limit_bytes=4 * MIB),
        name="combine",
    )(share, *results)


def plane_shift(value, count, offset):
    plane = count // EXPERTS
    return lax.ppermute(
        value, "dp", [(i, (i + offset * plane) % count) for i in range(count)]
    )


def swap(value, count, bit):
    return lax.ppermute(value, "dp", [(i, i ^ bit) for i in range(count)])


def body(
    queries,
    new_keys,
    new_values,
    cache_keys,
    cache_values,
    lengths,
    residual,
    norm_gain,
    router_weight,
    gate_weight,
    up_weight,
    down_weight,
    routes,
):
    count = lax.axis_size("dp")
    plane = count // EXPERTS
    bits = [1 << k for k in reversed(range(plane.bit_length() - 1))]
    attended, normed, share, down = attend(
        plane, queries, new_keys, new_values, cache_keys, cache_values, lengths, residual,
        norm_gain, router_weight, routes, down_weight,
    )

    gate, token = load(gate_weight, normed)
    gathered = join(token, normed, *[plane_shift(normed, count, k) for k in range(1, EXPERTS)])
    up, token = load(up_weight, gathered)
    for bit in bits:
        gathered = join(token, gathered, swap(gathered, count, bit))

    hidden = hidden_rows(gathered, gate, up)
    results = []
    for part in range(PARTS):
        held, send = down_rows(hidden, down, part)
        for bit in bits[:0:-1]:
            held, send = fold(held, swap(send, count, bit))
        terms = last_fold(held, swap(send, count, bits[0]))
        results += [terms[0]]
        results += [plane_shift(terms[k], count, -k) for k in range(1, EXPERTS)]
    return (attended, combine(share, results))


def solution(mesh):
    placed = (
        P(("group", "dp"), None),
        P(("group", "dp"), None),
        P(("group", "dp"), None),
        P(("group", "dp"), None, None),
        P(("group", "dp"), None, None),
        P(("group", "dp")),
        P(("group", "dp"), None),
        P(),
        P(),
        P(None, "dp"),
        P(None, "dp"),
        P("dp", None),
        P("group", None),
    )
    return jax.shard_map(
        body,
        mesh=mesh,
        in_specs=placed,
        out_specs=(P(("group", "dp"), None), P(("group", "dp"), None)),
        check_vma=False,
    )
```

```python
import functools

import jax
import jax.numpy as jnp
from jax import lax
from jax.experimental import pallas as pl
from jax.experimental.pallas import tpu as pltpu
from jax.sharding import PartitionSpec as P

HEADS = 32
KV_HEADS = 8
HEAD_DIM = 128
EXPERTS = 4
MIB = 1 << 20
WAYS = 4
PARTS = 2
MOST = 6
F32 = jnp.float32
BF16 = jnp.bfloat16
VMEM = pl.BlockSpec(memory_space=pltpu.VMEM)
ANY = pl.BlockSpec(memory_space=pl.ANY)


def dot(a, b, contract_last=False):
    dims = (((1,), (1 if contract_last else 0,)), ((), ()))
    return lax.dot_general(a, b, dims, preferred_element_type=F32)


def weight_copies(source, target, semaphores, first=0):
    step, columns = source.shape[0] // WAYS, target.shape[1]
    return [
        pltpu.make_async_copy(
            source.at[pl.ds(i * step, step), pl.ds(first, columns)],
            target.at[pl.ds(i * step, step)],
            semaphores.at[i],
        )
        for i in range(WAYS)
    ]


def one_hot(mask):
    return mask.astype(F32).astype(BF16)


def grid(shape):
    return [lax.broadcasted_iota(jnp.int32, shape, axis) for axis in (0, 1)]


def pack(picks, block):
    quarter = block.shape[1] // 4
    parts = [block[:, m * quarter : (m + 1) * quarter] for m in range(4)]
    return [
        (dot(picks[0], parts[m]) + dot(picks[1 + m], parts[3])).astype(BF16) for m in range(3)
    ]


def unpack(picks, block):
    quarter = block.shape[1] // 3
    parts = [block[:, m * quarter : (m + 1) * quarter] for m in range(3)]
    tail = dot(picks[1], parts[0]) + dot(picks[2], parts[1]) + dot(picks[3], parts[2])
    return [dot(picks[0], part) for part in parts] + [tail]


def attend_kernel(*refs):
    sources, (attended, packed, share, take), held, semaphores = (
        refs[:10], refs[11:15], refs[16:26], refs[26]
    )
    weight = weight_copies(refs[10], refs[15], refs[27])
    copies = [
        pltpu.make_async_copy(source, target, semaphores.at[i])
        for i, (source, target) in enumerate(zip(sources, held))
    ]
    for copy in copies + weight:
        copy.start()
    (queries, cache_keys, new_keys, lengths, cache_values, new_values, residual, gain, router,
     routes) = held
    for copy in copies:
        copy.wait()
    rows, width = queries.shape
    positions = cache_keys.shape[1]
    groups = HEADS // KV_HEADS
    scale = 1.0 / HEAD_DIM**0.5
    every = rows * positions
    block = groups * rows

    query = queries[...].astype(F32)
    stacked = jnp.concatenate(
        [query[:, h * HEAD_DIM : (h + 1) * HEAD_DIM] for h in range(HEADS)], axis=0
    )
    stacked_b = stacked.astype(BF16)
    keys = cache_keys[...].reshape(every, KV_HEADS * HEAD_DIM)
    values = cache_values[...].reshape(every, KV_HEADS * HEAD_DIM)
    newk = new_keys[...].astype(F32)
    newv = new_values[...].astype(F32)

    row_of = lax.broadcasted_iota(jnp.int32, (block, every), 0) % rows
    column = lax.broadcasted_iota(jnp.int32, (block, every), 1)
    position = column % positions
    column_row = column // positions
    limit = jnp.zeros((block, every), jnp.int32)
    for r in range(rows):
        limit = jnp.where(column_row == r, lengths[r], limit)
    valid = (row_of == column_row) & (position < limit)

    pieces = []
    for g in range(KV_HEADS):
        lanes = slice(g * HEAD_DIM, (g + 1) * HEAD_DIM)
        mine = slice(g * block, (g + 1) * block)
        scores = dot(stacked_b[mine], keys[:, lanes], contract_last=True) * scale
        scores = jnp.where(valid, scores, -jnp.inf)
        own_key = jnp.concatenate([newk[:, lanes]] * groups, axis=0)
        new_score = jnp.sum(stacked[mine] * own_key, axis=1, keepdims=True) * scale
        peak = jnp.maximum(jnp.max(scores, axis=1, keepdims=True), new_score)
        weights = jnp.exp(scores - peak)
        new_weight = jnp.exp(new_score - peak)
        total = jnp.sum(weights, axis=1, keepdims=True) + new_weight
        probs = (weights / total).astype(BF16)
        new_prob = (new_weight / total).astype(BF16).astype(F32)
        own_value = jnp.concatenate([newv[:, lanes]] * groups, axis=0)
        mixed = dot(probs, values[:, lanes]) + new_prob * own_value
        pieces += [mixed[j * rows : (j + 1) * rows] for j in range(groups)]

    states = (residual[...].astype(F32) + jnp.concatenate(pieces, axis=1)).astype(BF16)
    attended[...] = states
    states = states.astype(F32)
    norm = lax.rsqrt(jnp.mean(states * states, axis=1, keepdims=True) + 1e-05)
    gains = gain[...].astype(F32)
    logits = [jnp.zeros((rows, 128), F32) for _ in range(EXPERTS)]
    parts = []
    for c in range(width // 128):
        lanes = slice(c * 128, (c + 1) * 128)
        part = (states[:, lanes] * norm * gains[c : c + 1]).astype(BF16).astype(F32)
        parts.append(part)
        for e in range(EXPERTS):
            logits[e] += part * router[e : e + 1, lanes].astype(F32)
    logits = [jnp.sum(value, axis=1, keepdims=True) for value in logits]

    base = lax.axis_index("dp") * rows
    sub, lane = grid((2 * rows, 128))
    expert_down = jnp.zeros((2 * rows, 128), jnp.int32)
    slot_down = jnp.zeros((2 * rows, 128), jnp.int32)
    across = lax.broadcasted_iota(jnp.int32, (8, 128), 1)
    expert_across = jnp.zeros((8, 128), jnp.int32)
    slot_across = jnp.zeros((8, 128), jnp.int32)
    counts = [jnp.int32(0)] * EXPERTS
    for r in range(rows):
        names = [routes[0, base + r], routes[1, base + r]]
        for choice, name in ((r, names[0]), (rows + r, names[1])):
            slot = jnp.int32(0)
            for e in range(EXPERTS):
                slot = jnp.where(name == e, counts[e], slot)
            expert_down = jnp.where(sub == choice, name, expert_down)
            slot_down = jnp.where(sub == choice, slot, slot_down)
            expert_across = jnp.where(across == choice, name, expert_across)
            slot_across = jnp.where(across == choice, slot, slot_across)
        for e in range(EXPERTS):
            named = (names[0] == e) | (names[1] == e)
            counts[e] = counts[e] + jnp.where(named, 1, 0)

    late = jnp.where(slot_down >= 3, 1, 0)
    take[0] = one_hot(lane == expert_down * 8 + slot_down)
    for m in range(3):
        take[1 + m] = one_hot((lane == expert_down * 8 + 6 + late) & (slot_down - 3 * late == m))
    place, choice = grid((8 * EXPERTS, 128))
    expert, slot = expert_across[0:1], slot_across[0:1]
    late = jnp.where(slot >= 3, 1, 0)
    chosen = choice < 2 * rows
    picks = [one_hot((place == expert * 8 + slot) & chosen)]
    for m in range(3):
        picks.append(one_hot((place == expert * 8 + 6 + late) & (slot - 3 * late == m) & chosen))
    normed = jnp.concatenate(parts, axis=1)
    normed = jnp.concatenate([normed, normed], axis=0).astype(BF16)
    quarter = width // 4
    for m, value in enumerate(pack([pick[:, : 2 * rows] for pick in picks], normed)):
        packed[:, m * quarter : (m + 1) * quarter] = value

    chosen_logits = jnp.zeros((2 * rows, 1), F32)
    for e in range(EXPERTS):
        both = jnp.concatenate([logits[e], logits[e]], axis=0)
        chosen_logits = jnp.where(expert_down[:, :1] == e, both, chosen_logits)
    other = jnp.concatenate([chosen_logits[rows:], chosen_logits[:rows]], axis=0)
    share[...] = jnp.broadcast_to(1.0 / (1.0 + jnp.exp(other - chosen_logits)), share.shape)
    for copy in weight:
        copy.wait()


def attend(queries, new_keys, new_values, cache_keys, cache_values, lengths, residual,
           norm_gain, router_weight, routes, weight):
    rows, width = queries.shape
    operands = (
        queries,
        cache_keys,
        new_keys,
        lengths,
        cache_values,
        new_values,
        residual,
        norm_gain.reshape(-1, 128),
        router_weight.T,
        routes.T,
    )
    in_smem = (3, 9)
    return pl.pallas_call(
        attend_kernel,
        out_shape=(
            jax.ShapeDtypeStruct((rows, width), BF16),
            jax.ShapeDtypeStruct((8 * EXPERTS, width * 3 // 4), BF16),
            jax.ShapeDtypeStruct((2 * rows, 128), F32),
            jax.ShapeDtypeStruct((4, 2 * rows, 128), BF16),
            pltpu.VMEM((weight.shape[0], weight.shape[1] // PARTS), weight.dtype),
        ),
        in_specs=[ANY] * (len(operands) + 1),
        out_specs=(VMEM,) * 5,
        scratch_shapes=[
            (pltpu.SMEM if i in in_smem else pltpu.VMEM)(operand.shape, operand.dtype)
            for i, operand in enumerate(operands)
        ]
        + [pltpu.SemaphoreType.DMA((len(operands),)), pltpu.SemaphoreType.DMA((WAYS,))],
        compiler_params=pltpu.CompilerParams(vmem_limit_bytes=5 * MIB),
        name="attend",
    )(*[pltpu.with_memory_space_constraint(x, pltpu.HBM) for x in (*operands, weight)])


def hidden_kernel(inputs, gate_weight, up_weight, hidden):
    columns = gate_weight.shape[1]
    step = 256 if columns % 256 == 0 else columns
    x = inputs[...]
    for f in range(0, columns, step):
        gate = dot(x, gate_weight[:, f : f + step])
        upper = dot(x, up_weight[:, f : f + step])
        hidden[:, f : f + step] = (gate / (1.0 + jnp.exp(-gate)) * upper).astype(BF16)


def hidden_rows(inputs, gate_weight, up_weight):
    rows, width = inputs.shape
    columns = gate_weight.shape[1]
    return pl.pallas_call(
        hidden_kernel,
        out_shape=jax.ShapeDtypeStruct((rows, columns), BF16),
        in_specs=[VMEM] * 3,
        out_specs=VMEM,
        compiler_params=pltpu.CompilerParams(vmem_limit_bytes=4 * MIB * max(1, rows // 128)),
        cost_estimate=pl.CostEstimate(
            flops=4 * rows * width * columns, bytes_accessed=0, transcendentals=rows * columns
        ),
        name="hidden",
    )(inputs, gate_weight, up_weight)


def down_kernel(hidden, down_weight, keep, send):
    half, width = keep.shape
    h = hidden[...]
    for n in range(0, width, 512):
        terms = dot(h, down_weight[:, n : n + 512])
        keep[:, n : n + 512] = terms[:half]
        send[:, n : n + 512] = terms[half:].astype(BF16)


def down_rows(hidden, down_weight):
    rows, columns = hidden.shape
    half, width = rows // 2, down_weight.shape[1]
    return pl.pallas_call(
        down_kernel,
        out_shape=(
            jax.ShapeDtypeStruct((half, width), F32),
            jax.ShapeDtypeStruct((half, width), BF16),
        ),
        in_specs=[VMEM] * 2,
        out_specs=(VMEM, VMEM),
        compiler_params=pltpu.CompilerParams(vmem_limit_bytes=4 * MIB * max(1, rows // 128)),
        cost_estimate=pl.CostEstimate(
            flops=2 * rows * width * columns, bytes_accessed=0, transcendentals=0
        ),
        name="down",
    )(hidden, down_weight)


def load_kernel(first, source, after, target, token, semaphores):
    copies = weight_copies(source, target, semaphores, first)
    for copy in copies:
        copy.start()
    token[...] = jnp.zeros(token.shape, token.dtype)
    for copy in copies:
        copy.wait()


def load(source, after, first=0):
    shape = (source.shape[0], source.shape[1] - first)
    return pl.pallas_call(
        functools.partial(load_kernel, first),
        out_shape=(
            pltpu.VMEM(shape, source.dtype),
            jax.ShapeDtypeStruct((8, 128), F32),
        ),
        in_specs=[ANY, ANY],
        out_specs=(VMEM, VMEM),
        scratch_shapes=[pltpu.SemaphoreType.DMA((WAYS,))],
        compiler_params=pltpu.CompilerParams(vmem_limit_bytes=MIB),
        cost_estimate=pl.CostEstimate(
            flops=0, bytes_accessed=2 * shape[0] * shape[1], transcendentals=0
        ),
        name="load",
    )(pltpu.with_memory_space_constraint(source, pltpu.HBM), after)


def collect_kernel(arrived, token, gathered):
    row, lane = grid((MOST * EXPERTS, 8 * EXPERTS))
    plane = sum([jnp.where(row >= MOST * e, 1, 0) for e in range(1, EXPERTS)])
    slot = row - MOST * plane
    late = jnp.where(slot >= 3, 1, 0)
    picks = [one_hot(lane == plane * 8 + slot)]
    for m in range(3):
        picks.append(one_hot((lane == plane * 8 + 6 + late) & (slot - 3 * late == m)))
    quarter = gathered.shape[1] // 4
    for m, value in enumerate(unpack(picks, arrived[...])):
        gathered[:, m * quarter : (m + 1) * quarter] = value.astype(BF16)


def collect(arrived, token):
    return pl.pallas_call(
        collect_kernel,
        out_shape=jax.ShapeDtypeStruct((MOST * EXPERTS, arrived.shape[1] // 3 * 4), BF16),
        in_specs=[VMEM, ANY],
        out_specs=VMEM,
        compiler_params=pltpu.CompilerParams(vmem_limit_bytes=2 * MIB),
        name="collect",
    )(arrived, token)


def join_kernel(*refs):
    out, row = refs[-1], 0
    for piece in refs[1:-1]:
        out[row : row + piece.shape[0]] = piece[...]
        row += piece.shape[0]


def join(after, *pieces):
    rows = sum(piece.shape[0] for piece in pieces)
    return pl.pallas_call(
        join_kernel,
        out_shape=jax.ShapeDtypeStruct((rows, pieces[0].shape[1]), BF16),
        in_specs=[ANY] + [VMEM] * len(pieces),
        out_specs=VMEM,
        compiler_params=pltpu.CompilerParams(vmem_limit_bytes=1 * MIB),
        name="join",
    )(after, *pieces)


def fold_kernel(held, arrived, keep, send):
    half = keep.shape[0]
    keep[...] = held[:half] + arrived[:half].astype(F32)
    send[...] = (held[half:] + arrived[half:].astype(F32)).astype(BF16)


def fold(held, arrived):
    half, width = held.shape[0] // 2, held.shape[1]
    return pl.pallas_call(
        fold_kernel,
        out_shape=(
            jax.ShapeDtypeStruct((half, width), F32),
            jax.ShapeDtypeStruct((half, width), BF16),
        ),
        in_specs=[VMEM] * 2,
        out_specs=(VMEM, VMEM),
        compiler_params=pltpu.CompilerParams(vmem_limit_bytes=4 * MIB * max(1, half // 32)),
        name="fold",
    )(held, arrived)


def last_fold_kernel(held, arrived, packed):
    block = (held[...] + arrived[...].astype(F32)).astype(BF16)
    place, row = grid((8 * EXPERTS, MOST * EXPERTS))
    plane, slot = place // 8, place % 8
    picks = [one_hot((row == plane * MOST + slot) & (slot < MOST))]
    for m in range(3):
        picks.append(one_hot((row == plane * MOST + 3 * (slot - 6) + m) & (slot >= MOST)))
    quarter = block.shape[1] // 4
    for m, value in enumerate(pack(picks, block)):
        packed[:, m * quarter : (m + 1) * quarter] = value


def last_fold(held, arrived):
    return pl.pallas_call(
        last_fold_kernel,
        out_shape=jax.ShapeDtypeStruct((8 * EXPERTS, held.shape[1] // 4 * 3), BF16),
        in_specs=[VMEM] * 2,
        out_specs=VMEM,
        compiler_params=pltpu.CompilerParams(vmem_limit_bytes=2 * MIB),
        name="last_fold",
    )(held, arrived)


def combine_kernel(share, take, *refs):
    results, out = refs[:-1], refs[-1]
    rows = out.shape[0]
    quarter = results[0].shape[1] // 3
    picks = [take[i][:, : 8 * EXPERTS] for i in range(4)]
    shares = share[:, :1]
    for part, result in enumerate(results):
        for m, value in enumerate(unpack(picks, result[...])):
            value = value * shares
            first = (part * 4 + m) * quarter
            out[:, first : first + quarter] = (value[:rows] + value[rows:]).astype(BF16)


def combine(share, take, results):
    width = results[0].shape[1] // 3 * 4
    return pl.pallas_call(
        combine_kernel,
        out_shape=jax.ShapeDtypeStruct((share.shape[0] // 2, width * PARTS), BF16),
        in_specs=[VMEM] * (2 + len(results)),
        out_specs=VMEM,
        compiler_params=pltpu.CompilerParams(vmem_limit_bytes=2 * MIB),
        name="combine",
    )(share, take, *results)


def between_planes(value, count):
    plane = count // EXPERTS
    groups = [[e * plane + p for e in range(EXPERTS)] for p in range(plane)]
    return lax.all_to_all(
        value, "dp", split_axis=0, concat_axis=0, axis_index_groups=groups, tiled=True
    )


def swap(value, count, bit):
    return lax.ppermute(value, "dp", [(i, i ^ bit) for i in range(count)])


def body(
    queries,
    new_keys,
    new_values,
    cache_keys,
    cache_values,
    lengths,
    residual,
    norm_gain,
    router_weight,
    gate_weight,
    up_weight,
    down_weight,
    routes,
):
    count = lax.axis_size("dp")
    plane = count // EXPERTS
    bits = [1 << k for k in reversed(range(plane.bit_length() - 1))]
    attended, packed, share, take, down = attend(
        queries, new_keys, new_values, cache_keys, cache_values, lengths, residual, norm_gain,
        router_weight, routes, down_weight,
    )

    gate, token = load(gate_weight, packed)
    gathered = collect(between_planes(packed, count), token)
    up, token = load(up_weight, gathered)
    gathered = join(token, gathered, swap(gathered, count, bits[0]))
    down_rest, token = load(down_weight, gathered, down.shape[1])
    for bit in bits[1:]:
        gathered = join(token, gathered, swap(gathered, count, bit))

    hidden = hidden_rows(gathered, gate, up)
    results = []
    for weight in (down, down_rest):
        held, send = down_rows(hidden, weight)
        for bit in bits[:0:-1]:
            held, send = fold(held, swap(send, count, bit))
        results.append(between_planes(last_fold(held, swap(send, count, bits[0])), count))
    return (attended, combine(share, take, results))


def solution(mesh):
    placed = (
        P(("group", "dp"), None),
        P(("group", "dp"), None),
        P(("group", "dp"), None),
        P(("group", "dp"), None, None),
        P(("group", "dp"), None, None),
        P(("group", "dp")),
        P(("group", "dp"), None),
        P(),
        P(),
        P(None, "dp"),
        P(None, "dp"),
        P("dp", None),
        P("group", None),
    )
    return jax.shard_map(
        body,
        mesh=mesh,
        in_specs=placed,
        out_specs=(P(("group", "dp"), None), P(("group", "dp"), None)),
        check_vma=False,
    )
```

```python
import functools

import jax
import jax.numpy as jnp
from jax import lax
from jax.experimental import pallas as pl
from jax.experimental.pallas import tpu as pltpu
from jax.sharding import PartitionSpec as P

HEADS = 32
KV_HEADS = 8
HEAD_DIM = 128
EXPERTS = 4
MIB = 1 << 20
WAYS = 4
PARTS = 2
MOST = 6
F32 = jnp.float32
BF16 = jnp.bfloat16
VMEM = pl.BlockSpec(memory_space=pltpu.VMEM)
ANY = pl.BlockSpec(memory_space=pl.ANY)


def dot(a, b, contract_last=False):
    dims = (((1,), (1 if contract_last else 0,)), ((), ()))
    return lax.dot_general(a, b, dims, preferred_element_type=F32)


def weight_copies(source, target, semaphores, first=0):
    step, columns = source.shape[0] // WAYS, target.shape[1]
    return [
        pltpu.make_async_copy(
            source.at[pl.ds(i * step, step), pl.ds(first, columns)],
            target.at[pl.ds(i * step, step)],
            semaphores.at[i],
        )
        for i in range(WAYS)
    ]


def one_hot(mask):
    return mask.astype(F32).astype(BF16)


def grid(shape):
    return [lax.broadcasted_iota(jnp.int32, shape, axis) for axis in (0, 1)]


def pack(picks, block):
    quarter = block.shape[1] // 4
    parts = [block[:, m * quarter : (m + 1) * quarter] for m in range(4)]
    return [
        (dot(picks[0], parts[m]) + dot(picks[1 + m], parts[3])).astype(BF16) for m in range(3)
    ]


def unpack(picks, block):
    quarter = block.shape[1] // 3
    parts = [block[:, m * quarter : (m + 1) * quarter] for m in range(3)]
    tail = dot(picks[1], parts[0]) + dot(picks[2], parts[1]) + dot(picks[3], parts[2])
    return [dot(picks[0], part) for part in parts] + [tail]


def attend_kernel(plane, *refs):
    sources, attended, packed, (share, take), held, semaphores = (
        refs[:10], refs[11], refs[12:16], refs[16:18], refs[19:29], refs[29]
    )
    weight = weight_copies(refs[10], refs[18], refs[30])
    copies = [
        pltpu.make_async_copy(source, target, semaphores.at[i])
        for i, (source, target) in enumerate(zip(sources, held))
    ]
    for copy in copies + weight:
        copy.start()
    (queries, cache_keys, new_keys, lengths, cache_values, new_values, residual, gain, router,
     routes) = held
    for copy in copies[:4] + copies[9:]:
        copy.wait()
    rows, width = queries.shape
    positions = cache_keys.shape[1]
    groups = HEADS // KV_HEADS
    scale = 1.0 / HEAD_DIM**0.5
    every = rows * positions
    block = groups * rows

    query = queries[...].astype(F32)
    stacked = jnp.concatenate(
        [query[:, h * HEAD_DIM : (h + 1) * HEAD_DIM] for h in range(HEADS)], axis=0
    )
    stacked_b = stacked.astype(BF16)
    keys = cache_keys[...].reshape(every, KV_HEADS * HEAD_DIM)
    newk = new_keys[...].astype(F32)

    row_of = lax.broadcasted_iota(jnp.int32, (block, every), 0) % rows
    column = lax.broadcasted_iota(jnp.int32, (block, every), 1)
    position = column % positions
    column_row = column // positions
    limit = jnp.zeros((block, every), jnp.int32)
    for r in range(rows):
        limit = jnp.where(column_row == r, lengths[r], limit)
    valid = (row_of == column_row) & (position < limit)

    heads = range(KV_HEADS)
    lanes = [slice(g * HEAD_DIM, (g + 1) * HEAD_DIM) for g in heads]
    mine = [slice(g * block, (g + 1) * block) for g in heads]
    scores = [dot(stacked_b[mine[g]], keys[:, lanes[g]], contract_last=True) for g in heads]
    scores = [jnp.where(valid, score * scale, -jnp.inf) for score in scores]
    own_keys = [jnp.concatenate([newk[:, lanes[g]]] * groups, axis=0) for g in heads]
    new_scores = [
        jnp.sum(stacked[mine[g]] * own_keys[g], axis=1, keepdims=True) * scale for g in heads
    ]
    peaks = [
        jnp.maximum(jnp.max(score, axis=1, keepdims=True), new)
        for score, new in zip(scores, new_scores)
    ]
    weights = [jnp.exp(score - peak) for score, peak in zip(scores, peaks)]
    new_weights = [jnp.exp(new - peak) for new, peak in zip(new_scores, peaks)]
    totals = [
        jnp.sum(weight, axis=1, keepdims=True) + new
        for weight, new in zip(weights, new_weights)
    ]
    probs = [(weight / total).astype(BF16) for weight, total in zip(weights, totals)]
    new_probs = [
        (new / total).astype(BF16).astype(F32) for new, total in zip(new_weights, totals)
    ]
    for copy in copies[4:9]:
        copy.wait()
    values = cache_values[...].reshape(every, KV_HEADS * HEAD_DIM)
    newv = new_values[...].astype(F32)
    mixed = [
        dot(probs[g], values[:, lanes[g]])
        + new_probs[g] * jnp.concatenate([newv[:, lanes[g]]] * groups, axis=0)
        for g in heads
    ]
    pieces = [value[j * rows : (j + 1) * rows] for value in mixed for j in range(groups)]

    states = (residual[...].astype(F32) + jnp.concatenate(pieces, axis=1)).astype(BF16)
    attended[...] = states
    states = states.astype(F32)
    norm = lax.rsqrt(jnp.mean(states * states, axis=1, keepdims=True) + 1e-05)
    gains = gain[...].astype(F32)
    logits = [jnp.zeros((rows, 128), F32) for _ in range(EXPERTS)]
    parts = []
    for c in range(width // 128):
        lanes = slice(c * 128, (c + 1) * 128)
        part = (states[:, lanes] * norm * gains[c : c + 1]).astype(BF16).astype(F32)
        parts.append(part)
        for e in range(EXPERTS):
            logits[e] += part * router[e : e + 1, lanes].astype(F32)
    logits = [jnp.sum(value, axis=1, keepdims=True) for value in logits]

    index = lax.axis_index("dp")
    base = index * rows
    own = index // plane
    sub, lane = grid((2 * rows, 128))
    expert_down = jnp.zeros((2 * rows, 128), jnp.int32)
    slot_down = jnp.zeros((2 * rows, 128), jnp.int32)
    across = lax.broadcasted_iota(jnp.int32, (8, 128), 1)
    expert_across = jnp.zeros((8, 128), jnp.int32)
    slot_across = jnp.zeros((8, 128), jnp.int32)
    counts = [jnp.int32(0)] * EXPERTS
    for r in range(rows):
        names = [(routes[c, base + r] + EXPERTS - own) % EXPERTS for c in range(2)]
        for choice, name in ((r, names[0]), (rows + r, names[1])):
            slot = jnp.int32(0)
            for e in range(EXPERTS):
                slot = jnp.where(name == e, counts[e], slot)
            expert_down = jnp.where(sub == choice, name, expert_down)
            slot_down = jnp.where(sub == choice, slot, slot_down)
            expert_across = jnp.where(across == choice, name, expert_across)
            slot_across = jnp.where(across == choice, slot, slot_across)
        for e in range(EXPERTS):
            named = (names[0] == e) | (names[1] == e)
            counts[e] = counts[e] + jnp.where(named, 1, 0)

    late = jnp.where(slot_down >= 3, 1, 0)
    take[0] = one_hot(lane == expert_down * 8 + slot_down)
    for m in range(3):
        take[1 + m] = one_hot((lane == expert_down * 8 + 6 + late) & (slot_down - 3 * late == m))
    place, choice = grid((8 * EXPERTS, 128))
    expert, slot = expert_across[0:1], slot_across[0:1]
    late = jnp.where(slot >= 3, 1, 0)
    chosen = choice < 2 * rows
    picks = [one_hot((place == expert * 8 + slot) & chosen)]
    for m in range(3):
        picks.append(one_hot((place == expert * 8 + 6 + late) & (slot - 3 * late == m) & chosen))
    normed = jnp.concatenate(parts, axis=1)
    normed = jnp.concatenate([normed, normed], axis=0).astype(BF16)
    quarter = width // 4
    for m, value in enumerate(pack([pick[:, : 2 * rows] for pick in picks], normed)):
        for k, target in enumerate(packed):
            target[:, m * quarter : (m + 1) * quarter] = value[8 * k : 8 * k + 8]

    chosen_logits = jnp.zeros((2 * rows, 1), F32)
    for e in range(EXPERTS):
        both = jnp.concatenate([logits[e], logits[e]], axis=0)
        relative = (e + EXPERTS - own) % EXPERTS
        chosen_logits = jnp.where(expert_down[:, :1] == relative, both, chosen_logits)
    other = jnp.concatenate([chosen_logits[rows:], chosen_logits[:rows]], axis=0)
    share[...] = jnp.broadcast_to(1.0 / (1.0 + jnp.exp(other - chosen_logits)), share.shape)
    for copy in weight:
        copy.wait()


def attend(plane, queries, new_keys, new_values, cache_keys, cache_values, lengths, residual,
           norm_gain, router_weight, routes, weight):
    rows, width = queries.shape
    operands = (
        queries,
        cache_keys,
        new_keys,
        lengths,
        cache_values,
        new_values,
        residual,
        norm_gain.reshape(-1, 128),
        router_weight.T,
        routes.T,
    )
    in_smem = (3, 9)
    return pl.pallas_call(
        functools.partial(attend_kernel, plane),
        out_shape=(
            jax.ShapeDtypeStruct((rows, width), BF16),
            *[jax.ShapeDtypeStruct((8, width * 3 // 4), BF16)] * EXPERTS,
            jax.ShapeDtypeStruct((2 * rows, 128), F32),
            jax.ShapeDtypeStruct((4, 2 * rows, 128), BF16),
            pltpu.VMEM((weight.shape[0], weight.shape[1] // PARTS), weight.dtype),
        ),
        in_specs=[ANY] * (len(operands) + 1),
        out_specs=(VMEM,) * (4 + EXPERTS),
        scratch_shapes=[
            (pltpu.SMEM if i in in_smem else pltpu.VMEM)(operand.shape, operand.dtype)
            for i, operand in enumerate(operands)
        ]
        + [pltpu.SemaphoreType.DMA((len(operands),)), pltpu.SemaphoreType.DMA((WAYS,))],
        compiler_params=pltpu.CompilerParams(vmem_limit_bytes=5 * MIB),
        name="attend",
    )(*[pltpu.with_memory_space_constraint(x, pltpu.HBM) for x in (*operands, weight)])


def hidden_kernel(inputs, gate_weight, up_weight, hidden):
    columns = gate_weight.shape[1]
    step = 256 if columns % 256 == 0 else columns
    x = padded(inputs[...])
    for f in range(0, columns, step):
        gate = dot(x, gate_weight[:, f : f + step])
        upper = dot(x, up_weight[:, f : f + step])
        hidden[:, f : f + step] = (gate / (1.0 + jnp.exp(-gate)) * upper).astype(BF16)


def padded(x):
    extra = -x.shape[0] % 128
    if extra == 0:
        return x
    return jnp.concatenate([x, jnp.zeros((extra, x.shape[1]), x.dtype)], axis=0)


def hidden_rows(inputs, gate_weight, up_weight):
    rows, width = inputs.shape
    columns = gate_weight.shape[1]
    return pl.pallas_call(
        hidden_kernel,
        out_shape=jax.ShapeDtypeStruct((rows + -rows % 128, columns), BF16),
        in_specs=[VMEM] * 3,
        out_specs=VMEM,
        compiler_params=pltpu.CompilerParams(vmem_limit_bytes=4 * MIB * max(1, rows // 128)),
        cost_estimate=pl.CostEstimate(
            flops=4 * rows * width * columns, bytes_accessed=0, transcendentals=rows * columns
        ),
        name="hidden",
    )(inputs, gate_weight, up_weight)


def down_kernel(hidden, down_weight, keep, send):
    half, width = keep.shape
    h = hidden[...]
    for n in range(0, width, 512):
        terms = dot(h, down_weight[:, n : n + 512])
        keep[:, n : n + 512] = terms[:half]
        send[:, n : n + 512] = terms[half : 2 * half].astype(BF16)


def down_rows(hidden, down_weight, rows):
    columns = hidden.shape[1]
    half, width = rows // 2, down_weight.shape[1]
    return pl.pallas_call(
        down_kernel,
        out_shape=(
            jax.ShapeDtypeStruct((half, width), F32),
            jax.ShapeDtypeStruct((half, width), BF16),
        ),
        in_specs=[VMEM] * 2,
        out_specs=(VMEM, VMEM),
        compiler_params=pltpu.CompilerParams(vmem_limit_bytes=4 * MIB * max(1, rows // 128)),
        cost_estimate=pl.CostEstimate(
            flops=2 * rows * width * columns, bytes_accessed=0, transcendentals=0
        ),
        name="down",
    )(hidden, down_weight)


def load_kernel(first, source, after, target, token, semaphores):
    copies = weight_copies(source, target, semaphores, first)
    for copy in copies:
        copy.start()
    token[...] = jnp.zeros(token.shape, token.dtype)
    for copy in copies:
        copy.wait()


def load(source, after, first=0):
    shape = (source.shape[0], source.shape[1] - first)
    return pl.pallas_call(
        functools.partial(load_kernel, first),
        out_shape=(
            pltpu.VMEM(shape, source.dtype),
            jax.ShapeDtypeStruct((8, 128), F32),
        ),
        in_specs=[ANY, ANY],
        out_specs=(VMEM, VMEM),
        scratch_shapes=[pltpu.SemaphoreType.DMA((WAYS,))],
        compiler_params=pltpu.CompilerParams(vmem_limit_bytes=MIB),
        cost_estimate=pl.CostEstimate(
            flops=0, bytes_accessed=2 * shape[0] * shape[1], transcendentals=0
        ),
        name="load",
    )(pltpu.with_memory_space_constraint(source, pltpu.HBM), after)


def collect_kernel(token, *refs):
    arrived, gathered = refs[:-1], refs[-1]
    row, lane = grid((MOST * EXPERTS, 8 * EXPERTS))
    plane = sum([jnp.where(row >= MOST * e, 1, 0) for e in range(1, EXPERTS)])
    slot = row - MOST * plane
    late = jnp.where(slot >= 3, 1, 0)
    picks = [one_hot(lane == plane * 8 + slot)]
    for m in range(3):
        picks.append(one_hot((lane == plane * 8 + 6 + late) & (slot - 3 * late == m)))
    quarter = gathered.shape[1] // 4
    for m, value in enumerate(unpack(picks, jnp.concatenate([x[...] for x in arrived], axis=0))):
        gathered[:, m * quarter : (m + 1) * quarter] = value.astype(BF16)


def collect(token, arrived):
    return pl.pallas_call(
        collect_kernel,
        out_shape=jax.ShapeDtypeStruct((MOST * EXPERTS, arrived[0].shape[1] // 3 * 4), BF16),
        in_specs=[ANY] + [VMEM] * EXPERTS,
        out_specs=VMEM,
        compiler_params=pltpu.CompilerParams(vmem_limit_bytes=2 * MIB),
        name="collect",
    )(token, *arrived)


def join_kernel(*refs):
    out, row = refs[-1], 0
    for piece in refs[1:-1]:
        out[row : row + piece.shape[0]] = piece[...]
        row += piece.shape[0]


def join(after, *pieces):
    rows = sum(piece.shape[0] for piece in pieces)
    return pl.pallas_call(
        join_kernel,
        out_shape=jax.ShapeDtypeStruct((rows, pieces[0].shape[1]), BF16),
        in_specs=[ANY] + [VMEM] * len(pieces),
        out_specs=VMEM,
        compiler_params=pltpu.CompilerParams(vmem_limit_bytes=1 * MIB),
        name="join",
    )(after, *pieces)


def fold_kernel(held, arrived, keep, send):
    half = keep.shape[0]
    keep[...] = held[:half] + arrived[:half].astype(F32)
    send[...] = (held[half:] + arrived[half:].astype(F32)).astype(BF16)


def fold(held, arrived):
    half, width = held.shape[0] // 2, held.shape[1]
    return pl.pallas_call(
        fold_kernel,
        out_shape=(
            jax.ShapeDtypeStruct((half, width), F32),
            jax.ShapeDtypeStruct((half, width), BF16),
        ),
        in_specs=[VMEM] * 2,
        out_specs=(VMEM, VMEM),
        compiler_params=pltpu.CompilerParams(vmem_limit_bytes=4 * MIB * max(1, half // 32)),
        name="fold",
    )(held, arrived)


def last_fold_kernel(held, arrived, *packed):
    block = (held[...] + arrived[...].astype(F32)).astype(BF16)
    place, row = grid((8 * EXPERTS, MOST * EXPERTS))
    plane, slot = place // 8, place % 8
    picks = [one_hot((row == plane * MOST + slot) & (slot < MOST))]
    for m in range(3):
        picks.append(one_hot((row == plane * MOST + 3 * (slot - 6) + m) & (slot >= MOST)))
    quarter = block.shape[1] // 4
    for m, value in enumerate(pack(picks, block)):
        for k, target in enumerate(packed):
            target[:, m * quarter : (m + 1) * quarter] = value[8 * k : 8 * k + 8]


def last_fold(held, arrived):
    return pl.pallas_call(
        last_fold_kernel,
        out_shape=[jax.ShapeDtypeStruct((8, held.shape[1] // 4 * 3), BF16)] * EXPERTS,
        in_specs=[VMEM] * 2,
        out_specs=[VMEM] * EXPERTS,
        compiler_params=pltpu.CompilerParams(vmem_limit_bytes=2 * MIB),
        name="last_fold",
    )(held, arrived)


def combine_kernel(share, take, *refs):
    out = refs[-1]
    results = [refs[p * EXPERTS : (p + 1) * EXPERTS] for p in range(PARTS)]
    rows = out.shape[0]
    quarter = refs[0].shape[1] // 3
    picks = [take[i][:, : 8 * EXPERTS] for i in range(4)]
    shares = share[:, :1]
    for part, result in enumerate(results):
        for m, value in enumerate(unpack(picks, jnp.concatenate([x[...] for x in result], axis=0))):
            value = value * shares
            first = (part * 4 + m) * quarter
            out[:, first : first + quarter] = (value[:rows] + value[rows:]).astype(BF16)


def combine(share, take, results):
    width = results[0].shape[1] // 3 * 4
    return pl.pallas_call(
        combine_kernel,
        out_shape=jax.ShapeDtypeStruct((share.shape[0] // 2, width * PARTS), BF16),
        in_specs=[VMEM] * (2 + len(results)),
        out_specs=VMEM,
        compiler_params=pltpu.CompilerParams(vmem_limit_bytes=2 * MIB),
        name="combine",
    )(share, take, *results)


def between_planes(blocks, count, direction):
    plane = count // EXPERTS
    return [blocks[0]] + [
        lax.ppermute(
            blocks[k], "dp", [(i, (i + direction * k * plane) % count) for i in range(count)]
        )
        for k in range(1, EXPERTS)
    ]


def swap(value, count, bit):
    return lax.ppermute(value, "dp", [(i, i ^ bit) for i in range(count)])


def body(
    queries,
    new_keys,
    new_values,
    cache_keys,
    cache_values,
    lengths,
    residual,
    norm_gain,
    router_weight,
    gate_weight,
    up_weight,
    down_weight,
    routes,
):
    count = lax.axis_size("dp")
    plane = count // EXPERTS
    bits = [1 << k for k in reversed(range(plane.bit_length() - 1))]
    attended, *packed, share, take, down = attend(
        plane, queries, new_keys, new_values, cache_keys, cache_values, lengths, residual, norm_gain,
        router_weight, routes, down_weight,
    )

    gate, token = load(gate_weight, packed[0])
    gathered = collect(token, between_planes(packed, count, 1))
    up, token = load(up_weight, gathered)
    gathered = join(token, gathered, swap(gathered, count, bits[0]))
    down_rest, token = load(down_weight, gathered, down.shape[1])
    for bit in bits[1:]:
        gathered = join(token, gathered, swap(gathered, count, bit))

    hidden = hidden_rows(gathered, gate, up)
    results = []
    for weight in (down, down_rest):
        held, send = down_rows(hidden, weight, gathered.shape[0])
        for bit in bits[:0:-1]:
            held, send = fold(held, swap(send, count, bit))
        blocks = last_fold(held, swap(send, count, bits[0]))
        results += between_planes(blocks, count, -1)
    return (attended, combine(share, take, results))


def solution(mesh):
    placed = (
        P(("group", "dp"), None),
        P(("group", "dp"), None),
        P(("group", "dp"), None),
        P(("group", "dp"), None, None),
        P(("group", "dp"), None, None),
        P(("group", "dp")),
        P(("group", "dp"), None),
        P(),
        P(),
        P(None, "dp"),
        P(None, "dp"),
        P("dp", None),
        P("group", None),
    )
    return jax.shard_map(
        body,
        mesh=mesh,
        in_specs=placed,
        out_specs=(P(("group", "dp"), None), P(("group", "dp"), None)),
        check_vma=False,
    )
```

```python
import functools

import jax
import jax.numpy as jnp
from jax import lax
from jax.experimental import pallas as pl
from jax.experimental.pallas import tpu as pltpu
from jax.sharding import PartitionSpec as P

HEADS = 32
KV_HEADS = 8
HEAD_DIM = 128
EXPERTS = 4
MIB = 1 << 20
WAYS = 4
PARTS = 2
MOST = 6
F32 = jnp.float32
BF16 = jnp.bfloat16
VMEM = pl.BlockSpec(memory_space=pltpu.VMEM)
ANY = pl.BlockSpec(memory_space=pl.ANY)


def dot(a, b, contract_last=False):
    dims = (((1,), (1 if contract_last else 0,)), ((), ()))
    return lax.dot_general(a, b, dims, preferred_element_type=F32)


def weight_copies(source, target, semaphores, first=0):
    step, columns = source.shape[0] // WAYS, target.shape[1]
    return [
        pltpu.make_async_copy(
            source.at[pl.ds(i * step, step), pl.ds(first, columns)],
            target.at[pl.ds(i * step, step)],
            semaphores.at[i],
        )
        for i in range(WAYS)
    ]


def one_hot(mask):
    return mask.astype(F32).astype(BF16)


def grid(shape):
    return [lax.broadcasted_iota(jnp.int32, shape, axis) for axis in (0, 1)]


def pack(picks, block):
    quarter = block.shape[1] // 4
    parts = [block[:, m * quarter : (m + 1) * quarter] for m in range(4)]
    return [
        (dot(picks[0], parts[m]) + dot(picks[1 + m], parts[3])).astype(BF16) for m in range(3)
    ]


def unpack(picks, block):
    quarter = block.shape[1] // 3
    parts = [block[:, m * quarter : (m + 1) * quarter] for m in range(3)]
    tail = dot(picks[1], parts[0]) + dot(picks[2], parts[1]) + dot(picks[3], parts[2])
    return [dot(picks[0], part) for part in parts] + [tail]


def attend_kernel(plane, *refs):
    sources, attended, packed, (share, take), held, semaphores = (
        refs[:10], refs[11], refs[12:16], refs[16:18], refs[19:29], refs[29]
    )
    weight = weight_copies(refs[10], refs[18], refs[30])
    copies = [
        pltpu.make_async_copy(source, target, semaphores.at[i])
        for i, (source, target) in enumerate(zip(sources, held))
    ]
    for copy in copies + weight:
        copy.start()
    (queries, cache_keys, new_keys, lengths, cache_values, new_values, residual, gain, router,
     routes) = held
    for copy in copies[:4] + copies[9:]:
        copy.wait()
    rows, width = queries.shape
    positions = cache_keys.shape[1]
    groups = HEADS // KV_HEADS
    scale = 1.0 / HEAD_DIM**0.5
    every = rows * positions
    block = groups * rows

    query = queries[...].astype(F32)
    stacked = jnp.concatenate(
        [query[:, h * HEAD_DIM : (h + 1) * HEAD_DIM] for h in range(HEADS)], axis=0
    )
    stacked_b = stacked.astype(BF16)
    keys = cache_keys[...].reshape(every, KV_HEADS * HEAD_DIM)
    newk = new_keys[...].astype(F32)

    row_of = lax.broadcasted_iota(jnp.int32, (block, every), 0) % rows
    column = lax.broadcasted_iota(jnp.int32, (block, every), 1)
    position = column % positions
    column_row = column // positions
    limit = jnp.zeros((block, every), jnp.int32)
    for r in range(rows):
        limit = jnp.where(column_row == r, lengths[r], limit)
    valid = (row_of == column_row) & (position < limit)

    heads = range(KV_HEADS)
    lanes = [slice(g * HEAD_DIM, (g + 1) * HEAD_DIM) for g in heads]
    mine = [slice(g * block, (g + 1) * block) for g in heads]
    scores = [dot(stacked_b[mine[g]], keys[:, lanes[g]], contract_last=True) for g in heads]
    scores = [jnp.where(valid, score * scale, -jnp.inf) for score in scores]
    own_keys = [jnp.concatenate([newk[:, lanes[g]]] * groups, axis=0) for g in heads]
    new_scores = [
        jnp.sum(stacked[mine[g]] * own_keys[g], axis=1, keepdims=True) * scale for g in heads
    ]
    peaks = [
        jnp.maximum(jnp.max(score, axis=1, keepdims=True), new)
        for score, new in zip(scores, new_scores)
    ]
    weights = [jnp.exp(score - peak) for score, peak in zip(scores, peaks)]
    new_weights = [jnp.exp(new - peak) for new, peak in zip(new_scores, peaks)]
    totals = [
        jnp.sum(weight, axis=1, keepdims=True) + new
        for weight, new in zip(weights, new_weights)
    ]
    probs = [(weight / total).astype(BF16) for weight, total in zip(weights, totals)]
    new_probs = [
        (new / total).astype(BF16).astype(F32) for new, total in zip(new_weights, totals)
    ]
    for copy in copies[4:9]:
        copy.wait()
    values = cache_values[...].reshape(every, KV_HEADS * HEAD_DIM)
    newv = new_values[...].astype(F32)
    mixed = [
        dot(probs[g], values[:, lanes[g]])
        + new_probs[g] * jnp.concatenate([newv[:, lanes[g]]] * groups, axis=0)
        for g in heads
    ]
    pieces = [value[j * rows : (j + 1) * rows] for value in mixed for j in range(groups)]

    states = (residual[...].astype(F32) + jnp.concatenate(pieces, axis=1)).astype(BF16)
    attended[...] = states
    states = states.astype(F32)
    norm = lax.rsqrt(jnp.mean(states * states, axis=1, keepdims=True) + 1e-05)
    gains = gain[...].astype(F32)
    logits = [jnp.zeros((rows, 128), F32) for _ in range(EXPERTS)]
    parts = []
    for c in range(width // 128):
        lanes = slice(c * 128, (c + 1) * 128)
        part = (states[:, lanes] * norm * gains[c : c + 1]).astype(BF16).astype(F32)
        parts.append(part)
        for e in range(EXPERTS):
            logits[e] += part * router[e : e + 1, lanes].astype(F32)
    logits = [jnp.sum(value, axis=1, keepdims=True) for value in logits]

    index = lax.axis_index("dp")
    base = index * rows
    own = index // plane
    sub, lane = grid((2 * rows, 128))
    expert_down = jnp.zeros((2 * rows, 128), jnp.int32)
    slot_down = jnp.zeros((2 * rows, 128), jnp.int32)
    across = lax.broadcasted_iota(jnp.int32, (8, 128), 1)
    expert_across = jnp.zeros((8, 128), jnp.int32)
    slot_across = jnp.zeros((8, 128), jnp.int32)
    counts = [jnp.int32(0)] * EXPERTS
    for r in range(rows):
        names = [(routes[c, base + r] + EXPERTS - own) % EXPERTS for c in range(2)]
        for choice, name in ((r, names[0]), (rows + r, names[1])):
            slot = jnp.int32(0)
            for e in range(EXPERTS):
                slot = jnp.where(name == e, counts[e], slot)
            expert_down = jnp.where(sub == choice, name, expert_down)
            slot_down = jnp.where(sub == choice, slot, slot_down)
            expert_across = jnp.where(across == choice, name, expert_across)
            slot_across = jnp.where(across == choice, slot, slot_across)
        for e in range(EXPERTS):
            named = (names[0] == e) | (names[1] == e)
            counts[e] = counts[e] + jnp.where(named, 1, 0)

    late = jnp.where(slot_down >= 3, 1, 0)
    take[0] = one_hot(lane == expert_down * 8 + slot_down)
    for m in range(3):
        take[1 + m] = one_hot((lane == expert_down * 8 + 6 + late) & (slot_down - 3 * late == m))
    place, choice = grid((8 * EXPERTS, 128))
    expert, slot = expert_across[0:1], slot_across[0:1]
    late = jnp.where(slot >= 3, 1, 0)
    chosen = choice < 2 * rows
    picks = [one_hot((place == expert * 8 + slot) & chosen)]
    for m in range(3):
        picks.append(one_hot((place == expert * 8 + 6 + late) & (slot - 3 * late == m) & chosen))
    normed = jnp.concatenate(parts, axis=1)
    normed = jnp.concatenate([normed, normed], axis=0).astype(BF16)
    quarter = width // 4
    for m, value in enumerate(pack([pick[:, : 2 * rows] for pick in picks], normed)):
        for k, target in enumerate(packed):
            target[:, m * quarter : (m + 1) * quarter] = value[8 * k : 8 * k + 8]

    chosen_logits = jnp.zeros((2 * rows, 1), F32)
    for e in range(EXPERTS):
        both = jnp.concatenate([logits[e], logits[e]], axis=0)
        relative = (e + EXPERTS - own) % EXPERTS
        chosen_logits = jnp.where(expert_down[:, :1] == relative, both, chosen_logits)
    other = jnp.concatenate([chosen_logits[rows:], chosen_logits[:rows]], axis=0)
    share[...] = jnp.broadcast_to(1.0 / (1.0 + jnp.exp(other - chosen_logits)), share.shape)
    for copy in weight:
        copy.wait()


def attend(plane, queries, new_keys, new_values, cache_keys, cache_values, lengths, residual,
           norm_gain, router_weight, routes, weight):
    rows, width = queries.shape
    operands = (
        queries,
        cache_keys,
        new_keys,
        lengths,
        cache_values,
        new_values,
        residual,
        norm_gain.reshape(-1, 128),
        router_weight.T,
        routes.T,
    )
    in_smem = (3, 9)
    return pl.pallas_call(
        functools.partial(attend_kernel, plane),
        out_shape=(
            jax.ShapeDtypeStruct((rows, width), BF16),
            *[jax.ShapeDtypeStruct((8, width * 3 // 4), BF16)] * EXPERTS,
            jax.ShapeDtypeStruct((2 * rows, 128), F32),
            jax.ShapeDtypeStruct((4, 2 * rows, 128), BF16),
            pltpu.VMEM((weight.shape[0], weight.shape[1] // PARTS), weight.dtype),
        ),
        in_specs=[ANY] * (len(operands) + 1),
        out_specs=(VMEM,) * (4 + EXPERTS),
        scratch_shapes=[
            (pltpu.SMEM if i in in_smem else pltpu.VMEM)(operand.shape, operand.dtype)
            for i, operand in enumerate(operands)
        ]
        + [pltpu.SemaphoreType.DMA((len(operands),)), pltpu.SemaphoreType.DMA((WAYS,))],
        compiler_params=pltpu.CompilerParams(vmem_limit_bytes=5 * MIB),
        name="attend",
    )(*[pltpu.with_memory_space_constraint(x, pltpu.HBM) for x in (*operands, weight)])


def hidden_kernel(inputs, gate_weight, up_weight, hidden):
    columns = gate_weight.shape[1]
    step = 256 if columns % 256 == 0 else columns
    x = padded(inputs[...])
    for f in range(0, columns, step):
        gate = dot(x, gate_weight[:, f : f + step])
        upper = dot(x, up_weight[:, f : f + step])
        hidden[:, f : f + step] = (gate / (1.0 + jnp.exp(-gate)) * upper).astype(BF16)


def padded(x):
    extra = -x.shape[0] % 128
    if extra == 0:
        return x
    return jnp.concatenate([x, jnp.zeros((extra, x.shape[1]), x.dtype)], axis=0)


def hidden_rows(inputs, gate_weight, up_weight):
    rows, width = inputs.shape
    columns = gate_weight.shape[1]
    return pl.pallas_call(
        hidden_kernel,
        out_shape=jax.ShapeDtypeStruct((rows + -rows % 128, columns), BF16),
        in_specs=[VMEM] * 3,
        out_specs=VMEM,
        compiler_params=pltpu.CompilerParams(vmem_limit_bytes=4 * MIB * max(1, rows // 128)),
        cost_estimate=pl.CostEstimate(
            flops=4 * rows * width * columns, bytes_accessed=0, transcendentals=rows * columns
        ),
        name="hidden",
    )(inputs, gate_weight, up_weight)


def down_kernel(hidden, down_weight, keep, send):
    half, width = keep.shape
    h = hidden[...]
    for n in range(0, width, 512):
        terms = dot(h, down_weight[:, n : n + 512])
        keep[:, n : n + 512] = terms[:half]
        send[:, n : n + 512] = terms[half : 2 * half].astype(BF16)


def down_rows(hidden, down_weight, rows):
    columns = hidden.shape[1]
    half, width = rows // 2, down_weight.shape[1]
    return pl.pallas_call(
        down_kernel,
        out_shape=(
            jax.ShapeDtypeStruct((half, width), F32),
            jax.ShapeDtypeStruct((half, width), BF16),
        ),
        in_specs=[VMEM] * 2,
        out_specs=(VMEM, VMEM),
        compiler_params=pltpu.CompilerParams(vmem_limit_bytes=4 * MIB * max(1, rows // 128)),
        cost_estimate=pl.CostEstimate(
            flops=2 * rows * width * columns, bytes_accessed=0, transcendentals=0
        ),
        name="down",
    )(hidden, down_weight)


def load_kernel(first, source, after, target, token, semaphores):
    copies = weight_copies(source, target, semaphores, first)
    for copy in copies:
        copy.start()
    token[...] = jnp.zeros(token.shape, token.dtype)
    for copy in copies:
        copy.wait()


def load(source, after, first=0):
    shape = (source.shape[0], source.shape[1] - first)
    return pl.pallas_call(
        functools.partial(load_kernel, first),
        out_shape=(
            pltpu.VMEM(shape, source.dtype),
            jax.ShapeDtypeStruct((8, 128), F32),
        ),
        in_specs=[ANY, ANY],
        out_specs=(VMEM, VMEM),
        scratch_shapes=[pltpu.SemaphoreType.DMA((WAYS,))],
        compiler_params=pltpu.CompilerParams(vmem_limit_bytes=MIB),
        cost_estimate=pl.CostEstimate(
            flops=0, bytes_accessed=2 * shape[0] * shape[1], transcendentals=0
        ),
        name="load",
    )(pltpu.with_memory_space_constraint(source, pltpu.HBM), after)


def collect_kernel(token, *refs):
    arrived, gathered = refs[:-1], refs[-1]
    row, lane = grid((MOST * EXPERTS, 8 * EXPERTS))
    plane = sum([jnp.where(row >= MOST * e, 1, 0) for e in range(1, EXPERTS)])
    slot = row - MOST * plane
    late = jnp.where(slot >= 3, 1, 0)
    picks = [one_hot(lane == plane * 8 + slot)]
    for m in range(3):
        picks.append(one_hot((lane == plane * 8 + 6 + late) & (slot - 3 * late == m)))
    quarter = gathered.shape[1] // 4
    for m, value in enumerate(unpack(picks, jnp.concatenate([x[...] for x in arrived], axis=0))):
        gathered[:, m * quarter : (m + 1) * quarter] = value.astype(BF16)


def collect(token, arrived):
    return pl.pallas_call(
        collect_kernel,
        out_shape=jax.ShapeDtypeStruct((MOST * EXPERTS, arrived[0].shape[1] // 3 * 4), BF16),
        in_specs=[ANY] + [VMEM] * EXPERTS,
        out_specs=VMEM,
        compiler_params=pltpu.CompilerParams(vmem_limit_bytes=2 * MIB),
        name="collect",
    )(token, *arrived)


def join_kernel(*refs):
    out, row = refs[-1], 0
    for piece in refs[1:-1]:
        out[row : row + piece.shape[0]] = piece[...]
        row += piece.shape[0]


def join(after, *pieces):
    rows = sum(piece.shape[0] for piece in pieces)
    return pl.pallas_call(
        join_kernel,
        out_shape=jax.ShapeDtypeStruct((rows, pieces[0].shape[1]), BF16),
        in_specs=[ANY] + [VMEM] * len(pieces),
        out_specs=VMEM,
        compiler_params=pltpu.CompilerParams(vmem_limit_bytes=1 * MIB),
        name="join",
    )(after, *pieces)


def fold_kernel(held, arrived, keep, send):
    half = keep.shape[0]
    keep[...] = held[:half] + arrived[:half].astype(F32)
    send[...] = (held[half:] + arrived[half:].astype(F32)).astype(BF16)


def fold(held, arrived):
    half, width = held.shape[0] // 2, held.shape[1]
    return pl.pallas_call(
        fold_kernel,
        out_shape=(
            jax.ShapeDtypeStruct((half, width), F32),
            jax.ShapeDtypeStruct((half, width), BF16),
        ),
        in_specs=[VMEM] * 2,
        out_specs=(VMEM, VMEM),
        compiler_params=pltpu.CompilerParams(vmem_limit_bytes=4 * MIB * max(1, half // 32)),
        name="fold",
    )(held, arrived)


def last_fold_kernel(held, arrived, *packed):
    block = (held[...] + arrived[...].astype(F32)).astype(BF16)
    place, row = grid((8 * EXPERTS, MOST * EXPERTS))
    plane, slot = place // 8, place % 8
    picks = [one_hot((row == plane * MOST + slot) & (slot < MOST))]
    for m in range(3):
        picks.append(one_hot((row == plane * MOST + 3 * (slot - 6) + m) & (slot >= MOST)))
    quarter = block.shape[1] // 4
    for m, value in enumerate(pack(picks, block)):
        for k, target in enumerate(packed):
            target[:, m * quarter : (m + 1) * quarter] = value[8 * k : 8 * k + 8]


def last_fold(held, arrived):
    return pl.pallas_call(
        last_fold_kernel,
        out_shape=[jax.ShapeDtypeStruct((8, held.shape[1] // 4 * 3), BF16)] * EXPERTS,
        in_specs=[VMEM] * 2,
        out_specs=[VMEM] * EXPERTS,
        compiler_params=pltpu.CompilerParams(vmem_limit_bytes=2 * MIB),
        name="last_fold",
    )(held, arrived)


def combine_kernel(share, take, *refs):
    out = refs[-1]
    results = [refs[p * EXPERTS : (p + 1) * EXPERTS] for p in range(PARTS)]
    rows = out.shape[0]
    quarter = refs[0].shape[1] // 3
    picks = [take[i][:, : 8 * EXPERTS] for i in range(4)]
    shares = share[:, :1]
    for part, result in enumerate(results):
        for m, value in enumerate(unpack(picks, jnp.concatenate([x[...] for x in result], axis=0))):
            value = value * shares
            first = (part * 4 + m) * quarter
            out[:, first : first + quarter] = (value[:rows] + value[rows:]).astype(BF16)


def combine(share, take, results):
    width = results[0].shape[1] // 3 * 4
    return pl.pallas_call(
        combine_kernel,
        out_shape=jax.ShapeDtypeStruct((share.shape[0] // 2, width * PARTS), BF16),
        in_specs=[VMEM] * (2 + len(results)),
        out_specs=VMEM,
        compiler_params=pltpu.CompilerParams(vmem_limit_bytes=2 * MIB),
        name="combine",
    )(share, take, *results)


def between_planes(blocks, count, direction):
    plane = count // EXPERTS
    return [blocks[0]] + [
        lax.ppermute(
            blocks[k], "dp", [(i, (i + direction * k * plane) % count) for i in range(count)]
        )
        for k in range(1, EXPERTS)
    ]


def swap(value, count, bit):
    return lax.ppermute(value, "dp", [(i, i ^ bit) for i in range(count)])


def body(
    queries,
    new_keys,
    new_values,
    cache_keys,
    cache_values,
    lengths,
    residual,
    norm_gain,
    router_weight,
    gate_weight,
    up_weight,
    down_weight,
    routes,
):
    count = lax.axis_size("dp")
    plane = count // EXPERTS
    bits = [1 << k for k in reversed(range(plane.bit_length() - 1))]
    attended, *packed, share, take, down = attend(
        plane, queries, new_keys, new_values, cache_keys, cache_values, lengths, residual, norm_gain,
        router_weight, routes, down_weight,
    )

    gathered = collect(share, between_planes(packed, count, 1))
    down_rest, token = load(down_weight, gathered, down.shape[1])
    for bit in bits:
        gathered = join(token, gathered, swap(gathered, count, bit))

    hidden = hidden_rows(gathered, gate_weight, up_weight)
    results = []
    for weight in (down, down_rest):
        held, send = down_rows(hidden, weight, gathered.shape[0])
        for bit in bits[:0:-1]:
            held, send = fold(held, swap(send, count, bit))
        blocks = last_fold(held, swap(send, count, bits[0]))
        results += between_planes(blocks, count, -1)
    return (attended, combine(share, take, results))


def solution(mesh):
    placed = (
        P(("group", "dp"), None),
        P(("group", "dp"), None),
        P(("group", "dp"), None),
        P(("group", "dp"), None, None),
        P(("group", "dp"), None, None),
        P(("group", "dp")),
        P(("group", "dp"), None),
        P(),
        P(),
        P(None, "dp"),
        P(None, "dp"),
        P("dp", None),
        P("group", None),
    )
    return jax.shard_map(
        body,
        mesh=mesh,
        in_specs=placed,
        out_specs=(P(("group", "dp"), None), P(("group", "dp"), None)),
        check_vma=False,
    )
```

```python
import functools

import jax
import jax.numpy as jnp
from jax import lax
from jax.experimental import pallas as pl
from jax.experimental.pallas import tpu as pltpu
from jax.sharding import PartitionSpec as P

HEADS = 32
KV_HEADS = 8
HEAD_DIM = 128
EXPERTS = 4
MIB = 1 << 20
WAYS = 4
PARTS = 2
MOST = 6
F32 = jnp.float32
BF16 = jnp.bfloat16
VMEM = pl.BlockSpec(memory_space=pltpu.VMEM)
ANY = pl.BlockSpec(memory_space=pl.ANY)


def dot(a, b, contract_last=False):
    dims = (((1,), (1 if contract_last else 0,)), ((), ()))
    return lax.dot_general(a, b, dims, preferred_element_type=F32)


def weight_copies(source, target, semaphores, first=0):
    step, columns = source.shape[0] // WAYS, target.shape[1]
    return [
        pltpu.make_async_copy(
            source.at[pl.ds(i * step, step), pl.ds(first, columns)],
            target.at[pl.ds(i * step, step)],
            semaphores.at[i],
        )
        for i in range(WAYS)
    ]


def one_hot(mask):
    return mask.astype(F32).astype(BF16)


def grid(shape):
    return [lax.broadcasted_iota(jnp.int32, shape, axis) for axis in (0, 1)]


def pack(picks, block):
    quarter = block.shape[1] // 4
    parts = [block[:, m * quarter : (m + 1) * quarter] for m in range(4)]
    return [
        (dot(picks[0], parts[m]) + dot(picks[1 + m], parts[3])).astype(BF16) for m in range(3)
    ]


def unpack(picks, block):
    quarter = block.shape[1] // 3
    parts = [block[:, m * quarter : (m + 1) * quarter] for m in range(3)]
    tail = dot(picks[1], parts[0]) + dot(picks[2], parts[1]) + dot(picks[3], parts[2])
    return [dot(picks[0], part) for part in parts] + [tail]


def attend_kernel(plane, *refs):
    sources, attended, packed, (share, take), held, semaphores = (
        refs[:10], refs[11], refs[12:16], refs[16:18], refs[19:29], refs[29]
    )
    weight = weight_copies(refs[10], refs[18], refs[30])
    copies = [
        pltpu.make_async_copy(source, target, semaphores.at[i])
        for i, (source, target) in enumerate(zip(sources, held))
    ]
    for copy in copies + weight:
        copy.start()
    (queries, cache_keys, new_keys, lengths, cache_values, new_values, residual, gain, router,
     routes) = held
    for copy in copies[:4] + copies[9:]:
        copy.wait()
    rows, width = queries.shape
    positions = cache_keys.shape[1]
    groups = HEADS // KV_HEADS
    scale = 1.0 / HEAD_DIM**0.5
    every = rows * positions
    block = groups * rows

    query = queries[...].astype(F32)
    stacked = jnp.concatenate(
        [query[:, h * HEAD_DIM : (h + 1) * HEAD_DIM] for h in range(HEADS)], axis=0
    )
    stacked_b = stacked.astype(BF16)
    keys = cache_keys[...].reshape(every, KV_HEADS * HEAD_DIM)
    newk = new_keys[...].astype(F32)

    row_of = lax.broadcasted_iota(jnp.int32, (block, every), 0) % rows
    column = lax.broadcasted_iota(jnp.int32, (block, every), 1)
    position = column % positions
    column_row = column // positions
    limit = jnp.zeros((block, every), jnp.int32)
    for r in range(rows):
        limit = jnp.where(column_row == r, lengths[r], limit)
    valid = (row_of == column_row) & (position < limit)

    heads = range(KV_HEADS)
    lanes = [slice(g * HEAD_DIM, (g + 1) * HEAD_DIM) for g in heads]
    mine = [slice(g * block, (g + 1) * block) for g in heads]
    scores = [dot(stacked_b[mine[g]], keys[:, lanes[g]], contract_last=True) for g in heads]
    scores = [jnp.where(valid, score * scale, -jnp.inf) for score in scores]
    own_keys = [jnp.concatenate([newk[:, lanes[g]]] * groups, axis=0) for g in heads]
    new_scores = [
        jnp.sum(stacked[mine[g]] * own_keys[g], axis=1, keepdims=True) * scale for g in heads
    ]
    peaks = [
        jnp.maximum(jnp.max(score, axis=1, keepdims=True), new)
        for score, new in zip(scores, new_scores)
    ]
    weights = [jnp.exp(score - peak) for score, peak in zip(scores, peaks)]
    new_weights = [jnp.exp(new - peak) for new, peak in zip(new_scores, peaks)]
    totals = [
        jnp.sum(weight, axis=1, keepdims=True) + new
        for weight, new in zip(weights, new_weights)
    ]
    probs = [(weight / total).astype(BF16) for weight, total in zip(weights, totals)]
    new_probs = [
        (new / total).astype(BF16).astype(F32) for new, total in zip(new_weights, totals)
    ]
    for copy in copies[4:9]:
        copy.wait()
    values = cache_values[...].reshape(every, KV_HEADS * HEAD_DIM)
    newv = new_values[...].astype(F32)
    mixed = [
        dot(probs[g], values[:, lanes[g]])
        + new_probs[g] * jnp.concatenate([newv[:, lanes[g]]] * groups, axis=0)
        for g in heads
    ]
    pieces = [value[j * rows : (j + 1) * rows] for value in mixed for j in range(groups)]

    states = (residual[...].astype(F32) + jnp.concatenate(pieces, axis=1)).astype(BF16)
    attended[...] = states
    states = states.astype(F32)
    norm = lax.rsqrt(jnp.mean(states * states, axis=1, keepdims=True) + 1e-05)
    gains = gain[...].astype(F32)
    logits = [jnp.zeros((rows, 128), F32) for _ in range(EXPERTS)]
    parts = []
    for c in range(width // 128):
        lanes = slice(c * 128, (c + 1) * 128)
        part = (states[:, lanes] * norm * gains[c : c + 1]).astype(BF16).astype(F32)
        parts.append(part)
        for e in range(EXPERTS):
            logits[e] += part * router[e : e + 1, lanes].astype(F32)
    logits = [jnp.sum(value, axis=1, keepdims=True) for value in logits]

    index = lax.axis_index("dp")
    base = index * rows
    own = index // plane
    sub, lane = grid((2 * rows, 128))
    expert_down = jnp.zeros((2 * rows, 128), jnp.int32)
    slot_down = jnp.zeros((2 * rows, 128), jnp.int32)
    across = lax.broadcasted_iota(jnp.int32, (8, 128), 1)
    expert_across = jnp.zeros((8, 128), jnp.int32)
    slot_across = jnp.zeros((8, 128), jnp.int32)
    counts = [jnp.int32(0)] * EXPERTS
    for r in range(rows):
        names = [routes[c, base + r] ^ own for c in range(2)]
        for choice, name in ((r, names[0]), (rows + r, names[1])):
            slot = jnp.int32(0)
            for e in range(EXPERTS):
                slot = jnp.where(name == e, counts[e], slot)
            expert_down = jnp.where(sub == choice, name, expert_down)
            slot_down = jnp.where(sub == choice, slot, slot_down)
            expert_across = jnp.where(across == choice, name, expert_across)
            slot_across = jnp.where(across == choice, slot, slot_across)
        for e in range(EXPERTS):
            named = (names[0] == e) | (names[1] == e)
            counts[e] = counts[e] + jnp.where(named, 1, 0)

    late = jnp.where(slot_down >= 3, 1, 0)
    take[0] = one_hot(lane == expert_down * 8 + slot_down)
    for m in range(3):
        take[1 + m] = one_hot((lane == expert_down * 8 + 6 + late) & (slot_down - 3 * late == m))
    place, choice = grid((8 * EXPERTS, 128))
    expert, slot = expert_across[0:1], slot_across[0:1]
    late = jnp.where(slot >= 3, 1, 0)
    chosen = choice < 2 * rows
    picks = [one_hot((place == expert * 8 + slot) & chosen)]
    for m in range(3):
        picks.append(one_hot((place == expert * 8 + 6 + late) & (slot - 3 * late == m) & chosen))
    normed = jnp.concatenate(parts, axis=1)
    normed = jnp.concatenate([normed, normed], axis=0).astype(BF16)
    quarter = width // 4
    for m, value in enumerate(pack([pick[:, : 2 * rows] for pick in picks], normed)):
        for k, target in enumerate(packed):
            target[:, m * quarter : (m + 1) * quarter] = value[8 * k : 8 * k + 8]

    chosen_logits = jnp.zeros((2 * rows, 1), F32)
    for e in range(EXPERTS):
        both = jnp.concatenate([logits[e], logits[e]], axis=0)
        chosen_logits = jnp.where(expert_down[:, :1] == (own ^ e), both, chosen_logits)
    other = jnp.concatenate([chosen_logits[rows:], chosen_logits[:rows]], axis=0)
    share[...] = jnp.broadcast_to(1.0 / (1.0 + jnp.exp(other - chosen_logits)), share.shape)
    for copy in weight:
        copy.wait()


def attend(plane, queries, new_keys, new_values, cache_keys, cache_values, lengths, residual,
           norm_gain, router_weight, routes, weight):
    rows, width = queries.shape
    operands = (
        queries,
        cache_keys,
        new_keys,
        lengths,
        cache_values,
        new_values,
        residual,
        norm_gain.reshape(-1, 128),
        router_weight.T,
        routes.T,
    )
    in_smem = (3, 9)
    return pl.pallas_call(
        functools.partial(attend_kernel, plane),
        out_shape=(
            jax.ShapeDtypeStruct((rows, width), BF16),
            *[jax.ShapeDtypeStruct((8, width * 3 // 4), BF16)] * EXPERTS,
            jax.ShapeDtypeStruct((2 * rows, 128), F32),
            jax.ShapeDtypeStruct((4, 2 * rows, 128), BF16),
            pltpu.VMEM((weight.shape[0], weight.shape[1] // PARTS), weight.dtype),
        ),
        in_specs=[ANY] * (len(operands) + 1),
        out_specs=(VMEM,) * (4 + EXPERTS),
        scratch_shapes=[
            (pltpu.SMEM if i in in_smem else pltpu.VMEM)(operand.shape, operand.dtype)
            for i, operand in enumerate(operands)
        ]
        + [pltpu.SemaphoreType.DMA((len(operands),)), pltpu.SemaphoreType.DMA((WAYS,))],
        compiler_params=pltpu.CompilerParams(vmem_limit_bytes=5 * MIB),
        name="attend",
    )(*[pltpu.with_memory_space_constraint(x, pltpu.HBM) for x in (*operands, weight)])


def hidden_kernel(inputs, gate_weight, up_weight, hidden):
    columns = gate_weight.shape[1]
    step = 256 if columns % 256 == 0 else columns
    x = padded(inputs[...])
    for f in range(0, columns, step):
        gate = dot(x, gate_weight[:, f : f + step])
        upper = dot(x, up_weight[:, f : f + step])
        hidden[:, f : f + step] = (gate / (1.0 + jnp.exp(-gate)) * upper).astype(BF16)


def padded(x):
    extra = -x.shape[0] % 128
    if extra == 0:
        return x
    return jnp.concatenate([x, jnp.zeros((extra, x.shape[1]), x.dtype)], axis=0)


def hidden_rows(inputs, gate_weight, up_weight):
    rows, width = inputs.shape
    columns = gate_weight.shape[1]
    return pl.pallas_call(
        hidden_kernel,
        out_shape=jax.ShapeDtypeStruct((rows + -rows % 128, columns), BF16),
        in_specs=[VMEM] * 3,
        out_specs=VMEM,
        compiler_params=pltpu.CompilerParams(vmem_limit_bytes=4 * MIB * max(1, rows // 128)),
        cost_estimate=pl.CostEstimate(
            flops=4 * rows * width * columns, bytes_accessed=0, transcendentals=rows * columns
        ),
        name="hidden",
    )(inputs, gate_weight, up_weight)


def down_kernel(hidden, *refs):
    weights, (keep, send) = refs[:PARTS], refs[PARTS:]
    half = keep.shape[0]
    h = hidden[...]
    first = 0
    for weight in weights:
        for n in range(0, weight.shape[1], 512):
            terms = dot(h, weight[:, n : n + 512])
            keep[:, first : first + 512] = terms[:half]
            send[:, first : first + 512] = terms[half : 2 * half].astype(BF16)
            first += 512


def down_rows(hidden, weights, rows):
    columns = hidden.shape[1]
    half, width = rows // 2, sum(weight.shape[1] for weight in weights)
    return pl.pallas_call(
        down_kernel,
        out_shape=(
            jax.ShapeDtypeStruct((half, width), F32),
            jax.ShapeDtypeStruct((half, width), BF16),
        ),
        in_specs=[VMEM] * (1 + PARTS),
        out_specs=(VMEM, VMEM),
        compiler_params=pltpu.CompilerParams(vmem_limit_bytes=4 * MIB * max(1, rows // 128)),
        cost_estimate=pl.CostEstimate(
            flops=2 * rows * width * columns, bytes_accessed=0, transcendentals=0
        ),
        name="down",
    )(hidden, *weights)


def load_kernel(first, source, after, target, token, semaphores):
    copies = weight_copies(source, target, semaphores, first)
    for copy in copies:
        copy.start()
    token[...] = jnp.zeros(token.shape, token.dtype)
    for copy in copies:
        copy.wait()


def load(source, after, first=0):
    shape = (source.shape[0], source.shape[1] - first)
    return pl.pallas_call(
        functools.partial(load_kernel, first),
        out_shape=(
            pltpu.VMEM(shape, source.dtype),
            jax.ShapeDtypeStruct((8, 128), F32),
        ),
        in_specs=[ANY, ANY],
        out_specs=(VMEM, VMEM),
        scratch_shapes=[pltpu.SemaphoreType.DMA((WAYS,))],
        compiler_params=pltpu.CompilerParams(vmem_limit_bytes=MIB),
        cost_estimate=pl.CostEstimate(
            flops=0, bytes_accessed=2 * shape[0] * shape[1], transcendentals=0
        ),
        name="load",
    )(pltpu.with_memory_space_constraint(source, pltpu.HBM), after)


def collect_kernel(token, *refs):
    arrived, gathered = refs[:-1], refs[-1]
    row, lane = grid((MOST * EXPERTS, 8 * EXPERTS))
    plane = sum([jnp.where(row >= MOST * e, 1, 0) for e in range(1, EXPERTS)])
    slot = row - MOST * plane
    late = jnp.where(slot >= 3, 1, 0)
    picks = [one_hot(lane == plane * 8 + slot)]
    for m in range(3):
        picks.append(one_hot((lane == plane * 8 + 6 + late) & (slot - 3 * late == m)))
    quarter = gathered.shape[1] // 4
    for m, value in enumerate(unpack(picks, jnp.concatenate([x[...] for x in arrived], axis=0))):
        gathered[:, m * quarter : (m + 1) * quarter] = value.astype(BF16)


def collect(token, arrived):
    return pl.pallas_call(
        collect_kernel,
        out_shape=jax.ShapeDtypeStruct((MOST * EXPERTS, arrived[0].shape[1] // 3 * 4), BF16),
        in_specs=[ANY] + [VMEM] * EXPERTS,
        out_specs=VMEM,
        compiler_params=pltpu.CompilerParams(vmem_limit_bytes=2 * MIB),
        name="collect",
    )(token, *arrived)


def join_kernel(*refs):
    out, row = refs[-1], 0
    for piece in refs[1:-1]:
        out[row : row + piece.shape[0]] = piece[...]
        row += piece.shape[0]


def join(after, *pieces):
    rows = sum(piece.shape[0] for piece in pieces)
    return pl.pallas_call(
        join_kernel,
        out_shape=jax.ShapeDtypeStruct((rows, pieces[0].shape[1]), BF16),
        in_specs=[ANY] + [VMEM] * len(pieces),
        out_specs=VMEM,
        compiler_params=pltpu.CompilerParams(vmem_limit_bytes=1 * MIB),
        name="join",
    )(after, *pieces)


def fold_kernel(held, arrived, keep, send):
    half = keep.shape[0]
    keep[...] = held[:half] + arrived[:half].astype(F32)
    send[...] = (held[half:] + arrived[half:].astype(F32)).astype(BF16)


def fold(held, arrived):
    half, width = held.shape[0] // 2, held.shape[1]
    return pl.pallas_call(
        fold_kernel,
        out_shape=(
            jax.ShapeDtypeStruct((half, width), F32),
            jax.ShapeDtypeStruct((half, width), BF16),
        ),
        in_specs=[VMEM] * 2,
        out_specs=(VMEM, VMEM),
        compiler_params=pltpu.CompilerParams(vmem_limit_bytes=4 * MIB * max(1, half // 32)),
        name="fold",
    )(held, arrived)


def last_fold_kernel(held, arrived, *packed):
    block = (held[...] + arrived[...].astype(F32)).astype(BF16)
    place, row = grid((8 * EXPERTS, MOST * EXPERTS))
    plane, slot = place // 8, place % 8
    picks = [one_hot((row == plane * MOST + slot) & (slot < MOST))]
    for m in range(3):
        picks.append(one_hot((row == plane * MOST + 3 * (slot - 6) + m) & (slot >= MOST)))
    quarter = block.shape[1] // 4
    for m, value in enumerate(pack(picks, block)):
        for k, target in enumerate(packed):
            target[:, m * quarter : (m + 1) * quarter] = value[8 * k : 8 * k + 8]


def last_fold(held, arrived):
    return pl.pallas_call(
        last_fold_kernel,
        out_shape=[jax.ShapeDtypeStruct((8, held.shape[1] // 4 * 3), BF16)] * EXPERTS,
        in_specs=[VMEM] * 2,
        out_specs=[VMEM] * EXPERTS,
        compiler_params=pltpu.CompilerParams(vmem_limit_bytes=2 * MIB),
        name="last_fold",
    )(held, arrived)


def combine_kernel(share, take, *refs):
    results, out = refs[:-1], refs[-1]
    rows = out.shape[0]
    quarter = results[0].shape[1] // 3
    picks = [take[i][:, : 8 * EXPERTS] for i in range(4)]
    shares = share[:, :1]
    block = jnp.concatenate([x[...] for x in results], axis=0)
    for m, value in enumerate(unpack(picks, block)):
        value = value * shares
        out[:, m * quarter : (m + 1) * quarter] = (value[:rows] + value[rows:]).astype(BF16)


def combine(share, take, results):
    return pl.pallas_call(
        combine_kernel,
        out_shape=jax.ShapeDtypeStruct((share.shape[0] // 2, results[0].shape[1] // 3 * 4), BF16),
        in_specs=[VMEM] * (2 + EXPERTS),
        out_specs=VMEM,
        compiler_params=pltpu.CompilerParams(vmem_limit_bytes=2 * MIB),
        name="combine",
    )(share, take, *results)


def between_planes(blocks, count):
    plane = count // EXPERTS
    return [blocks[0]] + [swap(blocks[k], count, k * plane) for k in range(1, EXPERTS)]


def swap(value, count, bit):
    return lax.ppermute(value, "dp", [(i, i ^ bit) for i in range(count)])


def body(
    queries,
    new_keys,
    new_values,
    cache_keys,
    cache_values,
    lengths,
    residual,
    norm_gain,
    router_weight,
    gate_weight,
    up_weight,
    down_weight,
    routes,
):
    count = lax.axis_size("dp")
    plane = count // EXPERTS
    bits = [1 << k for k in reversed(range(plane.bit_length() - 1))]
    attended, *packed, share, take, down = attend(
        plane, queries, new_keys, new_values, cache_keys, cache_values, lengths, residual, norm_gain,
        router_weight, routes, down_weight,
    )

    gathered = collect(share, between_planes(packed, count))
    down_rest, token = load(down_weight, gathered, down.shape[1])
    for bit in bits:
        gathered = join(token, gathered, swap(gathered, count, bit))

    hidden = hidden_rows(gathered, gate_weight, up_weight)
    held, send = down_rows(hidden, (down, down_rest), gathered.shape[0])
    for bit in bits[:0:-1]:
        held, send = fold(held, swap(send, count, bit))
    results = between_planes(last_fold(held, swap(send, count, bits[0])), count)
    return (attended, combine(share, take, results))


def solution(mesh):
    placed = (
        P(("group", "dp"), None),
        P(("group", "dp"), None),
        P(("group", "dp"), None),
        P(("group", "dp"), None, None),
        P(("group", "dp"), None, None),
        P(("group", "dp")),
        P(("group", "dp"), None),
        P(),
        P(),
        P(None, "dp"),
        P(None, "dp"),
        P("dp", None),
        P("group", None),
    )
    return jax.shard_map(
        body,
        mesh=mesh,
        in_specs=placed,
        out_specs=(P(("group", "dp"), None), P(("group", "dp"), None)),
        check_vma=False,
    )
```

```python
import functools

import jax
import jax.numpy as jnp
from jax import lax
from jax.experimental import pallas as pl
from jax.experimental.pallas import tpu as pltpu
from jax.sharding import PartitionSpec as P

HEADS = 32
KV_HEADS = 8
HEAD_DIM = 128
EXPERTS = 4
MIB = 1 << 20
WAYS = 4
PARTS = 2
MOST = 6
F32 = jnp.float32
BF16 = jnp.bfloat16
VMEM = pl.BlockSpec(memory_space=pltpu.VMEM)
ANY = pl.BlockSpec(memory_space=pl.ANY)


def dot(a, b, contract_last=False):
    dims = (((1,), (1 if contract_last else 0,)), ((), ()))
    return lax.dot_general(a, b, dims, preferred_element_type=F32)


def weight_copies(source, target, semaphores, first=0):
    step, columns = source.shape[0] // WAYS, target.shape[1]
    return [
        pltpu.make_async_copy(
            source.at[pl.ds(i * step, step), pl.ds(first, columns)],
            target.at[pl.ds(i * step, step)],
            semaphores.at[i],
        )
        for i in range(WAYS)
    ]


def one_hot(mask):
    return mask.astype(F32).astype(BF16)


def grid(shape):
    return [lax.broadcasted_iota(jnp.int32, shape, axis) for axis in (0, 1)]


def pack(picks, block):
    quarter = block.shape[1] // 4
    parts = [block[:, m * quarter : (m + 1) * quarter] for m in range(4)]
    return [
        (dot(picks[0], parts[m]) + dot(picks[1 + m], parts[3])).astype(BF16) for m in range(3)
    ]


def unpack(picks, block):
    quarter = block.shape[1] // 3
    parts = [block[:, m * quarter : (m + 1) * quarter] for m in range(3)]
    tail = dot(picks[1], parts[0]) + dot(picks[2], parts[1]) + dot(picks[3], parts[2])
    return [dot(picks[0], part) for part in parts] + [tail]


def attend_kernel(plane, *refs):
    sources, attended, packed, (share, take), held, semaphores = (
        refs[:10], refs[11], refs[12:16], refs[16:18], refs[19:29], refs[29]
    )
    weight = weight_copies(refs[10], refs[18], refs[30])
    copies = [
        pltpu.make_async_copy(source, target, semaphores.at[i])
        for i, (source, target) in enumerate(zip(sources, held))
    ]
    for copy in copies + weight:
        copy.start()
    (queries, cache_keys, new_keys, lengths, cache_values, new_values, residual, gain, router,
     routes) = held
    for copy in copies[:4] + copies[9:]:
        copy.wait()
    rows, width = queries.shape
    positions = cache_keys.shape[1]
    groups = HEADS // KV_HEADS
    scale = 1.0 / HEAD_DIM**0.5
    every = rows * positions
    block = groups * rows

    query = queries[...].astype(F32)
    stacked = jnp.concatenate(
        [query[:, h * HEAD_DIM : (h + 1) * HEAD_DIM] for h in range(HEADS)], axis=0
    )
    stacked_b = stacked.astype(BF16)
    keys = cache_keys[...].reshape(every, KV_HEADS * HEAD_DIM)
    newk = new_keys[...].astype(F32)

    row_of = lax.broadcasted_iota(jnp.int32, (block, every), 0) % rows
    column = lax.broadcasted_iota(jnp.int32, (block, every), 1)
    position = column % positions
    column_row = column // positions
    limit = jnp.zeros((block, every), jnp.int32)
    for r in range(rows):
        limit = jnp.where(column_row == r, lengths[r], limit)
    valid = (row_of == column_row) & (position < limit)

    heads = range(KV_HEADS)
    lanes = [slice(g * HEAD_DIM, (g + 1) * HEAD_DIM) for g in heads]
    mine = [slice(g * block, (g + 1) * block) for g in heads]
    scores = [dot(stacked_b[mine[g]], keys[:, lanes[g]], contract_last=True) for g in heads]
    scores = [jnp.where(valid, score * scale, -jnp.inf) for score in scores]
    own_keys = [jnp.concatenate([newk[:, lanes[g]]] * groups, axis=0) for g in heads]
    new_scores = [
        jnp.sum(stacked[mine[g]] * own_keys[g], axis=1, keepdims=True) * scale for g in heads
    ]
    peaks = [
        jnp.maximum(jnp.max(score, axis=1, keepdims=True), new)
        for score, new in zip(scores, new_scores)
    ]
    weights = [jnp.exp(score - peak) for score, peak in zip(scores, peaks)]
    new_weights = [jnp.exp(new - peak) for new, peak in zip(new_scores, peaks)]
    totals = [
        jnp.sum(weight, axis=1, keepdims=True) + new
        for weight, new in zip(weights, new_weights)
    ]
    probs = [(weight / total).astype(BF16) for weight, total in zip(weights, totals)]
    new_probs = [
        (new / total).astype(BF16).astype(F32) for new, total in zip(new_weights, totals)
    ]
    for copy in copies[4:9]:
        copy.wait()
    values = cache_values[...].reshape(every, KV_HEADS * HEAD_DIM)
    newv = new_values[...].astype(F32)
    mixed = [
        dot(probs[g], values[:, lanes[g]])
        + new_probs[g] * jnp.concatenate([newv[:, lanes[g]]] * groups, axis=0)
        for g in heads
    ]
    pieces = [value[j * rows : (j + 1) * rows] for value in mixed for j in range(groups)]

    states = (residual[...].astype(F32) + jnp.concatenate(pieces, axis=1)).astype(BF16)
    attended[...] = states
    states = states.astype(F32)
    norm = lax.rsqrt(jnp.mean(states * states, axis=1, keepdims=True) + 1e-05)
    gains = gain[...].astype(F32)
    logits = [jnp.zeros((rows, 128), F32) for _ in range(EXPERTS)]
    parts = []
    for c in range(width // 128):
        lanes = slice(c * 128, (c + 1) * 128)
        part = (states[:, lanes] * norm * gains[c : c + 1]).astype(BF16).astype(F32)
        parts.append(part)
        for e in range(EXPERTS):
            logits[e] += part * router[e : e + 1, lanes].astype(F32)
    logits = [jnp.sum(value, axis=1, keepdims=True) for value in logits]

    index = lax.axis_index("dp")
    base = index * rows
    own = index // plane
    sub, lane = grid((2 * rows, 128))
    expert_down = jnp.zeros((2 * rows, 128), jnp.int32)
    slot_down = jnp.zeros((2 * rows, 128), jnp.int32)
    across = lax.broadcasted_iota(jnp.int32, (8, 128), 1)
    expert_across = jnp.zeros((8, 128), jnp.int32)
    slot_across = jnp.zeros((8, 128), jnp.int32)
    counts = [jnp.int32(0)] * EXPERTS
    for r in range(rows):
        names = [routes[c, base + r] ^ own for c in range(2)]
        for choice, name in ((r, names[0]), (rows + r, names[1])):
            slot = jnp.int32(0)
            for e in range(EXPERTS):
                slot = jnp.where(name == e, counts[e], slot)
            expert_down = jnp.where(sub == choice, name, expert_down)
            slot_down = jnp.where(sub == choice, slot, slot_down)
            expert_across = jnp.where(across == choice, name, expert_across)
            slot_across = jnp.where(across == choice, slot, slot_across)
        for e in range(EXPERTS):
            named = (names[0] == e) | (names[1] == e)
            counts[e] = counts[e] + jnp.where(named, 1, 0)

    late = jnp.where(slot_down >= 3, 1, 0)
    take[0] = one_hot(lane == expert_down * 8 + slot_down)
    for m in range(3):
        take[1 + m] = one_hot((lane == expert_down * 8 + 6 + late) & (slot_down - 3 * late == m))
    place, choice = grid((8 * EXPERTS, 128))
    expert, slot = expert_across[0:1], slot_across[0:1]
    late = jnp.where(slot >= 3, 1, 0)
    chosen = choice < 2 * rows
    picks = [one_hot((place == expert * 8 + slot) & chosen)]
    for m in range(3):
        picks.append(one_hot((place == expert * 8 + 6 + late) & (slot - 3 * late == m) & chosen))
    normed = jnp.concatenate(parts, axis=1)
    normed = jnp.concatenate([normed, normed], axis=0).astype(BF16)
    quarter = width // 4
    for m, value in enumerate(pack([pick[:, : 2 * rows] for pick in picks], normed)):
        for k, target in enumerate(packed):
            target[:, m * quarter : (m + 1) * quarter] = value[8 * k : 8 * k + 8]

    chosen_logits = jnp.zeros((2 * rows, 1), F32)
    for e in range(EXPERTS):
        both = jnp.concatenate([logits[e], logits[e]], axis=0)
        chosen_logits = jnp.where(expert_down[:, :1] == (own ^ e), both, chosen_logits)
    other = jnp.concatenate([chosen_logits[rows:], chosen_logits[:rows]], axis=0)
    share[...] = jnp.broadcast_to(1.0 / (1.0 + jnp.exp(other - chosen_logits)), share.shape)
    for copy in weight:
        copy.wait()


def attend(plane, queries, new_keys, new_values, cache_keys, cache_values, lengths, residual,
           norm_gain, router_weight, routes, weight):
    rows, width = queries.shape
    operands = (
        queries,
        cache_keys,
        new_keys,
        lengths,
        cache_values,
        new_values,
        residual,
        norm_gain.reshape(-1, 128),
        router_weight.T,
        routes.T,
    )
    in_smem = (3, 9)
    return pl.pallas_call(
        functools.partial(attend_kernel, plane),
        out_shape=(
            jax.ShapeDtypeStruct((rows, width), BF16),
            *[jax.ShapeDtypeStruct((8, width * 3 // 4), BF16)] * EXPERTS,
            jax.ShapeDtypeStruct((2 * rows, 128), F32),
            jax.ShapeDtypeStruct((4, 2 * rows, 128), BF16),
            pltpu.VMEM((weight.shape[0], weight.shape[1] // PARTS), weight.dtype),
        ),
        in_specs=[ANY] * (len(operands) + 1),
        out_specs=(VMEM,) * (4 + EXPERTS),
        scratch_shapes=[
            (pltpu.SMEM if i in in_smem else pltpu.VMEM)(operand.shape, operand.dtype)
            for i, operand in enumerate(operands)
        ]
        + [pltpu.SemaphoreType.DMA((len(operands),)), pltpu.SemaphoreType.DMA((WAYS,))],
        compiler_params=pltpu.CompilerParams(vmem_limit_bytes=5 * MIB),
        name="attend",
    )(*[pltpu.with_memory_space_constraint(x, pltpu.HBM) for x in (*operands, weight)])


def hidden_kernel(near, far, gate_weight, up_weight, hidden):
    columns = gate_weight.shape[1]
    step = 256 if columns % 256 == 0 else columns
    quarter = near.shape[1] // 3
    blocks = jnp.concatenate([near[...], far[...]], axis=0)
    size = 128
    row, lane = grid((size, size))
    slot = row & 7
    late = jnp.where(slot >= 3, 1, 0)
    picks = [
        one_hot((lane == row - slot + 6 + late) & (slot - 3 * late == m)) for m in range(3)
    ]
    tails = []
    for first in range(0, blocks.shape[0], size):
        some = blocks[first : first + size]
        parts = [dot(picks[m], some[:, m * quarter : (m + 1) * quarter]) for m in range(3)]
        tails.append((parts[0] + parts[1] + parts[2]).astype(BF16))
    x = jnp.concatenate([blocks, jnp.concatenate(tails, axis=0)], axis=1)
    for f in range(0, columns, step):
        gate = dot(x, gate_weight[:, f : f + step])
        upper = dot(x, up_weight[:, f : f + step])
        hidden[:, f : f + step] = (gate / (1.0 + jnp.exp(-gate)) * upper).astype(BF16)


def hidden_rows(near, far, gate_weight, up_weight):
    rows = near.shape[0] + far.shape[0]
    width, columns = gate_weight.shape
    return pl.pallas_call(
        hidden_kernel,
        out_shape=jax.ShapeDtypeStruct((rows, columns), BF16),
        in_specs=[VMEM] * 4,
        out_specs=VMEM,
        compiler_params=pltpu.CompilerParams(vmem_limit_bytes=4 * MIB * max(1, rows // 128)),
        cost_estimate=pl.CostEstimate(
            flops=4 * rows * width * columns, bytes_accessed=0, transcendentals=rows * columns
        ),
        name="hidden",
    )(near, far, gate_weight, up_weight)


def down_kernel(hidden, *refs):
    weights, outs = refs[:PARTS], refs[PARTS:]
    rows = hidden.shape[0]
    quarter = outs[0].shape[1] // 3
    size = 128
    row, lane = grid((size, size))
    slot = row & 7
    picks = [one_hot((lane == row - slot + 3 * (slot - 6) + m) & (slot >= MOST)) for m in range(3)]
    h = hidden[...]

    def terms(first, count):
        part, first = divmod(first, weights[0].shape[1])
        return dot(h, weights[part][:, first : first + count])

    step = min(512, quarter)
    is_row = (lax.broadcasted_iota(jnp.int32, (rows, step), 0) & 7) < MOST
    each = rows // len(outs)
    for n in range(0, quarter, step):
        tail = terms(3 * quarter + n, step).astype(BF16)
        for m in range(3):
            moved = jnp.concatenate(
                [dot(picks[m], tail[i : i + size]) for i in range(0, rows, size)], axis=0
            )
            value = jnp.where(is_row, terms(m * quarter + n, step), moved).astype(BF16)
            for k, out in enumerate(outs):
                out[:, m * quarter + n : m * quarter + n + step] = value[k * each : (k + 1) * each]


def down_rows(hidden, weights):
    rows, columns = hidden.shape
    width = sum(weight.shape[1] for weight in weights)
    return pl.pallas_call(
        down_kernel,
        out_shape=[jax.ShapeDtypeStruct((rows // 4, width // 4 * 3), BF16)] * 4,
        in_specs=[VMEM] * (1 + PARTS),
        out_specs=[VMEM] * 4,
        compiler_params=pltpu.CompilerParams(vmem_limit_bytes=4 * MIB * max(1, rows // 128)),
        cost_estimate=pl.CostEstimate(
            flops=2 * rows * width * columns, bytes_accessed=0, transcendentals=0
        ),
        name="down",
    )(hidden, *weights)


def load_kernel(first, source, after, target, token, semaphores):
    copies = weight_copies(source, target, semaphores, first)
    for copy in copies:
        copy.start()
    token[...] = jnp.zeros(token.shape, token.dtype)
    for copy in copies:
        copy.wait()


def load(source, after, first=0):
    shape = (source.shape[0], source.shape[1] - first)
    return pl.pallas_call(
        functools.partial(load_kernel, first),
        out_shape=(
            pltpu.VMEM(shape, source.dtype),
            jax.ShapeDtypeStruct((8, 128), F32),
        ),
        in_specs=[ANY, ANY],
        out_specs=(VMEM, VMEM),
        scratch_shapes=[pltpu.SemaphoreType.DMA((WAYS,))],
        compiler_params=pltpu.CompilerParams(vmem_limit_bytes=MIB),
        cost_estimate=pl.CostEstimate(
            flops=0, bytes_accessed=2 * shape[0] * shape[1], transcendentals=0
        ),
        name="load",
    )(pltpu.with_memory_space_constraint(source, pltpu.HBM), after)


def join_kernel(*refs):
    out, row = refs[-1], 0
    for piece in refs[1:-1]:
        out[row : row + piece.shape[0]] = piece[...]
        row += piece.shape[0]


def join(after, *pieces):
    rows = sum(piece.shape[0] for piece in pieces)
    return pl.pallas_call(
        join_kernel,
        out_shape=jax.ShapeDtypeStruct((rows, pieces[0].shape[1]), BF16),
        in_specs=[ANY] + [VMEM] * len(pieces),
        out_specs=VMEM,
        compiler_params=pltpu.CompilerParams(vmem_limit_bytes=1 * MIB),
        name="join",
    )(after, *pieces)


def fold_kernel(held, arrived, after, *outs):
    each = outs[0].shape[0]
    for k, out in enumerate(outs):
        block = slice(k * each, (k + 1) * each)
        out[...] = (held[block].astype(F32) + arrived[block].astype(F32)).astype(BF16)


def fold(held, arrived, after):
    rows, width = held.shape
    return pl.pallas_call(
        fold_kernel,
        out_shape=[jax.ShapeDtypeStruct((rows // 2, width), BF16)] * 2,
        in_specs=[VMEM] * 2 + [ANY],
        out_specs=[VMEM] * 2,
        compiler_params=pltpu.CompilerParams(vmem_limit_bytes=MIB * max(1, rows // 64)),
        cost_estimate=pl.CostEstimate(flops=0, bytes_accessed=16 * MIB, transcendentals=0),
        name="fold",
    )(held, arrived, after)


def combine_kernel(first, share, take, *refs):
    results, before, out = refs[:2], refs[2:-1], refs[-1]
    rows = out.shape[0]
    quarter = results[0].shape[1] // 3
    picks = [take[i][:, 8 * first : 8 * first + 16] for i in range(4)]
    shares = share[:, :1]
    block = jnp.concatenate([x[...] for x in results], axis=0)
    for m, value in enumerate(unpack(picks, block)):
        lanes = slice(m * quarter, (m + 1) * quarter)
        value = value * shares
        value = value[:rows] + value[rows:]
        for x in before:
            value = value + x[:, lanes]
        out[:, lanes] = value.astype(out.dtype)


def combine(first, share, take, results, before, dtype):
    width = results[0].shape[1] // 3 * 4
    return pl.pallas_call(
        functools.partial(combine_kernel, first),
        out_shape=jax.ShapeDtypeStruct((share.shape[0] // 2, width), dtype),
        in_specs=[VMEM] * (4 + len(before)),
        out_specs=VMEM,
        compiler_params=pltpu.CompilerParams(vmem_limit_bytes=2 * MIB),
        cost_estimate=pl.CostEstimate(flops=0, bytes_accessed=16 * MIB, transcendentals=0),
        name="combine",
    )(share, take, *results, *before)


def swap(value, count, bit):
    return lax.ppermute(value, "dp", [(i, i ^ bit) for i in range(count)])


def body(
    queries,
    new_keys,
    new_values,
    cache_keys,
    cache_values,
    lengths,
    residual,
    norm_gain,
    router_weight,
    gate_weight,
    up_weight,
    down_weight,
    routes,
):
    count = lax.axis_size("dp")
    plane = count // EXPERTS
    bits = [1 << k for k in reversed(range(plane.bit_length() - 1))]
    attended, *packed, share, take, down = attend(
        plane, queries, new_keys, new_values, cache_keys, cache_values, lengths, residual, norm_gain,
        router_weight, routes, down_weight,
    )

    packed = [packed[0]] + [swap(packed[k], count, k * plane) for k in range(1, EXPERTS)]
    near = join(share, *packed[:2])
    down_rest, token = load(down_weight, near, down.shape[1])
    far = join(token, *packed[2:])
    for bit in bits:
        near = join(share, near, swap(near, count, bit))
        far = join(share, far, swap(far, count, bit))

    hidden = hidden_rows(near, far, gate_weight, up_weight)
    near, near_send, far, far_send = down_rows(hidden, (down, down_rest))
    for bit in reversed(bits):
        far, far_send = fold(far, swap(far_send, count, bit), share)
        near, near_send = fold(near, swap(near_send, count, bit), far)
    far = swap(far, count, 2 * plane)
    far_send = swap(far_send, count, 3 * plane)
    near_send = swap(near_send, count, plane)
    total = combine(2, share, take, [far, far_send], [], F32)
    return (attended, combine(0, share, take, [near, near_send], [total], BF16))


def solution(mesh):
    placed = (
        P(("group", "dp"), None),
        P(("group", "dp"), None),
        P(("group", "dp"), None),
        P(("group", "dp"), None, None),
        P(("group", "dp"), None, None),
        P(("group", "dp")),
        P(("group", "dp"), None),
        P(),
        P(),
        P(None, "dp"),
        P(None, "dp"),
        P("dp", None),
        P("group", None),
    )
    return jax.shard_map(
        body,
        mesh=mesh,
        in_specs=placed,
        out_specs=(P(("group", "dp"), None), P(("group", "dp"), None)),
        check_vma=False,
    )
```

```python
import functools

import jax
import jax.numpy as jnp
from jax import lax
from jax.experimental import pallas as pl
from jax.experimental.pallas import tpu as pltpu
from jax.sharding import PartitionSpec as P

HEADS = 32
KV_HEADS = 8
HEAD_DIM = 128
EXPERTS = 4
MIB = 1 << 20
WAYS = 4
PARTS = (2, 1, 1)
MOST = 6
F32 = jnp.float32
BF16 = jnp.bfloat16
VMEM = pl.BlockSpec(memory_space=pltpu.VMEM)
ANY = pl.BlockSpec(memory_space=pl.ANY)


def dot(a, b, contract_last=False):
    dims = (((1,), (1 if contract_last else 0,)), ((), ()))
    return lax.dot_general(a, b, dims, preferred_element_type=F32)


def weight_copies(source, target, semaphores, first=0):
    step, columns = source.shape[0] // WAYS, target.shape[1]
    return [
        pltpu.make_async_copy(
            source.at[pl.ds(i * step, step), pl.ds(first, columns)],
            target.at[pl.ds(i * step, step)],
            semaphores.at[i],
        )
        for i in range(WAYS)
    ]


def one_hot(mask):
    return mask.astype(F32).astype(BF16)


def grid(shape):
    return [lax.broadcasted_iota(jnp.int32, shape, axis) for axis in (0, 1)]


def pack(picks, block):
    quarter = block.shape[1] // 4
    parts = [block[:, m * quarter : (m + 1) * quarter] for m in range(4)]
    return [
        (dot(picks[0], parts[m]) + dot(picks[1 + m], parts[3])).astype(BF16) for m in range(3)
    ]


def unpack(picks, block):
    quarter = block.shape[1] // 3
    parts = [block[:, m * quarter : (m + 1) * quarter] for m in range(3)]
    tail = dot(picks[1], parts[0]) + dot(picks[2], parts[1]) + dot(picks[3], parts[2])
    return [dot(picks[0], part) for part in parts] + [tail]


def attend_kernel(plane, *refs):
    sources, attended, packed, (share, take), held, semaphores = (
        refs[:10], refs[11], refs[12:16], refs[16:18], refs[19:29], refs[29]
    )
    weight = weight_copies(refs[10], refs[18], refs[30])
    copies = [
        pltpu.make_async_copy(source, target, semaphores.at[i])
        for i, (source, target) in enumerate(zip(sources, held))
    ]
    for copy in copies[9:] + copies[:9] + weight:
        copy.start()
    (queries, cache_keys, new_keys, lengths, cache_values, new_values, residual, gain, router,
     routes) = held
    rows, width = queries.shape
    positions = cache_keys.shape[1]
    groups = HEADS // KV_HEADS
    scale = 1.0 / HEAD_DIM**0.5
    every = rows * positions
    block = groups * rows

    copies[9].wait()
    index = lax.axis_index("dp")
    base = index * rows
    own = index // plane
    sub, lane = grid((2 * rows, 128))
    expert_down = jnp.zeros((2 * rows, 128), jnp.int32)
    slot_down = jnp.zeros((2 * rows, 128), jnp.int32)
    across = lax.broadcasted_iota(jnp.int32, (8, 128), 1)
    expert_across = jnp.zeros((8, 128), jnp.int32)
    slot_across = jnp.zeros((8, 128), jnp.int32)
    counts = [jnp.int32(0)] * EXPERTS
    for r in range(rows):
        names = [routes[c, base + r] ^ own for c in range(2)]
        for choice, name in ((r, names[0]), (rows + r, names[1])):
            slot = jnp.int32(0)
            for e in range(EXPERTS):
                slot = jnp.where(name == e, counts[e], slot)
            expert_down = jnp.where(sub == choice, name, expert_down)
            slot_down = jnp.where(sub == choice, slot, slot_down)
            expert_across = jnp.where(across == choice, name, expert_across)
            slot_across = jnp.where(across == choice, slot, slot_across)
        for e in range(EXPERTS):
            named = (names[0] == e) | (names[1] == e)
            counts[e] = counts[e] + jnp.where(named, 1, 0)

    late = jnp.where(slot_down >= 3, 1, 0)
    take[0] = one_hot(lane == expert_down * 8 + slot_down)
    for m in range(3):
        take[1 + m] = one_hot((lane == expert_down * 8 + 6 + late) & (slot_down - 3 * late == m))
    place, choice = grid((8 * EXPERTS, 128))
    expert, slot = expert_across[0:1], slot_across[0:1]
    late = jnp.where(slot >= 3, 1, 0)
    chosen = choice < 2 * rows
    picks = [one_hot((place == expert * 8 + slot) & chosen)]
    for m in range(3):
        picks.append(one_hot((place == expert * 8 + 6 + late) & (slot - 3 * late == m) & chosen))
    for copy in copies[:4]:
        copy.wait()

    query = queries[...].astype(F32)
    stacked = jnp.concatenate(
        [query[:, h * HEAD_DIM : (h + 1) * HEAD_DIM] for h in range(HEADS)], axis=0
    )
    stacked_b = stacked.astype(BF16)
    keys = cache_keys[...].reshape(every, KV_HEADS * HEAD_DIM)
    newk = new_keys[...].astype(F32)

    row_of = lax.broadcasted_iota(jnp.int32, (block, every), 0) % rows
    column = lax.broadcasted_iota(jnp.int32, (block, every), 1)
    position = column % positions
    column_row = column // positions
    limit = jnp.zeros((block, every), jnp.int32)
    for r in range(rows):
        limit = jnp.where(column_row == r, lengths[r], limit)
    valid = (row_of == column_row) & (position < limit)

    heads = range(KV_HEADS)
    lanes = [slice(g * HEAD_DIM, (g + 1) * HEAD_DIM) for g in heads]
    mine = [slice(g * block, (g + 1) * block) for g in heads]
    scores = [dot(stacked_b[mine[g]], keys[:, lanes[g]], contract_last=True) for g in heads]
    scores = [jnp.where(valid, score * scale, -jnp.inf) for score in scores]
    own_keys = [jnp.concatenate([newk[:, lanes[g]]] * groups, axis=0) for g in heads]
    new_scores = [
        jnp.sum(stacked[mine[g]] * own_keys[g], axis=1, keepdims=True) * scale for g in heads
    ]
    peaks = [
        jnp.maximum(jnp.max(score, axis=1, keepdims=True), new)
        for score, new in zip(scores, new_scores)
    ]
    weights = [jnp.exp(score - peak) for score, peak in zip(scores, peaks)]
    new_weights = [jnp.exp(new - peak) for new, peak in zip(new_scores, peaks)]
    totals = [
        jnp.sum(weight, axis=1, keepdims=True) + new
        for weight, new in zip(weights, new_weights)
    ]
    inverses = [1.0 / total for total in totals]
    probs = [(weight * inverse).astype(BF16) for weight, inverse in zip(weights, inverses)]
    new_probs = [
        (new * inverse).astype(BF16).astype(F32) for new, inverse in zip(new_weights, inverses)
    ]
    for copy in copies[4:9]:
        copy.wait()
    values = cache_values[...].reshape(every, KV_HEADS * HEAD_DIM)
    newv = new_values[...].astype(F32)
    mixed = [
        dot(probs[g], values[:, lanes[g]])
        + new_probs[g] * jnp.concatenate([newv[:, lanes[g]]] * groups, axis=0)
        for g in heads
    ]
    pieces = [value[j * rows : (j + 1) * rows] for value in mixed for j in range(groups)]

    states = (residual[...].astype(F32) + jnp.concatenate(pieces, axis=1)).astype(BF16)
    attended[...] = states
    states = states.astype(F32)
    norm = lax.rsqrt(jnp.mean(states * states, axis=1, keepdims=True) + 1e-05)
    gains = gain[...].astype(F32)
    logits = [jnp.zeros((rows, 128), F32) for _ in range(EXPERTS)]
    parts = []
    for c in range(width // 128):
        lanes = slice(c * 128, (c + 1) * 128)
        part = (states[:, lanes] * norm * gains[c : c + 1]).astype(BF16).astype(F32)
        parts.append(part)
        for e in range(EXPERTS):
            logits[e] += part * router[e : e + 1, lanes].astype(F32)
    logits = [jnp.sum(value, axis=1, keepdims=True) for value in logits]

    normed = jnp.concatenate(parts, axis=1)
    normed = jnp.concatenate([normed, normed], axis=0).astype(BF16)
    quarter = width // 4
    for m, value in enumerate(pack([pick[:, : 2 * rows] for pick in picks], normed)):
        for k, target in enumerate(packed):
            target[:, m * quarter : (m + 1) * quarter] = value[8 * k : 8 * k + 8]

    chosen_logits = jnp.zeros((2 * rows, 1), F32)
    for e in range(EXPERTS):
        both = jnp.concatenate([logits[e], logits[e]], axis=0)
        chosen_logits = jnp.where(expert_down[:, :1] == (own ^ e), both, chosen_logits)
    other = jnp.concatenate([chosen_logits[rows:], chosen_logits[:rows]], axis=0)
    share[...] = jnp.broadcast_to(1.0 / (1.0 + jnp.exp(other - chosen_logits)), share.shape)
    for copy in weight:
        copy.wait()


def attend(plane, queries, new_keys, new_values, cache_keys, cache_values, lengths, residual,
           norm_gain, router_weight, routes, weight):
    rows, width = queries.shape
    operands = (
        queries,
        cache_keys,
        new_keys,
        lengths,
        cache_values,
        new_values,
        residual,
        norm_gain.reshape(-1, 128),
        router_weight.T,
        routes.T,
    )
    in_smem = (3, 9)
    return pl.pallas_call(
        functools.partial(attend_kernel, plane),
        out_shape=(
            jax.ShapeDtypeStruct((rows, width), BF16),
            *[jax.ShapeDtypeStruct((8, width * 3 // 4), BF16)] * EXPERTS,
            jax.ShapeDtypeStruct((2 * rows, 128), F32),
            jax.ShapeDtypeStruct((4, 2 * rows, 128), BF16),
            pltpu.VMEM((weight.shape[0], weight.shape[1] // 4 * PARTS[0]), weight.dtype),
        ),
        in_specs=[ANY] * (len(operands) + 1),
        out_specs=(VMEM,) * (4 + EXPERTS),
        scratch_shapes=[
            (pltpu.SMEM if i in in_smem else pltpu.VMEM)(operand.shape, operand.dtype)
            for i, operand in enumerate(operands)
        ]
        + [pltpu.SemaphoreType.DMA((len(operands),)), pltpu.SemaphoreType.DMA((WAYS,))],
        compiler_params=pltpu.CompilerParams(vmem_limit_bytes=5 * MIB),
        name="attend",
    )(*[pltpu.with_memory_space_constraint(x, pltpu.HBM) for x in (*operands, weight)])


def hidden_kernel(near, far, gate_weight, up_weight, hidden):
    columns = gate_weight.shape[1]
    step = 256 if columns % 256 == 0 else columns
    quarter = near.shape[1] // 3
    blocks = jnp.concatenate([near[...], far[...]], axis=0)
    size = 128
    row, lane = grid((size, size))
    slot = row & 7
    late = jnp.where(slot >= 3, 1, 0)
    picks = [
        one_hot((lane == row - slot + 6 + late) & (slot - 3 * late == m)) for m in range(3)
    ]
    picks = jnp.concatenate(picks, axis=1)
    tails = []
    for first in range(0, blocks.shape[0], size):
        some = blocks[first : first + size]
        parts = [some[:, m * quarter : (m + 1) * quarter] for m in range(3)]
        tails.append(dot(picks, jnp.concatenate(parts, axis=0)).astype(BF16))
    x = jnp.concatenate([blocks, jnp.concatenate(tails, axis=0)], axis=1)
    for f in range(0, columns, step):
        gate = dot(x, gate_weight[:, f : f + step])
        upper = dot(x, up_weight[:, f : f + step])
        hidden[:, f : f + step] = (gate / (1.0 + jnp.exp(-gate)) * upper).astype(BF16)


def hidden_rows(near, far, gate_weight, up_weight):
    rows = near.shape[0] + far.shape[0]
    width, columns = gate_weight.shape
    return pl.pallas_call(
        hidden_kernel,
        out_shape=jax.ShapeDtypeStruct((rows, columns), BF16),
        in_specs=[VMEM] * 4,
        out_specs=VMEM,
        compiler_params=pltpu.CompilerParams(vmem_limit_bytes=4 * MIB * max(1, rows // 128)),
        cost_estimate=pl.CostEstimate(
            flops=4 * rows * width * columns, bytes_accessed=0, transcendentals=rows * columns
        ),
        name="hidden",
    )(near, far, gate_weight, up_weight)


def down_kernel(hidden, *refs):
    weights, outs = refs[: len(PARTS)], refs[len(PARTS) :]
    rows = hidden.shape[0]
    quarter = outs[0].shape[1] // 3
    size = 128
    row, lane = grid((size, size))
    slot = row & 7
    picks = [one_hot((lane == row - slot + 3 * (slot - 6) + m) & (slot >= MOST)) for m in range(3)]
    picks = jnp.concatenate(picks, axis=0)
    h = hidden[...]

    def terms(first, count):
        for weight in weights:
            if first < weight.shape[1]:
                return dot(h, weight[:, first : first + count])
            first -= weight.shape[1]

    step = min(512, quarter)
    is_row = (lax.broadcasted_iota(jnp.int32, (rows, step), 0) & 7) < MOST
    each = rows // len(outs)
    for n in range(0, quarter, step):
        tail = terms(3 * quarter + n, step).astype(BF16)
        tails = [dot(picks, tail[i : i + size]) for i in range(0, rows, size)]
        for m in range(3):
            moved = jnp.concatenate([x[m * size : (m + 1) * size] for x in tails], axis=0)
            value = jnp.where(is_row, terms(m * quarter + n, step), moved).astype(BF16)
            for k, out in enumerate(outs):
                out[:, m * quarter + n : m * quarter + n + step] = value[k * each : (k + 1) * each]


def down_rows(hidden, weights):
    rows, columns = hidden.shape
    width = sum(weight.shape[1] for weight in weights)
    return pl.pallas_call(
        down_kernel,
        out_shape=[jax.ShapeDtypeStruct((rows // 4, width // 4 * 3), BF16)] * 4,
        in_specs=[VMEM] * (1 + len(PARTS)),
        out_specs=[VMEM] * 4,
        compiler_params=pltpu.CompilerParams(vmem_limit_bytes=4 * MIB * max(1, rows // 128)),
        cost_estimate=pl.CostEstimate(
            flops=2 * rows * width * columns, bytes_accessed=0, transcendentals=0
        ),
        name="down",
    )(hidden, *weights)


def load_kernel(first, source, after, target, token, semaphores):
    copies = weight_copies(source, target, semaphores, first)
    for copy in copies:
        copy.start()
    token[...] = jnp.zeros(token.shape, token.dtype)
    for copy in copies:
        copy.wait()


def load(source, after, first, columns):
    shape = (source.shape[0], columns)
    return pl.pallas_call(
        functools.partial(load_kernel, first),
        out_shape=(
            pltpu.VMEM(shape, source.dtype),
            jax.ShapeDtypeStruct((8, 128), F32),
        ),
        in_specs=[ANY, ANY],
        out_specs=(VMEM, VMEM),
        scratch_shapes=[pltpu.SemaphoreType.DMA((WAYS,))],
        compiler_params=pltpu.CompilerParams(vmem_limit_bytes=MIB),
        cost_estimate=pl.CostEstimate(
            flops=0, bytes_accessed=2 * shape[0] * shape[1], transcendentals=0
        ),
        name="load",
    )(pltpu.with_memory_space_constraint(source, pltpu.HBM), after)


def join_kernel(*refs):
    out, row = refs[-1], 0
    for piece in refs[1:-1]:
        out[row : row + piece.shape[0]] = piece[...]
        row += piece.shape[0]


def join(after, *pieces):
    rows = sum(piece.shape[0] for piece in pieces)
    return pl.pallas_call(
        join_kernel,
        out_shape=jax.ShapeDtypeStruct((rows, pieces[0].shape[1]), BF16),
        in_specs=[ANY] + [VMEM] * len(pieces),
        out_specs=VMEM,
        compiler_params=pltpu.CompilerParams(vmem_limit_bytes=1 * MIB),
        name="join",
    )(after, *pieces)


def fold_kernel(held, arrived, after, *outs):
    each = outs[0].shape[0]
    for k, out in enumerate(outs):
        block = slice(k * each, (k + 1) * each)
        out[...] = (held[block].astype(F32) + arrived[block].astype(F32)).astype(BF16)


def fold(held, arrived, after):
    rows, width = held.shape
    return pl.pallas_call(
        fold_kernel,
        out_shape=[jax.ShapeDtypeStruct((rows // 2, width), BF16)] * 2,
        in_specs=[VMEM] * 2 + [ANY],
        out_specs=[VMEM] * 2,
        compiler_params=pltpu.CompilerParams(vmem_limit_bytes=MIB * max(1, rows // 64)),
        cost_estimate=pl.CostEstimate(flops=0, bytes_accessed=16 * MIB, transcendentals=0),
        name="fold",
    )(held, arrived, after)


def combine_kernel(first, share, take, *refs):
    results, before, out = refs[:2], refs[2:-1], refs[-1]
    rows = out.shape[0]
    quarter = results[0].shape[1] // 3
    picks = [take[i][:, 8 * first : 8 * first + 16] for i in range(4)]
    shares = share[:, :1]
    block = jnp.concatenate([x[...] for x in results], axis=0)
    for m, value in enumerate(unpack(picks, block)):
        lanes = slice(m * quarter, (m + 1) * quarter)
        value = value * shares
        value = value[:rows] + value[rows:]
        for x in before:
            value = value + x[:, lanes]
        out[:, lanes] = value.astype(out.dtype)


def combine(first, share, take, results, before, dtype):
    width = results[0].shape[1] // 3 * 4
    return pl.pallas_call(
        functools.partial(combine_kernel, first),
        out_shape=jax.ShapeDtypeStruct((share.shape[0] // 2, width), dtype),
        in_specs=[VMEM] * (4 + len(before)),
        out_specs=VMEM,
        compiler_params=pltpu.CompilerParams(vmem_limit_bytes=2 * MIB),
        cost_estimate=pl.CostEstimate(flops=0, bytes_accessed=16 * MIB, transcendentals=0),
        name="combine",
    )(share, take, *results, *before)


def swap(value, count, bit):
    return lax.ppermute(value, "dp", [(i, i ^ bit) for i in range(count)])


def body(
    queries,
    new_keys,
    new_values,
    cache_keys,
    cache_values,
    lengths,
    residual,
    norm_gain,
    router_weight,
    gate_weight,
    up_weight,
    down_weight,
    routes,
):
    count = lax.axis_size("dp")
    plane = count // EXPERTS
    bits = [1 << k for k in reversed(range(plane.bit_length() - 1))]
    attended, *packed, share, take, down = attend(
        plane, queries, new_keys, new_values, cache_keys, cache_values, lengths, residual, norm_gain,
        router_weight, routes, down_weight,
    )

    packed = [packed[0]] + [swap(packed[k], count, k * plane) for k in range(1, EXPERTS)]
    near = join(share, *packed[:2])
    quarter = down_weight.shape[1] // 4
    down_2, token = load(down_weight, near, quarter * PARTS[0], quarter * PARTS[1])
    far = join(token, *packed[2:])
    down_3, token = load(down_weight, far, quarter * sum(PARTS[:2]), quarter * PARTS[2])
    for bit in bits:
        near = join(share, near, swap(near, count, bit))
        far = join(token, far, swap(far, count, bit))

    hidden = hidden_rows(near, far, gate_weight, up_weight)
    near, near_send, far, far_send = down_rows(hidden, (down, down_2, down_3))
    for bit in reversed(bits):
        far, far_send = fold(far, swap(far_send, count, bit), share)
    for bit in reversed(bits):
        near, near_send = fold(near, swap(near_send, count, bit), far)
    far = swap(far, count, 2 * plane)
    far_send = swap(far_send, count, 3 * plane)
    near_send = swap(near_send, count, plane)
    total = combine(2, share, take, [far, far_send], [], F32)
    return (attended, combine(0, share, take, [near, near_send], [total], BF16))


def solution(mesh):
    placed = (
        P(("group", "dp"), None),
        P(("group", "dp"), None),
        P(("group", "dp"), None),
        P(("group", "dp"), None, None),
        P(("group", "dp"), None, None),
        P(("group", "dp")),
        P(("group", "dp"), None),
        P(),
        P(),
        P(None, "dp"),
        P(None, "dp"),
        P("dp", None),
        P("group", None),
    )
    return jax.shard_map(
        body,
        mesh=mesh,
        in_specs=placed,
        out_specs=(P(("group", "dp"), None), P(("group", "dp"), None)),
        check_vma=False,
    )
```

```python
import functools

import jax
import jax.numpy as jnp
from jax import lax
from jax.experimental import pallas as pl
from jax.experimental.pallas import tpu as pltpu
from jax.sharding import PartitionSpec as P

HEADS = 32
KV_HEADS = 8
HEAD_DIM = 128
EXPERTS = 4
MIB = 1 << 20
HINTS = 3
MOST = 6
F32 = jnp.float32
BF16 = jnp.bfloat16
VMEM = pl.BlockSpec(memory_space=pltpu.VMEM)
ANY = pl.BlockSpec(memory_space=pl.ANY)


def dot(a, b, contract_last=False):
    dims = (((1,), (1 if contract_last else 0,)), ((), ()))
    return lax.dot_general(a, b, dims, preferred_element_type=F32)


def one_hot(mask):
    return mask.astype(F32).astype(BF16)


def grid(shape):
    return [lax.broadcasted_iota(jnp.int32, shape, axis) for axis in (0, 1)]


def pack(picks, block):
    quarter = block.shape[1] // 4
    parts = [block[:, m * quarter : (m + 1) * quarter] for m in range(4)]
    return [
        (dot(picks[0], parts[m]) + dot(picks[1 + m], parts[3])).astype(BF16) for m in range(3)
    ]


def unpack(picks, block):
    quarter = block.shape[1] // 3
    parts = [block[:, m * quarter : (m + 1) * quarter] for m in range(3)]
    tail = dot(picks[1], parts[0]) + dot(picks[2], parts[1]) + dot(picks[3], parts[2])
    return [dot(picks[0], part) for part in parts] + [tail]


def attend_kernel(plane, *refs):
    refs = refs[:10] + refs[10 + HINTS :]
    sources, attended, packed, (share, take), held, semaphores = (
        refs[:10], refs[10], refs[11:15], refs[15:17], refs[17:27], refs[27]
    )
    copies = [
        pltpu.make_async_copy(source, target, semaphores.at[i])
        for i, (source, target) in enumerate(zip(sources, held))
    ]
    for copy in copies[9:] + copies[:9]:
        copy.start()
    (queries, cache_keys, new_keys, lengths, cache_values, new_values, residual, gain, router,
     routes) = held
    rows, width = queries.shape
    positions = cache_keys.shape[1]
    groups = HEADS // KV_HEADS
    scale = 1.0 / HEAD_DIM**0.5
    every = rows * positions
    block = groups * rows

    copies[9].wait()
    index = lax.axis_index("dp")
    base = index * rows
    own = index // plane
    sub, lane = grid((2 * rows, 128))
    expert_down = jnp.zeros((2 * rows, 128), jnp.int32)
    slot_down = jnp.zeros((2 * rows, 128), jnp.int32)
    across = lax.broadcasted_iota(jnp.int32, (8, 128), 1)
    expert_across = jnp.zeros((8, 128), jnp.int32)
    slot_across = jnp.zeros((8, 128), jnp.int32)
    counts = [jnp.int32(0)] * EXPERTS
    for r in range(rows):
        names = [routes[c, base + r] ^ own for c in range(2)]
        for choice, name in ((r, names[0]), (rows + r, names[1])):
            slot = jnp.int32(0)
            for e in range(EXPERTS):
                slot = jnp.where(name == e, counts[e], slot)
            expert_down = jnp.where(sub == choice, name, expert_down)
            slot_down = jnp.where(sub == choice, slot, slot_down)
            expert_across = jnp.where(across == choice, name, expert_across)
            slot_across = jnp.where(across == choice, slot, slot_across)
        for e in range(EXPERTS):
            named = (names[0] == e) | (names[1] == e)
            counts[e] = counts[e] + jnp.where(named, 1, 0)

    late = jnp.where(slot_down >= 3, 1, 0)
    take[0] = one_hot(lane == expert_down * 8 + slot_down)
    for m in range(3):
        take[1 + m] = one_hot((lane == expert_down * 8 + 6 + late) & (slot_down - 3 * late == m))
    place, choice = grid((8 * EXPERTS, 128))
    expert, slot = expert_across[0:1], slot_across[0:1]
    late = jnp.where(slot >= 3, 1, 0)
    chosen = choice < 2 * rows
    picks = [one_hot((place == expert * 8 + slot) & chosen)]
    for m in range(3):
        picks.append(one_hot((place == expert * 8 + 6 + late) & (slot - 3 * late == m) & chosen))
    for copy in copies[:4]:
        copy.wait()

    query = queries[...].astype(F32)
    stacked = jnp.concatenate(
        [query[:, h * HEAD_DIM : (h + 1) * HEAD_DIM] for h in range(HEADS)], axis=0
    )
    stacked_b = stacked.astype(BF16)
    keys = cache_keys[...].reshape(every, KV_HEADS * HEAD_DIM)
    newk = new_keys[...].astype(F32)

    row_of = lax.broadcasted_iota(jnp.int32, (block, every), 0) % rows
    column = lax.broadcasted_iota(jnp.int32, (block, every), 1)
    position = column % positions
    column_row = column // positions
    limit = jnp.zeros((block, every), jnp.int32)
    for r in range(rows):
        limit = jnp.where(column_row == r, lengths[r], limit)
    valid = (row_of == column_row) & (position < limit)

    heads = range(KV_HEADS)
    lanes = [slice(g * HEAD_DIM, (g + 1) * HEAD_DIM) for g in heads]
    mine = [slice(g * block, (g + 1) * block) for g in heads]
    scores = [dot(stacked_b[mine[g]], keys[:, lanes[g]], contract_last=True) for g in heads]
    scores = [jnp.where(valid, score * scale, -jnp.inf) for score in scores]
    own_keys = [jnp.concatenate([newk[:, lanes[g]]] * groups, axis=0) for g in heads]
    new_scores = [
        jnp.sum(stacked[mine[g]] * own_keys[g], axis=1, keepdims=True) * scale for g in heads
    ]
    peaks = [
        jnp.maximum(jnp.max(score, axis=1, keepdims=True), new)
        for score, new in zip(scores, new_scores)
    ]
    weights = [jnp.exp(score - peak) for score, peak in zip(scores, peaks)]
    new_weights = [jnp.exp(new - peak) for new, peak in zip(new_scores, peaks)]
    totals = [
        jnp.sum(weight, axis=1, keepdims=True) + new
        for weight, new in zip(weights, new_weights)
    ]
    inverses = [1.0 / total for total in totals]
    probs = [(weight * inverse).astype(BF16) for weight, inverse in zip(weights, inverses)]
    new_probs = [
        (new * inverse).astype(BF16).astype(F32) for new, inverse in zip(new_weights, inverses)
    ]
    for copy in copies[4:9]:
        copy.wait()
    values = cache_values[...].reshape(every, KV_HEADS * HEAD_DIM)
    newv = new_values[...].astype(F32)
    mixed = [
        dot(probs[g], values[:, lanes[g]])
        + new_probs[g] * jnp.concatenate([newv[:, lanes[g]]] * groups, axis=0)
        for g in heads
    ]
    pieces = [value[j * rows : (j + 1) * rows] for value in mixed for j in range(groups)]

    states = (residual[...].astype(F32) + jnp.concatenate(pieces, axis=1)).astype(BF16)
    attended[...] = states
    states = states.astype(F32)
    norm = lax.rsqrt(jnp.mean(states * states, axis=1, keepdims=True) + 1e-05)
    gains = gain[...].astype(F32)
    logits = [jnp.zeros((rows, 128), F32) for _ in range(EXPERTS)]
    parts = []
    for c in range(width // 128):
        lanes = slice(c * 128, (c + 1) * 128)
        part = (states[:, lanes] * norm * gains[c : c + 1]).astype(BF16).astype(F32)
        parts.append(part)
        for e in range(EXPERTS):
            logits[e] += part * router[e : e + 1, lanes].astype(F32)
    logits = [jnp.sum(value, axis=1, keepdims=True) for value in logits]

    normed = jnp.concatenate(parts, axis=1)
    normed = jnp.concatenate([normed, normed], axis=0).astype(BF16)
    quarter = width // 4
    for m, value in enumerate(pack([pick[:, : 2 * rows] for pick in picks], normed)):
        for k, target in enumerate(packed):
            target[:, m * quarter : (m + 1) * quarter] = value[8 * k : 8 * k + 8]

    chosen_logits = jnp.zeros((2 * rows, 1), F32)
    for e in range(EXPERTS):
        both = jnp.concatenate([logits[e], logits[e]], axis=0)
        chosen_logits = jnp.where(expert_down[:, :1] == (own ^ e), both, chosen_logits)
    other = jnp.concatenate([chosen_logits[rows:], chosen_logits[:rows]], axis=0)
    share[...] = jnp.broadcast_to(1.0 / (1.0 + jnp.exp(other - chosen_logits)), share.shape)


def attend(plane, queries, new_keys, new_values, cache_keys, cache_values, lengths, residual,
           norm_gain, router_weight, routes, weight):
    rows, width = queries.shape
    operands = (
        queries,
        cache_keys,
        new_keys,
        lengths,
        cache_values,
        new_values,
        residual,
        norm_gain.reshape(-1, 128),
        router_weight.T,
        routes.T,
    )
    in_smem = (3, 9)
    return pl.pallas_call(
        functools.partial(attend_kernel, plane),
        out_shape=(
            jax.ShapeDtypeStruct((rows, width), BF16),
            *[jax.ShapeDtypeStruct((8, width * 3 // 4), BF16)] * EXPERTS,
            jax.ShapeDtypeStruct((2 * rows, 128), F32),
            jax.ShapeDtypeStruct((4, 2 * rows, 128), BF16),
        ),
        in_specs=[ANY] * (len(operands) + HINTS),
        out_specs=(VMEM,) * (3 + EXPERTS),
        scratch_shapes=[
            (pltpu.SMEM if i in in_smem else pltpu.VMEM)(operand.shape, operand.dtype)
            for i, operand in enumerate(operands)
        ]
        + [pltpu.SemaphoreType.DMA((len(operands),))],
        compiler_params=pltpu.CompilerParams(vmem_limit_bytes=5 * MIB),
        name="attend",
    )(*[pltpu.with_memory_space_constraint(x, pltpu.HBM) for x in operands + (weight,) * HINTS])


def expert_kernel(near, far, gate_weight, up_weight, down_weight, *refs):
    outs, (hidden, down, semaphores) = refs[:4], refs[4:]
    rows = near.shape[0] + far.shape[0]
    width, columns = gate_weight.shape
    quarter = width // 4
    order = (3, 0, 1, 2)
    copies = {}
    for m in order:
        lanes = pl.ds(m * quarter, quarter)
        copies[m] = pltpu.make_async_copy(down_weight.at[:, lanes], down.at[m], semaphores.at[m])
        copies[m].start()

    size = 128
    row, lane = grid((size, size))
    slot = row & 7
    late = jnp.where(slot >= 3, 1, 0)
    picks = [
        one_hot((lane == row - slot + 6 + late) & (slot - 3 * late == m)) for m in range(3)
    ]
    picks = jnp.concatenate(picks, axis=1)
    blocks = jnp.concatenate([near[...], far[...]], axis=0)
    tails = []
    for first in range(0, rows, size):
        some = blocks[first : first + size]
        parts = [some[:, m * quarter : (m + 1) * quarter] for m in range(3)]
        tails.append(dot(picks, jnp.concatenate(parts, axis=0)).astype(BF16))
    x = jnp.concatenate([blocks, jnp.concatenate(tails, axis=0)], axis=1)
    step = 256 if columns % 256 == 0 else columns
    for f in range(0, columns, step):
        gate = dot(x, gate_weight[:, f : f + step])
        upper = dot(x, up_weight[:, f : f + step])
        hidden[:, f : f + step] = (gate / (1.0 + jnp.exp(-gate)) * upper).astype(BF16)

    picks = [one_hot((lane == row - slot + 3 * (slot - 6) + m) & (slot >= MOST)) for m in range(3)]
    picks = jnp.concatenate(picks, axis=0)
    h = hidden[...]
    step = min(512, quarter)
    is_row = (lax.broadcasted_iota(jnp.int32, (rows, step), 0) & 7) < MOST
    each = rows // len(outs)
    moved = {}
    for m in order:
        copies[m].wait()
        for n in range(0, quarter, step):
            terms = dot(h, down[m, :, n : n + step])
            if m == 3:
                tail = terms.astype(BF16)
                tails = [dot(picks, tail[i : i + size]) for i in range(0, rows, size)]
                for k in range(3):
                    moved[k, n] = jnp.concatenate(
                        [t[k * size : (k + 1) * size] for t in tails], axis=0
                    ).astype(BF16)
                continue
            value = jnp.where(is_row, terms, moved[m, n].astype(F32)).astype(BF16)
            for k, out in enumerate(outs):
                out[:, m * quarter + n : m * quarter + n + step] = value[k * each : (k + 1) * each]


def expert_rows(near, far, gate_weight, up_weight, down_weight):
    rows = near.shape[0] + far.shape[0]
    width, columns = gate_weight.shape
    return pl.pallas_call(
        expert_kernel,
        out_shape=[jax.ShapeDtypeStruct((rows // 4, width // 4 * 3), BF16)] * 4,
        in_specs=[VMEM] * 4 + [ANY],
        out_specs=[VMEM] * 4,
        scratch_shapes=[
            pltpu.VMEM((rows, columns), BF16),
            pltpu.VMEM((4, columns, width // 4), BF16),
            pltpu.SemaphoreType.DMA((4,)),
        ],
        compiler_params=pltpu.CompilerParams(
            vmem_limit_bytes=2 * columns * width + 4 * MIB * max(1, rows // 128)
        ),
        cost_estimate=pl.CostEstimate(
            flops=6 * rows * width * columns, bytes_accessed=0, transcendentals=rows * columns
        ),
        name="experts",
    )(near, far, gate_weight, up_weight, pltpu.with_memory_space_constraint(down_weight, pltpu.HBM))


def join_kernel(*refs):
    out, row = refs[-1], 0
    for piece in refs[:-1]:
        out[row : row + piece.shape[0]] = piece[...]
        row += piece.shape[0]


def join(*pieces):
    rows = sum(piece.shape[0] for piece in pieces)
    return pl.pallas_call(
        join_kernel,
        out_shape=jax.ShapeDtypeStruct((rows, pieces[0].shape[1]), BF16),
        in_specs=[VMEM] * len(pieces),
        out_specs=VMEM,
        compiler_params=pltpu.CompilerParams(vmem_limit_bytes=1 * MIB),
        name="join",
    )(*pieces)


def fold_kernel(held, arrived, after, *outs):
    each = outs[0].shape[0]
    for k, out in enumerate(outs):
        block = slice(k * each, (k + 1) * each)
        out[...] = (held[block].astype(F32) + arrived[block].astype(F32)).astype(BF16)


def fold(held, arrived, after):
    rows, width = held.shape
    return pl.pallas_call(
        fold_kernel,
        out_shape=[jax.ShapeDtypeStruct((rows // 2, width), BF16)] * 2,
        in_specs=[VMEM] * 2 + [ANY],
        out_specs=[VMEM] * 2,
        compiler_params=pltpu.CompilerParams(vmem_limit_bytes=MIB * max(1, rows // 64)),
        cost_estimate=pl.CostEstimate(flops=0, bytes_accessed=16 * MIB, transcendentals=0),
        name="fold",
    )(held, arrived, after)


def combine_kernel(first, share, take, *refs):
    results, before, out = refs[:2], refs[2:-1], refs[-1]
    rows = out.shape[0]
    quarter = results[0].shape[1] // 3
    picks = [take[i][:, 8 * first : 8 * first + 16] for i in range(4)]
    shares = share[:, :1]
    block = jnp.concatenate([x[...] for x in results], axis=0)
    for m, value in enumerate(unpack(picks, block)):
        lanes = slice(m * quarter, (m + 1) * quarter)
        value = value * shares
        value = value[:rows] + value[rows:]
        for x in before:
            value = value + x[:, lanes]
        out[:, lanes] = value.astype(out.dtype)


def combine(first, share, take, results, before, dtype):
    width = results[0].shape[1] // 3 * 4
    return pl.pallas_call(
        functools.partial(combine_kernel, first),
        out_shape=jax.ShapeDtypeStruct((share.shape[0] // 2, width), dtype),
        in_specs=[VMEM] * (4 + len(before)),
        out_specs=VMEM,
        compiler_params=pltpu.CompilerParams(vmem_limit_bytes=2 * MIB),
        cost_estimate=pl.CostEstimate(flops=0, bytes_accessed=16 * MIB, transcendentals=0),
        name="combine",
    )(share, take, *results, *before)


def swap(value, count, bit):
    return lax.ppermute(value, "dp", [(i, i ^ bit) for i in range(count)])


def body(
    queries,
    new_keys,
    new_values,
    cache_keys,
    cache_values,
    lengths,
    residual,
    norm_gain,
    router_weight,
    gate_weight,
    up_weight,
    down_weight,
    routes,
):
    count = lax.axis_size("dp")
    plane = count // EXPERTS
    bits = [1 << k for k in reversed(range(plane.bit_length() - 1))]
    attended, *packed, share, take = attend(
        plane, queries, new_keys, new_values, cache_keys, cache_values, lengths, residual, norm_gain,
        router_weight, routes, down_weight,
    )

    packed = [packed[0]] + [swap(packed[k], count, k * plane) for k in range(1, EXPERTS)]
    near = join(*packed[:2])
    far = join(*packed[2:])
    for bit in bits:
        near = join(near, swap(near, count, bit))
        far = join(far, swap(far, count, bit))

    near, near_send, far, far_send = expert_rows(
        near, far, gate_weight, up_weight, down_weight
    )
    for bit in reversed(bits):
        far, far_send = fold(far, swap(far_send, count, bit), share)
    for bit in reversed(bits):
        near, near_send = fold(near, swap(near_send, count, bit), far)
    far = swap(far, count, 2 * plane)
    far_send = swap(far_send, count, 3 * plane)
    near_send = swap(near_send, count, plane)
    total = combine(2, share, take, [far, far_send], [], F32)
    return (attended, combine(0, share, take, [near, near_send], [total], BF16))


def solution(mesh):
    placed = (
        P(("group", "dp"), None),
        P(("group", "dp"), None),
        P(("group", "dp"), None),
        P(("group", "dp"), None, None),
        P(("group", "dp"), None, None),
        P(("group", "dp")),
        P(("group", "dp"), None),
        P(),
        P(),
        P(None, "dp"),
        P(None, "dp"),
        P("dp", None),
        P("group", None),
    )
    return jax.shard_map(
        body,
        mesh=mesh,
        in_specs=placed,
        out_specs=(P(("group", "dp"), None), P(("group", "dp"), None)),
        check_vma=False,
    )
```

```python
import functools

import jax
import jax.numpy as jnp
from jax import lax
from jax.experimental import pallas as pl
from jax.experimental.pallas import tpu as pltpu
from jax.sharding import PartitionSpec as P

HEADS = 32
KV_HEADS = 8
HEAD_DIM = 128
EXPERTS = 4
MIB = 1 << 20
HINTS = 4
WAYS = 2
MOST = 6
F32 = jnp.float32
BF16 = jnp.bfloat16
VMEM = pl.BlockSpec(memory_space=pltpu.VMEM)
ANY = pl.BlockSpec(memory_space=pl.ANY)


def dot(a, b, contract_last=False):
    dims = (((1,), (1 if contract_last else 0,)), ((), ()))
    return lax.dot_general(a, b, dims, preferred_element_type=F32)


def one_hot(mask):
    return mask.astype(F32).astype(BF16)


def grid(shape):
    return [lax.broadcasted_iota(jnp.int32, shape, axis) for axis in (0, 1)]


def pack(picks, block):
    quarter = block.shape[1] // 4
    parts = [block[:, m * quarter : (m + 1) * quarter] for m in range(4)]
    return [
        (dot(picks[0], parts[m]) + dot(picks[1 + m], parts[3])).astype(BF16) for m in range(3)
    ]


def unpack(picks, block):
    quarter = block.shape[1] // 3
    parts = [block[:, m * quarter : (m + 1) * quarter] for m in range(3)]
    tail = dot(picks[1], parts[0]) + dot(picks[2], parts[1]) + dot(picks[3], parts[2])
    return [dot(picks[0], part) for part in parts] + [tail]


def attend_kernel(plane, *refs):
    refs = refs[:10] + refs[10 + HINTS :]
    sources, attended, packed, (share, take), held, semaphores = (
        refs[:10], refs[10], refs[11:15], refs[15:17], refs[17:27], refs[27]
    )
    copies = [
        pltpu.make_async_copy(source, target, semaphores.at[i])
        for i, (source, target) in enumerate(zip(sources, held))
    ]
    for copy in copies[9:] + copies[:9]:
        copy.start()
    (queries, cache_keys, new_keys, lengths, cache_values, new_values, residual, gain, router,
     routes) = held
    rows, width = queries.shape
    positions = cache_keys.shape[1]
    groups = HEADS // KV_HEADS
    scale = 1.0 / HEAD_DIM**0.5
    every = rows * positions
    block = groups * rows

    copies[9].wait()
    index = lax.axis_index("dp")
    base = index * rows
    own = index // plane
    sub, lane = grid((2 * rows, 128))
    expert_down = jnp.zeros((2 * rows, 128), jnp.int32)
    slot_down = jnp.zeros((2 * rows, 128), jnp.int32)
    across = lax.broadcasted_iota(jnp.int32, (8, 128), 1)
    expert_across = jnp.zeros((8, 128), jnp.int32)
    slot_across = jnp.zeros((8, 128), jnp.int32)
    counts = [jnp.int32(0)] * EXPERTS
    for r in range(rows):
        names = [routes[c, base + r] ^ own for c in range(2)]
        for choice, name in ((r, names[0]), (rows + r, names[1])):
            slot = jnp.int32(0)
            for e in range(EXPERTS):
                slot = jnp.where(name == e, counts[e], slot)
            expert_down = jnp.where(sub == choice, name, expert_down)
            slot_down = jnp.where(sub == choice, slot, slot_down)
            expert_across = jnp.where(across == choice, name, expert_across)
            slot_across = jnp.where(across == choice, slot, slot_across)
        for e in range(EXPERTS):
            named = (names[0] == e) | (names[1] == e)
            counts[e] = counts[e] + jnp.where(named, 1, 0)

    late = jnp.where(slot_down >= 3, 1, 0)
    take[0] = one_hot(lane == expert_down * 8 + slot_down)
    for m in range(3):
        take[1 + m] = one_hot((lane == expert_down * 8 + 6 + late) & (slot_down - 3 * late == m))
    place, choice = grid((8 * EXPERTS, 128))
    expert, slot = expert_across[0:1], slot_across[0:1]
    late = jnp.where(slot >= 3, 1, 0)
    chosen = choice < 2 * rows
    picks = [one_hot((place == expert * 8 + slot) & chosen)]
    for m in range(3):
        picks.append(one_hot((place == expert * 8 + 6 + late) & (slot - 3 * late == m) & chosen))
    for copy in copies[:4]:
        copy.wait()

    query = queries[...].astype(F32)
    stacked = jnp.concatenate(
        [query[:, h * HEAD_DIM : (h + 1) * HEAD_DIM] for h in range(HEADS)], axis=0
    )
    stacked_b = stacked.astype(BF16)
    keys = cache_keys[...].reshape(every, KV_HEADS * HEAD_DIM)
    newk = new_keys[...].astype(F32)

    row_of = lax.broadcasted_iota(jnp.int32, (block, every), 0) % rows
    column = lax.broadcasted_iota(jnp.int32, (block, every), 1)
    position = column % positions
    column_row = column // positions
    limit = jnp.zeros((block, every), jnp.int32)
    for r in range(rows):
        limit = jnp.where(column_row == r, lengths[r], limit)
    valid = (row_of == column_row) & (position < limit)

    heads = range(KV_HEADS)
    lanes = [slice(g * HEAD_DIM, (g + 1) * HEAD_DIM) for g in heads]
    mine = [slice(g * block, (g + 1) * block) for g in heads]
    scores = [dot(stacked_b[mine[g]], keys[:, lanes[g]], contract_last=True) for g in heads]
    scores = [jnp.where(valid, score * scale, -jnp.inf) for score in scores]
    own_keys = [jnp.concatenate([newk[:, lanes[g]]] * groups, axis=0) for g in heads]
    new_scores = [
        jnp.sum(stacked[mine[g]] * own_keys[g], axis=1, keepdims=True) * scale for g in heads
    ]
    peaks = [
        jnp.maximum(jnp.max(score, axis=1, keepdims=True), new)
        for score, new in zip(scores, new_scores)
    ]
    weights = [jnp.exp(score - peak) for score, peak in zip(scores, peaks)]
    new_weights = [jnp.exp(new - peak) for new, peak in zip(new_scores, peaks)]
    totals = [
        jnp.sum(weight, axis=1, keepdims=True) + new
        for weight, new in zip(weights, new_weights)
    ]
    inverses = [1.0 / total for total in totals]
    probs = [(weight * inverse).astype(BF16) for weight, inverse in zip(weights, inverses)]
    new_probs = [
        (new * inverse).astype(BF16).astype(F32) for new, inverse in zip(new_weights, inverses)
    ]
    for copy in copies[4:9]:
        copy.wait()
    values = cache_values[...].reshape(every, KV_HEADS * HEAD_DIM)
    newv = new_values[...].astype(F32)
    mixed = [
        dot(probs[g], values[:, lanes[g]])
        + new_probs[g] * jnp.concatenate([newv[:, lanes[g]]] * groups, axis=0)
        for g in heads
    ]
    pieces = [value[j * rows : (j + 1) * rows] for value in mixed for j in range(groups)]

    states = (residual[...].astype(F32) + jnp.concatenate(pieces, axis=1)).astype(BF16)
    attended[...] = states
    states = states.astype(F32)
    norm = lax.rsqrt(jnp.mean(states * states, axis=1, keepdims=True) + 1e-05)
    gains = gain[...].astype(F32)
    logits = [jnp.zeros((rows, 128), F32) for _ in range(EXPERTS)]
    parts = []
    for c in range(width // 128):
        lanes = slice(c * 128, (c + 1) * 128)
        part = (states[:, lanes] * norm * gains[c : c + 1]).astype(BF16).astype(F32)
        parts.append(part)
        for e in range(EXPERTS):
            logits[e] += part * router[e : e + 1, lanes].astype(F32)
    logits = [jnp.sum(value, axis=1, keepdims=True) for value in logits]

    normed = jnp.concatenate(parts, axis=1)
    normed = jnp.concatenate([normed, normed], axis=0).astype(BF16)
    quarter = width // 4
    for m, value in enumerate(pack([pick[:, : 2 * rows] for pick in picks], normed)):
        for k, target in enumerate(packed):
            target[:, m * quarter : (m + 1) * quarter] = value[8 * k : 8 * k + 8]

    chosen_logits = jnp.zeros((2 * rows, 1), F32)
    for e in range(EXPERTS):
        both = jnp.concatenate([logits[e], logits[e]], axis=0)
        chosen_logits = jnp.where(expert_down[:, :1] == (own ^ e), both, chosen_logits)
    other = jnp.concatenate([chosen_logits[rows:], chosen_logits[:rows]], axis=0)
    share[...] = jnp.broadcast_to(1.0 / (1.0 + jnp.exp(other - chosen_logits)), share.shape)


def attend(plane, queries, new_keys, new_values, cache_keys, cache_values, lengths, residual,
           norm_gain, router_weight, routes, weight):
    rows, width = queries.shape
    operands = (
        queries,
        cache_keys,
        new_keys,
        lengths,
        cache_values,
        new_values,
        residual,
        norm_gain.reshape(-1, 128),
        router_weight.T,
        routes.T,
    )
    in_smem = (3, 9)
    return pl.pallas_call(
        functools.partial(attend_kernel, plane),
        out_shape=(
            jax.ShapeDtypeStruct((rows, width), BF16),
            *[jax.ShapeDtypeStruct((8, width * 3 // 4), BF16)] * EXPERTS,
            jax.ShapeDtypeStruct((2 * rows, 128), F32),
            jax.ShapeDtypeStruct((4, 2 * rows, 128), BF16),
        ),
        in_specs=[ANY] * (len(operands) + HINTS),
        out_specs=(VMEM,) * (3 + EXPERTS),
        scratch_shapes=[
            (pltpu.SMEM if i in in_smem else pltpu.VMEM)(operand.shape, operand.dtype)
            for i, operand in enumerate(operands)
        ]
        + [pltpu.SemaphoreType.DMA((len(operands),))],
        compiler_params=pltpu.CompilerParams(vmem_limit_bytes=5 * MIB),
        name="attend",
    )(*[pltpu.with_memory_space_constraint(x, pltpu.HBM) for x in operands + (weight,) * HINTS])


def row_copies(source, target, semaphores, first):
    step = target.shape[0] // WAYS
    return [
        pltpu.make_async_copy(
            source.at[pl.ds(first + i * step, step)],
            target.at[pl.ds(i * step, step)],
            semaphores.at[i],
        )
        for i in range(WAYS)
    ]


def load_kernel(source, after, target, token, semaphores):
    copies = row_copies(source, target, semaphores, 0)
    for copy in copies:
        copy.start()
    token[...] = jnp.zeros(token.shape, token.dtype)
    for copy in copies:
        copy.wait()


def load(source, rows, after):
    return pl.pallas_call(
        load_kernel,
        out_shape=(
            pltpu.VMEM((rows, source.shape[1]), source.dtype),
            jax.ShapeDtypeStruct((8, 128), F32),
        ),
        in_specs=[ANY, ANY],
        out_specs=(VMEM, VMEM),
        scratch_shapes=[pltpu.SemaphoreType.DMA((WAYS,))],
        compiler_params=pltpu.CompilerParams(vmem_limit_bytes=MIB),
        cost_estimate=pl.CostEstimate(
            flops=0, bytes_accessed=2 * rows * source.shape[1], transcendentals=0
        ),
        name="load",
    )(pltpu.with_memory_space_constraint(source, pltpu.HBM), after)


def expert_kernel(near, far, gate_weight, up_weight, down_top, down_weight, *refs):
    outs, (hidden, down_rest, semaphores) = refs[:4], refs[4:]
    rows = near.shape[0] + far.shape[0]
    width, columns = gate_weight.shape
    top = down_top.shape[0]
    quarter = width // 4
    order = (3, 0, 1, 2)
    copies = row_copies(down_weight, down_rest, semaphores, top)
    for copy in copies:
        copy.start()

    size = 128
    row, lane = grid((size, size))
    slot = row & 7
    late = jnp.where(slot >= 3, 1, 0)
    picks = [
        one_hot((lane == row - slot + 6 + late) & (slot - 3 * late == m)) for m in range(3)
    ]
    picks = jnp.concatenate(picks, axis=1)
    blocks = jnp.concatenate([near[...], far[...]], axis=0)
    tails = []
    for first in range(0, rows, size):
        some = blocks[first : first + size]
        parts = [some[:, m * quarter : (m + 1) * quarter] for m in range(3)]
        tails.append(dot(picks, jnp.concatenate(parts, axis=0)).astype(BF16))
    x = jnp.concatenate([blocks, jnp.concatenate(tails, axis=0)], axis=1)
    step = 256 if columns % 256 == 0 else columns
    for f in range(0, columns, step):
        gate = dot(x, gate_weight[:, f : f + step])
        upper = dot(x, up_weight[:, f : f + step])
        hidden[:, f : f + step] = (gate / (1.0 + jnp.exp(-gate)) * upper).astype(BF16)

    picks = [one_hot((lane == row - slot + 3 * (slot - 6) + m) & (slot >= MOST)) for m in range(3)]
    picks = jnp.concatenate(picks, axis=0)
    h = hidden[...]
    for copy in copies:
        copy.wait()
    step = min(512, quarter)
    is_row = (lax.broadcasted_iota(jnp.int32, (rows, step), 0) & 7) < MOST
    each = rows // len(outs)
    moved = {}
    for m in order:
        for n in range(0, quarter, step):
            lanes = slice(m * quarter + n, m * quarter + n + step)
            terms = dot(h[:, :top], down_top[:, lanes]) + dot(h[:, top:], down_rest[:, lanes])
            if m == 3:
                tail = terms.astype(BF16)
                tails = [dot(picks, tail[i : i + size]) for i in range(0, rows, size)]
                for k in range(3):
                    moved[k, n] = jnp.concatenate(
                        [t[k * size : (k + 1) * size] for t in tails], axis=0
                    ).astype(BF16)
                continue
            value = jnp.where(is_row, terms, moved[m, n].astype(F32)).astype(BF16)
            for k, out in enumerate(outs):
                out[:, lanes] = value[k * each : (k + 1) * each]


def expert_rows(near, far, gate_weight, up_weight, down_top, down_weight):
    rows = near.shape[0] + far.shape[0]
    width, columns = gate_weight.shape
    return pl.pallas_call(
        expert_kernel,
        out_shape=[jax.ShapeDtypeStruct((rows // 4, width // 4 * 3), BF16)] * 4,
        in_specs=[VMEM] * 5 + [ANY],
        out_specs=[VMEM] * 4,
        scratch_shapes=[
            pltpu.VMEM((rows, columns), BF16),
            pltpu.VMEM((columns - down_top.shape[0], width), BF16),
            pltpu.SemaphoreType.DMA((WAYS,)),
        ],
        compiler_params=pltpu.CompilerParams(
            vmem_limit_bytes=2 * (columns - down_top.shape[0]) * width
            + 4 * MIB * max(1, rows // 128)
        ),
        cost_estimate=pl.CostEstimate(
            flops=6 * rows * width * columns, bytes_accessed=0, transcendentals=rows * columns
        ),
        name="experts",
    )(
        near,
        far,
        gate_weight,
        up_weight,
        down_top,
        pltpu.with_memory_space_constraint(down_weight, pltpu.HBM),
    )


def join_kernel(*refs):
    out, row = refs[-1], 0
    for piece in refs[1:-1]:
        out[row : row + piece.shape[0]] = piece[...]
        row += piece.shape[0]


def join(after, *pieces):
    rows = sum(piece.shape[0] for piece in pieces)
    return pl.pallas_call(
        join_kernel,
        out_shape=jax.ShapeDtypeStruct((rows, pieces[0].shape[1]), BF16),
        in_specs=[ANY] + [VMEM] * len(pieces),
        out_specs=VMEM,
        compiler_params=pltpu.CompilerParams(vmem_limit_bytes=1 * MIB),
        name="join",
    )(after, *pieces)


def fold_kernel(held, arrived, after, *outs):
    each = outs[0].shape[0]
    for k, out in enumerate(outs):
        block = slice(k * each, (k + 1) * each)
        out[...] = (held[block].astype(F32) + arrived[block].astype(F32)).astype(BF16)


def fold(held, arrived, after):
    rows, width = held.shape
    return pl.pallas_call(
        fold_kernel,
        out_shape=[jax.ShapeDtypeStruct((rows // 2, width), BF16)] * 2,
        in_specs=[VMEM] * 2 + [ANY],
        out_specs=[VMEM] * 2,
        compiler_params=pltpu.CompilerParams(vmem_limit_bytes=MIB * max(1, rows // 64)),
        cost_estimate=pl.CostEstimate(flops=0, bytes_accessed=16 * MIB, transcendentals=0),
        name="fold",
    )(held, arrived, after)


def combine_kernel(first, share, take, *refs):
    results, before, out = refs[:2], refs[2:-1], refs[-1]
    rows = out.shape[0]
    quarter = results[0].shape[1] // 3
    picks = [take[i][:, 8 * first : 8 * first + 16] for i in range(4)]
    shares = share[:, :1]
    block = jnp.concatenate([x[...] for x in results], axis=0)
    for m, value in enumerate(unpack(picks, block)):
        lanes = slice(m * quarter, (m + 1) * quarter)
        value = value * shares
        value = value[:rows] + value[rows:]
        for x in before:
            value = value + x[:, lanes]
        out[:, lanes] = value.astype(out.dtype)


def combine(first, share, take, results, before, dtype):
    width = results[0].shape[1] // 3 * 4
    return pl.pallas_call(
        functools.partial(combine_kernel, first),
        out_shape=jax.ShapeDtypeStruct((share.shape[0] // 2, width), dtype),
        in_specs=[VMEM] * (4 + len(before)),
        out_specs=VMEM,
        compiler_params=pltpu.CompilerParams(vmem_limit_bytes=2 * MIB),
        cost_estimate=pl.CostEstimate(flops=0, bytes_accessed=16 * MIB, transcendentals=0),
        name="combine",
    )(share, take, *results, *before)


def swap(value, count, bit):
    return lax.ppermute(value, "dp", [(i, i ^ bit) for i in range(count)])


def body(
    queries,
    new_keys,
    new_values,
    cache_keys,
    cache_values,
    lengths,
    residual,
    norm_gain,
    router_weight,
    gate_weight,
    up_weight,
    down_weight,
    routes,
):
    count = lax.axis_size("dp")
    plane = count // EXPERTS
    bits = [1 << k for k in reversed(range(plane.bit_length() - 1))]
    attended, *packed, share, take = attend(
        plane, queries, new_keys, new_values, cache_keys, cache_values, lengths, residual, norm_gain,
        router_weight, routes, down_weight,
    )

    packed = [packed[0]] + [swap(packed[k], count, k * plane) for k in range(1, EXPERTS)]
    near = join(share, *packed[:2])
    far = join(share, *packed[2:])
    columns = down_weight.shape[0]
    down_top, token = load(down_weight, max(256, columns // 512 * 256), far)
    for bit in bits:
        near = join(share, near, swap(near, count, bit))
        far = join(token, far, swap(far, count, bit))

    near, near_send, far, far_send = expert_rows(
        near, far, gate_weight, up_weight, down_top, down_weight
    )
    for bit in reversed(bits):
        far, far_send = fold(far, swap(far_send, count, bit), share)
    for bit in reversed(bits):
        near, near_send = fold(near, swap(near_send, count, bit), far)
    far = swap(far, count, 2 * plane)
    far_send = swap(far_send, count, 3 * plane)
    near_send = swap(near_send, count, plane)
    total = combine(2, share, take, [far, far_send], [], F32)
    return (attended, combine(0, share, take, [near, near_send], [total], BF16))


def solution(mesh):
    placed = (
        P(("group", "dp"), None),
        P(("group", "dp"), None),
        P(("group", "dp"), None),
        P(("group", "dp"), None, None),
        P(("group", "dp"), None, None),
        P(("group", "dp")),
        P(("group", "dp"), None),
        P(),
        P(),
        P(None, "dp"),
        P(None, "dp"),
        P("dp", None),
        P("group", None),
    )
    return jax.shard_map(
        body,
        mesh=mesh,
        in_specs=placed,
        out_specs=(P(("group", "dp"), None), P(("group", "dp"), None)),
        check_vma=False,
    )
```

```python
import functools

import jax
import jax.numpy as jnp
from jax import lax
from jax.experimental import pallas as pl
from jax.experimental.pallas import tpu as pltpu
from jax.sharding import PartitionSpec as P

HEADS = 32
KV_HEADS = 8
HEAD_DIM = 128
EXPERTS = 4
MIB = 1 << 20
HINTS = 4
MOST = 6
F32 = jnp.float32
BF16 = jnp.bfloat16
VMEM = pl.BlockSpec(memory_space=pltpu.VMEM)
ANY = pl.BlockSpec(memory_space=pl.ANY)


def dot(a, b, contract_last=False):
    dims = (((1,), (1 if contract_last else 0,)), ((), ()))
    return lax.dot_general(a, b, dims, preferred_element_type=F32)


def one_hot(mask):
    return mask.astype(F32).astype(BF16)


def grid(shape):
    return [lax.broadcasted_iota(jnp.int32, shape, axis) for axis in (0, 1)]


def pack(picks, block):
    quarter = block.shape[1] // 4
    parts = [block[:, m * quarter : (m + 1) * quarter] for m in range(4)]
    return [
        (dot(picks[0], parts[m]) + dot(picks[1 + m], parts[3])).astype(BF16) for m in range(3)
    ]


def unpack(picks, block):
    quarter = block.shape[1] // 3
    parts = [block[:, m * quarter : (m + 1) * quarter] for m in range(3)]
    tail = dot(picks[1], parts[0]) + dot(picks[2], parts[1]) + dot(picks[3], parts[2])
    return [dot(picks[0], part) for part in parts] + [tail]


def attend_kernel(plane, *refs):
    refs = refs[:10] + refs[10 + HINTS :]
    sources, attended, packed, (share, take), held, semaphores = (
        refs[:10], refs[10], refs[11:15], refs[15:17], refs[17:27], refs[27]
    )
    copies = [
        pltpu.make_async_copy(source, target, semaphores.at[i])
        for i, (source, target) in enumerate(zip(sources, held))
    ]
    for copy in copies[9:] + copies[:9]:
        copy.start()
    (queries, cache_keys, new_keys, lengths, cache_values, new_values, residual, gain, router,
     routes) = held
    rows, width = queries.shape
    positions = cache_keys.shape[1]
    groups = HEADS // KV_HEADS
    scale = 1.0 / HEAD_DIM**0.5
    every = rows * positions
    block = groups * rows

    copies[9].wait()
    index = lax.axis_index("dp")
    base = index * rows
    own = index // plane
    sub, lane = grid((2 * rows, 128))
    expert_down = jnp.zeros((2 * rows, 128), jnp.int32)
    slot_down = jnp.zeros((2 * rows, 128), jnp.int32)
    across = lax.broadcasted_iota(jnp.int32, (8, 128), 1)
    expert_across = jnp.zeros((8, 128), jnp.int32)
    slot_across = jnp.zeros((8, 128), jnp.int32)
    counts = [jnp.int32(0)] * EXPERTS
    for r in range(rows):
        names = [routes[c, base + r] ^ own for c in range(2)]
        for choice, name in ((r, names[0]), (rows + r, names[1])):
            slot = jnp.int32(0)
            for e in range(EXPERTS):
                slot = jnp.where(name == e, counts[e], slot)
            expert_down = jnp.where(sub == choice, name, expert_down)
            slot_down = jnp.where(sub == choice, slot, slot_down)
            expert_across = jnp.where(across == choice, name, expert_across)
            slot_across = jnp.where(across == choice, slot, slot_across)
        for e in range(EXPERTS):
            named = (names[0] == e) | (names[1] == e)
            counts[e] = counts[e] + jnp.where(named, 1, 0)

    late = jnp.where(slot_down >= 3, 1, 0)
    take[0] = one_hot(lane == expert_down * 8 + slot_down)
    for m in range(3):
        take[1 + m] = one_hot((lane == expert_down * 8 + 6 + late) & (slot_down - 3 * late == m))
    place, choice = grid((8 * EXPERTS, 128))
    expert, slot = expert_across[0:1], slot_across[0:1]
    late = jnp.where(slot >= 3, 1, 0)
    chosen = choice < 2 * rows
    picks = [one_hot((place == expert * 8 + slot) & chosen)]
    for m in range(3):
        picks.append(one_hot((place == expert * 8 + 6 + late) & (slot - 3 * late == m) & chosen))
    for copy in copies[:4]:
        copy.wait()

    query = queries[...].astype(F32)
    stacked = jnp.concatenate(
        [query[:, h * HEAD_DIM : (h + 1) * HEAD_DIM] for h in range(HEADS)], axis=0
    )
    stacked_b = stacked.astype(BF16)
    keys = cache_keys[...].reshape(every, KV_HEADS * HEAD_DIM)
    newk = new_keys[...].astype(F32)

    row_of = lax.broadcasted_iota(jnp.int32, (block, every), 0) % rows
    column = lax.broadcasted_iota(jnp.int32, (block, every), 1)
    position = column % positions
    column_row = column // positions
    limit = jnp.zeros((block, every), jnp.int32)
    for r in range(rows):
        limit = jnp.where(column_row == r, lengths[r], limit)
    valid = (row_of == column_row) & (position < limit)

    heads = range(KV_HEADS)
    lanes = [slice(g * HEAD_DIM, (g + 1) * HEAD_DIM) for g in heads]
    mine = [slice(g * block, (g + 1) * block) for g in heads]
    scores = [dot(stacked_b[mine[g]], keys[:, lanes[g]], contract_last=True) for g in heads]
    scores = [jnp.where(valid, score * scale, -jnp.inf) for score in scores]
    own_keys = [jnp.concatenate([newk[:, lanes[g]]] * groups, axis=0) for g in heads]
    new_scores = [
        jnp.sum(stacked[mine[g]] * own_keys[g], axis=1, keepdims=True) * scale for g in heads
    ]
    peaks = [
        jnp.maximum(jnp.max(score, axis=1, keepdims=True), new)
        for score, new in zip(scores, new_scores)
    ]
    weights = [jnp.exp(score - peak) for score, peak in zip(scores, peaks)]
    new_weights = [jnp.exp(new - peak) for new, peak in zip(new_scores, peaks)]
    totals = [
        jnp.sum(weight, axis=1, keepdims=True) + new
        for weight, new in zip(weights, new_weights)
    ]
    inverses = [1.0 / total for total in totals]
    probs = [(weight * inverse).astype(BF16) for weight, inverse in zip(weights, inverses)]
    new_probs = [
        (new * inverse).astype(BF16).astype(F32) for new, inverse in zip(new_weights, inverses)
    ]
    for copy in copies[4:9]:
        copy.wait()
    values = cache_values[...].reshape(every, KV_HEADS * HEAD_DIM)
    newv = new_values[...].astype(F32)
    mixed = [
        dot(probs[g], values[:, lanes[g]])
        + new_probs[g] * jnp.concatenate([newv[:, lanes[g]]] * groups, axis=0)
        for g in heads
    ]
    pieces = [value[j * rows : (j + 1) * rows] for value in mixed for j in range(groups)]

    states = (residual[...].astype(F32) + jnp.concatenate(pieces, axis=1)).astype(BF16)
    attended[...] = states
    states = states.astype(F32)
    norm = lax.rsqrt(jnp.mean(states * states, axis=1, keepdims=True) + 1e-05)
    gains = gain[...].astype(F32)
    logits = [jnp.zeros((rows, 128), F32) for _ in range(EXPERTS)]
    parts = []
    for c in range(width // 128):
        lanes = slice(c * 128, (c + 1) * 128)
        part = (states[:, lanes] * norm * gains[c : c + 1]).astype(BF16).astype(F32)
        parts.append(part)
        for e in range(EXPERTS):
            logits[e] += part * router[e : e + 1, lanes].astype(F32)
    logits = [jnp.sum(value, axis=1, keepdims=True) for value in logits]

    normed = jnp.concatenate(parts, axis=1)
    normed = jnp.concatenate([normed, normed], axis=0).astype(BF16)
    quarter = width // 4
    for m, value in enumerate(pack([pick[:, : 2 * rows] for pick in picks], normed)):
        for k, target in enumerate(packed):
            target[:, m * quarter : (m + 1) * quarter] = value[8 * k : 8 * k + 8]

    chosen_logits = jnp.zeros((2 * rows, 1), F32)
    for e in range(EXPERTS):
        both = jnp.concatenate([logits[e], logits[e]], axis=0)
        chosen_logits = jnp.where(expert_down[:, :1] == (own ^ e), both, chosen_logits)
    other = jnp.concatenate([chosen_logits[rows:], chosen_logits[:rows]], axis=0)
    share[...] = jnp.broadcast_to(1.0 / (1.0 + jnp.exp(other - chosen_logits)), share.shape)


def attend(plane, queries, new_keys, new_values, cache_keys, cache_values, lengths, residual,
           norm_gain, router_weight, routes, weight):
    rows, width = queries.shape
    operands = (
        queries,
        cache_keys,
        new_keys,
        lengths,
        cache_values,
        new_values,
        residual,
        norm_gain.reshape(-1, 128),
        router_weight.T,
        routes.T,
    )
    in_smem = (3, 9)
    return pl.pallas_call(
        functools.partial(attend_kernel, plane),
        out_shape=(
            jax.ShapeDtypeStruct((rows, width), BF16),
            *[jax.ShapeDtypeStruct((8, width * 3 // 4), BF16)] * EXPERTS,
            jax.ShapeDtypeStruct((2 * rows, 128), F32),
            jax.ShapeDtypeStruct((4, 2 * rows, 128), BF16),
        ),
        in_specs=[ANY] * (len(operands) + HINTS),
        out_specs=(VMEM,) * (3 + EXPERTS),
        scratch_shapes=[
            (pltpu.SMEM if i in in_smem else pltpu.VMEM)(operand.shape, operand.dtype)
            for i, operand in enumerate(operands)
        ]
        + [pltpu.SemaphoreType.DMA((len(operands),))],
        compiler_params=pltpu.CompilerParams(vmem_limit_bytes=5 * MIB),
        name="attend",
    )(*[pltpu.with_memory_space_constraint(x, pltpu.HBM) for x in operands + (weight,) * HINTS])


def hidden_kernel(near, far, gate_weight, up_weight, down_weight, hidden):
    columns = gate_weight.shape[1]
    step = 256 if columns % 256 == 0 else columns
    quarter = near.shape[1] // 3
    blocks = jnp.concatenate([near[...], far[...]], axis=0)
    size = 128
    row, lane = grid((size, size))
    slot = row & 7
    late = jnp.where(slot >= 3, 1, 0)
    picks = [
        one_hot((lane == row - slot + 6 + late) & (slot - 3 * late == m)) for m in range(3)
    ]
    picks = jnp.concatenate(picks, axis=1)
    tails = []
    for first in range(0, blocks.shape[0], size):
        some = blocks[first : first + size]
        parts = [some[:, m * quarter : (m + 1) * quarter] for m in range(3)]
        tails.append(dot(picks, jnp.concatenate(parts, axis=0)).astype(BF16))
    x = jnp.concatenate([blocks, jnp.concatenate(tails, axis=0)], axis=1)
    for f in range(0, columns, step):
        gate = dot(x, gate_weight[:, f : f + step])
        upper = dot(x, up_weight[:, f : f + step])
        hidden[:, f : f + step] = (gate / (1.0 + jnp.exp(-gate)) * upper).astype(BF16)


def hidden_rows(near, far, gate_weight, up_weight, down_weight):
    rows = near.shape[0] + far.shape[0]
    width, columns = gate_weight.shape
    return pl.pallas_call(
        hidden_kernel,
        out_shape=jax.ShapeDtypeStruct((rows, columns), BF16),
        in_specs=[VMEM] * 5,
        out_specs=VMEM,
        compiler_params=pltpu.CompilerParams(vmem_limit_bytes=4 * MIB * max(1, rows // 128)),
        cost_estimate=pl.CostEstimate(
            flops=4 * rows * width * columns, bytes_accessed=0, transcendentals=rows * columns
        ),
        name="hidden",
    )(near, far, gate_weight, up_weight, down_weight)


def down_kernel(hidden, weight, *outs):
    rows = hidden.shape[0]
    quarter = outs[0].shape[1] // 3
    size = 128
    row, lane = grid((size, size))
    slot = row & 7
    picks = [one_hot((lane == row - slot + 3 * (slot - 6) + m) & (slot >= MOST)) for m in range(3)]
    picks = jnp.concatenate(picks, axis=0)
    h = hidden[...]

    def terms(first, count):
        return dot(h, weight[:, first : first + count])

    step = min(512, quarter)
    is_row = (lax.broadcasted_iota(jnp.int32, (rows, step), 0) & 7) < MOST
    each = rows // len(outs)
    for n in range(0, quarter, step):
        tail = terms(3 * quarter + n, step).astype(BF16)
        tails = [dot(picks, tail[i : i + size]) for i in range(0, rows, size)]
        for m in range(3):
            moved = jnp.concatenate([x[m * size : (m + 1) * size] for x in tails], axis=0)
            value = jnp.where(is_row, terms(m * quarter + n, step), moved).astype(BF16)
            for k, out in enumerate(outs):
                out[:, m * quarter + n : m * quarter + n + step] = value[k * each : (k + 1) * each]


def down_rows(hidden, weight):
    rows, columns = hidden.shape
    width = weight.shape[1]
    return pl.pallas_call(
        down_kernel,
        out_shape=[jax.ShapeDtypeStruct((rows // 4, width // 4 * 3), BF16)] * 4,
        in_specs=[VMEM] * 2,
        out_specs=[VMEM] * 4,
        compiler_params=pltpu.CompilerParams(vmem_limit_bytes=4 * MIB * max(1, rows // 128)),
        cost_estimate=pl.CostEstimate(
            flops=2 * rows * width * columns, bytes_accessed=0, transcendentals=0
        ),
        name="down",
    )(hidden, weight)


def join_kernel(*refs):
    out, row = refs[-1], 0
    for piece in refs[:-1]:
        out[row : row + piece.shape[0]] = piece[...]
        row += piece.shape[0]


def join(*pieces):
    rows = sum(piece.shape[0] for piece in pieces)
    return pl.pallas_call(
        join_kernel,
        out_shape=jax.ShapeDtypeStruct((rows, pieces[0].shape[1]), BF16),
        in_specs=[VMEM] * len(pieces),
        out_specs=VMEM,
        compiler_params=pltpu.CompilerParams(vmem_limit_bytes=1 * MIB),
        name="join",
    )(*pieces)


def fold_kernel(held, arrived, after, *outs):
    each = outs[0].shape[0]
    for k, out in enumerate(outs):
        block = slice(k * each, (k + 1) * each)
        out[...] = (held[block].astype(F32) + arrived[block].astype(F32)).astype(BF16)


def fold(held, arrived, after):
    rows, width = held.shape
    return pl.pallas_call(
        fold_kernel,
        out_shape=[jax.ShapeDtypeStruct((rows // 2, width), BF16)] * 2,
        in_specs=[VMEM] * 2 + [ANY],
        out_specs=[VMEM] * 2,
        compiler_params=pltpu.CompilerParams(vmem_limit_bytes=MIB * max(1, rows // 64)),
        cost_estimate=pl.CostEstimate(flops=0, bytes_accessed=16 * MIB, transcendentals=0),
        name="fold",
    )(held, arrived, after)


def combine_kernel(first, share, take, *refs):
    results, before, out = refs[:2], refs[2:-1], refs[-1]
    rows = out.shape[0]
    quarter = results[0].shape[1] // 3
    picks = [take[i][:, 8 * first : 8 * first + 16] for i in range(4)]
    shares = share[:, :1]
    block = jnp.concatenate([x[...] for x in results], axis=0)
    for m, value in enumerate(unpack(picks, block)):
        lanes = slice(m * quarter, (m + 1) * quarter)
        value = value * shares
        value = value[:rows] + value[rows:]
        for x in before:
            value = value + x[:, lanes]
        out[:, lanes] = value.astype(out.dtype)


def combine(first, share, take, results, before, dtype):
    width = results[0].shape[1] // 3 * 4
    return pl.pallas_call(
        functools.partial(combine_kernel, first),
        out_shape=jax.ShapeDtypeStruct((share.shape[0] // 2, width), dtype),
        in_specs=[VMEM] * (4 + len(before)),
        out_specs=VMEM,
        compiler_params=pltpu.CompilerParams(vmem_limit_bytes=2 * MIB),
        cost_estimate=pl.CostEstimate(flops=0, bytes_accessed=16 * MIB, transcendentals=0),
        name="combine",
    )(share, take, *results, *before)


def swap(value, count, bit):
    return lax.ppermute(value, "dp", [(i, i ^ bit) for i in range(count)])


def body(
    queries,
    new_keys,
    new_values,
    cache_keys,
    cache_values,
    lengths,
    residual,
    norm_gain,
    router_weight,
    gate_weight,
    up_weight,
    down_weight,
    routes,
):
    count = lax.axis_size("dp")
    plane = count // EXPERTS
    bits = [1 << k for k in reversed(range(plane.bit_length() - 1))]
    attended, *packed, share, take = attend(
        plane, queries, new_keys, new_values, cache_keys, cache_values, lengths, residual, norm_gain,
        router_weight, routes, down_weight,
    )

    packed = [packed[0]] + [swap(packed[k], count, k * plane) for k in range(1, EXPERTS)]
    near = join(*packed[:2])
    far = join(*packed[2:])
    for bit in bits:
        near = join(near, swap(near, count, bit))
        far = join(far, swap(far, count, bit))

    hidden = hidden_rows(near, far, gate_weight, up_weight, down_weight)
    near, near_send, far, far_send = down_rows(hidden, down_weight)
    for bit in reversed(bits):
        far, far_send = fold(far, swap(far_send, count, bit), share)
    for bit in reversed(bits):
        near, near_send = fold(near, swap(near_send, count, bit), far)
    far = swap(far, count, 2 * plane)
    far_send = swap(far_send, count, 3 * plane)
    near_send = swap(near_send, count, plane)
    total = combine(2, share, take, [far, far_send], [], F32)
    return (attended, combine(0, share, take, [near, near_send], [total], BF16))


def solution(mesh):
    placed = (
        P(("group", "dp"), None),
        P(("group", "dp"), None),
        P(("group", "dp"), None),
        P(("group", "dp"), None, None),
        P(("group", "dp"), None, None),
        P(("group", "dp")),
        P(("group", "dp"), None),
        P(),
        P(),
        P(None, "dp"),
        P(None, "dp"),
        P("dp", None),
        P("group", None),
    )
    return jax.shard_map(
        body,
        mesh=mesh,
        in_specs=placed,
        out_specs=(P(("group", "dp"), None), P(("group", "dp"), None)),
        check_vma=False,
    )
```

```python
import functools

import jax
import jax.numpy as jnp
from jax import lax
from jax.experimental import pallas as pl
from jax.experimental.pallas import tpu as pltpu
from jax.sharding import PartitionSpec as P

HEADS = 32
KV_HEADS = 8
HEAD_DIM = 128
EXPERTS = 4
MIB = 1 << 20
HINTS = 4
MOST = 6
F32 = jnp.float32
BF16 = jnp.bfloat16
VMEM = pl.BlockSpec(memory_space=pltpu.VMEM)
ANY = pl.BlockSpec(memory_space=pl.ANY)


def dot(a, b, contract_last=False):
    dims = (((1,), (1 if contract_last else 0,)), ((), ()))
    return lax.dot_general(a, b, dims, preferred_element_type=F32)


def one_hot(mask):
    return mask.astype(F32).astype(BF16)


def grid(shape):
    return [lax.broadcasted_iota(jnp.int32, shape, axis) for axis in (0, 1)]


def pack(picks, block):
    quarter = block.shape[1] // 4
    parts = [block[:, m * quarter : (m + 1) * quarter] for m in range(4)]
    return [
        (dot(picks[0], parts[m]) + dot(picks[1 + m], parts[3])).astype(BF16) for m in range(3)
    ]


def unpack(picks, block):
    quarter = block.shape[1] // 3
    parts = [block[:, m * quarter : (m + 1) * quarter] for m in range(3)]
    tail = dot(picks[1], parts[0]) + dot(picks[2], parts[1]) + dot(picks[3], parts[2])
    return [dot(picks[0], part) for part in parts] + [tail]


def attend_kernel(plane, *refs):
    refs = refs[:10] + refs[10 + HINTS :]
    sources, attended, packed, (share, take), held, semaphores = (
        refs[:10], refs[10], refs[11:15], refs[15:17], refs[17:27], refs[27]
    )
    copies = [
        pltpu.make_async_copy(source, target, semaphores.at[i])
        for i, (source, target) in enumerate(zip(sources, held))
    ]
    for copy in copies[9:] + copies[:9]:
        copy.start()
    (queries, cache_keys, new_keys, lengths, cache_values, new_values, residual, gain, router,
     routes) = held
    rows, width = queries.shape
    positions = cache_keys.shape[1]
    groups = HEADS // KV_HEADS
    scale = 1.0 / HEAD_DIM**0.5
    every = rows * positions
    block = groups * rows

    copies[9].wait()
    index = lax.axis_index("dp")
    base = index * rows
    own = index // plane
    sub, lane = grid((2 * rows, 128))
    expert_down = jnp.zeros((2 * rows, 128), jnp.int32)
    slot_down = jnp.zeros((2 * rows, 128), jnp.int32)
    across = lax.broadcasted_iota(jnp.int32, (8, 128), 1)
    expert_across = jnp.zeros((8, 128), jnp.int32)
    slot_across = jnp.zeros((8, 128), jnp.int32)
    counts = [jnp.int32(0)] * EXPERTS
    for r in range(rows):
        names = [routes[c, base + r] ^ own for c in range(2)]
        for choice, name in ((r, names[0]), (rows + r, names[1])):
            slot = jnp.int32(0)
            for e in range(EXPERTS):
                slot = jnp.where(name == e, counts[e], slot)
            expert_down = jnp.where(sub == choice, name, expert_down)
            slot_down = jnp.where(sub == choice, slot, slot_down)
            expert_across = jnp.where(across == choice, name, expert_across)
            slot_across = jnp.where(across == choice, slot, slot_across)
        for e in range(EXPERTS):
            named = (names[0] == e) | (names[1] == e)
            counts[e] = counts[e] + jnp.where(named, 1, 0)

    late = jnp.where(slot_down >= 3, 1, 0)
    take[0] = one_hot(lane == expert_down * 8 + slot_down)
    for m in range(3):
        take[1 + m] = one_hot((lane == expert_down * 8 + 6 + late) & (slot_down - 3 * late == m))
    place, choice = grid((8 * EXPERTS, 128))
    expert, slot = expert_across[0:1], slot_across[0:1]
    late = jnp.where(slot >= 3, 1, 0)
    chosen = choice < 2 * rows
    picks = [one_hot((place == expert * 8 + slot) & chosen)]
    for m in range(3):
        picks.append(one_hot((place == expert * 8 + 6 + late) & (slot - 3 * late == m) & chosen))
    for copy in copies[:4]:
        copy.wait()

    query = queries[...].astype(F32)
    stacked = jnp.concatenate(
        [query[:, h * HEAD_DIM : (h + 1) * HEAD_DIM] for h in range(HEADS)], axis=0
    )
    stacked_b = stacked.astype(BF16)
    keys = cache_keys[...].reshape(every, KV_HEADS * HEAD_DIM)
    newk = new_keys[...].astype(F32)

    row_of = lax.broadcasted_iota(jnp.int32, (block, every), 0) % rows
    column = lax.broadcasted_iota(jnp.int32, (block, every), 1)
    position = column % positions
    column_row = column // positions
    limit = jnp.zeros((block, every), jnp.int32)
    for r in range(rows):
        limit = jnp.where(column_row == r, lengths[r], limit)
    valid = (row_of == column_row) & (position < limit)

    heads = range(KV_HEADS)
    lanes = [slice(g * HEAD_DIM, (g + 1) * HEAD_DIM) for g in heads]
    mine = [slice(g * block, (g + 1) * block) for g in heads]
    scores = [dot(stacked_b[mine[g]], keys[:, lanes[g]], contract_last=True) for g in heads]
    scores = [jnp.where(valid, score * scale, -jnp.inf) for score in scores]
    own_keys = [jnp.concatenate([newk[:, lanes[g]]] * groups, axis=0) for g in heads]
    new_scores = [
        jnp.sum(stacked[mine[g]] * own_keys[g], axis=1, keepdims=True) * scale for g in heads
    ]
    peaks = [
        jnp.maximum(jnp.max(score, axis=1, keepdims=True), new)
        for score, new in zip(scores, new_scores)
    ]
    weights = [jnp.exp(score - peak) for score, peak in zip(scores, peaks)]
    new_weights = [jnp.exp(new - peak) for new, peak in zip(new_scores, peaks)]
    totals = [
        jnp.sum(weight, axis=1, keepdims=True) + new
        for weight, new in zip(weights, new_weights)
    ]
    inverses = [1.0 / total for total in totals]
    probs = [(weight * inverse).astype(BF16) for weight, inverse in zip(weights, inverses)]
    new_probs = [
        (new * inverse).astype(BF16).astype(F32) for new, inverse in zip(new_weights, inverses)
    ]
    for copy in copies[4:9]:
        copy.wait()
    values = cache_values[...].reshape(every, KV_HEADS * HEAD_DIM)
    newv = new_values[...].astype(F32)
    mixed = [
        dot(probs[g], values[:, lanes[g]])
        + new_probs[g] * jnp.concatenate([newv[:, lanes[g]]] * groups, axis=0)
        for g in heads
    ]
    pieces = [value[j * rows : (j + 1) * rows] for value in mixed for j in range(groups)]

    states = (residual[...].astype(F32) + jnp.concatenate(pieces, axis=1)).astype(BF16)
    attended[...] = states
    states = states.astype(F32)
    norm = lax.rsqrt(jnp.mean(states * states, axis=1, keepdims=True) + 1e-05)
    gains = gain[...].astype(F32)
    logits = [jnp.zeros((rows, 128), F32) for _ in range(EXPERTS)]
    parts = []
    for c in range(width // 128):
        lanes = slice(c * 128, (c + 1) * 128)
        part = (states[:, lanes] * norm * gains[c : c + 1]).astype(BF16).astype(F32)
        parts.append(part)
        for e in range(EXPERTS):
            logits[e] += part * router[e : e + 1, lanes].astype(F32)
    logits = [jnp.sum(value, axis=1, keepdims=True) for value in logits]

    normed = jnp.concatenate(parts, axis=1)
    normed = jnp.concatenate([normed, normed], axis=0).astype(BF16)
    quarter = width // 4
    for m, value in enumerate(pack([pick[:, : 2 * rows] for pick in picks], normed)):
        for k, target in enumerate(packed):
            target[:, m * quarter : (m + 1) * quarter] = value[8 * k : 8 * k + 8]

    chosen_logits = jnp.zeros((2 * rows, 1), F32)
    for e in range(EXPERTS):
        both = jnp.concatenate([logits[e], logits[e]], axis=0)
        chosen_logits = jnp.where(expert_down[:, :1] == (own ^ e), both, chosen_logits)
    other = jnp.concatenate([chosen_logits[rows:], chosen_logits[:rows]], axis=0)
    share[...] = jnp.broadcast_to(1.0 / (1.0 + jnp.exp(other - chosen_logits)), share.shape)


def attend(plane, queries, new_keys, new_values, cache_keys, cache_values, lengths, residual,
           norm_gain, router_weight, routes, weight):
    rows, width = queries.shape
    operands = (
        queries,
        cache_keys,
        new_keys,
        lengths,
        cache_values,
        new_values,
        residual,
        norm_gain.reshape(-1, 128),
        router_weight.T,
        routes.T,
    )
    in_smem = (3, 9)
    return pl.pallas_call(
        functools.partial(attend_kernel, plane),
        out_shape=(
            jax.ShapeDtypeStruct((rows, width), BF16),
            *[jax.ShapeDtypeStruct((8, width * 3 // 4), BF16)] * EXPERTS,
            jax.ShapeDtypeStruct((2 * rows, 128), F32),
            jax.ShapeDtypeStruct((4, 2 * rows, 128), BF16),
        ),
        in_specs=[ANY] * (len(operands) + HINTS),
        out_specs=(VMEM,) * (3 + EXPERTS),
        scratch_shapes=[
            (pltpu.SMEM if i in in_smem else pltpu.VMEM)(operand.shape, operand.dtype)
            for i, operand in enumerate(operands)
        ]
        + [pltpu.SemaphoreType.DMA((len(operands),))],
        compiler_params=pltpu.CompilerParams(vmem_limit_bytes=5 * MIB),
        name="attend",
    )(*[pltpu.with_memory_space_constraint(x, pltpu.HBM) for x in operands + (weight,) * HINTS])


def hidden_kernel(gate_weight, up_weight, down_weight, *refs):
    waves, hidden = refs[:-1], refs[-1]
    columns = gate_weight.shape[1]
    step = 256 if columns % 256 == 0 else columns
    quarter = waves[0].shape[1] // 3
    blocks = jnp.concatenate([wave[...] for wave in waves], axis=0)
    size = 128
    row, lane = grid((size, size))
    slot = row & 7
    late = jnp.where(slot >= 3, 1, 0)
    picks = [
        one_hot((lane == row - slot + 6 + late) & (slot - 3 * late == m)) for m in range(3)
    ]
    picks = jnp.concatenate(picks, axis=1)
    tails = []
    for first in range(0, blocks.shape[0], size):
        some = blocks[first : first + size]
        parts = [some[:, m * quarter : (m + 1) * quarter] for m in range(3)]
        tails.append(dot(picks, jnp.concatenate(parts, axis=0)).astype(BF16))
    x = jnp.concatenate([blocks, jnp.concatenate(tails, axis=0)], axis=1)
    for f in range(0, columns, step):
        gate = dot(x, gate_weight[:, f : f + step])
        upper = dot(x, up_weight[:, f : f + step])
        hidden[:, f : f + step] = (gate / (1.0 + jnp.exp(-gate)) * upper).astype(BF16)


def hidden_rows(waves, gate_weight, up_weight, down_weight):
    rows = sum(wave.shape[0] for wave in waves)
    width, columns = gate_weight.shape
    return pl.pallas_call(
        hidden_kernel,
        out_shape=jax.ShapeDtypeStruct((rows, columns), BF16),
        in_specs=[VMEM] * (3 + len(waves)),
        out_specs=VMEM,
        compiler_params=pltpu.CompilerParams(vmem_limit_bytes=4 * MIB * max(1, rows // 128)),
        cost_estimate=pl.CostEstimate(
            flops=4 * rows * width * columns, bytes_accessed=0, transcendentals=rows * columns
        ),
        name="hidden",
    )(gate_weight, up_weight, down_weight, *waves)


def down_kernel(hidden, weight, *outs):
    rows = hidden.shape[0]
    quarter = outs[0].shape[1] // 3
    size = 128
    row, lane = grid((size, size))
    slot = row & 7
    picks = [one_hot((lane == row - slot + 3 * (slot - 6) + m) & (slot >= MOST)) for m in range(3)]
    picks = jnp.concatenate(picks, axis=0)
    h = hidden[...]

    def terms(first, count):
        return dot(h, weight[:, first : first + count])

    step = min(512, quarter)
    is_row = (lax.broadcasted_iota(jnp.int32, (rows, step), 0) & 7) < MOST
    for n in range(0, quarter, step):
        tail = terms(3 * quarter + n, step).astype(BF16)
        tails = [dot(picks, tail[i : i + size]) for i in range(0, rows, size)]
        for m in range(3):
            moved = jnp.concatenate([x[m * size : (m + 1) * size] for x in tails], axis=0)
            value = jnp.where(is_row, terms(m * quarter + n, step), moved).astype(BF16)
            lanes = slice(m * quarter + n, m * quarter + n + step)
            for out, blocks in zip(outs, ways_back(rows // 32)):
                for i, b in enumerate(blocks):
                    out[8 * i : 8 * i + 8, lanes] = value[8 * b : 8 * b + 8]


def ways_back(places):
    near = [2 * p + j for high in range(0, places, 2) for j in (0, 1) for p in (high, high + 1)]
    two = [2 * places + 2 * p for p in range(places)]
    three = [b + 1 for b in two]
    return [half for w in (near, two, three) for half in (w[: len(w) // 2], w[len(w) // 2 :])]


def down_rows(hidden, weight):
    rows, columns = hidden.shape
    width = weight.shape[1]
    sizes = [8 * len(blocks) for blocks in ways_back(rows // 32)]
    outs = pl.pallas_call(
        down_kernel,
        out_shape=[jax.ShapeDtypeStruct((size, width // 4 * 3), BF16) for size in sizes],
        in_specs=[VMEM] * 2,
        out_specs=[VMEM] * len(sizes),
        compiler_params=pltpu.CompilerParams(vmem_limit_bytes=4 * MIB * max(1, rows // 128)),
        cost_estimate=pl.CostEstimate(
            flops=2 * rows * width * columns, bytes_accessed=0, transcendentals=0
        ),
        name="down",
    )(hidden, weight)
    return outs[0:2], outs[2:4], outs[4:6]


def join_kernel(*refs):
    out, row = refs[-1], 0
    for piece in refs[1:-1]:
        out[row : row + piece.shape[0]] = piece[...]
        row += piece.shape[0]


def join(after, *pieces):
    rows = sum(piece.shape[0] for piece in pieces)
    return pl.pallas_call(
        join_kernel,
        out_shape=jax.ShapeDtypeStruct((rows, pieces[0].shape[1]), BF16),
        in_specs=[ANY] + [VMEM] * len(pieces),
        out_specs=VMEM,
        compiler_params=pltpu.CompilerParams(vmem_limit_bytes=1 * MIB),
        cost_estimate=pl.CostEstimate(flops=0, bytes_accessed=0, transcendentals=0),
        name="join",
    )(after, *pieces)


def fold_kernel(held, arrived, after, *outs):
    each = outs[0].shape[0]
    for k, out in enumerate(outs):
        block = slice(k * each, (k + 1) * each)
        out[...] = (held[block].astype(F32) + arrived[block].astype(F32)).astype(BF16)


def fold(held, arrived, after, parts):
    rows, width = held.shape
    return pl.pallas_call(
        fold_kernel,
        out_shape=[jax.ShapeDtypeStruct((rows // parts, width), BF16)] * parts,
        in_specs=[VMEM] * 2 + [ANY],
        out_specs=[VMEM] * parts,
        compiler_params=pltpu.CompilerParams(vmem_limit_bytes=MIB * max(1, rows // 64)),
        cost_estimate=pl.CostEstimate(flops=0, bytes_accessed=0, transcendentals=0),
        name="fold",
    )(held, arrived, after)


def combine_kernel(first, share, take, *refs):
    results, before, out = refs[:2], refs[2:-1], refs[-1]
    rows = out.shape[0]
    quarter = results[0].shape[1] // 3
    picks = [take[i][:, 8 * first : 8 * first + 16] for i in range(4)]
    shares = share[:, :1]
    block = jnp.concatenate([x[...] for x in results], axis=0)
    for m, value in enumerate(unpack(picks, block)):
        lanes = slice(m * quarter, (m + 1) * quarter)
        value = value * shares
        value = value[:rows] + value[rows:]
        for x in before:
            value = value + x[:, lanes]
        out[:, lanes] = value.astype(out.dtype)


def combine(first, share, take, results, before, dtype):
    width = results[0].shape[1] // 3 * 4
    return pl.pallas_call(
        functools.partial(combine_kernel, first),
        out_shape=jax.ShapeDtypeStruct((share.shape[0] // 2, width), dtype),
        in_specs=[VMEM] * (4 + len(before)),
        out_specs=VMEM,
        compiler_params=pltpu.CompilerParams(vmem_limit_bytes=2 * MIB),
        cost_estimate=pl.CostEstimate(flops=0, bytes_accessed=16 * MIB, transcendentals=0),
        name="combine",
    )(share, take, *results, *before)


def swap(value, count, bit):
    return lax.ppermute(value, "dp", [(i, i ^ bit) for i in range(count)])


def body(
    queries,
    new_keys,
    new_values,
    cache_keys,
    cache_values,
    lengths,
    residual,
    norm_gain,
    router_weight,
    gate_weight,
    up_weight,
    down_weight,
    routes,
):
    count = lax.axis_size("dp")
    plane = count // EXPERTS
    bits = [1 << k for k in reversed(range(plane.bit_length() - 1))]
    attended, *packed, share, take = attend(
        plane, queries, new_keys, new_values, cache_keys, cache_values, lengths, residual, norm_gain,
        router_weight, routes, down_weight,
    )

    packed = [packed[0]] + [swap(packed[k], count, k * plane) for k in range(1, EXPERTS)]
    waves = [join(share, *packed[:2]), join(share, *packed[2:])]
    for bit in bits:
        waves = [join(share, wave, swap(wave, count, bit)) for wave in waves]

    hidden = hidden_rows(waves, gate_weight, up_weight, down_weight)

    near, two, three = down_rows(hidden, down_weight)

    def back(wave, stage, after, parts=2):
        return fold(wave[0], swap(wave[1], count, bits[-1 - stage]), after, parts)

    last = len(bits) - 1
    token = share
    for stage in range(last):
        two = back(two, stage, token)
        three = back(three, stage, two[0])
        token = three[0]
        near = back(near, stage, token, 4 if stage == last - 1 else 2)
    two = back(two, last, near[0], 1)
    three = back(three, last, two[0], 1)
    one = back(near[2:4], last, three[0], 1)
    zero = back(near[0:2], last, one[0], 1)
    results = [
        zero[0],
        swap(one[0], count, plane),
        swap(two[0], count, 2 * plane),
        swap(three[0], count, 3 * plane),
    ]
    total = combine(2, share, take, results[2:], [], F32)
    return (attended, combine(0, share, take, results[:2], [total], BF16))


def solution(mesh):
    placed = (
        P(("group", "dp"), None),
        P(("group", "dp"), None),
        P(("group", "dp"), None),
        P(("group", "dp"), None, None),
        P(("group", "dp"), None, None),
        P(("group", "dp")),
        P(("group", "dp"), None),
        P(),
        P(),
        P(None, "dp"),
        P(None, "dp"),
        P("dp", None),
        P("group", None),
    )
    return jax.shard_map(
        body,
        mesh=mesh,
        in_specs=placed,
        out_specs=(P(("group", "dp"), None), P(("group", "dp"), None)),
        check_vma=False,
    )
```

```python
import functools

import jax
import jax.numpy as jnp
from jax import lax
from jax.experimental import pallas as pl
from jax.experimental.pallas import tpu as pltpu
from jax.sharding import PartitionSpec as P

HEADS = 32
KV_HEADS = 8
HEAD_DIM = 128
EXPERTS = 4
MIB = 1 << 20
HINTS = 4
MOST = 6
F32 = jnp.float32
BF16 = jnp.bfloat16
VMEM = pl.BlockSpec(memory_space=pltpu.VMEM)
ANY = pl.BlockSpec(memory_space=pl.ANY)


def dot(a, b, contract_last=False):
    dims = (((1,), (1 if contract_last else 0,)), ((), ()))
    return lax.dot_general(a, b, dims, preferred_element_type=F32)


def one_hot(mask):
    return mask.astype(F32).astype(BF16)


def grid(shape):
    return [lax.broadcasted_iota(jnp.int32, shape, axis) for axis in (0, 1)]


def pack(picks, block):
    quarter = block.shape[1] // 4
    parts = [block[:, m * quarter : (m + 1) * quarter] for m in range(4)]
    return [
        (dot(picks[0], parts[m]) + dot(picks[1 + m], parts[3])).astype(BF16) for m in range(3)
    ]


def unpack(picks, block):
    quarter = block.shape[1] // 3
    parts = [block[:, m * quarter : (m + 1) * quarter] for m in range(3)]
    tail = dot(picks[1], parts[0]) + dot(picks[2], parts[1]) + dot(picks[3], parts[2])
    return [dot(picks[0], part) for part in parts] + [tail]


def attend_kernel(plane, *refs):
    refs = refs[:10] + refs[10 + HINTS :]
    sources, attended, packed, (share, take), held, semaphores = (
        refs[:10], refs[10], refs[11:15], refs[15:17], refs[17:27], refs[27]
    )
    copies = [
        pltpu.make_async_copy(source, target, semaphores.at[i])
        for i, (source, target) in enumerate(zip(sources, held))
    ]
    for copy in copies[9:] + copies[:9]:
        copy.start()
    (queries, cache_keys, new_keys, lengths, cache_values, new_values, residual, gain, router,
     routes) = held
    rows, width = queries.shape
    positions = cache_keys.shape[1]
    groups = HEADS // KV_HEADS
    scale = 1.0 / HEAD_DIM**0.5
    every = rows * positions
    block = groups * rows

    copies[9].wait()
    index = lax.axis_index("dp")
    base = index * rows
    own = index // plane
    sub, lane = grid((2 * rows, 128))
    expert_down = jnp.zeros((2 * rows, 128), jnp.int32)
    slot_down = jnp.zeros((2 * rows, 128), jnp.int32)
    across = lax.broadcasted_iota(jnp.int32, (8, 128), 1)
    expert_across = jnp.zeros((8, 128), jnp.int32)
    slot_across = jnp.zeros((8, 128), jnp.int32)
    counts = [jnp.int32(0)] * EXPERTS
    for r in range(rows):
        names = [routes[c, base + r] ^ own for c in range(2)]
        for choice, name in ((r, names[0]), (rows + r, names[1])):
            slot = jnp.int32(0)
            for e in range(EXPERTS):
                slot = jnp.where(name == e, counts[e], slot)
            expert_down = jnp.where(sub == choice, name, expert_down)
            slot_down = jnp.where(sub == choice, slot, slot_down)
            expert_across = jnp.where(across == choice, name, expert_across)
            slot_across = jnp.where(across == choice, slot, slot_across)
        for e in range(EXPERTS):
            named = (names[0] == e) | (names[1] == e)
            counts[e] = counts[e] + jnp.where(named, 1, 0)

    late = jnp.where(slot_down >= 3, 1, 0)
    take[0] = one_hot(lane == expert_down * 8 + slot_down)
    for m in range(3):
        take[1 + m] = one_hot((lane == expert_down * 8 + 6 + late) & (slot_down - 3 * late == m))
    place, choice = grid((8 * EXPERTS, 128))
    expert, slot = expert_across[0:1], slot_across[0:1]
    late = jnp.where(slot >= 3, 1, 0)
    chosen = choice < 2 * rows
    picks = [one_hot((place == expert * 8 + slot) & chosen)]
    for m in range(3):
        picks.append(one_hot((place == expert * 8 + 6 + late) & (slot - 3 * late == m) & chosen))
    for copy in copies[:4]:
        copy.wait()

    query = queries[...].astype(F32)
    stacked = jnp.concatenate(
        [query[:, h * HEAD_DIM : (h + 1) * HEAD_DIM] for h in range(HEADS)], axis=0
    )
    stacked_b = stacked.astype(BF16)
    keys = cache_keys[...].reshape(every, KV_HEADS * HEAD_DIM)
    newk = new_keys[...].astype(F32)

    row_of = lax.broadcasted_iota(jnp.int32, (block, every), 0) % rows
    column = lax.broadcasted_iota(jnp.int32, (block, every), 1)
    position = column % positions
    column_row = column // positions
    limit = jnp.zeros((block, every), jnp.int32)
    for r in range(rows):
        limit = jnp.where(column_row == r, lengths[r], limit)
    valid = (row_of == column_row) & (position < limit)

    heads = range(KV_HEADS)
    lanes = [slice(g * HEAD_DIM, (g + 1) * HEAD_DIM) for g in heads]
    mine = [slice(g * block, (g + 1) * block) for g in heads]
    scores = [dot(stacked_b[mine[g]], keys[:, lanes[g]], contract_last=True) for g in heads]
    scores = [jnp.where(valid, score * scale, -jnp.inf) for score in scores]
    own_keys = [jnp.concatenate([newk[:, lanes[g]]] * groups, axis=0) for g in heads]
    new_scores = [
        jnp.sum(stacked[mine[g]] * own_keys[g], axis=1, keepdims=True) * scale for g in heads
    ]
    peaks = [
        jnp.maximum(jnp.max(score, axis=1, keepdims=True), new)
        for score, new in zip(scores, new_scores)
    ]
    weights = [jnp.exp(score - peak) for score, peak in zip(scores, peaks)]
    new_weights = [jnp.exp(new - peak) for new, peak in zip(new_scores, peaks)]
    totals = [
        jnp.sum(weight, axis=1, keepdims=True) + new
        for weight, new in zip(weights, new_weights)
    ]
    inverses = [1.0 / total for total in totals]
    probs = [(weight * inverse).astype(BF16) for weight, inverse in zip(weights, inverses)]
    new_probs = [
        (new * inverse).astype(BF16).astype(F32) for new, inverse in zip(new_weights, inverses)
    ]
    for copy in copies[4:9]:
        copy.wait()
    values = cache_values[...].reshape(every, KV_HEADS * HEAD_DIM)
    newv = new_values[...].astype(F32)
    mixed = [
        dot(probs[g], values[:, lanes[g]])
        + new_probs[g] * jnp.concatenate([newv[:, lanes[g]]] * groups, axis=0)
        for g in heads
    ]
    pieces = [value[j * rows : (j + 1) * rows] for value in mixed for j in range(groups)]

    states = (residual[...].astype(F32) + jnp.concatenate(pieces, axis=1)).astype(BF16)
    attended[...] = states
    states = states.astype(F32)
    norm = lax.rsqrt(jnp.mean(states * states, axis=1, keepdims=True) + 1e-05)
    gains = gain[...].astype(F32)
    logits = [jnp.zeros((rows, 128), F32) for _ in range(EXPERTS)]
    parts = []
    for c in range(width // 128):
        lanes = slice(c * 128, (c + 1) * 128)
        part = (states[:, lanes] * norm * gains[c : c + 1]).astype(BF16).astype(F32)
        parts.append(part)
        for e in range(EXPERTS):
            logits[e] += part * router[e : e + 1, lanes].astype(F32)
    logits = [jnp.sum(value, axis=1, keepdims=True) for value in logits]

    normed = jnp.concatenate(parts, axis=1)
    normed = jnp.concatenate([normed, normed], axis=0).astype(BF16)
    quarter = width // 4
    for m, value in enumerate(pack([pick[:, : 2 * rows] for pick in picks], normed)):
        for k, target in enumerate(packed):
            target[:, m * quarter : (m + 1) * quarter] = value[8 * k : 8 * k + 8]

    chosen_logits = jnp.zeros((2 * rows, 1), F32)
    for e in range(EXPERTS):
        both = jnp.concatenate([logits[e], logits[e]], axis=0)
        chosen_logits = jnp.where(expert_down[:, :1] == (own ^ e), both, chosen_logits)
    other = jnp.concatenate([chosen_logits[rows:], chosen_logits[:rows]], axis=0)
    share[...] = jnp.broadcast_to(1.0 / (1.0 + jnp.exp(other - chosen_logits)), share.shape)


def attend(plane, queries, new_keys, new_values, cache_keys, cache_values, lengths, residual,
           norm_gain, router_weight, routes, weight):
    rows, width = queries.shape
    operands = (
        queries,
        cache_keys,
        new_keys,
        lengths,
        cache_values,
        new_values,
        residual,
        norm_gain.reshape(-1, 128),
        router_weight.T,
        routes.T,
    )
    in_smem = (3, 9)
    return pl.pallas_call(
        functools.partial(attend_kernel, plane),
        out_shape=(
            jax.ShapeDtypeStruct((rows, width), BF16),
            *[jax.ShapeDtypeStruct((8, width * 3 // 4), BF16)] * EXPERTS,
            jax.ShapeDtypeStruct((2 * rows, 128), F32),
            jax.ShapeDtypeStruct((4, 2 * rows, 128), BF16),
        ),
        in_specs=[ANY] * (len(operands) + HINTS),
        out_specs=(VMEM,) * (3 + EXPERTS),
        scratch_shapes=[
            (pltpu.SMEM if i in in_smem else pltpu.VMEM)(operand.shape, operand.dtype)
            for i, operand in enumerate(operands)
        ]
        + [pltpu.SemaphoreType.DMA((len(operands),))],
        compiler_params=pltpu.CompilerParams(vmem_limit_bytes=5 * MIB),
        name="attend",
    )(*[pltpu.with_memory_space_constraint(x, pltpu.HBM) for x in operands + (weight,) * HINTS])


def hidden_kernel(gate_weight, up_weight, down_weight, *refs):
    waves, hidden = refs[:-1], refs[-1]
    columns = gate_weight.shape[1]
    step = 256 if columns % 256 == 0 else columns
    quarter = waves[0].shape[1] // 3
    blocks = jnp.concatenate([wave[...] for wave in waves], axis=0)
    size = 128
    row, lane = grid((size, size))
    slot = row & 7
    late = jnp.where(slot >= 3, 1, 0)
    picks = [
        one_hot((lane == row - slot + 6 + late) & (slot - 3 * late == m)) for m in range(3)
    ]
    picks = jnp.concatenate(picks, axis=1)
    tails = []
    for first in range(0, blocks.shape[0], size):
        some = blocks[first : first + size]
        parts = [some[:, m * quarter : (m + 1) * quarter] for m in range(3)]
        tails.append(dot(picks, jnp.concatenate(parts, axis=0)).astype(BF16))
    x = jnp.concatenate([blocks, jnp.concatenate(tails, axis=0)], axis=1)
    for f in range(0, columns, step):
        gate = dot(x, gate_weight[:, f : f + step])
        upper = dot(x, up_weight[:, f : f + step])
        hidden[:, f : f + step] = (gate / (1.0 + jnp.exp(-gate)) * upper).astype(BF16)


def hidden_rows(waves, gate_weight, up_weight, down_weight):
    rows = sum(wave.shape[0] for wave in waves)
    width, columns = gate_weight.shape
    return pl.pallas_call(
        hidden_kernel,
        out_shape=jax.ShapeDtypeStruct((rows, columns), BF16),
        in_specs=[VMEM] * (3 + len(waves)),
        out_specs=VMEM,
        compiler_params=pltpu.CompilerParams(vmem_limit_bytes=4 * MIB * max(1, rows // 128)),
        cost_estimate=pl.CostEstimate(
            flops=4 * rows * width * columns, bytes_accessed=0, transcendentals=rows * columns
        ),
        name="hidden",
    )(gate_weight, up_weight, down_weight, *waves)


def down_kernel(hidden, weight, *outs):
    rows = hidden.shape[0]
    quarter = outs[0].shape[1] // 3
    size = 128
    row, lane = grid((size, size))
    slot = row & 7
    picks = [one_hot((lane == row - slot + 3 * (slot - 6) + m) & (slot >= MOST)) for m in range(3)]
    picks = jnp.concatenate(picks, axis=0)
    h = hidden[...]

    def terms(first, count):
        return dot(h, weight[:, first : first + count])

    step = min(512, quarter)
    is_row = (lax.broadcasted_iota(jnp.int32, (rows, step), 0) & 7) < MOST
    for n in range(0, quarter, step):
        tail = terms(3 * quarter + n, step).astype(BF16)
        tails = [dot(picks, tail[i : i + size]) for i in range(0, rows, size)]
        for m in range(3):
            moved = jnp.concatenate([x[m * size : (m + 1) * size] for x in tails], axis=0)
            value = jnp.where(is_row, terms(m * quarter + n, step), moved).astype(BF16)
            lanes = slice(m * quarter + n, m * quarter + n + step)
            for out, blocks in zip(outs, ways_back(rows // 32)):
                for i, b in enumerate(blocks):
                    out[8 * i : 8 * i + 8, lanes] = value[8 * b : 8 * b + 8]


def ways_back(places):
    near = [2 * p + j for high in range(0, places, 2) for j in (0, 1) for p in (high, high + 1)]
    two = [2 * places + 2 * p for p in range(places)]
    three = [b + 1 for b in two]
    return [half for w in (near, two, three) for half in (w[: len(w) // 2], w[len(w) // 2 :])]


def down_rows(hidden, weight):
    rows, columns = hidden.shape
    width = weight.shape[1]
    sizes = [8 * len(blocks) for blocks in ways_back(rows // 32)]
    outs = pl.pallas_call(
        down_kernel,
        out_shape=[jax.ShapeDtypeStruct((size, width // 4 * 3), BF16) for size in sizes],
        in_specs=[VMEM] * 2,
        out_specs=[VMEM] * len(sizes),
        compiler_params=pltpu.CompilerParams(vmem_limit_bytes=4 * MIB * max(1, rows // 128)),
        cost_estimate=pl.CostEstimate(
            flops=2 * rows * width * columns, bytes_accessed=0, transcendentals=0
        ),
        name="down",
    )(hidden, weight)
    return outs[0:2], outs[2:4], outs[4:6]


def join_kernel(*refs):
    out, row = refs[-1], 0
    for piece in refs[1:-1]:
        out[row : row + piece.shape[0]] = piece[...]
        row += piece.shape[0]


def join(after, *pieces):
    rows = sum(piece.shape[0] for piece in pieces)
    return pl.pallas_call(
        join_kernel,
        out_shape=jax.ShapeDtypeStruct((rows, pieces[0].shape[1]), BF16),
        in_specs=[ANY] + [VMEM] * len(pieces),
        out_specs=VMEM,
        compiler_params=pltpu.CompilerParams(vmem_limit_bytes=1 * MIB),
        cost_estimate=pl.CostEstimate(flops=0, bytes_accessed=0, transcendentals=0),
        name="join",
    )(after, *pieces)


def fold_kernel(held, arrived, after, *outs):
    each = outs[0].shape[0]
    for k, out in enumerate(outs):
        block = slice(k * each, (k + 1) * each)
        out[...] = (held[block].astype(F32) + arrived[block].astype(F32)).astype(BF16)


def fold(held, arrived, after, parts):
    rows, width = held.shape
    return pl.pallas_call(
        fold_kernel,
        out_shape=[jax.ShapeDtypeStruct((rows // parts, width), BF16)] * parts,
        in_specs=[VMEM] * 2 + [ANY],
        out_specs=[VMEM] * parts,
        compiler_params=pltpu.CompilerParams(vmem_limit_bytes=MIB * max(1, rows // 64)),
        cost_estimate=pl.CostEstimate(flops=0, bytes_accessed=0, transcendentals=0),
        name="fold",
    )(held, arrived, after)


def combine_kernel(first, share, take, *refs):
    results, before, out = refs[:2], refs[2:-1], refs[-1]
    rows = out.shape[0]
    quarter = results[0].shape[1] // 3
    picks = [take[i][:, 8 * first : 8 * first + 16] for i in range(4)]
    shares = share[:, :1]
    block = jnp.concatenate([x[...] for x in results], axis=0)
    for m, value in enumerate(unpack(picks, block)):
        lanes = slice(m * quarter, (m + 1) * quarter)
        value = value * shares
        value = value[:rows] + value[rows:]
        for x in before:
            value = value + x[:, lanes]
        out[:, lanes] = value.astype(out.dtype)


def combine(first, share, take, results, before, dtype):
    width = results[0].shape[1] // 3 * 4
    return pl.pallas_call(
        functools.partial(combine_kernel, first),
        out_shape=jax.ShapeDtypeStruct((share.shape[0] // 2, width), dtype),
        in_specs=[VMEM] * (4 + len(before)),
        out_specs=VMEM,
        compiler_params=pltpu.CompilerParams(vmem_limit_bytes=2 * MIB),
        cost_estimate=pl.CostEstimate(flops=0, bytes_accessed=16 * MIB, transcendentals=0),
        name="combine",
    )(share, take, *results, *before)


def swap(value, count, bit):
    return lax.ppermute(value, "dp", [(i, i ^ bit) for i in range(count)])


def body(
    queries,
    new_keys,
    new_values,
    cache_keys,
    cache_values,
    lengths,
    residual,
    norm_gain,
    router_weight,
    gate_weight,
    up_weight,
    down_weight,
    routes,
):
    count = lax.axis_size("dp")
    plane = count // EXPERTS
    bits = [1 << k for k in reversed(range(plane.bit_length() - 1))]
    attended, *packed, share, take = attend(
        plane, queries, new_keys, new_values, cache_keys, cache_values, lengths, residual, norm_gain,
        router_weight, routes, down_weight,
    )

    packed = [packed[0]] + [swap(packed[k], count, k * plane) for k in range(1, EXPERTS)]
    waves = [join(share, *packed[:2]), join(share, *packed[2:])]
    for bit in bits:
        waves = [join(share, wave, swap(wave, count, bit)) for wave in waves]

    hidden = hidden_rows(waves, gate_weight, up_weight, down_weight)

    near, two, three = down_rows(hidden, down_weight)

    def back(wave, stage, after, parts=2):
        return fold(wave[0], swap(wave[1], count, bits[-1 - stage]), after, parts)

    last = len(bits) - 1
    token = share
    for stage in range(last):
        two = back(two, stage, token)
        three = back(three, stage, two[0])
        token = three[0]
    two = back(two, last, token, 1)
    for stage in range(last):
        near = back(near, stage, two[0], 4 if stage == last - 1 else 2)
    three = back(three, last, near[0], 1)
    one = back(near[2:4], last, three[0], 1)
    zero = back(near[0:2], last, one[0], 1)
    results = [
        zero[0],
        swap(one[0], count, plane),
        swap(two[0], count, 2 * plane),
        swap(three[0], count, 3 * plane),
    ]
    total = combine(2, share, take, results[2:], [], F32)
    return (attended, combine(0, share, take, results[:2], [total], BF16))


def solution(mesh):
    placed = (
        P(("group", "dp"), None),
        P(("group", "dp"), None),
        P(("group", "dp"), None),
        P(("group", "dp"), None, None),
        P(("group", "dp"), None, None),
        P(("group", "dp")),
        P(("group", "dp"), None),
        P(),
        P(),
        P(None, "dp"),
        P(None, "dp"),
        P("dp", None),
        P("group", None),
    )
    return jax.shard_map(
        body,
        mesh=mesh,
        in_specs=placed,
        out_specs=(P(("group", "dp"), None), P(("group", "dp"), None)),
        check_vma=False,
    )
```

```python
import functools

import jax
import jax.numpy as jnp
from jax import lax
from jax.experimental import pallas as pl
from jax.experimental.pallas import tpu as pltpu
from jax.sharding import PartitionSpec as P

HEADS = 32
KV_HEADS = 8
HEAD_DIM = 128
EXPERTS = 4
MIB = 1 << 20
HINTS = 4
MOST = 6
F32 = jnp.float32
BF16 = jnp.bfloat16
VMEM = pl.BlockSpec(memory_space=pltpu.VMEM)
ANY = pl.BlockSpec(memory_space=pl.ANY)


def dot(a, b, contract_last=False):
    dims = (((1,), (1 if contract_last else 0,)), ((), ()))
    return lax.dot_general(a, b, dims, preferred_element_type=F32)


def one_hot(mask):
    return mask.astype(F32).astype(BF16)


def grid(shape):
    return [lax.broadcasted_iota(jnp.int32, shape, axis) for axis in (0, 1)]


def pack(picks, block):
    quarter = block.shape[1] // 4
    parts = [block[:, m * quarter : (m + 1) * quarter] for m in range(4)]
    return [
        (dot(picks[0], parts[m]) + dot(picks[1 + m], parts[3])).astype(BF16) for m in range(3)
    ]


def unpack(picks, block):
    quarter = block.shape[1] // 3
    parts = [block[:, m * quarter : (m + 1) * quarter] for m in range(3)]
    tail = dot(picks[1], parts[0]) + dot(picks[2], parts[1]) + dot(picks[3], parts[2])
    return [dot(picks[0], part) for part in parts] + [tail]


def attend_kernel(plane, *refs):
    refs = refs[:10] + refs[10 + HINTS :]
    sources, attended, packed, (share, take), held, semaphores = (
        refs[:10], refs[10], refs[11:15], refs[15:17], refs[17:27], refs[27]
    )
    copies = [
        pltpu.make_async_copy(source, target, semaphores.at[i])
        for i, (source, target) in enumerate(zip(sources, held))
    ]
    for copy in copies[9:] + copies[:9]:
        copy.start()
    (queries, cache_keys, new_keys, lengths, cache_values, new_values, residual, gain, router,
     routes) = held
    rows, width = queries.shape
    positions = cache_keys.shape[1]
    groups = HEADS // KV_HEADS
    scale = 1.0 / HEAD_DIM**0.5
    every = rows * positions
    block = groups * rows

    copies[9].wait()
    index = lax.axis_index("dp")
    base = index * rows
    own = index // plane
    sub, lane = grid((2 * rows, 128))
    expert_down = jnp.zeros((2 * rows, 128), jnp.int32)
    slot_down = jnp.zeros((2 * rows, 128), jnp.int32)
    across = lax.broadcasted_iota(jnp.int32, (8, 128), 1)
    expert_across = jnp.zeros((8, 128), jnp.int32)
    slot_across = jnp.zeros((8, 128), jnp.int32)
    counts = [jnp.int32(0)] * EXPERTS
    for r in range(rows):
        names = [routes[c, base + r] ^ own for c in range(2)]
        for choice, name in ((r, names[0]), (rows + r, names[1])):
            slot = jnp.int32(0)
            for e in range(EXPERTS):
                slot = jnp.where(name == e, counts[e], slot)
            expert_down = jnp.where(sub == choice, name, expert_down)
            slot_down = jnp.where(sub == choice, slot, slot_down)
            expert_across = jnp.where(across == choice, name, expert_across)
            slot_across = jnp.where(across == choice, slot, slot_across)
        for e in range(EXPERTS):
            named = (names[0] == e) | (names[1] == e)
            counts[e] = counts[e] + jnp.where(named, 1, 0)

    late = jnp.where(slot_down >= 3, 1, 0)
    take[0] = one_hot(lane == expert_down * 8 + slot_down)
    for m in range(3):
        take[1 + m] = one_hot((lane == expert_down * 8 + 6 + late) & (slot_down - 3 * late == m))
    place, choice = grid((8 * EXPERTS, 128))
    expert, slot = expert_across[0:1], slot_across[0:1]
    late = jnp.where(slot >= 3, 1, 0)
    chosen = choice < 2 * rows
    picks = [one_hot((place == expert * 8 + slot) & chosen)]
    for m in range(3):
        picks.append(one_hot((place == expert * 8 + 6 + late) & (slot - 3 * late == m) & chosen))
    for copy in copies[:4]:
        copy.wait()

    query = queries[...].astype(F32)
    stacked = jnp.concatenate(
        [query[:, h * HEAD_DIM : (h + 1) * HEAD_DIM] for h in range(HEADS)], axis=0
    )
    stacked_b = stacked.astype(BF16)
    keys = cache_keys[...].reshape(every, KV_HEADS * HEAD_DIM)
    newk = new_keys[...].astype(F32)

    row_of = lax.broadcasted_iota(jnp.int32, (block, every), 0) % rows
    column = lax.broadcasted_iota(jnp.int32, (block, every), 1)
    position = column % positions
    column_row = column // positions
    limit = jnp.zeros((block, every), jnp.int32)
    for r in range(rows):
        limit = jnp.where(column_row == r, lengths[r], limit)
    valid = (row_of == column_row) & (position < limit)

    heads = range(KV_HEADS)
    lanes = [slice(g * HEAD_DIM, (g + 1) * HEAD_DIM) for g in heads]
    mine = [slice(g * block, (g + 1) * block) for g in heads]
    scores = [dot(stacked_b[mine[g]], keys[:, lanes[g]], contract_last=True) for g in heads]
    scores = [jnp.where(valid, score * scale, -jnp.inf) for score in scores]
    own_keys = [jnp.concatenate([newk[:, lanes[g]]] * groups, axis=0) for g in heads]
    new_scores = [
        jnp.sum(stacked[mine[g]] * own_keys[g], axis=1, keepdims=True) * scale for g in heads
    ]
    peaks = [
        jnp.maximum(jnp.max(score, axis=1, keepdims=True), new)
        for score, new in zip(scores, new_scores)
    ]
    weights = [jnp.exp(score - peak) for score, peak in zip(scores, peaks)]
    new_weights = [jnp.exp(new - peak) for new, peak in zip(new_scores, peaks)]
    totals = [
        jnp.sum(weight, axis=1, keepdims=True) + new
        for weight, new in zip(weights, new_weights)
    ]
    inverses = [1.0 / total for total in totals]
    probs = [(weight * inverse).astype(BF16) for weight, inverse in zip(weights, inverses)]
    new_probs = [
        (new * inverse).astype(BF16).astype(F32) for new, inverse in zip(new_weights, inverses)
    ]
    for copy in copies[4:9]:
        copy.wait()
    values = cache_values[...].reshape(every, KV_HEADS * HEAD_DIM)
    newv = new_values[...].astype(F32)
    mixed = [
        dot(probs[g], values[:, lanes[g]])
        + new_probs[g] * jnp.concatenate([newv[:, lanes[g]]] * groups, axis=0)
        for g in heads
    ]
    pieces = [value[j * rows : (j + 1) * rows] for value in mixed for j in range(groups)]

    states = (residual[...].astype(F32) + jnp.concatenate(pieces, axis=1)).astype(BF16)
    attended[...] = states
    states = states.astype(F32)
    norm = lax.rsqrt(jnp.mean(states * states, axis=1, keepdims=True) + 1e-05)
    gains = gain[...].astype(F32)
    logits = [jnp.zeros((rows, 128), F32) for _ in range(EXPERTS)]
    parts = []
    for c in range(width // 128):
        lanes = slice(c * 128, (c + 1) * 128)
        part = (states[:, lanes] * norm * gains[c : c + 1]).astype(BF16).astype(F32)
        parts.append(part)
        for e in range(EXPERTS):
            logits[e] += part * router[e : e + 1, lanes].astype(F32)
    logits = [jnp.sum(value, axis=1, keepdims=True) for value in logits]

    normed = jnp.concatenate(parts, axis=1)
    normed = jnp.concatenate([normed, normed], axis=0).astype(BF16)
    quarter = width // 4
    for m, value in enumerate(pack([pick[:, : 2 * rows] for pick in picks], normed)):
        for k, target in enumerate(packed):
            target[:, m * quarter : (m + 1) * quarter] = value[8 * k : 8 * k + 8]

    chosen_logits = jnp.zeros((2 * rows, 1), F32)
    for e in range(EXPERTS):
        both = jnp.concatenate([logits[e], logits[e]], axis=0)
        chosen_logits = jnp.where(expert_down[:, :1] == (own ^ e), both, chosen_logits)
    other = jnp.concatenate([chosen_logits[rows:], chosen_logits[:rows]], axis=0)
    share[...] = jnp.broadcast_to(1.0 / (1.0 + jnp.exp(other - chosen_logits)), share.shape)


def attend(plane, queries, new_keys, new_values, cache_keys, cache_values, lengths, residual,
           norm_gain, router_weight, routes, weight):
    rows, width = queries.shape
    operands = (
        queries,
        cache_keys,
        new_keys,
        lengths,
        cache_values,
        new_values,
        residual,
        norm_gain.reshape(-1, 128),
        router_weight.T,
        routes.T,
    )
    in_smem = (3, 9)
    return pl.pallas_call(
        functools.partial(attend_kernel, plane),
        out_shape=(
            jax.ShapeDtypeStruct((rows, width), BF16),
            *[jax.ShapeDtypeStruct((8, width * 3 // 4), BF16)] * EXPERTS,
            jax.ShapeDtypeStruct((2 * rows, 128), F32),
            jax.ShapeDtypeStruct((4, 2 * rows, 128), BF16),
        ),
        in_specs=[ANY] * (len(operands) + HINTS),
        out_specs=(VMEM,) * (3 + EXPERTS),
        scratch_shapes=[
            (pltpu.SMEM if i in in_smem else pltpu.VMEM)(operand.shape, operand.dtype)
            for i, operand in enumerate(operands)
        ]
        + [pltpu.SemaphoreType.DMA((len(operands),))],
        compiler_params=pltpu.CompilerParams(vmem_limit_bytes=5 * MIB),
        name="attend",
    )(*[pltpu.with_memory_space_constraint(x, pltpu.HBM) for x in operands + (weight,) * HINTS])


def hidden_kernel(gate_weight, up_weight, down_weight, *refs):
    waves, hidden = refs[:-1], refs[-1]
    columns = gate_weight.shape[1]
    step = 256 if columns % 256 == 0 else columns
    quarter = waves[0].shape[1] // 3
    blocks = jnp.concatenate([wave[...] for wave in waves], axis=0)
    size = 128
    row, lane = grid((size, size))
    slot = row & 7
    late = jnp.where(slot >= 3, 1, 0)
    picks = [
        one_hot((lane == row - slot + 6 + late) & (slot - 3 * late == m)) for m in range(3)
    ]
    picks = jnp.concatenate(picks, axis=1)
    tails = []
    for first in range(0, blocks.shape[0], size):
        some = blocks[first : first + size]
        parts = [some[:, m * quarter : (m + 1) * quarter] for m in range(3)]
        tails.append(dot(picks, jnp.concatenate(parts, axis=0)).astype(BF16))
    x = jnp.concatenate([blocks, jnp.concatenate(tails, axis=0)], axis=1)
    for f in range(0, columns, step):
        gate = dot(x, gate_weight[:, f : f + step])
        upper = dot(x, up_weight[:, f : f + step])
        hidden[:, f : f + step] = (gate / (1.0 + jnp.exp(-gate)) * upper).astype(BF16)


def hidden_rows(waves, gate_weight, up_weight, down_weight):
    rows = sum(wave.shape[0] for wave in waves)
    width, columns = gate_weight.shape
    return pl.pallas_call(
        hidden_kernel,
        out_shape=jax.ShapeDtypeStruct((rows, columns), BF16),
        in_specs=[VMEM] * (3 + len(waves)),
        out_specs=VMEM,
        compiler_params=pltpu.CompilerParams(vmem_limit_bytes=4 * MIB * max(1, rows // 128)),
        cost_estimate=pl.CostEstimate(
            flops=4 * rows * width * columns, bytes_accessed=0, transcendentals=rows * columns
        ),
        name="hidden",
    )(gate_weight, up_weight, down_weight, *waves)


def down_kernel(hidden, weight, *outs):
    rows = hidden.shape[0]
    quarter = outs[0].shape[1] // 3
    size = 128
    row, lane = grid((size, size))
    slot = row & 7
    picks = [one_hot((lane == row - slot + 3 * (slot - 6) + m) & (slot >= MOST)) for m in range(3)]
    picks = jnp.concatenate(picks, axis=0)
    h = hidden[...]

    def terms(first, count):
        return dot(h, weight[:, first : first + count])

    step = min(512, quarter)
    is_row = (lax.broadcasted_iota(jnp.int32, (rows, step), 0) & 7) < MOST
    for n in range(0, quarter, step):
        tail = terms(3 * quarter + n, step).astype(BF16)
        tails = [dot(picks, tail[i : i + size]) for i in range(0, rows, size)]
        for m in range(3):
            moved = jnp.concatenate([x[m * size : (m + 1) * size] for x in tails], axis=0)
            value = jnp.where(is_row, terms(m * quarter + n, step), moved).astype(BF16)
            lanes = slice(m * quarter + n, m * quarter + n + step)
            for out, blocks in zip(outs, ways_back(rows // 32)):
                for i, b in enumerate(blocks):
                    out[8 * i : 8 * i + 8, lanes] = value[8 * b : 8 * b + 8]


def ways_back(places):
    blocks = []
    for k in range(EXPERTS):
        groups = [k // 2 * 2 * places + 2 * p + k % 2 for p in range(places)]
        blocks += [groups[: places // 2], groups[places // 2 :]]
    return blocks


def down_rows(hidden, weight):
    rows, columns = hidden.shape
    width = weight.shape[1]
    sizes = [8 * len(blocks) for blocks in ways_back(rows // 32)]
    outs = pl.pallas_call(
        down_kernel,
        out_shape=[jax.ShapeDtypeStruct((size, width // 4 * 3), BF16) for size in sizes],
        in_specs=[VMEM] * 2,
        out_specs=[VMEM] * len(sizes),
        compiler_params=pltpu.CompilerParams(vmem_limit_bytes=4 * MIB * max(1, rows // 128)),
        cost_estimate=pl.CostEstimate(
            flops=2 * rows * width * columns, bytes_accessed=0, transcendentals=0
        ),
        name="down",
    )(hidden, weight)
    return [outs[2 * k : 2 * k + 2] for k in range(EXPERTS)]


def join_kernel(*refs):
    out, row = refs[-1], 0
    for piece in refs[1:-1]:
        out[row : row + piece.shape[0]] = piece[...]
        row += piece.shape[0]


def join(after, *pieces):
    rows = sum(piece.shape[0] for piece in pieces)
    return pl.pallas_call(
        join_kernel,
        out_shape=jax.ShapeDtypeStruct((rows, pieces[0].shape[1]), BF16),
        in_specs=[ANY] + [VMEM] * len(pieces),
        out_specs=VMEM,
        compiler_params=pltpu.CompilerParams(vmem_limit_bytes=1 * MIB),
        cost_estimate=pl.CostEstimate(flops=0, bytes_accessed=0, transcendentals=0),
        name="join",
    )(after, *pieces)


def fold_kernel(held, arrived, after, *outs):
    each = outs[0].shape[0]
    for k, out in enumerate(outs):
        block = slice(k * each, (k + 1) * each)
        out[...] = (held[block].astype(F32) + arrived[block].astype(F32)).astype(BF16)


def fold(held, arrived, after, parts):
    rows, width = held.shape
    return pl.pallas_call(
        fold_kernel,
        out_shape=[jax.ShapeDtypeStruct((rows // parts, width), BF16)] * parts,
        in_specs=[VMEM] * 2 + [ANY],
        out_specs=[VMEM] * parts,
        compiler_params=pltpu.CompilerParams(vmem_limit_bytes=MIB * max(1, rows // 64)),
        cost_estimate=pl.CostEstimate(flops=0, bytes_accessed=0, transcendentals=0),
        name="fold",
    )(held, arrived, after)


def combine_kernel(first, share, take, *refs):
    results, before, out = refs[:2], refs[2:-1], refs[-1]
    rows = out.shape[0]
    quarter = results[0].shape[1] // 3
    picks = [take[i][:, 8 * first : 8 * first + 16] for i in range(4)]
    shares = share[:, :1]
    block = jnp.concatenate([x[...] for x in results], axis=0)
    for m, value in enumerate(unpack(picks, block)):
        lanes = slice(m * quarter, (m + 1) * quarter)
        value = value * shares
        value = value[:rows] + value[rows:]
        for x in before:
            value = value + x[:, lanes]
        out[:, lanes] = value.astype(out.dtype)


def combine(first, share, take, results, before, dtype):
    width = results[0].shape[1] // 3 * 4
    return pl.pallas_call(
        functools.partial(combine_kernel, first),
        out_shape=jax.ShapeDtypeStruct((share.shape[0] // 2, width), dtype),
        in_specs=[VMEM] * (4 + len(before)),
        out_specs=VMEM,
        compiler_params=pltpu.CompilerParams(vmem_limit_bytes=2 * MIB),
        cost_estimate=pl.CostEstimate(flops=0, bytes_accessed=16 * MIB, transcendentals=0),
        name="combine",
    )(share, take, *results, *before)


def swap(value, count, bit):
    return lax.ppermute(value, "dp", [(i, i ^ bit) for i in range(count)])


def body(
    queries,
    new_keys,
    new_values,
    cache_keys,
    cache_values,
    lengths,
    residual,
    norm_gain,
    router_weight,
    gate_weight,
    up_weight,
    down_weight,
    routes,
):
    count = lax.axis_size("dp")
    plane = count // EXPERTS
    bits = [1 << k for k in reversed(range(plane.bit_length() - 1))]
    attended, *packed, share, take = attend(
        plane, queries, new_keys, new_values, cache_keys, cache_values, lengths, residual, norm_gain,
        router_weight, routes, down_weight,
    )

    packed = [packed[0]] + [swap(packed[k], count, k * plane) for k in range(1, EXPERTS)]
    waves = [join(share, *packed[:2]), join(share, *packed[2:])]
    for bit in bits:
        waves = [join(share, wave, swap(wave, count, bit)) for wave in waves]

    hidden = hidden_rows(waves, gate_weight, up_weight, down_weight)

    blocks = down_rows(hidden, down_weight)

    def back(k, stage, after):
        held, send = blocks[k]
        parts = 1 if stage == last else 2
        blocks[k] = fold(held, swap(send, count, bits[-1 - stage]), after, parts)
        return blocks[k][0]

    last = len(bits) - 1
    token = share
    for stage in range(last):
        for k in (3, 2, 1):
            token = back(k, stage, token)
    token = back(3, last, token)
    for stage in range(last):
        back(0, stage, token)
    token = back(2, last, token)
    token = back(1, last, token)
    back(0, last, token)
    results = [blocks[0][0]] + [swap(blocks[k][0], count, k * plane) for k in (1, 2, 3)]
    total = combine(2, share, take, results[2:], [], F32)
    return (attended, combine(0, share, take, results[:2], [total], BF16))


def solution(mesh):
    placed = (
        P(("group", "dp"), None),
        P(("group", "dp"), None),
        P(("group", "dp"), None),
        P(("group", "dp"), None, None),
        P(("group", "dp"), None, None),
        P(("group", "dp")),
        P(("group", "dp"), None),
        P(),
        P(),
        P(None, "dp"),
        P(None, "dp"),
        P("dp", None),
        P("group", None),
    )
    return jax.shard_map(
        body,
        mesh=mesh,
        in_specs=placed,
        out_specs=(P(("group", "dp"), None), P(("group", "dp"), None)),
        check_vma=False,
    )
```

```python
import functools

import jax
import jax.numpy as jnp
from jax import lax
from jax.experimental import pallas as pl
from jax.experimental.pallas import tpu as pltpu
from jax.sharding import PartitionSpec as P

HEADS = 32
KV_HEADS = 8
HEAD_DIM = 128
EXPERTS = 4
MIB = 1 << 20
HINTS = 4
MOST = 6
F32 = jnp.float32
BF16 = jnp.bfloat16
VMEM = pl.BlockSpec(memory_space=pltpu.VMEM)
ANY = pl.BlockSpec(memory_space=pl.ANY)


def dot(a, b, contract_last=False):
    dims = (((1,), (1 if contract_last else 0,)), ((), ()))
    return lax.dot_general(a, b, dims, preferred_element_type=F32)


def one_hot(mask):
    return mask.astype(F32).astype(BF16)


def grid(shape):
    return [lax.broadcasted_iota(jnp.int32, shape, axis) for axis in (0, 1)]


def pack(picks, block):
    quarter = block.shape[1] // 4
    parts = [block[:, m * quarter : (m + 1) * quarter] for m in range(4)]
    return [
        (dot(picks[0], parts[m]) + dot(picks[1 + m], parts[3])).astype(BF16) for m in range(3)
    ]


def unpack(picks, block):
    quarter = block.shape[1] // 3
    parts = [block[:, m * quarter : (m + 1) * quarter] for m in range(3)]
    tail = dot(picks[1], parts[0]) + dot(picks[2], parts[1]) + dot(picks[3], parts[2])
    return [dot(picks[0], part) for part in parts] + [tail]


def attend_kernel(plane, *refs):
    refs = refs[:10] + refs[10 + HINTS :]
    sources, attended, packed, (share, take), held, semaphores = (
        refs[:10], refs[10], refs[11:15], refs[15:17], refs[17:27], refs[28]
    )
    kept = refs[27]
    copies = [
        pltpu.make_async_copy(source, target, semaphores.at[i])
        for i, (source, target) in enumerate(zip(sources, held))
    ]
    for copy in copies[9:] + copies[:9]:
        copy.start()
    (queries, cache_keys, new_keys, lengths, cache_values, new_values, residual, gain, router,
     routes) = held
    rows, width = queries.shape
    positions = cache_keys.shape[1]
    groups = HEADS // KV_HEADS
    scale = 1.0 / HEAD_DIM**0.5
    every = rows * positions
    block = groups * rows

    copies[9].wait()
    index = lax.axis_index("dp")
    base = index * rows
    own = index // plane
    sub, lane = grid((2 * rows, 128))
    expert_down = jnp.zeros((2 * rows, 128), jnp.int32)
    slot_down = jnp.zeros((2 * rows, 128), jnp.int32)
    across = lax.broadcasted_iota(jnp.int32, (8, 128), 1)
    expert_across = jnp.zeros((8, 128), jnp.int32)
    slot_across = jnp.zeros((8, 128), jnp.int32)
    counts = [jnp.int32(0)] * EXPERTS
    for r in range(rows):
        names = [routes[c, base + r] ^ own for c in range(2)]
        for choice, name in ((r, names[0]), (rows + r, names[1])):
            slot = jnp.int32(0)
            for e in range(EXPERTS):
                slot = jnp.where(name == e, counts[e], slot)
            expert_down = jnp.where(sub == choice, name, expert_down)
            slot_down = jnp.where(sub == choice, slot, slot_down)
            expert_across = jnp.where(across == choice, name, expert_across)
            slot_across = jnp.where(across == choice, slot, slot_across)
        for e in range(EXPERTS):
            named = (names[0] == e) | (names[1] == e)
            counts[e] = counts[e] + jnp.where(named, 1, 0)

    late = jnp.where(slot_down >= 3, 1, 0)
    take[0] = one_hot(lane == expert_down * 8 + slot_down)
    for m in range(3):
        take[1 + m] = one_hot((lane == expert_down * 8 + 6 + late) & (slot_down - 3 * late == m))
    place, choice = grid((8 * EXPERTS, 128))
    expert, slot = expert_across[0:1], slot_across[0:1]
    late = jnp.where(slot >= 3, 1, 0)
    chosen = choice < 2 * rows
    picks = [one_hot((place == expert * 8 + slot) & chosen)]
    for m in range(3):
        picks.append(one_hot((place == expert * 8 + 6 + late) & (slot - 3 * late == m) & chosen))
    for copy in copies[:4]:
        copy.wait()

    query = queries[...].astype(F32)
    stacked = jnp.concatenate(
        [query[:, h * HEAD_DIM : (h + 1) * HEAD_DIM] for h in range(HEADS)], axis=0
    )
    stacked_b = stacked.astype(BF16)
    keys = cache_keys[...].reshape(every, KV_HEADS * HEAD_DIM)
    newk = new_keys[...].astype(F32)

    row_of = lax.broadcasted_iota(jnp.int32, (block, every), 0) % rows
    column = lax.broadcasted_iota(jnp.int32, (block, every), 1)
    position = column % positions
    column_row = column // positions
    limit = jnp.zeros((block, every), jnp.int32)
    for r in range(rows):
        limit = jnp.where(column_row == r, lengths[r], limit)
    valid = (row_of == column_row) & (position < limit)

    heads = range(KV_HEADS)
    lanes = [slice(g * HEAD_DIM, (g + 1) * HEAD_DIM) for g in heads]
    mine = [slice(g * block, (g + 1) * block) for g in heads]
    scores = [dot(stacked_b[mine[g]], keys[:, lanes[g]], contract_last=True) for g in heads]
    scores = [jnp.where(valid, score * scale, -jnp.inf) for score in scores]
    own_keys = [jnp.concatenate([newk[:, lanes[g]]] * groups, axis=0) for g in heads]
    new_scores = [
        jnp.sum(stacked[mine[g]] * own_keys[g], axis=1, keepdims=True) * scale for g in heads
    ]
    peaks = [
        jnp.maximum(jnp.max(score, axis=1, keepdims=True), new)
        for score, new in zip(scores, new_scores)
    ]
    weights = [jnp.exp(score - peak) for score, peak in zip(scores, peaks)]
    new_weights = [jnp.exp(new - peak) for new, peak in zip(new_scores, peaks)]
    totals = [
        jnp.sum(weight, axis=1, keepdims=True) + new
        for weight, new in zip(weights, new_weights)
    ]
    inverses = [1.0 / total for total in totals]
    probs = [(weight * inverse).astype(BF16) for weight, inverse in zip(weights, inverses)]
    new_probs = [
        (new * inverse).astype(BF16).astype(F32) for new, inverse in zip(new_weights, inverses)
    ]
    for copy in copies[4:9]:
        copy.wait()
    values = cache_values[...].reshape(every, KV_HEADS * HEAD_DIM)
    newv = new_values[...].astype(F32)
    mixed = [
        dot(probs[g], values[:, lanes[g]])
        + new_probs[g] * jnp.concatenate([newv[:, lanes[g]]] * groups, axis=0)
        for g in heads
    ]
    pieces = [value[j * rows : (j + 1) * rows] for value in mixed for j in range(groups)]

    states = (residual[...].astype(F32) + jnp.concatenate(pieces, axis=1)).astype(BF16)
    attended_copy = pltpu.make_async_copy(kept, attended, semaphores.at[len(copies)])
    kept[...] = states
    attended_copy.start()
    states = states.astype(F32)
    norm = lax.rsqrt(jnp.mean(states * states, axis=1, keepdims=True) + 1e-05)
    gains = gain[...].astype(F32)
    logits = [jnp.zeros((rows, 128), F32) for _ in range(EXPERTS)]
    parts = []
    for c in range(width // 128):
        lanes = slice(c * 128, (c + 1) * 128)
        part = (states[:, lanes] * norm * gains[c : c + 1]).astype(BF16).astype(F32)
        parts.append(part)
        for e in range(EXPERTS):
            logits[e] += part * router[e : e + 1, lanes].astype(F32)
    logits = [jnp.sum(value, axis=1, keepdims=True) for value in logits]

    normed = jnp.concatenate(parts, axis=1)
    normed = jnp.concatenate([normed, normed], axis=0).astype(BF16)
    quarter = width // 4
    for m, value in enumerate(pack([pick[:, : 2 * rows] for pick in picks], normed)):
        for k, target in enumerate(packed):
            target[:, m * quarter : (m + 1) * quarter] = value[8 * k : 8 * k + 8]

    chosen_logits = jnp.zeros((2 * rows, 1), F32)
    for e in range(EXPERTS):
        both = jnp.concatenate([logits[e], logits[e]], axis=0)
        chosen_logits = jnp.where(expert_down[:, :1] == (own ^ e), both, chosen_logits)
    other = jnp.concatenate([chosen_logits[rows:], chosen_logits[:rows]], axis=0)
    share[...] = jnp.broadcast_to(1.0 / (1.0 + jnp.exp(other - chosen_logits)), share.shape)
    attended_copy.wait()


def attend(plane, queries, new_keys, new_values, cache_keys, cache_values, lengths, residual,
           norm_gain, router_weight, routes, weight):
    rows, width = queries.shape
    operands = (
        queries,
        cache_keys,
        new_keys,
        lengths,
        cache_values,
        new_values,
        residual,
        norm_gain.reshape(-1, 128),
        router_weight.T,
        routes.T,
    )
    in_smem = (3, 9)
    return pl.pallas_call(
        functools.partial(attend_kernel, plane),
        out_shape=(
            jax.ShapeDtypeStruct((rows, width), BF16),
            *[jax.ShapeDtypeStruct((8, width * 3 // 4), BF16)] * EXPERTS,
            jax.ShapeDtypeStruct((2 * rows, 128), F32),
            jax.ShapeDtypeStruct((4, 2 * rows, 128), BF16),
        ),
        in_specs=[ANY] * (len(operands) + HINTS),
        out_specs=(ANY,) + (VMEM,) * (2 + EXPERTS),
        scratch_shapes=[
            (pltpu.SMEM if i in in_smem else pltpu.VMEM)(operand.shape, operand.dtype)
            for i, operand in enumerate(operands)
        ]
        + [pltpu.VMEM((rows, width), BF16), pltpu.SemaphoreType.DMA((len(operands) + 1,))],
        compiler_params=pltpu.CompilerParams(vmem_limit_bytes=5 * MIB),
        name="attend",
    )(*[pltpu.with_memory_space_constraint(x, pltpu.HBM) for x in operands + (weight,) * HINTS])


def hidden_kernel(gate_weight, up_weight, down_weight, *refs):
    waves, hidden = refs[:-1], refs[-1]
    columns = gate_weight.shape[1]
    step = 512
    quarter = waves[0].shape[1] // 3
    blocks = jnp.concatenate([wave[...] for wave in waves], axis=0)
    size = 128
    row, lane = grid((size, size))
    slot = row & 7
    late = jnp.where(slot >= 3, 1, 0)
    picks = [
        one_hot((lane == row - slot + 6 + late) & (slot - 3 * late == m)) for m in range(3)
    ]
    picks = jnp.concatenate(picks, axis=1)
    tails = []
    for first in range(0, blocks.shape[0], size):
        some = blocks[first : first + size]
        parts = [some[:, m * quarter : (m + 1) * quarter] for m in range(3)]
        tails.append(dot(picks, jnp.concatenate(parts, axis=0)).astype(BF16))
    x = jnp.concatenate([blocks, jnp.concatenate(tails, axis=0)], axis=1)
    for f in range(0, columns, step):
        last = min(f + step, columns)
        gate = dot(x, gate_weight[:, f:last])
        upper = dot(x, up_weight[:, f:last])
        hidden[:, f:last] = (gate / (1.0 + jnp.exp(-gate)) * upper).astype(BF16)


def hidden_rows(waves, gate_weight, up_weight, down_weight):
    rows = sum(wave.shape[0] for wave in waves)
    width, columns = gate_weight.shape
    return pl.pallas_call(
        hidden_kernel,
        out_shape=jax.ShapeDtypeStruct((rows, columns), BF16),
        in_specs=[VMEM] * (3 + len(waves)),
        out_specs=VMEM,
        compiler_params=pltpu.CompilerParams(vmem_limit_bytes=4 * MIB * max(1, rows // 128)),
        cost_estimate=pl.CostEstimate(
            flops=4 * rows * width * columns, bytes_accessed=0, transcendentals=rows * columns
        ),
        name="hidden",
    )(gate_weight, up_weight, down_weight, *waves)


def down_kernel(hidden, weight, *outs):
    rows = hidden.shape[0]
    quarter = outs[0].shape[1] // 3
    size = 128
    row, lane = grid((size, size))
    slot = row & 7
    picks = [one_hot((lane == row - slot + 3 * (slot - 6) + m) & (slot >= MOST)) for m in range(3)]
    picks = jnp.concatenate(picks, axis=0)
    h = hidden[...]

    def terms(first, count):
        return dot(h, weight[:, first : first + count])

    step = min(1024, quarter)
    is_row = (lax.broadcasted_iota(jnp.int32, (rows, step), 0) & 7) < MOST
    for n in range(0, quarter, step):
        tail = terms(3 * quarter + n, step).astype(BF16)
        tails = [dot(picks, tail[i : i + size]) for i in range(0, rows, size)]
        for m in range(3):
            moved = jnp.concatenate([x[m * size : (m + 1) * size] for x in tails], axis=0)
            value = jnp.where(is_row, terms(m * quarter + n, step), moved).astype(BF16)
            lanes = slice(m * quarter + n, m * quarter + n + step)
            for out, blocks in zip(outs, ways_back(rows // 32)):
                for i, b in enumerate(blocks):
                    out[8 * i : 8 * i + 8, lanes] = value[8 * b : 8 * b + 8]


def ways_back(places):
    near = [2 * p + j for high in range(0, places, 2) for j in (0, 1) for p in (high, high + 1)]
    two = [2 * places + 2 * p for p in range(places)]
    three = [b + 1 for b in two]
    return [half for w in (near, two, three) for half in (w[: len(w) // 2], w[len(w) // 2 :])]


def down_rows(hidden, weight):
    rows, columns = hidden.shape
    width = weight.shape[1]
    sizes = [8 * len(blocks) for blocks in ways_back(rows // 32)]
    outs = pl.pallas_call(
        down_kernel,
        out_shape=[jax.ShapeDtypeStruct((size, width // 4 * 3), BF16) for size in sizes],
        in_specs=[VMEM] * 2,
        out_specs=[VMEM] * len(sizes),
        compiler_params=pltpu.CompilerParams(vmem_limit_bytes=4 * MIB * max(1, rows // 128)),
        cost_estimate=pl.CostEstimate(
            flops=2 * rows * width * columns, bytes_accessed=0, transcendentals=0
        ),
        name="down",
    )(hidden, weight)
    return outs[0:2], outs[2:4], outs[4:6]


def join_kernel(*refs):
    out, row = refs[-1], 0
    for piece in refs[1:-1]:
        out[row : row + piece.shape[0]] = piece[...]
        row += piece.shape[0]


def join(after, *pieces):
    rows = sum(piece.shape[0] for piece in pieces)
    return pl.pallas_call(
        join_kernel,
        out_shape=jax.ShapeDtypeStruct((rows, pieces[0].shape[1]), BF16),
        in_specs=[ANY] + [VMEM] * len(pieces),
        out_specs=VMEM,
        compiler_params=pltpu.CompilerParams(vmem_limit_bytes=1 * MIB),
        cost_estimate=pl.CostEstimate(flops=0, bytes_accessed=0, transcendentals=0),
        name="join",
    )(after, *pieces)


def fold_kernel(held, arrived, after, *outs):
    each = outs[0].shape[0]
    for k, out in enumerate(outs):
        block = slice(k * each, (k + 1) * each)
        out[...] = (held[block].astype(F32) + arrived[block].astype(F32)).astype(BF16)


def fold(held, arrived, after, parts):
    rows, width = held.shape
    return pl.pallas_call(
        fold_kernel,
        out_shape=[jax.ShapeDtypeStruct((rows // parts, width), BF16)] * parts,
        in_specs=[VMEM] * 2 + [ANY],
        out_specs=[VMEM] * parts,
        compiler_params=pltpu.CompilerParams(vmem_limit_bytes=MIB * max(1, rows // 64)),
        cost_estimate=pl.CostEstimate(flops=0, bytes_accessed=0, transcendentals=0),
        name="fold",
    )(held, arrived, after)


def combined(first, share, take, results):
    picks = [take[i][:, 8 * first : 8 * first + 16] for i in range(4)]
    rows = share.shape[0] // 2
    block = jnp.concatenate([x[...] for x in results], axis=0)
    values = [value * share[:, :1] for value in unpack(picks, block)]
    return [value[:rows] + value[rows:] for value in values]


def combine_far_kernel(share, take, two, three, total):
    quarter = two.shape[1] // 3
    for m, value in enumerate(combined(2, share, take, (two, three))):
        total[:, m * quarter : (m + 1) * quarter] = value


def combine_kernel(share, take, zero, one, total, out, held, semaphores):
    quarter = zero.shape[1] // 3
    copies = []
    for m, value in enumerate(combined(0, share, take, (zero, one))):
        lanes = pl.ds(m * quarter, quarter)
        held[:, lanes] = (value + total[:, lanes]).astype(BF16)
        copies.append(
            pltpu.make_async_copy(held.at[:, lanes], out.at[:, lanes], semaphores.at[m])
        )
        copies[m].start()
    for copy in copies:
        copy.wait()


def combine(share, take, results):
    rows, width = share.shape[0] // 2, results[0].shape[1] // 3 * 4
    params = pltpu.CompilerParams(vmem_limit_bytes=2 * MIB)
    cost = pl.CostEstimate(flops=0, bytes_accessed=16 * MIB, transcendentals=0)
    total = pl.pallas_call(
        combine_far_kernel,
        out_shape=jax.ShapeDtypeStruct((rows, width), F32),
        in_specs=[VMEM] * 4,
        out_specs=VMEM,
        compiler_params=params,
        cost_estimate=cost,
        name="combine_far",
    )(share, take, *results[2:])
    return pl.pallas_call(
        combine_kernel,
        out_shape=jax.ShapeDtypeStruct((rows, width), BF16),
        in_specs=[VMEM] * 5,
        out_specs=ANY,
        scratch_shapes=[pltpu.VMEM((rows, width), BF16), pltpu.SemaphoreType.DMA((4,))],
        compiler_params=params,
        cost_estimate=cost,
        name="combine",
    )(share, take, *results[:2], total)


def swap(value, count, bit):
    return lax.ppermute(value, "dp", [(i, i ^ bit) for i in range(count)])


def body(
    queries,
    new_keys,
    new_values,
    cache_keys,
    cache_values,
    lengths,
    residual,
    norm_gain,
    router_weight,
    gate_weight,
    up_weight,
    down_weight,
    routes,
):
    count = lax.axis_size("dp")
    plane = count // EXPERTS
    bits = [1 << k for k in reversed(range(plane.bit_length() - 1))]
    attended, *packed, share, take = attend(
        plane, queries, new_keys, new_values, cache_keys, cache_values, lengths, residual, norm_gain,
        router_weight, routes, down_weight,
    )

    packed = [packed[0]] + [swap(packed[k], count, k * plane) for k in range(1, EXPERTS)]
    waves = [join(share, *packed[:2]), join(share, *packed[2:])]
    for bit in bits:
        waves = [join(share, wave, swap(wave, count, bit)) for wave in waves]

    hidden = hidden_rows(waves, gate_weight, up_weight, down_weight)

    near, two, three = down_rows(hidden, down_weight)

    def back(wave, stage, after, parts=2):
        return fold(wave[0], swap(wave[1], count, bits[-1 - stage]), after, parts)

    last = len(bits) - 1
    token = share
    for stage in range(last):
        two = back(two, stage, token)
        three = back(three, stage, two[0])
        token = three[0]
        near = back(near, stage, token, 4 if stage == last - 1 else 2)
    two = back(two, last, near[0], 1)
    three = back(three, last, two[0], 1)
    one = back(near[2:4], last, three[0], 1)
    zero = back(near[0:2], last, one[0], 1)
    results = [
        zero[0],
        swap(one[0], count, plane),
        swap(two[0], count, 2 * plane),
        swap(three[0], count, 3 * plane),
    ]
    return (attended, combine(share, take, results))


def solution(mesh):
    placed = (
        P(("group", "dp"), None),
        P(("group", "dp"), None),
        P(("group", "dp"), None),
        P(("group", "dp"), None, None),
        P(("group", "dp"), None, None),
        P(("group", "dp")),
        P(("group", "dp"), None),
        P(),
        P(),
        P(None, "dp"),
        P(None, "dp"),
        P("dp", None),
        P("group", None),
    )
    return jax.shard_map(
        body,
        mesh=mesh,
        in_specs=placed,
        out_specs=(P(("group", "dp"), None), P(("group", "dp"), None)),
        check_vma=False,
    )
```

```python
import functools

import jax
import jax.numpy as jnp
from jax import lax
from jax.experimental import pallas as pl
from jax.experimental.pallas import tpu as pltpu
from jax.sharding import PartitionSpec as P

HEADS = 32
KV_HEADS = 8
HEAD_DIM = 128
EXPERTS = 4
MIB = 1 << 20
HINTS = 4
MOST = 6
F32 = jnp.float32
BF16 = jnp.bfloat16
VMEM = pl.BlockSpec(memory_space=pltpu.VMEM)
ANY = pl.BlockSpec(memory_space=pl.ANY)


def dot(a, b, contract_last=False):
    dims = (((1,), (1 if contract_last else 0,)), ((), ()))
    return lax.dot_general(a, b, dims, preferred_element_type=F32)


def one_hot(mask):
    return mask.astype(F32).astype(BF16)


def grid(shape):
    return [lax.broadcasted_iota(jnp.int32, shape, axis) for axis in (0, 1)]


def pack(picks, block):
    quarter = block.shape[1] // 4
    parts = [block[:, m * quarter : (m + 1) * quarter] for m in range(4)]
    return [
        (dot(picks[0], parts[m]) + dot(picks[1 + m], parts[3])).astype(BF16) for m in range(3)
    ]


def unpack(picks, block):
    quarter = block.shape[1] // 3
    parts = [block[:, m * quarter : (m + 1) * quarter] for m in range(3)]
    tail = dot(picks[1], parts[0]) + dot(picks[2], parts[1]) + dot(picks[3], parts[2])
    return [dot(picks[0], part) for part in parts] + [tail]


def attend_kernel(plane, *refs):
    refs = refs[:10] + refs[10 + HINTS :]
    sources, attended, packed, (share, take), held, semaphores = (
        refs[:10], refs[10], refs[11:15], refs[15:17], refs[17:27], refs[28]
    )
    kept = refs[27]
    copies = [
        pltpu.make_async_copy(source, target, semaphores.at[i])
        for i, (source, target) in enumerate(zip(sources, held))
    ]
    for copy in copies[9:] + copies[:9]:
        copy.start()
    (queries, cache_keys, new_keys, lengths, cache_values, new_values, residual, gain, router,
     routes) = held
    rows, width = queries.shape
    positions = cache_keys.shape[1]
    groups = HEADS // KV_HEADS
    scale = 1.0 / HEAD_DIM**0.5
    every = rows * positions
    block = groups * rows

    copies[9].wait()
    index = lax.axis_index("dp")
    base = index * rows
    own = index // plane
    sub, lane = grid((2 * rows, 128))
    expert_down = jnp.zeros((2 * rows, 128), jnp.int32)
    slot_down = jnp.zeros((2 * rows, 128), jnp.int32)
    across = lax.broadcasted_iota(jnp.int32, (8, 128), 1)
    expert_across = jnp.zeros((8, 128), jnp.int32)
    slot_across = jnp.zeros((8, 128), jnp.int32)
    counts = [jnp.int32(0)] * EXPERTS
    for r in range(rows):
        names = [routes[c, base + r] ^ own for c in range(2)]
        for choice, name in ((r, names[0]), (rows + r, names[1])):
            slot = jnp.int32(0)
            for e in range(EXPERTS):
                slot = jnp.where(name == e, counts[e], slot)
            expert_down = jnp.where(sub == choice, name, expert_down)
            slot_down = jnp.where(sub == choice, slot, slot_down)
            expert_across = jnp.where(across == choice, name, expert_across)
            slot_across = jnp.where(across == choice, slot, slot_across)
        for e in range(EXPERTS):
            named = (names[0] == e) | (names[1] == e)
            counts[e] = counts[e] + jnp.where(named, 1, 0)

    late = jnp.where(slot_down >= 3, 1, 0)
    take[0] = one_hot(lane == expert_down * 8 + slot_down)
    for m in range(3):
        take[1 + m] = one_hot((lane == expert_down * 8 + 6 + late) & (slot_down - 3 * late == m))
    place, choice = grid((8 * EXPERTS, 128))
    expert, slot = expert_across[0:1], slot_across[0:1]
    late = jnp.where(slot >= 3, 1, 0)
    chosen = choice < 2 * rows
    picks = [one_hot((place == expert * 8 + slot) & chosen)]
    for m in range(3):
        picks.append(one_hot((place == expert * 8 + 6 + late) & (slot - 3 * late == m) & chosen))
    for copy in copies[:4]:
        copy.wait()

    query = queries[...].astype(F32)
    stacked = jnp.concatenate(
        [query[:, h * HEAD_DIM : (h + 1) * HEAD_DIM] for h in range(HEADS)], axis=0
    )
    stacked_b = stacked.astype(BF16)
    keys = cache_keys[...].reshape(every, KV_HEADS * HEAD_DIM)
    newk = new_keys[...].astype(F32)

    row_of = lax.broadcasted_iota(jnp.int32, (block, every), 0) % rows
    column = lax.broadcasted_iota(jnp.int32, (block, every), 1)
    position = column % positions
    column_row = column // positions
    limit = jnp.zeros((block, every), jnp.int32)
    for r in range(rows):
        limit = jnp.where(column_row == r, lengths[r], limit)
    valid = (row_of == column_row) & (position < limit)

    heads = range(KV_HEADS)
    lanes = [slice(g * HEAD_DIM, (g + 1) * HEAD_DIM) for g in heads]
    mine = [slice(g * block, (g + 1) * block) for g in heads]
    scores = [dot(stacked_b[mine[g]], keys[:, lanes[g]], contract_last=True) for g in heads]
    scores = [jnp.where(valid, score * scale, -jnp.inf) for score in scores]
    own_keys = [jnp.concatenate([newk[:, lanes[g]]] * groups, axis=0) for g in heads]
    new_scores = [
        jnp.sum(stacked[mine[g]] * own_keys[g], axis=1, keepdims=True) * scale for g in heads
    ]
    peaks = [
        jnp.maximum(jnp.max(score, axis=1, keepdims=True), new)
        for score, new in zip(scores, new_scores)
    ]
    weights = [jnp.exp(score - peak) for score, peak in zip(scores, peaks)]
    new_weights = [jnp.exp(new - peak) for new, peak in zip(new_scores, peaks)]
    totals = [
        jnp.sum(weight, axis=1, keepdims=True) + new
        for weight, new in zip(weights, new_weights)
    ]
    inverses = [1.0 / total for total in totals]
    probs = [(weight * inverse).astype(BF16) for weight, inverse in zip(weights, inverses)]
    new_probs = [
        (new * inverse).astype(BF16).astype(F32) for new, inverse in zip(new_weights, inverses)
    ]
    for copy in copies[4:9]:
        copy.wait()
    values = cache_values[...].reshape(every, KV_HEADS * HEAD_DIM)
    newv = new_values[...].astype(F32)
    mixed = [
        dot(probs[g], values[:, lanes[g]])
        + new_probs[g] * jnp.concatenate([newv[:, lanes[g]]] * groups, axis=0)
        for g in heads
    ]
    pieces = [value[j * rows : (j + 1) * rows] for value in mixed for j in range(groups)]

    states = (residual[...].astype(F32) + jnp.concatenate(pieces, axis=1)).astype(BF16)
    attended_copy = pltpu.make_async_copy(kept, attended, semaphores.at[len(copies)])
    kept[...] = states
    attended_copy.start()
    states = states.astype(F32)
    norm = lax.rsqrt(jnp.mean(states * states, axis=1, keepdims=True) + 1e-05)
    gains = gain[...].astype(F32)
    logits = [jnp.zeros((rows, 128), F32) for _ in range(EXPERTS)]
    parts = []
    for c in range(width // 128):
        lanes = slice(c * 128, (c + 1) * 128)
        part = (states[:, lanes] * norm * gains[c : c + 1]).astype(BF16).astype(F32)
        parts.append(part)
        for e in range(EXPERTS):
            logits[e] += part * router[e : e + 1, lanes].astype(F32)
    logits = [jnp.sum(value, axis=1, keepdims=True) for value in logits]

    normed = jnp.concatenate(parts, axis=1)
    normed = jnp.concatenate([normed, normed], axis=0).astype(BF16)
    quarter = width // 4
    for m, value in enumerate(pack([pick[:, : 2 * rows] for pick in picks], normed)):
        for k, target in enumerate(packed):
            target[:, m * quarter : (m + 1) * quarter] = value[8 * k : 8 * k + 8]

    chosen_logits = jnp.zeros((2 * rows, 1), F32)
    for e in range(EXPERTS):
        both = jnp.concatenate([logits[e], logits[e]], axis=0)
        chosen_logits = jnp.where(expert_down[:, :1] == (own ^ e), both, chosen_logits)
    other = jnp.concatenate([chosen_logits[rows:], chosen_logits[:rows]], axis=0)
    share[...] = jnp.broadcast_to(1.0 / (1.0 + jnp.exp(other - chosen_logits)), share.shape)
    attended_copy.wait()


def attend(plane, queries, new_keys, new_values, cache_keys, cache_values, lengths, residual,
           norm_gain, router_weight, routes, weight):
    rows, width = queries.shape
    operands = (
        queries,
        cache_keys,
        new_keys,
        lengths,
        cache_values,
        new_values,
        residual,
        norm_gain.reshape(-1, 128),
        router_weight.T,
        routes.T,
    )
    in_smem = (3, 9)
    return pl.pallas_call(
        functools.partial(attend_kernel, plane),
        out_shape=(
            jax.ShapeDtypeStruct((rows, width), BF16),
            *[jax.ShapeDtypeStruct((8, width * 3 // 4), BF16)] * EXPERTS,
            jax.ShapeDtypeStruct((2 * rows, 128), F32),
            jax.ShapeDtypeStruct((4, 2 * rows, 128), BF16),
        ),
        in_specs=[ANY] * (len(operands) + HINTS),
        out_specs=(ANY,) + (VMEM,) * (2 + EXPERTS),
        scratch_shapes=[
            (pltpu.SMEM if i in in_smem else pltpu.VMEM)(operand.shape, operand.dtype)
            for i, operand in enumerate(operands)
        ]
        + [pltpu.VMEM((rows, width), BF16), pltpu.SemaphoreType.DMA((len(operands) + 1,))],
        compiler_params=pltpu.CompilerParams(vmem_limit_bytes=5 * MIB),
        name="attend",
    )(*[pltpu.with_memory_space_constraint(x, pltpu.HBM) for x in operands + (weight,) * HINTS])


def hidden_kernel(gate_weight, up_weight, down_weight, *refs):
    waves, hidden = refs[:-1], refs[-1]
    columns = gate_weight.shape[1]
    step = 512
    quarter = waves[0].shape[1] // 3
    blocks = jnp.concatenate([wave[...] for wave in waves], axis=0)
    size = 128
    row, lane = grid((size, size))
    slot = row & 7
    late = jnp.where(slot >= 3, 1, 0)
    picks = [
        one_hot((lane == row - slot + 6 + late) & (slot - 3 * late == m)) for m in range(3)
    ]
    picks = jnp.concatenate(picks, axis=1)
    tails = []
    for first in range(0, blocks.shape[0], size):
        some = blocks[first : first + size]
        parts = [some[:, m * quarter : (m + 1) * quarter] for m in range(3)]
        tails.append(dot(picks, jnp.concatenate(parts, axis=0)).astype(BF16))
    x = jnp.concatenate([blocks, jnp.concatenate(tails, axis=0)], axis=1)
    for f in range(0, columns, step):
        last = min(f + step, columns)
        gate = dot(x, gate_weight[:, f:last])
        upper = dot(x, up_weight[:, f:last])
        hidden[:, f:last] = (gate / (1.0 + jnp.exp(-gate)) * upper).astype(BF16)


def hidden_rows(waves, gate_weight, up_weight, down_weight):
    rows = sum(wave.shape[0] for wave in waves)
    width, columns = gate_weight.shape
    return pl.pallas_call(
        hidden_kernel,
        out_shape=jax.ShapeDtypeStruct((rows, columns), BF16),
        in_specs=[VMEM] * (3 + len(waves)),
        out_specs=VMEM,
        compiler_params=pltpu.CompilerParams(vmem_limit_bytes=4 * MIB * max(1, rows // 128)),
        cost_estimate=pl.CostEstimate(
            flops=4 * rows * width * columns, bytes_accessed=0, transcendentals=rows * columns
        ),
        name="hidden",
    )(gate_weight, up_weight, down_weight, *waves)


def down_kernel(hidden, weight, *outs):
    rows = hidden.shape[0]
    quarter = outs[0].shape[1] // 3
    size = 128
    row, lane = grid((size, size))
    slot = row & 7
    picks = [one_hot((lane == row - slot + 3 * (slot - 6) + m) & (slot >= MOST)) for m in range(3)]
    picks = jnp.concatenate(picks, axis=0)
    h = hidden[...]

    def terms(first, count):
        return dot(h, weight[:, first : first + count])

    step = min(1024, quarter)
    is_row = (lax.broadcasted_iota(jnp.int32, (rows, step), 0) & 7) < MOST
    for n in range(0, quarter, step):
        tail = terms(3 * quarter + n, step).astype(BF16)
        tails = [dot(picks, tail[i : i + size]) for i in range(0, rows, size)]
        for m in range(3):
            moved = jnp.concatenate([x[m * size : (m + 1) * size] for x in tails], axis=0)
            value = jnp.where(is_row, terms(m * quarter + n, step), moved).astype(BF16)
            lanes = slice(m * quarter + n, m * quarter + n + step)
            for out, blocks in zip(outs, ways_back(rows // 32)):
                for i, b in enumerate(blocks):
                    out[8 * i : 8 * i + 8, lanes] = value[8 * b : 8 * b + 8]


def ways_back(places):
    halves = []
    for w in (0, 1):
        groups = [
            2 * places * w + 2 * p + j
            for high in range(0, places, 2)
            for j in (0, 1)
            for p in (high, high + 1)
        ]
        halves += [groups[:places], groups[places:]]
    return halves


def down_rows(hidden, weight):
    rows, columns = hidden.shape
    width = weight.shape[1]
    sizes = [8 * len(blocks) for blocks in ways_back(rows // 32)]
    outs = pl.pallas_call(
        down_kernel,
        out_shape=[jax.ShapeDtypeStruct((size, width // 4 * 3), BF16) for size in sizes],
        in_specs=[VMEM] * 2,
        out_specs=[VMEM] * len(sizes),
        compiler_params=pltpu.CompilerParams(vmem_limit_bytes=4 * MIB * max(1, rows // 128)),
        cost_estimate=pl.CostEstimate(
            flops=2 * rows * width * columns, bytes_accessed=0, transcendentals=0
        ),
        name="down",
    )(hidden, weight)
    return outs[0:2], outs[2:4]


def join_kernel(*refs):
    out, row = refs[-1], 0
    for piece in refs[1:-1]:
        out[row : row + piece.shape[0]] = piece[...]
        row += piece.shape[0]


def join(after, *pieces):
    rows = sum(piece.shape[0] for piece in pieces)
    return pl.pallas_call(
        join_kernel,
        out_shape=jax.ShapeDtypeStruct((rows, pieces[0].shape[1]), BF16),
        in_specs=[ANY] + [VMEM] * len(pieces),
        out_specs=VMEM,
        compiler_params=pltpu.CompilerParams(vmem_limit_bytes=1 * MIB),
        cost_estimate=pl.CostEstimate(flops=0, bytes_accessed=0, transcendentals=0),
        name="join",
    )(after, *pieces)


def fold_kernel(held, arrived, after, *outs):
    each = outs[0].shape[0]
    for k, out in enumerate(outs):
        block = slice(k * each, (k + 1) * each)
        out[...] = (held[block].astype(F32) + arrived[block].astype(F32)).astype(BF16)


def fold(held, arrived, after, parts):
    rows, width = held.shape
    return pl.pallas_call(
        fold_kernel,
        out_shape=[jax.ShapeDtypeStruct((rows // parts, width), BF16)] * parts,
        in_specs=[VMEM] * 2 + [ANY],
        out_specs=[VMEM] * parts,
        compiler_params=pltpu.CompilerParams(vmem_limit_bytes=MIB * max(1, rows // 64)),
        cost_estimate=pl.CostEstimate(flops=0, bytes_accessed=0, transcendentals=0),
        name="fold",
    )(held, arrived, after)


def combined(first, share, take, results):
    picks = [take[i][:, 8 * first : 8 * first + 16] for i in range(4)]
    rows = share.shape[0] // 2
    block = jnp.concatenate([x[...] for x in results], axis=0)
    values = [value * share[:, :1] for value in unpack(picks, block)]
    return [value[:rows] + value[rows:] for value in values]


def combine_far_kernel(share, take, two, three, total):
    quarter = two.shape[1] // 3
    for m, value in enumerate(combined(2, share, take, (two, three))):
        total[:, m * quarter : (m + 1) * quarter] = value


def combine_kernel(share, take, zero, one, total, out, held, semaphores):
    quarter = zero.shape[1] // 3
    copies = []
    for m, value in enumerate(combined(0, share, take, (zero, one))):
        lanes = pl.ds(m * quarter, quarter)
        held[:, lanes] = (value + total[:, lanes]).astype(BF16)
        copies.append(
            pltpu.make_async_copy(held.at[:, lanes], out.at[:, lanes], semaphores.at[m])
        )
        copies[m].start()
    for copy in copies:
        copy.wait()


def combine(share, take, results):
    rows, width = share.shape[0] // 2, results[0].shape[1] // 3 * 4
    params = pltpu.CompilerParams(vmem_limit_bytes=2 * MIB)
    cost = pl.CostEstimate(flops=0, bytes_accessed=16 * MIB, transcendentals=0)
    total = pl.pallas_call(
        combine_far_kernel,
        out_shape=jax.ShapeDtypeStruct((rows, width), F32),
        in_specs=[VMEM] * 4,
        out_specs=VMEM,
        compiler_params=params,
        cost_estimate=cost,
        name="combine_far",
    )(share, take, *results[2:])
    return pl.pallas_call(
        combine_kernel,
        out_shape=jax.ShapeDtypeStruct((rows, width), BF16),
        in_specs=[VMEM] * 5,
        out_specs=ANY,
        scratch_shapes=[pltpu.VMEM((rows, width), BF16), pltpu.SemaphoreType.DMA((4,))],
        compiler_params=params,
        cost_estimate=cost,
        name="combine",
    )(share, take, *results[:2], total)


def swap(value, count, bit):
    return lax.ppermute(value, "dp", [(i, i ^ bit) for i in range(count)])


def body(
    queries,
    new_keys,
    new_values,
    cache_keys,
    cache_values,
    lengths,
    residual,
    norm_gain,
    router_weight,
    gate_weight,
    up_weight,
    down_weight,
    routes,
):
    count = lax.axis_size("dp")
    plane = count // EXPERTS
    bits = [1 << k for k in reversed(range(plane.bit_length() - 1))]
    attended, *packed, share, take = attend(
        plane, queries, new_keys, new_values, cache_keys, cache_values, lengths, residual, norm_gain,
        router_weight, routes, down_weight,
    )

    packed = [packed[0]] + [swap(packed[k], count, k * plane) for k in range(1, EXPERTS)]
    waves = [join(share, *packed[:2]), join(share, *packed[2:])]
    for bit in bits:
        waves = [join(share, wave, swap(wave, count, bit)) for wave in waves]

    hidden = hidden_rows(waves, gate_weight, up_weight, down_weight)

    near, far = down_rows(hidden, down_weight)

    def back(wave, stage, after, parts=2):
        return fold(wave[0], swap(wave[1], count, bits[-1 - stage]), after, parts)

    last = len(bits) - 1
    token = share
    for stage in range(last):
        parts = 4 if stage == last - 1 else 2
        far = back(far, stage, token, parts)
        near = back(near, stage, far[0], parts)
        token = near[0]
    two = back(far[0:2], last, token, 1)
    three = back(far[2:4], last, two[0], 1)
    one = back(near[2:4], last, three[0], 1)
    zero = back(near[0:2], last, one[0], 1)
    results = [
        zero[0],
        swap(one[0], count, plane),
        swap(two[0], count, 2 * plane),
        swap(three[0], count, 3 * plane),
    ]
    return (attended, combine(share, take, results))


def solution(mesh):
    placed = (
        P(("group", "dp"), None),
        P(("group", "dp"), None),
        P(("group", "dp"), None),
        P(("group", "dp"), None, None),
        P(("group", "dp"), None, None),
        P(("group", "dp")),
        P(("group", "dp"), None),
        P(),
        P(),
        P(None, "dp"),
        P(None, "dp"),
        P("dp", None),
        P("group", None),
    )
    return jax.shard_map(
        body,
        mesh=mesh,
        in_specs=placed,
        out_specs=(P(("group", "dp"), None), P(("group", "dp"), None)),
        check_vma=False,
    )
```

```python
import functools

import jax
import jax.numpy as jnp
from jax import lax
from jax.experimental import pallas as pl
from jax.experimental.pallas import tpu as pltpu
from jax.sharding import PartitionSpec as P

HEADS = 32
KV_HEADS = 8
HEAD_DIM = 128
EXPERTS = 4
MIB = 1 << 20
HINTS = 4
MOST = 6
F32 = jnp.float32
BF16 = jnp.bfloat16
VMEM = pl.BlockSpec(memory_space=pltpu.VMEM)
ANY = pl.BlockSpec(memory_space=pl.ANY)


def dot(a, b, contract_last=False):
    dims = (((1,), (1 if contract_last else 0,)), ((), ()))
    return lax.dot_general(a, b, dims, preferred_element_type=F32)


def one_hot(mask):
    return mask.astype(F32).astype(BF16)


def grid(shape):
    return [lax.broadcasted_iota(jnp.int32, shape, axis) for axis in (0, 1)]


def pack(picks, block):
    quarter = block.shape[1] // 4
    parts = [block[:, m * quarter : (m + 1) * quarter] for m in range(4)]
    return [
        (dot(picks[0], parts[m]) + dot(picks[1 + m], parts[3])).astype(BF16) for m in range(3)
    ]


def unpack(picks, block):
    quarter = block.shape[1] // 3
    parts = [block[:, m * quarter : (m + 1) * quarter] for m in range(3)]
    tail = dot(picks[1], parts[0]) + dot(picks[2], parts[1]) + dot(picks[3], parts[2])
    return [dot(picks[0], part) for part in parts] + [tail]


def attend_kernel(plane, *refs):
    refs = refs[:10] + refs[10 + HINTS :]
    sources, attended, packed, (share, take), held, semaphores = (
        refs[:10], refs[10], refs[11:15], refs[15:17], refs[17:27], refs[28]
    )
    kept = refs[27]
    copies = [
        pltpu.make_async_copy(source, target, semaphores.at[i])
        for i, (source, target) in enumerate(zip(sources, held))
    ]
    for copy in copies[9:] + copies[:9]:
        copy.start()
    (queries, cache_keys, new_keys, lengths, cache_values, new_values, residual, gain, router,
     routes) = held
    rows, width = queries.shape
    positions = cache_keys.shape[1]
    groups = HEADS // KV_HEADS
    scale = 1.0 / HEAD_DIM**0.5
    every = rows * positions
    block = groups * rows

    copies[9].wait()
    index = lax.axis_index("dp")
    base = index * rows
    own = index // plane
    sub, lane = grid((2 * rows, 128))
    expert_down = jnp.zeros((2 * rows, 128), jnp.int32)
    slot_down = jnp.zeros((2 * rows, 128), jnp.int32)
    across = lax.broadcasted_iota(jnp.int32, (8, 128), 1)
    expert_across = jnp.zeros((8, 128), jnp.int32)
    slot_across = jnp.zeros((8, 128), jnp.int32)
    counts = [jnp.int32(0)] * EXPERTS
    for r in range(rows):
        names = [routes[c, base + r] ^ own for c in range(2)]
        for choice, name in ((r, names[0]), (rows + r, names[1])):
            slot = jnp.int32(0)
            for e in range(EXPERTS):
                slot = jnp.where(name == e, counts[e], slot)
            expert_down = jnp.where(sub == choice, name, expert_down)
            slot_down = jnp.where(sub == choice, slot, slot_down)
            expert_across = jnp.where(across == choice, name, expert_across)
            slot_across = jnp.where(across == choice, slot, slot_across)
        for e in range(EXPERTS):
            named = (names[0] == e) | (names[1] == e)
            counts[e] = counts[e] + jnp.where(named, 1, 0)

    late = jnp.where(slot_down >= 3, 1, 0)
    take[0] = one_hot(lane == expert_down * 8 + slot_down)
    for m in range(3):
        take[1 + m] = one_hot((lane == expert_down * 8 + 6 + late) & (slot_down - 3 * late == m))
    place, choice = grid((8 * EXPERTS, 128))
    expert, slot = expert_across[0:1], slot_across[0:1]
    late = jnp.where(slot >= 3, 1, 0)
    chosen = choice < 2 * rows
    picks = [one_hot((place == expert * 8 + slot) & chosen)]
    for m in range(3):
        picks.append(one_hot((place == expert * 8 + 6 + late) & (slot - 3 * late == m) & chosen))
    for copy in copies[:4]:
        copy.wait()

    query = queries[...].astype(F32)
    stacked = jnp.concatenate(
        [query[:, h * HEAD_DIM : (h + 1) * HEAD_DIM] for h in range(HEADS)], axis=0
    )
    stacked_b = stacked.astype(BF16)
    keys = cache_keys[...].reshape(every, KV_HEADS * HEAD_DIM)
    newk = new_keys[...].astype(F32)

    row_of = lax.broadcasted_iota(jnp.int32, (block, every), 0) % rows
    column = lax.broadcasted_iota(jnp.int32, (block, every), 1)
    position = column % positions
    column_row = column // positions
    limit = jnp.zeros((block, every), jnp.int32)
    for r in range(rows):
        limit = jnp.where(column_row == r, lengths[r], limit)
    valid = (row_of == column_row) & (position < limit)

    heads = range(KV_HEADS)
    lanes = [slice(g * HEAD_DIM, (g + 1) * HEAD_DIM) for g in heads]
    mine = [slice(g * block, (g + 1) * block) for g in heads]
    scores = [dot(stacked_b[mine[g]], keys[:, lanes[g]], contract_last=True) for g in heads]
    scores = [jnp.where(valid, score * scale, -jnp.inf) for score in scores]
    own_keys = [jnp.concatenate([newk[:, lanes[g]]] * groups, axis=0) for g in heads]
    new_scores = [
        jnp.sum(stacked[mine[g]] * own_keys[g], axis=1, keepdims=True) * scale for g in heads
    ]
    peaks = [
        jnp.maximum(jnp.max(score, axis=1, keepdims=True), new)
        for score, new in zip(scores, new_scores)
    ]
    weights = [jnp.exp(score - peak) for score, peak in zip(scores, peaks)]
    new_weights = [jnp.exp(new - peak) for new, peak in zip(new_scores, peaks)]
    totals = [
        jnp.sum(weight, axis=1, keepdims=True) + new
        for weight, new in zip(weights, new_weights)
    ]
    inverses = [1.0 / total for total in totals]
    probs = [(weight * inverse).astype(BF16) for weight, inverse in zip(weights, inverses)]
    new_probs = [
        (new * inverse).astype(BF16).astype(F32) for new, inverse in zip(new_weights, inverses)
    ]
    for copy in copies[4:9]:
        copy.wait()
    values = cache_values[...].reshape(every, KV_HEADS * HEAD_DIM)
    newv = new_values[...].astype(F32)
    mixed = [
        dot(probs[g], values[:, lanes[g]])
        + new_probs[g] * jnp.concatenate([newv[:, lanes[g]]] * groups, axis=0)
        for g in heads
    ]
    pieces = [value[j * rows : (j + 1) * rows] for value in mixed for j in range(groups)]

    states = (residual[...].astype(F32) + jnp.concatenate(pieces, axis=1)).astype(BF16)
    attended_copy = pltpu.make_async_copy(kept, attended, semaphores.at[len(copies)])
    kept[...] = states
    attended_copy.start()
    states = states.astype(F32)
    norm = lax.rsqrt(jnp.mean(states * states, axis=1, keepdims=True) + 1e-05)
    gains = gain[...].astype(F32)
    logits = [jnp.zeros((rows, 128), F32) for _ in range(EXPERTS)]
    parts = []
    for c in range(width // 128):
        lanes = slice(c * 128, (c + 1) * 128)
        part = (states[:, lanes] * norm * gains[c : c + 1]).astype(BF16).astype(F32)
        parts.append(part)
        for e in range(EXPERTS):
            logits[e] += part * router[e : e + 1, lanes].astype(F32)
    logits = [jnp.sum(value, axis=1, keepdims=True) for value in logits]

    normed = jnp.concatenate(parts, axis=1)
    normed = jnp.concatenate([normed, normed], axis=0).astype(BF16)
    quarter = width // 4
    for m, value in enumerate(pack([pick[:, : 2 * rows] for pick in picks], normed)):
        for k, target in enumerate(packed):
            target[:, m * quarter : (m + 1) * quarter] = value[8 * k : 8 * k + 8]

    chosen_logits = jnp.zeros((2 * rows, 1), F32)
    for e in range(EXPERTS):
        both = jnp.concatenate([logits[e], logits[e]], axis=0)
        chosen_logits = jnp.where(expert_down[:, :1] == (own ^ e), both, chosen_logits)
    other = jnp.concatenate([chosen_logits[rows:], chosen_logits[:rows]], axis=0)
    share[...] = jnp.broadcast_to(1.0 / (1.0 + jnp.exp(other - chosen_logits)), share.shape)
    attended_copy.wait()


def attend(plane, queries, new_keys, new_values, cache_keys, cache_values, lengths, residual,
           norm_gain, router_weight, routes, weight):
    rows, width = queries.shape
    operands = (
        queries,
        cache_keys,
        new_keys,
        lengths,
        cache_values,
        new_values,
        residual,
        norm_gain.reshape(-1, 128),
        router_weight.T,
        routes.T,
    )
    in_smem = (3, 9)
    return pl.pallas_call(
        functools.partial(attend_kernel, plane),
        out_shape=(
            jax.ShapeDtypeStruct((rows, width), BF16),
            *[jax.ShapeDtypeStruct((8, width * 3 // 4), BF16)] * EXPERTS,
            jax.ShapeDtypeStruct((2 * rows, 128), F32),
            jax.ShapeDtypeStruct((4, 2 * rows, 128), BF16),
        ),
        in_specs=[ANY] * (len(operands) + HINTS),
        out_specs=(ANY,) + (VMEM,) * (2 + EXPERTS),
        scratch_shapes=[
            (pltpu.SMEM if i in in_smem else pltpu.VMEM)(operand.shape, operand.dtype)
            for i, operand in enumerate(operands)
        ]
        + [pltpu.VMEM((rows, width), BF16), pltpu.SemaphoreType.DMA((len(operands) + 1,))],
        compiler_params=pltpu.CompilerParams(vmem_limit_bytes=5 * MIB),
        name="attend",
    )(*[pltpu.with_memory_space_constraint(x, pltpu.HBM) for x in operands + (weight,) * HINTS])


def hidden_kernel(gate_weight, up_weight, down_weight, *refs):
    waves, hidden = refs[:-1], refs[-1]
    columns = gate_weight.shape[1]
    step = 512
    quarter = waves[0].shape[1] // 3
    blocks = jnp.concatenate([wave[...] for wave in waves], axis=0)
    size = 128
    row, lane = grid((size, size))
    slot = row & 7
    late = jnp.where(slot >= 3, 1, 0)
    picks = [
        one_hot((lane == row - slot + 6 + late) & (slot - 3 * late == m)) for m in range(3)
    ]
    picks = jnp.concatenate(picks, axis=1)
    tails = []
    for first in range(0, blocks.shape[0], size):
        some = blocks[first : first + size]
        parts = [some[:, m * quarter : (m + 1) * quarter] for m in range(3)]
        tails.append(dot(picks, jnp.concatenate(parts, axis=0)).astype(BF16))
    x = jnp.concatenate([blocks, jnp.concatenate(tails, axis=0)], axis=1)
    for f in range(0, columns, step):
        last = min(f + step, columns)
        gate = dot(x, gate_weight[:, f:last])
        upper = dot(x, up_weight[:, f:last])
        hidden[:, f:last] = (gate / (1.0 + jnp.exp(-gate)) * upper).astype(BF16)


def hidden_rows(waves, gate_weight, up_weight, down_weight):
    rows = sum(wave.shape[0] for wave in waves)
    width, columns = gate_weight.shape
    return pl.pallas_call(
        hidden_kernel,
        out_shape=jax.ShapeDtypeStruct((rows, columns), BF16),
        in_specs=[VMEM] * (3 + len(waves)),
        out_specs=VMEM,
        compiler_params=pltpu.CompilerParams(vmem_limit_bytes=4 * MIB * max(1, rows // 128)),
        cost_estimate=pl.CostEstimate(
            flops=4 * rows * width * columns, bytes_accessed=0, transcendentals=rows * columns
        ),
        name="hidden",
    )(gate_weight, up_weight, down_weight, *waves)


def down_kernel(hidden, weight, *outs):
    rows = hidden.shape[0]
    quarter = outs[0].shape[1] // 3
    size = 128
    row, lane = grid((size, size))
    slot = row & 7
    picks = [one_hot((lane == row - slot + 3 * (slot - 6) + m) & (slot >= MOST)) for m in range(3)]
    picks = jnp.concatenate(picks, axis=0)
    h = hidden[...]

    def terms(first, count):
        return dot(h, weight[:, first : first + count])

    step = min(1024, quarter)
    is_row = (lax.broadcasted_iota(jnp.int32, (rows, step), 0) & 7) < MOST
    for n in range(0, quarter, step):
        tail = terms(3 * quarter + n, step).astype(BF16)
        tails = [dot(picks, tail[i : i + size]) for i in range(0, rows, size)]
        for m in range(3):
            moved = jnp.concatenate([x[m * size : (m + 1) * size] for x in tails], axis=0)
            value = jnp.where(is_row, terms(m * quarter + n, step), moved).astype(BF16)
            lanes = slice(m * quarter + n, m * quarter + n + step)
            for out, blocks in zip(outs, ways_back(rows // 32)):
                for i, b in enumerate(blocks):
                    out[8 * i : 8 * i + 8, lanes] = value[8 * b : 8 * b + 8]


def ways_back(places):
    halves = []
    for w in (0, 1):
        groups = [
            2 * places * w + 2 * p + j
            for high in range(0, places, 2)
            for j in (0, 1)
            for p in (high, high + 1)
        ]
        halves += [groups[:places], groups[places:]]
    return halves


def down_rows(hidden, weight):
    rows, columns = hidden.shape
    width = weight.shape[1]
    sizes = [8 * len(blocks) for blocks in ways_back(rows // 32)]
    outs = pl.pallas_call(
        down_kernel,
        out_shape=[jax.ShapeDtypeStruct((size, width // 4 * 3), BF16) for size in sizes],
        in_specs=[VMEM] * 2,
        out_specs=[VMEM] * len(sizes),
        compiler_params=pltpu.CompilerParams(vmem_limit_bytes=4 * MIB * max(1, rows // 128)),
        cost_estimate=pl.CostEstimate(
            flops=2 * rows * width * columns, bytes_accessed=0, transcendentals=0
        ),
        name="down",
    )(hidden, weight)
    return outs[0:2], outs[2:4]


def join_kernel(backwards, *refs):
    out, row = refs[-1], 0
    pieces = refs[1:-1][::-1] if backwards else refs[1:-1]
    for piece in pieces:
        out[row : row + piece.shape[0]] = piece[...]
        row += piece.shape[0]


def join(after, *pieces, backwards=False):
    rows = sum(piece.shape[0] for piece in pieces)
    return pl.pallas_call(
        functools.partial(join_kernel, backwards),
        out_shape=jax.ShapeDtypeStruct((rows, pieces[0].shape[1]), BF16),
        in_specs=[ANY] + [VMEM] * len(pieces),
        out_specs=VMEM,
        compiler_params=pltpu.CompilerParams(vmem_limit_bytes=1 * MIB),
        cost_estimate=pl.CostEstimate(flops=0, bytes_accessed=0, transcendentals=0),
        name="join",
    )(after, *pieces)


def fold_kernel(held, arrived, after, *outs):
    each = outs[0].shape[0]
    for k, out in enumerate(outs):
        block = slice(k * each, (k + 1) * each)
        out[...] = (held[block].astype(F32) + arrived[block].astype(F32)).astype(BF16)


def fold(held, arrived, after, parts):
    rows, width = held.shape
    return pl.pallas_call(
        fold_kernel,
        out_shape=[jax.ShapeDtypeStruct((rows // parts, width), BF16)] * parts,
        in_specs=[VMEM] * 2 + [ANY],
        out_specs=[VMEM] * parts,
        compiler_params=pltpu.CompilerParams(vmem_limit_bytes=MIB * max(1, rows // 64)),
        cost_estimate=pl.CostEstimate(flops=0, bytes_accessed=0, transcendentals=0),
        name="fold",
    )(held, arrived, after)


def combined(first, share, take, results):
    picks = [take[i][:, 8 * first : 8 * first + 16] for i in range(4)]
    rows = share.shape[0] // 2
    block = jnp.concatenate([x[...] for x in results], axis=0)
    values = [value * share[:, :1] for value in unpack(picks, block)]
    return [value[:rows] + value[rows:] for value in values]


def combine_far_kernel(share, take, two, three, total):
    quarter = two.shape[1] // 3
    for m, value in enumerate(combined(2, share, take, (two, three))):
        total[:, m * quarter : (m + 1) * quarter] = value


def combine_kernel(share, take, zero, one, total, out, held, semaphores):
    quarter = zero.shape[1] // 3
    copies = []
    for m, value in enumerate(combined(0, share, take, (zero, one))):
        lanes = pl.ds(m * quarter, quarter)
        held[:, lanes] = (value + total[:, lanes]).astype(BF16)
        copies.append(
            pltpu.make_async_copy(held.at[:, lanes], out.at[:, lanes], semaphores.at[m])
        )
        copies[m].start()
    for copy in copies:
        copy.wait()


def combine(share, take, results):
    rows, width = share.shape[0] // 2, results[0].shape[1] // 3 * 4
    params = pltpu.CompilerParams(vmem_limit_bytes=2 * MIB)
    cost = pl.CostEstimate(flops=0, bytes_accessed=16 * MIB, transcendentals=0)
    total = pl.pallas_call(
        combine_far_kernel,
        out_shape=jax.ShapeDtypeStruct((rows, width), F32),
        in_specs=[VMEM] * 4,
        out_specs=VMEM,
        compiler_params=params,
        cost_estimate=cost,
        name="combine_far",
    )(share, take, *results[2:])
    return pl.pallas_call(
        combine_kernel,
        out_shape=jax.ShapeDtypeStruct((rows, width), BF16),
        in_specs=[VMEM] * 5,
        out_specs=ANY,
        scratch_shapes=[pltpu.VMEM((rows, width), BF16), pltpu.SemaphoreType.DMA((4,))],
        compiler_params=params,
        cost_estimate=cost,
        name="combine",
    )(share, take, *results[:2], total)


def swap(value, count, bit):
    return lax.ppermute(value, "dp", [(i, i ^ bit) for i in range(count)])


def body(
    queries,
    new_keys,
    new_values,
    cache_keys,
    cache_values,
    lengths,
    residual,
    norm_gain,
    router_weight,
    gate_weight,
    up_weight,
    down_weight,
    routes,
):
    count = lax.axis_size("dp")
    plane = count // EXPERTS
    bits = [1 << k for k in reversed(range(plane.bit_length() - 1))]
    attended, *packed, share, take = attend(
        plane, queries, new_keys, new_values, cache_keys, cache_values, lengths, residual, norm_gain,
        router_weight, routes, down_weight,
    )

    for k in (1, 3, 2):
        packed[k] = swap(packed[k], count, k * plane)
    waves = [join(share, *packed[:2]), join(share, packed[3], packed[2], backwards=True)]
    for bit in bits:
        waves = [join(share, wave, swap(wave, count, bit)) for wave in waves]

    hidden = hidden_rows(waves, gate_weight, up_weight, down_weight)

    near, far = down_rows(hidden, down_weight)

    def back(wave, stage, after, parts=2):
        return fold(wave[0], swap(wave[1], count, bits[-1 - stage]), after, parts)

    last = len(bits) - 1
    token = share
    for stage in range(last):
        parts = 4 if stage == last - 1 else 2
        far = back(far, stage, token, parts)
        near = back(near, stage, far[0], parts)
        token = near[0]
    two = back(far[0:2], last, token, 1)
    three = back(far[2:4], last, two[0], 1)
    one = back(near[2:4], last, three[0], 1)
    zero = back(near[0:2], last, one[0], 1)
    results = [
        zero[0],
        swap(one[0], count, plane),
        swap(two[0], count, 2 * plane),
        swap(three[0], count, 3 * plane),
    ]
    return (attended, combine(share, take, results))


def solution(mesh):
    placed = (
        P(("group", "dp"), None),
        P(("group", "dp"), None),
        P(("group", "dp"), None),
        P(("group", "dp"), None, None),
        P(("group", "dp"), None, None),
        P(("group", "dp")),
        P(("group", "dp"), None),
        P(),
        P(),
        P(None, "dp"),
        P(None, "dp"),
        P("dp", None),
        P("group", None),
    )
    return jax.shard_map(
        body,
        mesh=mesh,
        in_specs=placed,
        out_specs=(P(("group", "dp"), None), P(("group", "dp"), None)),
        check_vma=False,
    )
```

```python
import functools

import jax
import jax.numpy as jnp
from jax import lax
from jax.experimental import pallas as pl
from jax.experimental.pallas import tpu as pltpu
from jax.sharding import PartitionSpec as P

HEADS = 32
KV_HEADS = 8
HEAD_DIM = 128
EXPERTS = 4
MIB = 1 << 20
HINTS = 4
MOST = 6
F32 = jnp.float32
BF16 = jnp.bfloat16
VMEM = pl.BlockSpec(memory_space=pltpu.VMEM)
ANY = pl.BlockSpec(memory_space=pl.ANY)


def dot(a, b, contract_last=False):
    dims = (((1,), (1 if contract_last else 0,)), ((), ()))
    return lax.dot_general(a, b, dims, preferred_element_type=F32)


def one_hot(mask):
    return mask.astype(F32).astype(BF16)


def grid(shape):
    return [lax.broadcasted_iota(jnp.int32, shape, axis) for axis in (0, 1)]


def pack(picks, block):
    quarter = block.shape[1] // 4
    parts = [block[:, m * quarter : (m + 1) * quarter] for m in range(4)]
    return [dot(picks[0], parts[m]) + dot(picks[1 + m], parts[3]) for m in range(3)]


def unpack(picks, block):
    quarter = block.shape[1] // 3
    parts = [block[:, m * quarter : (m + 1) * quarter] for m in range(3)]
    tail = dot(picks[1], parts[0]) + dot(picks[2], parts[1]) + dot(picks[3], parts[2])
    return [dot(picks[0], part) for part in parts] + [tail]


def attend_kernel(plane, *refs):
    refs = refs[:10] + refs[10 + HINTS :]
    sources, attended, packed, (share, take), held, semaphores = (
        refs[:10], refs[10], refs[11:15], refs[15:17], refs[17:27], refs[27]
    )
    copies = [
        pltpu.make_async_copy(source, target, semaphores.at[i])
        for i, (source, target) in enumerate(zip(sources, held))
    ]
    for copy in copies[9:] + copies[:9]:
        copy.start()
    (queries, cache_keys, new_keys, lengths, cache_values, new_values, residual, gain, router,
     routes) = held
    rows, width = queries.shape
    positions = cache_keys.shape[1]
    groups = HEADS // KV_HEADS
    scale = 1.0 / HEAD_DIM**0.5
    every = rows * positions
    block = groups * rows

    copies[9].wait()
    index = lax.axis_index("dp")
    base = index * rows
    own = index // plane
    sub, lane = grid((2 * rows, 128))
    expert_down = jnp.zeros((2 * rows, 128), jnp.int32)
    slot_down = jnp.zeros((2 * rows, 128), jnp.int32)
    across = lax.broadcasted_iota(jnp.int32, (8, 128), 1)
    expert_across = jnp.zeros((8, 128), jnp.int32)
    slot_across = jnp.zeros((8, 128), jnp.int32)
    counts = [jnp.int32(0)] * EXPERTS
    for r in range(rows):
        names = [routes[c, base + r] ^ own for c in range(2)]
        for choice, name in ((r, names[0]), (rows + r, names[1])):
            slot = jnp.int32(0)
            for e in range(EXPERTS):
                slot = jnp.where(name == e, counts[e], slot)
            expert_down = jnp.where(sub == choice, name, expert_down)
            slot_down = jnp.where(sub == choice, slot, slot_down)
            expert_across = jnp.where(across == choice, name, expert_across)
            slot_across = jnp.where(across == choice, slot, slot_across)
        for e in range(EXPERTS):
            named = (names[0] == e) | (names[1] == e)
            counts[e] = counts[e] + jnp.where(named, 1, 0)

    late = jnp.where(slot_down >= 3, 1, 0)
    take[0] = one_hot(lane == expert_down * 8 + slot_down)
    for m in range(3):
        take[1 + m] = one_hot((lane == expert_down * 8 + 6 + late) & (slot_down - 3 * late == m))
    place, choice = grid((8 * EXPERTS, 128))
    expert, slot = expert_across[0:1], slot_across[0:1]
    late = jnp.where(slot >= 3, 1, 0)
    chosen = choice < 2 * rows
    picks = [one_hot((place == expert * 8 + slot) & chosen)]
    for m in range(3):
        picks.append(one_hot((place == expert * 8 + 6 + late) & (slot - 3 * late == m) & chosen))
    for copy in copies[:4]:
        copy.wait()

    query = queries[...].astype(F32)
    stacked = jnp.concatenate(
        [query[:, h * HEAD_DIM : (h + 1) * HEAD_DIM] for h in range(HEADS)], axis=0
    )
    stacked_b = stacked.astype(BF16)
    keys = cache_keys[...].reshape(every, KV_HEADS * HEAD_DIM)
    newk = new_keys[...].astype(F32)

    row_of = lax.broadcasted_iota(jnp.int32, (block, every), 0) % rows
    column = lax.broadcasted_iota(jnp.int32, (block, every), 1)
    position = column % positions
    column_row = column // positions
    limit = jnp.zeros((block, every), jnp.int32)
    for r in range(rows):
        limit = jnp.where(column_row == r, lengths[r], limit)
    valid = (row_of == column_row) & (position < limit)

    heads = range(KV_HEADS)
    lanes = [slice(g * HEAD_DIM, (g + 1) * HEAD_DIM) for g in heads]
    mine = [slice(g * block, (g + 1) * block) for g in heads]
    scores = [dot(stacked_b[mine[g]], keys[:, lanes[g]], contract_last=True) for g in heads]
    scores = [jnp.where(valid, score * scale, -jnp.inf) for score in scores]
    own_keys = [jnp.concatenate([newk[:, lanes[g]]] * groups, axis=0) for g in heads]
    new_scores = [
        jnp.sum(stacked[mine[g]] * own_keys[g], axis=1, keepdims=True) * scale for g in heads
    ]
    peaks = [
        jnp.maximum(jnp.max(score, axis=1, keepdims=True), new)
        for score, new in zip(scores, new_scores)
    ]
    weights = [jnp.exp(score - peak) for score, peak in zip(scores, peaks)]
    new_weights = [jnp.exp(new - peak) for new, peak in zip(new_scores, peaks)]
    totals = [
        jnp.sum(weight, axis=1, keepdims=True) + new
        for weight, new in zip(weights, new_weights)
    ]
    inverses = [1.0 / total for total in totals]
    probs = [(weight * inverse).astype(BF16) for weight, inverse in zip(weights, inverses)]
    new_probs = [
        (new * inverse).astype(BF16).astype(F32) for new, inverse in zip(new_weights, inverses)
    ]
    for copy in copies[4:9]:
        copy.wait()
    values = cache_values[...].reshape(every, KV_HEADS * HEAD_DIM)
    newv = new_values[...].astype(F32)
    mixed = [
        dot(probs[g], values[:, lanes[g]])
        + new_probs[g] * jnp.concatenate([newv[:, lanes[g]]] * groups, axis=0)
        for g in heads
    ]
    pieces = [value[j * rows : (j + 1) * rows] for value in mixed for j in range(groups)]

    states = (residual[...].astype(F32) + jnp.concatenate(pieces, axis=1)).astype(BF16)
    attended[...] = states
    states = states.astype(F32)
    norm = lax.rsqrt(jnp.mean(states * states, axis=1, keepdims=True) + 1e-05)
    gains = gain[...].astype(F32)
    logits = [jnp.zeros((rows, 128), F32) for _ in range(EXPERTS)]
    parts = []
    for c in range(width // 128):
        lanes = slice(c * 128, (c + 1) * 128)
        part = (states[:, lanes] * norm * gains[c : c + 1]).astype(BF16).astype(F32)
        parts.append(part)
        for e in range(EXPERTS):
            logits[e] += part * router[e : e + 1, lanes].astype(F32)
    logits = [jnp.sum(value, axis=1, keepdims=True) for value in logits]

    normed = jnp.concatenate(parts, axis=1)
    normed = jnp.concatenate([normed, normed], axis=0).astype(BF16)
    quarter = width // 4
    for m, value in enumerate(pack([pick[:, : 2 * rows] for pick in picks], normed)):
        for k, target in enumerate(packed):
            target[:, m * quarter : (m + 1) * quarter] = value[8 * k : 8 * k + 8].astype(BF16)

    chosen_logits = jnp.zeros((2 * rows, 1), F32)
    for e in range(EXPERTS):
        both = jnp.concatenate([logits[e], logits[e]], axis=0)
        chosen_logits = jnp.where(expert_down[:, :1] == (own ^ e), both, chosen_logits)
    other = jnp.concatenate([chosen_logits[rows:], chosen_logits[:rows]], axis=0)
    share[...] = jnp.broadcast_to(1.0 / (1.0 + jnp.exp(other - chosen_logits)), share.shape)


def attend(plane, queries, new_keys, new_values, cache_keys, cache_values, lengths, residual,
           norm_gain, router_weight, routes, weight):
    rows, width = queries.shape
    operands = (
        queries,
        cache_keys,
        new_keys,
        lengths,
        cache_values,
        new_values,
        residual,
        norm_gain.reshape(-1, 128),
        router_weight.T,
        routes.T,
    )
    in_smem = (3, 9)
    return pl.pallas_call(
        functools.partial(attend_kernel, plane),
        out_shape=(
            jax.ShapeDtypeStruct((rows, width), BF16),
            *[jax.ShapeDtypeStruct((8, width * 3 // 4), BF16)] * EXPERTS,
            jax.ShapeDtypeStruct((2 * rows, 128), F32),
            jax.ShapeDtypeStruct((4, 2 * rows, 128), BF16),
        ),
        in_specs=[ANY] * (len(operands) + HINTS),
        out_specs=(VMEM,) * (3 + EXPERTS),
        scratch_shapes=[
            (pltpu.SMEM if i in in_smem else pltpu.VMEM)(operand.shape, operand.dtype)
            for i, operand in enumerate(operands)
        ]
        + [pltpu.SemaphoreType.DMA((len(operands),))],
        compiler_params=pltpu.CompilerParams(vmem_limit_bytes=5 * MIB),
        name="attend",
    )(*[pltpu.with_memory_space_constraint(x, pltpu.HBM) for x in operands + (weight,) * HINTS])


def hidden_kernel(gate_weight, up_weight, down_weight, *refs):
    waves, hidden = refs[:-1], refs[-1]
    columns = gate_weight.shape[1]
    step = 512
    quarter = waves[0].shape[1] // 3
    blocks = jnp.concatenate([wave[...] for wave in waves], axis=0)
    size = 128
    row, lane = grid((size, size))
    slot = row & 7
    late = jnp.where(slot >= 3, 1, 0)
    picks = [
        one_hot((lane == row - slot + 6 + late) & (slot - 3 * late == m)) for m in range(3)
    ]
    picks = jnp.concatenate(picks, axis=1)
    tails = []
    for first in range(0, blocks.shape[0], size):
        some = blocks[first : first + size]
        parts = [some[:, m * quarter : (m + 1) * quarter] for m in range(3)]
        tails.append(dot(picks, jnp.concatenate(parts, axis=0)).astype(BF16))
    x = jnp.concatenate([blocks, jnp.concatenate(tails, axis=0)], axis=1)
    for f in range(0, columns, step):
        last = min(f + step, columns)
        gate = dot(x, gate_weight[:, f:last])
        upper = dot(x, up_weight[:, f:last])
        hidden[:, f:last] = (gate / (1.0 + jnp.exp(-gate)) * upper).astype(BF16)


def hidden_rows(waves, gate_weight, up_weight, down_weight):
    rows = sum(wave.shape[0] for wave in waves)
    width, columns = gate_weight.shape
    return pl.pallas_call(
        hidden_kernel,
        out_shape=jax.ShapeDtypeStruct((rows, columns), BF16),
        in_specs=[VMEM] * (3 + len(waves)),
        out_specs=VMEM,
        compiler_params=pltpu.CompilerParams(vmem_limit_bytes=4 * MIB * max(1, rows // 128)),
        cost_estimate=pl.CostEstimate(
            flops=4 * rows * width * columns, bytes_accessed=0, transcendentals=rows * columns
        ),
        name="hidden",
    )(gate_weight, up_weight, down_weight, *waves)


def down_kernel(hidden, weight, *outs):
    rows = hidden.shape[0]
    quarter = outs[0].shape[1] // 3
    size = 128
    row, lane = grid((size, size))
    slot = row & 7
    picks = [one_hot((lane == row - slot + 3 * (slot - 6) + m) & (slot >= MOST)) for m in range(3)]
    picks = jnp.concatenate(picks, axis=0)
    h = hidden[...]

    def terms(first, count):
        return dot(h, weight[:, first : first + count])

    step = min(1024, quarter)
    is_row = (lax.broadcasted_iota(jnp.int32, (rows, step), 0) & 7) < MOST
    for n in range(0, quarter, step):
        tail = terms(3 * quarter + n, step).astype(BF16)
        tails = [dot(picks, tail[i : i + size]) for i in range(0, rows, size)]
        for m in range(3):
            moved = jnp.concatenate([x[m * size : (m + 1) * size] for x in tails], axis=0)
            value = jnp.where(is_row, terms(m * quarter + n, step), moved)
            lanes = slice(m * quarter + n, m * quarter + n + step)
            for out, blocks in zip(outs, ways_back(rows // 32)):
                chosen = [value[8 * b : 8 * b + 8] for b in blocks]
                out[:, lanes] = jnp.concatenate(chosen, axis=0).astype(BF16)


def ways_back(places):
    halves = []
    for w in (0, 1):
        groups = [
            2 * places * w + 2 * p + j
            for high in range(0, places, 2)
            for j in (0, 1)
            for p in (high, high + 1)
        ]
        halves += [groups[:places], groups[places:]]
    return halves


def down_rows(hidden, weight):
    rows, columns = hidden.shape
    width = weight.shape[1]
    sizes = [8 * len(blocks) for blocks in ways_back(rows // 32)]
    outs = pl.pallas_call(
        down_kernel,
        out_shape=[jax.ShapeDtypeStruct((size, width // 4 * 3), BF16) for size in sizes],
        in_specs=[VMEM] * 2,
        out_specs=[VMEM] * len(sizes),
        compiler_params=pltpu.CompilerParams(vmem_limit_bytes=4 * MIB * max(1, rows // 128)),
        cost_estimate=pl.CostEstimate(
            flops=2 * rows * width * columns, bytes_accessed=0, transcendentals=0
        ),
        name="down",
    )(hidden, weight)
    return outs[0:2], outs[2:4]


def join_kernel(backwards, *refs):
    pieces = refs[1:-1][::-1] if backwards else refs[1:-1]
    rows = [piece[...].astype(F32) for piece in pieces]
    refs[-1][...] = jnp.concatenate(rows, axis=0).astype(BF16)


def join(after, *pieces, backwards=False):
    rows = sum(piece.shape[0] for piece in pieces)
    return pl.pallas_call(
        functools.partial(join_kernel, backwards),
        out_shape=jax.ShapeDtypeStruct((rows, pieces[0].shape[1]), BF16),
        in_specs=[ANY] + [VMEM] * len(pieces),
        out_specs=VMEM,
        compiler_params=pltpu.CompilerParams(vmem_limit_bytes=1 * MIB),
        cost_estimate=pl.CostEstimate(flops=0, bytes_accessed=0, transcendentals=0),
        name="join",
    )(after, *pieces)


def fold_kernel(held, arrived, after, *outs):
    each = outs[0].shape[0]
    total = held[...].astype(F32) + arrived[...].astype(F32)
    for k, out in enumerate(outs):
        out[...] = total[k * each : (k + 1) * each].astype(BF16)


def fold(held, arrived, after, parts):
    rows, width = held.shape
    return pl.pallas_call(
        fold_kernel,
        out_shape=[jax.ShapeDtypeStruct((rows // parts, width), BF16)] * parts,
        in_specs=[VMEM] * 2 + [ANY],
        out_specs=[VMEM] * parts,
        compiler_params=pltpu.CompilerParams(vmem_limit_bytes=MIB * max(1, rows // 64)),
        cost_estimate=pl.CostEstimate(flops=0, bytes_accessed=0, transcendentals=0),
        name="fold",
    )(held, arrived, after)


def combined(first, share, take, results):
    picks = [take[i][:, 8 * first : 8 * first + 16] for i in range(4)]
    rows = share.shape[0] // 2
    block = jnp.concatenate([x[...].astype(F32) for x in results], axis=0).astype(BF16)
    values = [value * share[:, :1] for value in unpack(picks, block)]
    return [value[:rows] + value[rows:] for value in values]


def combine_far_kernel(share, take, two, three, total):
    quarter = two.shape[1] // 3
    for m, value in enumerate(combined(2, share, take, (two, three))):
        total[:, m * quarter : (m + 1) * quarter] = value


def combine_kernel(share, take, zero, one, total, out):
    quarter = zero.shape[1] // 3
    for m, value in enumerate(combined(0, share, take, (zero, one))):
        lanes = slice(m * quarter, (m + 1) * quarter)
        out[:, lanes] = (value + total[:, lanes]).astype(BF16)


def combine(share, take, results):
    rows, width = share.shape[0] // 2, results[0].shape[1] // 3 * 4
    params = pltpu.CompilerParams(vmem_limit_bytes=2 * MIB)
    cost = pl.CostEstimate(flops=0, bytes_accessed=16 * MIB, transcendentals=0)
    total = pl.pallas_call(
        combine_far_kernel,
        out_shape=jax.ShapeDtypeStruct((rows, width), F32),
        in_specs=[VMEM] * 4,
        out_specs=VMEM,
        compiler_params=params,
        cost_estimate=cost,
        name="combine_far",
    )(share, take, *results[2:])
    return pl.pallas_call(
        combine_kernel,
        out_shape=jax.ShapeDtypeStruct((rows, width), BF16),
        in_specs=[VMEM] * 5,
        out_specs=VMEM,
        compiler_params=params,
        cost_estimate=cost,
        name="combine",
    )(share, take, *results[:2], total)


def swap(value, count, bit):
    return lax.ppermute(value, "dp", [(i, i ^ bit) for i in range(count)])


def body(
    queries,
    new_keys,
    new_values,
    cache_keys,
    cache_values,
    lengths,
    residual,
    norm_gain,
    router_weight,
    gate_weight,
    up_weight,
    down_weight,
    routes,
):
    count = lax.axis_size("dp")
    plane = count // EXPERTS
    bits = [1 << k for k in reversed(range(plane.bit_length() - 1))]
    attended, *packed, share, take = attend(
        plane, queries, new_keys, new_values, cache_keys, cache_values, lengths, residual, norm_gain,
        router_weight, routes, down_weight,
    )

    for k in (1, 3, 2):
        packed[k] = swap(packed[k], count, k * plane)
    waves = [join(share, *packed[:2]), join(share, packed[3], packed[2], backwards=True)]
    for bit in bits:
        waves = [join(share, wave, swap(wave, count, bit)) for wave in waves]

    hidden = hidden_rows(waves, gate_weight, up_weight, down_weight)

    near, far = down_rows(hidden, down_weight)

    def back(wave, stage, after, parts=2):
        return fold(wave[0], swap(wave[1], count, bits[-1 - stage]), after, parts)

    last = len(bits) - 1
    token = share
    for stage in range(last):
        parts = 4 if stage == last - 1 else 2
        far = back(far, stage, token, parts)
        near = back(near, stage, far[0], parts)
        token = near[0]
    two = back(far[0:2], last, token, 1)
    three = back(far[2:4], last, two[0], 1)
    one = back(near[2:4], last, three[0], 1)
    zero = back(near[0:2], last, one[0], 1)
    results = [
        zero[0],
        swap(one[0], count, plane),
        swap(two[0], count, 2 * plane),
        swap(three[0], count, 3 * plane),
    ]
    return (attended, combine(share, take, results))


def solution(mesh):
    placed = (
        P(("group", "dp"), None),
        P(("group", "dp"), None),
        P(("group", "dp"), None),
        P(("group", "dp"), None, None),
        P(("group", "dp"), None, None),
        P(("group", "dp")),
        P(("group", "dp"), None),
        P(),
        P(),
        P(None, "dp"),
        P(None, "dp"),
        P("dp", None),
        P("group", None),
    )
    return jax.shard_map(
        body,
        mesh=mesh,
        in_specs=placed,
        out_specs=(P(("group", "dp"), None), P(("group", "dp"), None)),
        check_vma=False,
    )
```

```python
import functools

import jax
import jax.numpy as jnp
from jax import lax
from jax.experimental import pallas as pl
from jax.experimental.pallas import tpu as pltpu
from jax.sharding import PartitionSpec as P

HEADS = 32
KV_HEADS = 8
HEAD_DIM = 128
EXPERTS = 4
MIB = 1 << 20
HINTS = 4
MOST = 6
F32 = jnp.float32
BF16 = jnp.bfloat16
VMEM = pl.BlockSpec(memory_space=pltpu.VMEM)
ANY = pl.BlockSpec(memory_space=pl.ANY)


def dot(a, b, contract_last=False):
    dims = (((1,), (1 if contract_last else 0,)), ((), ()))
    return lax.dot_general(a, b, dims, preferred_element_type=F32)


def one_hot(mask):
    return mask.astype(F32).astype(BF16)


def grid(shape):
    return [lax.broadcasted_iota(jnp.int32, shape, axis) for axis in (0, 1)]


def pack(picks, block):
    quarter = block.shape[1] // 4
    parts = [block[:, m * quarter : (m + 1) * quarter] for m in range(4)]
    return [dot(picks[0], parts[m]) + dot(picks[1 + m], parts[3]) for m in range(3)]


def unpack(picks, block):
    quarter = block.shape[1] // 3
    parts = [block[:, m * quarter : (m + 1) * quarter] for m in range(3)]
    tail = dot(picks[1], parts[0]) + dot(picks[2], parts[1]) + dot(picks[3], parts[2])
    return [dot(picks[0], part) for part in parts] + [tail]


def attend_kernel(plane, *refs):
    refs = refs[:10] + refs[10 + HINTS :]
    sources, attended, packed, (share, take), held, semaphores = (
        refs[:10], refs[10], refs[11:15], refs[15:17], refs[17:27], refs[27]
    )
    copies = [
        pltpu.make_async_copy(source, target, semaphores.at[i])
        for i, (source, target) in enumerate(zip(sources, held))
    ]
    for copy in copies[9:] + copies[:9]:
        copy.start()
    (queries, cache_keys, new_keys, lengths, cache_values, new_values, residual, gain, router,
     routes) = held
    rows, width = queries.shape
    positions = cache_keys.shape[1]
    groups = HEADS // KV_HEADS
    scale = 1.0 / HEAD_DIM**0.5
    every = rows * positions
    block = groups * rows

    copies[9].wait()
    index = lax.axis_index("dp")
    base = index * rows
    own = index // plane
    sub, lane = grid((2 * rows, 128))
    expert_down = jnp.zeros((2 * rows, 128), jnp.int32)
    slot_down = jnp.zeros((2 * rows, 128), jnp.int32)
    across = lax.broadcasted_iota(jnp.int32, (8, 128), 1)
    expert_across = jnp.zeros((8, 128), jnp.int32)
    slot_across = jnp.zeros((8, 128), jnp.int32)
    counts = [jnp.int32(0)] * EXPERTS
    for r in range(rows):
        names = [routes[c, base + r] ^ own for c in range(2)]
        for choice, name in ((r, names[0]), (rows + r, names[1])):
            slot = jnp.int32(0)
            for e in range(EXPERTS):
                slot = jnp.where(name == e, counts[e], slot)
            expert_down = jnp.where(sub == choice, name, expert_down)
            slot_down = jnp.where(sub == choice, slot, slot_down)
            expert_across = jnp.where(across == choice, name, expert_across)
            slot_across = jnp.where(across == choice, slot, slot_across)
        for e in range(EXPERTS):
            named = (names[0] == e) | (names[1] == e)
            counts[e] = counts[e] + jnp.where(named, 1, 0)

    late = jnp.where(slot_down >= 3, 1, 0)
    take[0] = one_hot(lane == expert_down * 8 + slot_down)
    for m in range(3):
        take[1 + m] = one_hot((lane == expert_down * 8 + 6 + late) & (slot_down - 3 * late == m))
    place, choice = grid((8 * EXPERTS, 128))
    expert, slot = expert_across[0:1], slot_across[0:1]
    late = jnp.where(slot >= 3, 1, 0)
    chosen = choice < 2 * rows
    picks = [one_hot((place == expert * 8 + slot) & chosen)]
    for m in range(3):
        picks.append(one_hot((place == expert * 8 + 6 + late) & (slot - 3 * late == m) & chosen))
    for copy in copies[:4]:
        copy.wait()

    query = queries[...].astype(F32)
    stacked = jnp.concatenate(
        [query[:, h * HEAD_DIM : (h + 1) * HEAD_DIM] for h in range(HEADS)], axis=0
    )
    stacked_b = stacked.astype(BF16)
    keys = cache_keys[...].reshape(every, KV_HEADS * HEAD_DIM)
    newk = new_keys[...].astype(F32)

    row_of = lax.broadcasted_iota(jnp.int32, (block, every), 0) % rows
    column = lax.broadcasted_iota(jnp.int32, (block, every), 1)
    position = column % positions
    column_row = column // positions
    limit = jnp.zeros((block, every), jnp.int32)
    for r in range(rows):
        limit = jnp.where(column_row == r, lengths[r], limit)
    valid = (row_of == column_row) & (position < limit)

    heads = range(KV_HEADS)
    lanes = [slice(g * HEAD_DIM, (g + 1) * HEAD_DIM) for g in heads]
    mine = [slice(g * block, (g + 1) * block) for g in heads]
    scores = [dot(stacked_b[mine[g]], keys[:, lanes[g]], contract_last=True) for g in heads]
    scores = [jnp.where(valid, score * scale, -jnp.inf) for score in scores]
    own_keys = [jnp.concatenate([newk[:, lanes[g]]] * groups, axis=0) for g in heads]
    new_scores = [
        jnp.sum(stacked[mine[g]] * own_keys[g], axis=1, keepdims=True) * scale for g in heads
    ]
    peaks = [
        jnp.maximum(jnp.max(score, axis=1, keepdims=True), new)
        for score, new in zip(scores, new_scores)
    ]
    weights = [jnp.exp(score - peak) for score, peak in zip(scores, peaks)]
    new_weights = [jnp.exp(new - peak) for new, peak in zip(new_scores, peaks)]
    totals = [
        jnp.sum(weight, axis=1, keepdims=True) + new
        for weight, new in zip(weights, new_weights)
    ]
    inverses = [1.0 / total for total in totals]
    probs = [(weight * inverse).astype(BF16) for weight, inverse in zip(weights, inverses)]
    new_probs = [
        (new * inverse).astype(BF16).astype(F32) for new, inverse in zip(new_weights, inverses)
    ]
    for copy in copies[4:9]:
        copy.wait()
    values = cache_values[...].reshape(every, KV_HEADS * HEAD_DIM)
    newv = new_values[...].astype(F32)
    mixed = [
        dot(probs[g], values[:, lanes[g]])
        + new_probs[g] * jnp.concatenate([newv[:, lanes[g]]] * groups, axis=0)
        for g in heads
    ]
    pieces = [value[j * rows : (j + 1) * rows] for value in mixed for j in range(groups)]

    states = (residual[...].astype(F32) + jnp.concatenate(pieces, axis=1)).astype(BF16)
    attended[...] = states
    states = states.astype(F32)
    norm = lax.rsqrt(jnp.mean(states * states, axis=1, keepdims=True) + 1e-05)
    gains = gain[...].astype(F32)
    logits = [jnp.zeros((rows, 128), F32) for _ in range(EXPERTS)]
    parts = []
    for c in range(width // 128):
        lanes = slice(c * 128, (c + 1) * 128)
        part = (states[:, lanes] * norm * gains[c : c + 1]).astype(BF16).astype(F32)
        parts.append(part)
        for e in range(EXPERTS):
            logits[e] += part * router[e : e + 1, lanes].astype(F32)
    logits = [jnp.sum(value, axis=1, keepdims=True) for value in logits]

    normed = jnp.concatenate(parts, axis=1)
    normed = jnp.concatenate([normed, normed], axis=0).astype(BF16)
    quarter = width // 4
    for m, value in enumerate(pack([pick[:, : 2 * rows] for pick in picks], normed)):
        for k, target in enumerate(packed):
            target[:, m * quarter : (m + 1) * quarter] = value[8 * k : 8 * k + 8].astype(BF16)

    chosen_logits = jnp.zeros((2 * rows, 1), F32)
    for e in range(EXPERTS):
        both = jnp.concatenate([logits[e], logits[e]], axis=0)
        chosen_logits = jnp.where(expert_down[:, :1] == (own ^ e), both, chosen_logits)
    other = jnp.concatenate([chosen_logits[rows:], chosen_logits[:rows]], axis=0)
    share[...] = jnp.broadcast_to(1.0 / (1.0 + jnp.exp(other - chosen_logits)), share.shape)


def attend(plane, queries, new_keys, new_values, cache_keys, cache_values, lengths, residual,
           norm_gain, router_weight, routes, weight):
    rows, width = queries.shape
    operands = (
        queries,
        cache_keys,
        new_keys,
        lengths,
        cache_values,
        new_values,
        residual,
        norm_gain.reshape(-1, 128),
        router_weight.T,
        routes.T,
    )
    in_smem = (3, 9)
    return pl.pallas_call(
        functools.partial(attend_kernel, plane),
        out_shape=(
            jax.ShapeDtypeStruct((rows, width), BF16),
            *[jax.ShapeDtypeStruct((8, width * 3 // 4), BF16)] * EXPERTS,
            jax.ShapeDtypeStruct((2 * rows, 128), F32),
            jax.ShapeDtypeStruct((4, 2 * rows, 128), BF16),
        ),
        in_specs=[ANY] * (len(operands) + HINTS),
        out_specs=(VMEM,) * (3 + EXPERTS),
        scratch_shapes=[
            (pltpu.SMEM if i in in_smem else pltpu.VMEM)(operand.shape, operand.dtype)
            for i, operand in enumerate(operands)
        ]
        + [pltpu.SemaphoreType.DMA((len(operands),))],
        compiler_params=pltpu.CompilerParams(vmem_limit_bytes=5 * MIB),
        name="attend",
    )(*[pltpu.with_memory_space_constraint(x, pltpu.HBM) for x in operands + (weight,) * HINTS])


def hidden_kernel(gate_weight, up_weight, down_weight, *refs):
    waves, hidden = refs[:-1], refs[-1]
    columns = gate_weight.shape[1]
    step = 512
    quarter = waves[0].shape[1] // 3
    blocks = jnp.concatenate([wave[...] for wave in waves], axis=0)
    size = 128
    row, lane = grid((size, size))
    slot = row & 7
    late = jnp.where(slot >= 3, 1, 0)
    picks = [
        one_hot((lane == row - slot + 6 + late) & (slot - 3 * late == m)) for m in range(3)
    ]
    picks = jnp.concatenate(picks, axis=1)
    tails = []
    for first in range(0, blocks.shape[0], size):
        some = blocks[first : first + size]
        parts = [some[:, m * quarter : (m + 1) * quarter] for m in range(3)]
        tails.append(dot(picks, jnp.concatenate(parts, axis=0)).astype(BF16))
    x = jnp.concatenate([blocks, jnp.concatenate(tails, axis=0)], axis=1)
    for f in range(0, columns, step):
        last = min(f + step, columns)
        gate = dot(x, gate_weight[:, f:last])
        upper = dot(x, up_weight[:, f:last])
        hidden[:, f:last] = (gate / (1.0 + jnp.exp(-gate)) * upper).astype(BF16)


def hidden_rows(waves, gate_weight, up_weight, down_weight):
    rows = sum(wave.shape[0] for wave in waves)
    width, columns = gate_weight.shape
    return pl.pallas_call(
        hidden_kernel,
        out_shape=jax.ShapeDtypeStruct((rows, columns), BF16),
        in_specs=[VMEM] * (3 + len(waves)),
        out_specs=VMEM,
        compiler_params=pltpu.CompilerParams(vmem_limit_bytes=4 * MIB * max(1, rows // 128)),
        cost_estimate=pl.CostEstimate(
            flops=4 * rows * width * columns, bytes_accessed=0, transcendentals=rows * columns
        ),
        name="hidden",
    )(gate_weight, up_weight, down_weight, *waves)


def down_kernel(hidden, weight, *outs):
    rows = hidden.shape[0]
    quarter = outs[0].shape[1] // 3
    size = 128
    row, lane = grid((size, size))
    slot = row & 7
    picks = [one_hot((lane == row - slot + 3 * (slot - 6) + m) & (slot >= MOST)) for m in range(3)]
    picks = jnp.concatenate(picks, axis=0)
    h = hidden[...]

    def terms(first, count):
        return dot(h, weight[:, first : first + count])

    step = min(1024, quarter)
    is_row = (lax.broadcasted_iota(jnp.int32, (rows, step), 0) & 7) < MOST
    for n in range(0, quarter, step):
        tail = terms(3 * quarter + n, step).astype(BF16)
        tails = [dot(picks, tail[i : i + size]) for i in range(0, rows, size)]
        for m in range(3):
            moved = jnp.concatenate([x[m * size : (m + 1) * size] for x in tails], axis=0)
            value = jnp.where(is_row, terms(m * quarter + n, step), moved)
            lanes = slice(m * quarter + n, m * quarter + n + step)
            for out, blocks in zip(outs, ways_back(rows // 32)):
                chosen = [value[8 * b : 8 * b + 8] for b in blocks]
                out[:, lanes] = jnp.concatenate(chosen, axis=0).astype(BF16)


def ways_back(places):
    halves = []
    for w in (0, 1):
        groups = [
            2 * places * w + 2 * p + j
            for high in range(0, places, 2)
            for j in (0, 1)
            for p in (high, high + 1)
        ]
        halves += [groups[:places], groups[places:]]
    return halves


def down_rows(hidden, weight):
    rows, columns = hidden.shape
    width = weight.shape[1]
    sizes = [8 * len(blocks) for blocks in ways_back(rows // 32)]
    outs = pl.pallas_call(
        down_kernel,
        out_shape=[jax.ShapeDtypeStruct((size, width // 4 * 3), BF16) for size in sizes],
        in_specs=[VMEM] * 2,
        out_specs=[VMEM] * len(sizes),
        compiler_params=pltpu.CompilerParams(vmem_limit_bytes=4 * MIB * max(1, rows // 128)),
        cost_estimate=pl.CostEstimate(
            flops=2 * rows * width * columns, bytes_accessed=0, transcendentals=0
        ),
        name="down",
    )(hidden, weight)
    return outs[0:2], outs[2:4]


def join_kernel(backwards, *refs):
    pieces = refs[1:-1][::-1] if backwards else refs[1:-1]
    rows = [piece[...].astype(F32) for piece in pieces]
    refs[-1][...] = jnp.concatenate(rows, axis=0).astype(BF16)


def join(after, *pieces, backwards=False):
    rows = sum(piece.shape[0] for piece in pieces)
    return pl.pallas_call(
        functools.partial(join_kernel, backwards),
        out_shape=jax.ShapeDtypeStruct((rows, pieces[0].shape[1]), BF16),
        in_specs=[ANY] + [VMEM] * len(pieces),
        out_specs=VMEM,
        compiler_params=pltpu.CompilerParams(vmem_limit_bytes=1 * MIB),
        cost_estimate=pl.CostEstimate(flops=0, bytes_accessed=0, transcendentals=0),
        name="join",
    )(after, *pieces)


def fold_kernel(held, arrived, after, *outs):
    each = outs[0].shape[0]
    total = held[...].astype(F32) + arrived[...].astype(F32)
    for k, out in enumerate(outs):
        out[...] = total[k * each : (k + 1) * each].astype(BF16)


def fold(held, arrived, after, parts):
    rows, width = held.shape
    return pl.pallas_call(
        fold_kernel,
        out_shape=[jax.ShapeDtypeStruct((rows // parts, width), BF16)] * parts,
        in_specs=[VMEM] * 2 + [ANY],
        out_specs=[VMEM] * parts,
        compiler_params=pltpu.CompilerParams(vmem_limit_bytes=MIB * max(1, rows // 64)),
        cost_estimate=pl.CostEstimate(flops=0, bytes_accessed=0, transcendentals=0),
        name="fold",
    )(held, arrived, after)


def combined(first, share, take, results):
    picks = [take[i][:, 8 * first : 8 * first + 16] for i in range(4)]
    rows = share.shape[0] // 2
    block = jnp.concatenate([x[...].astype(F32) for x in results], axis=0).astype(BF16)
    values = [value * share[:, :1] for value in unpack(picks, block)]
    return [value[:rows] + value[rows:] for value in values]


def combine_far_kernel(share, take, two, three, total):
    quarter = two.shape[1] // 3
    for m, value in enumerate(combined(2, share, take, (two, three))):
        total[:, m * quarter : (m + 1) * quarter] = value


def combine_kernel(share, take, zero, one, total, out):
    quarter = zero.shape[1] // 3
    for m, value in enumerate(combined(0, share, take, (zero, one))):
        lanes = slice(m * quarter, (m + 1) * quarter)
        out[:, lanes] = (value + total[:, lanes]).astype(BF16)


def combine(share, take, results):
    rows, width = share.shape[0] // 2, results[0].shape[1] // 3 * 4
    params = pltpu.CompilerParams(vmem_limit_bytes=2 * MIB)
    cost = pl.CostEstimate(flops=0, bytes_accessed=16 * MIB, transcendentals=0)
    total = pl.pallas_call(
        combine_far_kernel,
        out_shape=jax.ShapeDtypeStruct((rows, width), F32),
        in_specs=[VMEM] * 4,
        out_specs=VMEM,
        compiler_params=params,
        cost_estimate=cost,
        name="combine_far",
    )(share, take, *results[2:])
    return pl.pallas_call(
        combine_kernel,
        out_shape=jax.ShapeDtypeStruct((rows, width), BF16),
        in_specs=[VMEM] * 5,
        out_specs=VMEM,
        compiler_params=params,
        cost_estimate=cost,
        name="combine",
    )(share, take, *results[:2], total)


def swap(value, count, bit):
    return lax.ppermute(value, "dp", [(i, i ^ bit) for i in range(count)])


def body(
    queries,
    new_keys,
    new_values,
    cache_keys,
    cache_values,
    lengths,
    residual,
    norm_gain,
    router_weight,
    gate_weight,
    up_weight,
    down_weight,
    routes,
):
    count = lax.axis_size("dp")
    plane = count // EXPERTS
    bits = [1 << k for k in reversed(range(plane.bit_length() - 1))]
    attended, *packed, share, take = attend(
        plane, queries, new_keys, new_values, cache_keys, cache_values, lengths, residual, norm_gain,
        router_weight, routes, down_weight,
    )

    for k in (1, 3, 2):
        packed[k] = swap(packed[k], count, k * plane)
    waves = [join(share, *packed[:2]), join(share, packed[3], packed[2], backwards=True)]
    for bit in bits[:-1]:
        waves = [join(share, wave, swap(wave, count, bit)) for wave in waves]
    waves = [piece for wave in waves for piece in (wave, swap(wave, count, bits[-1]))]

    hidden = hidden_rows(waves, gate_weight, up_weight, down_weight)

    near, far = down_rows(hidden, down_weight)

    def back(wave, stage, after, parts=2):
        return fold(wave[0], swap(wave[1], count, bits[-1 - stage]), after, parts)

    last = len(bits) - 1
    token = share
    for stage in range(last):
        parts = 4 if stage == last - 1 else 2
        far = back(far, stage, token, parts)
        near = back(near, stage, far[0], parts)
        token = near[0]
    two = back(far[0:2], last, token, 1)
    three = back(far[2:4], last, two[0], 1)
    one = back(near[2:4], last, three[0], 1)
    zero = back(near[0:2], last, one[0], 1)
    results = [
        zero[0],
        swap(one[0], count, plane),
        swap(two[0], count, 2 * plane),
        swap(three[0], count, 3 * plane),
    ]
    return (attended, combine(share, take, results))


def solution(mesh):
    placed = (
        P(("group", "dp"), None),
        P(("group", "dp"), None),
        P(("group", "dp"), None),
        P(("group", "dp"), None, None),
        P(("group", "dp"), None, None),
        P(("group", "dp")),
        P(("group", "dp"), None),
        P(),
        P(),
        P(None, "dp"),
        P(None, "dp"),
        P("dp", None),
        P("group", None),
    )
    return jax.shard_map(
        body,
        mesh=mesh,
        in_specs=placed,
        out_specs=(P(("group", "dp"), None), P(("group", "dp"), None)),
        check_vma=False,
    )
```

```python
import functools

import jax
import jax.numpy as jnp
from jax import lax
from jax.experimental import pallas as pl
from jax.experimental.pallas import tpu as pltpu
from jax.sharding import PartitionSpec as P

HEADS = 32
KV_HEADS = 8
HEAD_DIM = 128
EXPERTS = 4
MIB = 1 << 20
HINTS = 4
MOST = 6
F32 = jnp.float32
BF16 = jnp.bfloat16
VMEM = pl.BlockSpec(memory_space=pltpu.VMEM)
ANY = pl.BlockSpec(memory_space=pl.ANY)


def dot(a, b, contract_last=False):
    dims = (((1,), (1 if contract_last else 0,)), ((), ()))
    return lax.dot_general(a, b, dims, preferred_element_type=F32)


def one_hot(mask):
    return mask.astype(F32).astype(BF16)


def grid(shape):
    return [lax.broadcasted_iota(jnp.int32, shape, axis) for axis in (0, 1)]


def pack(picks, block):
    quarter = block.shape[1] // 4
    parts = [block[:, m * quarter : (m + 1) * quarter] for m in range(4)]
    return [dot(picks[0], parts[m]) + dot(picks[1 + m], parts[3]) for m in range(3)]


def unpack(picks, block):
    quarter = block.shape[1] // 3
    parts = [block[:, m * quarter : (m + 1) * quarter] for m in range(3)]
    tail = dot(picks[1], parts[0]) + dot(picks[2], parts[1]) + dot(picks[3], parts[2])
    return [dot(picks[0], part) for part in parts] + [tail]


def attend_kernel(plane, *refs):
    refs = refs[:10] + refs[10 + HINTS :]
    sources, attended, packed, (share, take), held, semaphores = (
        refs[:10], refs[10], refs[11:15], refs[15:17], refs[17:27], refs[27]
    )
    copies = [
        pltpu.make_async_copy(source, target, semaphores.at[i])
        for i, (source, target) in enumerate(zip(sources, held))
    ]
    for copy in copies[9:] + copies[:9]:
        copy.start()
    (queries, cache_keys, new_keys, lengths, cache_values, new_values, residual, gain, router,
     routes) = held
    rows, width = queries.shape
    positions = cache_keys.shape[1]
    groups = HEADS // KV_HEADS
    scale = 1.0 / HEAD_DIM**0.5
    every = rows * positions
    block = groups * rows

    copies[9].wait()
    index = lax.axis_index("dp")
    base = index * rows
    own = index // plane
    sub, lane = grid((2 * rows, 128))
    expert_down = jnp.zeros((2 * rows, 128), jnp.int32)
    slot_down = jnp.zeros((2 * rows, 128), jnp.int32)
    across = lax.broadcasted_iota(jnp.int32, (8, 128), 1)
    expert_across = jnp.zeros((8, 128), jnp.int32)
    slot_across = jnp.zeros((8, 128), jnp.int32)
    counts = [jnp.int32(0)] * EXPERTS
    for r in range(rows):
        names = [routes[c, base + r] ^ own for c in range(2)]
        for choice, name in ((r, names[0]), (rows + r, names[1])):
            slot = jnp.int32(0)
            for e in range(EXPERTS):
                slot = jnp.where(name == e, counts[e], slot)
            expert_down = jnp.where(sub == choice, name, expert_down)
            slot_down = jnp.where(sub == choice, slot, slot_down)
            expert_across = jnp.where(across == choice, name, expert_across)
            slot_across = jnp.where(across == choice, slot, slot_across)
        for e in range(EXPERTS):
            named = (names[0] == e) | (names[1] == e)
            counts[e] = counts[e] + jnp.where(named, 1, 0)

    late = jnp.where(slot_down >= 3, 1, 0)
    take[0] = one_hot(lane == expert_down * 8 + slot_down)
    for m in range(3):
        take[1 + m] = one_hot((lane == expert_down * 8 + 6 + late) & (slot_down - 3 * late == m))
    place, choice = grid((8 * EXPERTS, 128))
    expert, slot = expert_across[0:1], slot_across[0:1]
    late = jnp.where(slot >= 3, 1, 0)
    chosen = choice < 2 * rows
    picks = [one_hot((place == expert * 8 + slot) & chosen)]
    for m in range(3):
        picks.append(one_hot((place == expert * 8 + 6 + late) & (slot - 3 * late == m) & chosen))
    for copy in copies[:4]:
        copy.wait()

    query = queries[...].astype(F32)
    stacked = jnp.concatenate(
        [query[:, h * HEAD_DIM : (h + 1) * HEAD_DIM] for h in range(HEADS)], axis=0
    )
    stacked_b = stacked.astype(BF16)
    keys = cache_keys[...].reshape(every, KV_HEADS * HEAD_DIM)
    newk = new_keys[...].astype(F32)

    row_of = lax.broadcasted_iota(jnp.int32, (block, every), 0) % rows
    column = lax.broadcasted_iota(jnp.int32, (block, every), 1)
    position = column % positions
    column_row = column // positions
    limit = jnp.zeros((block, every), jnp.int32)
    for r in range(rows):
        limit = jnp.where(column_row == r, lengths[r], limit)
    valid = (row_of == column_row) & (position < limit)

    heads = range(KV_HEADS)
    lanes = [slice(g * HEAD_DIM, (g + 1) * HEAD_DIM) for g in heads]
    mine = [slice(g * block, (g + 1) * block) for g in heads]
    scores = [dot(stacked_b[mine[g]], keys[:, lanes[g]], contract_last=True) for g in heads]
    scores = [jnp.where(valid, score * scale, -jnp.inf) for score in scores]
    own_keys = [jnp.concatenate([newk[:, lanes[g]]] * groups, axis=0) for g in heads]
    new_scores = [
        jnp.sum(stacked[mine[g]] * own_keys[g], axis=1, keepdims=True) * scale for g in heads
    ]
    peaks = [
        jnp.maximum(jnp.max(score, axis=1, keepdims=True), new)
        for score, new in zip(scores, new_scores)
    ]
    weights = [jnp.exp(score - peak) for score, peak in zip(scores, peaks)]
    new_weights = [jnp.exp(new - peak) for new, peak in zip(new_scores, peaks)]
    totals = [
        jnp.sum(weight, axis=1, keepdims=True) + new
        for weight, new in zip(weights, new_weights)
    ]
    inverses = [1.0 / total for total in totals]
    probs = [(weight * inverse).astype(BF16) for weight, inverse in zip(weights, inverses)]
    new_probs = [
        (new * inverse).astype(BF16).astype(F32) for new, inverse in zip(new_weights, inverses)
    ]
    for copy in copies[4:9]:
        copy.wait()
    values = cache_values[...].reshape(every, KV_HEADS * HEAD_DIM)
    newv = new_values[...].astype(F32)
    mixed = [
        dot(probs[g], values[:, lanes[g]])
        + new_probs[g] * jnp.concatenate([newv[:, lanes[g]]] * groups, axis=0)
        for g in heads
    ]
    pieces = [value[j * rows : (j + 1) * rows] for value in mixed for j in range(groups)]

    states = (residual[...].astype(F32) + jnp.concatenate(pieces, axis=1)).astype(BF16)
    attended[...] = states
    states = states.astype(F32)
    norm = lax.rsqrt(jnp.mean(states * states, axis=1, keepdims=True) + 1e-05)
    gains = gain[...].astype(F32)
    logits = [jnp.zeros((rows, 128), F32) for _ in range(EXPERTS)]
    parts = []
    for c in range(width // 128):
        lanes = slice(c * 128, (c + 1) * 128)
        part = (states[:, lanes] * norm * gains[c : c + 1]).astype(BF16).astype(F32)
        parts.append(part)
        for e in range(EXPERTS):
            logits[e] += part * router[e : e + 1, lanes].astype(F32)
    logits = [jnp.sum(value, axis=1, keepdims=True) for value in logits]

    normed = jnp.concatenate(parts, axis=1)
    normed = jnp.concatenate([normed, normed], axis=0).astype(BF16)
    quarter = width // 4
    for m, value in enumerate(pack([pick[:, : 2 * rows] for pick in picks], normed)):
        for k, target in enumerate(packed):
            target[:, m * quarter : (m + 1) * quarter] = value[8 * k : 8 * k + 8].astype(BF16)

    chosen_logits = jnp.zeros((2 * rows, 1), F32)
    for e in range(EXPERTS):
        both = jnp.concatenate([logits[e], logits[e]], axis=0)
        chosen_logits = jnp.where(expert_down[:, :1] == (own ^ e), both, chosen_logits)
    other = jnp.concatenate([chosen_logits[rows:], chosen_logits[:rows]], axis=0)
    share[...] = jnp.broadcast_to(1.0 / (1.0 + jnp.exp(other - chosen_logits)), share.shape)


def attend(plane, queries, new_keys, new_values, cache_keys, cache_values, lengths, residual,
           norm_gain, router_weight, routes, weight):
    rows, width = queries.shape
    operands = (
        queries,
        cache_keys,
        new_keys,
        lengths,
        cache_values,
        new_values,
        residual,
        norm_gain.reshape(-1, 128),
        router_weight.T,
        routes.T,
    )
    in_smem = (3, 9)
    return pl.pallas_call(
        functools.partial(attend_kernel, plane),
        out_shape=(
            jax.ShapeDtypeStruct((rows, width), BF16),
            *[jax.ShapeDtypeStruct((8, width * 3 // 4), BF16)] * EXPERTS,
            jax.ShapeDtypeStruct((2 * rows, 128), F32),
            jax.ShapeDtypeStruct((4, 2 * rows, 128), BF16),
        ),
        in_specs=[ANY] * (len(operands) + HINTS),
        out_specs=(VMEM,) * (3 + EXPERTS),
        scratch_shapes=[
            (pltpu.SMEM if i in in_smem else pltpu.VMEM)(operand.shape, operand.dtype)
            for i, operand in enumerate(operands)
        ]
        + [pltpu.SemaphoreType.DMA((len(operands),))],
        compiler_params=pltpu.CompilerParams(vmem_limit_bytes=5 * MIB),
        name="attend",
    )(*[pltpu.with_memory_space_constraint(x, pltpu.HBM) for x in operands + (weight,) * HINTS])


def hidden_kernel(gate_weight, up_weight, down_weight, *refs):
    waves, hidden = refs[:-1], refs[-1]
    columns = gate_weight.shape[1]
    step = 896
    quarter = waves[0].shape[1] // 3
    blocks = jnp.concatenate([wave[...] for wave in waves], axis=0)
    size = 128
    row, lane = grid((size, size))
    slot = row & 7
    late = jnp.where(slot >= 3, 1, 0)
    picks = [
        one_hot((lane == row - slot + 6 + late) & (slot - 3 * late == m)) for m in range(3)
    ]
    picks = jnp.concatenate(picks, axis=1)
    tails = []
    for first in range(0, blocks.shape[0], size):
        some = blocks[first : first + size]
        parts = [some[:, m * quarter : (m + 1) * quarter] for m in range(3)]
        tails.append(dot(picks, jnp.concatenate(parts, axis=0)).astype(BF16))
    x = jnp.concatenate([blocks, jnp.concatenate(tails, axis=0)], axis=1)
    for f in range(0, columns, step):
        last = min(f + step, columns)
        gate = dot(x, gate_weight[:, f:last])
        upper = dot(x, up_weight[:, f:last])
        hidden[:, f:last] = (gate / (1.0 + jnp.exp(-gate)) * upper).astype(BF16)


def hidden_rows(waves, gate_weight, up_weight, down_weight):
    rows = sum(wave.shape[0] for wave in waves)
    width, columns = gate_weight.shape
    return pl.pallas_call(
        hidden_kernel,
        out_shape=jax.ShapeDtypeStruct((rows, columns), BF16),
        in_specs=[VMEM] * (3 + len(waves)),
        out_specs=VMEM,
        compiler_params=pltpu.CompilerParams(vmem_limit_bytes=4 * MIB * max(1, rows // 128)),
        cost_estimate=pl.CostEstimate(
            flops=4 * rows * width * columns, bytes_accessed=0, transcendentals=rows * columns
        ),
        name="hidden",
    )(gate_weight, up_weight, down_weight, *waves)


def down_kernel(hidden, weight, *outs):
    rows = hidden.shape[0]
    quarter = outs[0].shape[1] // 3
    size = 128
    row, lane = grid((size, size))
    slot = row & 7
    picks = [one_hot((lane == row - slot + 3 * (slot - 6) + m) & (slot >= MOST)) for m in range(3)]
    picks = jnp.concatenate(picks, axis=0)
    h = hidden[...]

    def terms(first, count):
        return dot(h, weight[:, first : first + count])

    step = min(1024, quarter)
    is_row = (lax.broadcasted_iota(jnp.int32, (rows, step), 0) & 7) < MOST
    for n in range(0, quarter, step):
        tail = terms(3 * quarter + n, step).astype(BF16)
        tails = [dot(picks, tail[i : i + size]) for i in range(0, rows, size)]
        for m in range(3):
            moved = jnp.concatenate([x[m * size : (m + 1) * size] for x in tails], axis=0)
            value = jnp.where(is_row, terms(m * quarter + n, step), moved)
            lanes = slice(m * quarter + n, m * quarter + n + step)
            for out, blocks in zip(outs, ways_back(rows // 32)):
                chosen = [value[8 * b : 8 * b + 8] for b in blocks]
                out[:, lanes] = jnp.concatenate(chosen, axis=0).astype(BF16)


def ways_back(places):
    halves = []
    for w in (0, 1):
        groups = [
            2 * places * w + 2 * p + j
            for high in range(0, places, 2)
            for j in (0, 1)
            for p in (high, high + 1)
        ]
        halves += [groups[:places], groups[places:]]
    return halves


def down_rows(hidden, weight):
    rows, columns = hidden.shape
    width = weight.shape[1]
    sizes = [8 * len(blocks) for blocks in ways_back(rows // 32)]
    outs = pl.pallas_call(
        down_kernel,
        out_shape=[jax.ShapeDtypeStruct((size, width // 4 * 3), BF16) for size in sizes],
        in_specs=[VMEM] * 2,
        out_specs=[VMEM] * len(sizes),
        compiler_params=pltpu.CompilerParams(vmem_limit_bytes=4 * MIB * max(1, rows // 128)),
        cost_estimate=pl.CostEstimate(
            flops=2 * rows * width * columns, bytes_accessed=0, transcendentals=0
        ),
        name="down",
    )(hidden, weight)
    return outs[0:2], outs[2:4]


def join_kernel(backwards, *refs):
    pieces = refs[1:-1][::-1] if backwards else refs[1:-1]
    rows = [piece[...].astype(F32) for piece in pieces]
    refs[-1][...] = jnp.concatenate(rows, axis=0).astype(BF16)


def join(after, *pieces, backwards=False):
    rows = sum(piece.shape[0] for piece in pieces)
    return pl.pallas_call(
        functools.partial(join_kernel, backwards),
        out_shape=jax.ShapeDtypeStruct((rows, pieces[0].shape[1]), BF16),
        in_specs=[ANY] + [VMEM] * len(pieces),
        out_specs=VMEM,
        compiler_params=pltpu.CompilerParams(vmem_limit_bytes=1 * MIB),
        cost_estimate=pl.CostEstimate(flops=0, bytes_accessed=0, transcendentals=0),
        name="join",
    )(after, *pieces)


def fold_kernel(held, arrived, after, *outs):
    each = outs[0].shape[0]
    total = held[...].astype(F32) + arrived[...].astype(F32)
    for k, out in enumerate(outs):
        out[...] = total[k * each : (k + 1) * each].astype(BF16)


def fold(held, arrived, after, parts):
    rows, width = held.shape
    return pl.pallas_call(
        fold_kernel,
        out_shape=[jax.ShapeDtypeStruct((rows // parts, width), BF16)] * parts,
        in_specs=[VMEM] * 2 + [ANY],
        out_specs=[VMEM] * parts,
        compiler_params=pltpu.CompilerParams(vmem_limit_bytes=MIB * max(1, rows // 64)),
        cost_estimate=pl.CostEstimate(flops=0, bytes_accessed=0, transcendentals=0),
        name="fold",
    )(held, arrived, after)


def combined(first, share, take, results):
    picks = [take[i][:, 8 * first : 8 * first + 16] for i in range(4)]
    rows = share.shape[0] // 2
    block = jnp.concatenate([x[...].astype(F32) for x in results], axis=0).astype(BF16)
    values = [value * share[:, :1] for value in unpack(picks, block)]
    return [value[:rows] + value[rows:] for value in values]


def combine_far_kernel(share, take, two, three, total):
    quarter = two.shape[1] // 3
    for m, value in enumerate(combined(2, share, take, (two, three))):
        total[:, m * quarter : (m + 1) * quarter] = value


def combine_kernel(share, take, zero, one, total, out):
    quarter = zero.shape[1] // 3
    for m, value in enumerate(combined(0, share, take, (zero, one))):
        lanes = slice(m * quarter, (m + 1) * quarter)
        out[:, lanes] = (value + total[:, lanes]).astype(BF16)


def combine(share, take, results):
    rows, width = share.shape[0] // 2, results[0].shape[1] // 3 * 4
    params = pltpu.CompilerParams(vmem_limit_bytes=2 * MIB)
    cost = pl.CostEstimate(flops=0, bytes_accessed=16 * MIB, transcendentals=0)
    total = pl.pallas_call(
        combine_far_kernel,
        out_shape=jax.ShapeDtypeStruct((rows, width), F32),
        in_specs=[VMEM] * 4,
        out_specs=VMEM,
        compiler_params=params,
        cost_estimate=cost,
        name="combine_far",
    )(share, take, *results[2:])
    return pl.pallas_call(
        combine_kernel,
        out_shape=jax.ShapeDtypeStruct((rows, width), BF16),
        in_specs=[VMEM] * 5,
        out_specs=VMEM,
        compiler_params=params,
        cost_estimate=cost,
        name="combine",
    )(share, take, *results[:2], total)


def swap(value, count, bit):
    return lax.ppermute(value, "dp", [(i, i ^ bit) for i in range(count)])


def body(
    queries,
    new_keys,
    new_values,
    cache_keys,
    cache_values,
    lengths,
    residual,
    norm_gain,
    router_weight,
    gate_weight,
    up_weight,
    down_weight,
    routes,
):
    count = lax.axis_size("dp")
    plane = count // EXPERTS
    bits = [1 << k for k in reversed(range(plane.bit_length() - 1))]
    attended, *packed, share, take = attend(
        plane, queries, new_keys, new_values, cache_keys, cache_values, lengths, residual, norm_gain,
        router_weight, routes, down_weight,
    )

    for k in (1, 3, 2):
        packed[k] = swap(packed[k], count, k * plane)
    waves = [join(share, *packed[:2]), join(share, packed[3], packed[2], backwards=True)]
    for bit in bits[:-1]:
        waves = [join(share, wave, swap(wave, count, bit)) for wave in waves]
    waves = [piece for wave in waves for piece in (wave, swap(wave, count, bits[-1]))]

    hidden = hidden_rows(waves, gate_weight, up_weight, down_weight)

    near, far = down_rows(hidden, down_weight)

    def back(wave, stage, after, parts=2):
        return fold(wave[0], swap(wave[1], count, bits[-1 - stage]), after, parts)

    last = len(bits) - 1
    token = share
    for stage in range(last):
        parts = 4 if stage == last - 1 else 2
        far = back(far, stage, token, parts)
        near = back(near, stage, far[0], parts)
        token = near[0]
    two = back(far[0:2], last, token, 1)
    three = back(far[2:4], last, two[0], 1)
    one = back(near[2:4], last, three[0], 1)
    zero = back(near[0:2], last, one[0], 1)
    results = [
        zero[0],
        swap(one[0], count, plane),
        swap(two[0], count, 2 * plane),
        swap(three[0], count, 3 * plane),
    ]
    return (attended, combine(share, take, results))


def solution(mesh):
    placed = (
        P(("group", "dp"), None),
        P(("group", "dp"), None),
        P(("group", "dp"), None),
        P(("group", "dp"), None, None),
        P(("group", "dp"), None, None),
        P(("group", "dp")),
        P(("group", "dp"), None),
        P(),
        P(),
        P(None, "dp"),
        P(None, "dp"),
        P("dp", None),
        P("group", None),
    )
    return jax.shard_map(
        body,
        mesh=mesh,
        in_specs=placed,
        out_specs=(P(("group", "dp"), None), P(("group", "dp"), None)),
        check_vma=False,
    )
```
